32 devices in a mesh: member: 2 (over y), lat: 4 (over z), lev: 2 (over x), fld: 2 (over core).
Axes of the slice: x: 2, y: 2, z: 4, core: 2. Of those that a mesh axis runs over, the one named last changes fastest.
Arguments:
- tracer: bfloat16 [8, 800, 1600], P('member', 'lat', ('lev', 'fld')), parts along dimension 0, may hold values from -6 to 6
- wind_east: bfloat16 [8, 800, 1600], P('member', 'lat', ('lev', 'fld')), parts along dimension 0, may hold values from -3 to 3
- wind_north: bfloat16 [8, 800, 1600], P('member', 'lat', ('lev', 'fld')), parts along dimension 0, may hold values from -3 to 3
- keep_m: int32 [800], P('lat'), may hold values from 9 to 400, as said below
- slot_wave: int32 [400], replicated, may hold values from 0 to 399, each once
Outputs:
- spectral: float32 [8, 400, 2, 400], P(('member', 'lev', 'fld'), 'lat'), parts along dimension 0
The draws below stay inside these ranges and needn't reach their ends.
There are 2 independent parts, one for each index of `member`. The reference program is written for one: setup_inputs(seed, part) draws one part's arguments, and reference() takes and returns one part's arrays. A program takes and returns all parts, laid end to end along the dimension named above; an argument that names none is the same for every part. Nothing has to cross between parts.
Inputs may be any that keep to these rules, and one draw needn't show every extreme that they name: keep_m equals 400 at rows 399 and 400, and 9 at rows 0 and 799. Slot s of the output holds wavenumber slot_wave[s]; values of 400 or more mark empty slots.
All inputs are finite; a program needn't handle non-finite values.
Results may differ from the reference program's by a relative error of at most 0.0003.
Values may be sent and summed in bfloat16 or wider, within the bound.
No kernel may reach another device: no remote copies, remote signals or barrier semaphores. Data moves between devices by JAX's collectives and lax.ppermute only.
A program may use at most 64 MiB of HBM per device.

```python
import math
import jax
import jax.numpy as jnp
from jax import lax

M = 400
LEV = 4
NLAT = 800
NLON = 1600
MSLOT = 400


def draw_keep_m(key, part):
    row_index = jnp.arange(NLAT, dtype=jnp.int32)
    distance = jnp.minimum(row_index, NLAT - 1 - row_index)
    jitter = jax.random.randint(key, (NLAT,), 0, M // 8 + 1, dtype=jnp.int32)
    jitter = jnp.where(distance > 0, jitter, 0)
    return jnp.minimum(M, 9 + distance + jitter).astype(jnp.int32)


def shard_levels(rng, shape, pieces, low, top_value):
    factor_of, own = 1.0, jax.random.fold_in(rng, 6)
    for position, parts in pieces:
        steps = jnp.exp(jax.random.uniform(jax.random.fold_in(own, position), (parts,), jnp.float32, low / len(pieces), top_value / len(pieces)))
        factor_of = factor_of * jnp.repeat(steps, shape[position] // parts).reshape([-1 if axis == position else 1 for axis in range(len(shape))])
    return factor_of


def noise(key, shape, scale, reach, split=(), held_as=jnp.bfloat16):
    values = scale * jax.random.normal(key, shape, jnp.float32)
    if split:
        values = values * shard_levels(key, shape, split, -0.22, 0.18)
    return jnp.clip(values, -reach, reach).astype(held_as)


def setup_inputs(seed: int = 0, part: int = 0) -> dict:
    splits = jax.random.split(jax.random.key(seed), 6)
    part_keys = jax.random.split(jax.random.fold_in(splits[5], part), 6)
    return {
        "tracer": noise(part_keys[0], (LEV, NLAT, NLON), 1.0, 6.0, ((1, 4), (2, 4))),
        "wind_east": noise(part_keys[1], (LEV, NLAT, NLON), 0.5, 3.0, ((1, 4), (2, 4))),
        "wind_north": noise(part_keys[2], (LEV, NLAT, NLON), 0.5, 3.0, ((1, 4), (2, 4))),
        "keep_m": draw_keep_m(jax.random.fold_in(splits[5], 71), part),
        "slot_wave": jax.random.permutation(splits[4], MSLOT).astype(jnp.int32),
    }


precise = lax.Precision.HIGHEST
block_rows = 16

def fourier_table(wave_ids, lon_count):
    grid_index = jnp.arange(lon_count, dtype=jnp.int32)
    phase_index = wave_ids.astype(jnp.int32)[:, None] * grid_index[None, :] % lon_count
    angles = 2.0 * math.pi / lon_count * phase_index.astype(jnp.float32)
    factor = 1.0 / math.sqrt(lon_count)
    return jnp.stack([jnp.cos(angles), -jnp.sin(angles)], axis=1) * factor

def advect(padded, east_wind, north_wind, first_row, lat_total):
    rows_here = padded.shape[1] - 2
    row_ids = first_row - 1 + jnp.arange(rows_here + 2, dtype=jnp.int32)
    inside = ((row_ids >= 0) & (row_ids < lat_total)).astype(jnp.float32)
    field_rows = padded.astype(jnp.float32) * inside[None, :, None]
    centre = field_rows[:, 1:-1, 1:-1]
    east_diff = field_rows[:, 1:-1, 2:] - field_rows[:, 1:-1, :-2]
    north_diff = field_rows[:, 2:, 1:-1] - field_rows[:, :-2, 1:-1]
    return centre - 0.5 * east_wind.astype(jnp.float32) * east_diff - 0.5 * north_wind.astype(jnp.float32) * north_diff

def legendre_setup(wave_ids, trunc_count, lat_total, lat_used):
    degree = jnp.minimum(wave_ids, trunc_count - 1).astype(jnp.float32)
    counter = jnp.arange(1, trunc_count, dtype=jnp.float32)
    log_terms = jnp.log1p(0.5 / counter)
    log_norm = lax.optimization_barrier(jnp.sum(jnp.where(counter[None, :] <= degree[:, None], log_terms[None, :], 0.0), axis=1))
    colatitude = math.pi / lat_total * (jnp.arange(lat_used, dtype=jnp.float32) + 0.5)
    sine_rows = jnp.sin(colatitude)
    cosines = jnp.cos(colatitude)
    start_log = 0.5 * (log_norm[:, None] - math.log(2.0)) + degree[:, None] * jnp.log(sine_rows)[None, :]
    return (degree, cosines, start_log)

def legendre_rows(recurrence, degree, cosines, first_order):
    before, current, log_scale = recurrence
    rows_list = [current]
    for offset in range(1, block_rows + 1):
        order_value = (first_order + offset).astype(jnp.float32)
        total_degree = degree[:, None] + order_value
        growth = jnp.sqrt((4.0 * total_degree * total_degree - 1.0) / (total_degree * total_degree - degree[:, None] * degree[:, None]))
        lower_degree = total_degree - 1.0
        damping = jnp.sqrt((lower_degree * lower_degree - degree[:, None] * degree[:, None]) / jnp.maximum(4.0 * lower_degree * lower_degree - 1.0, 1.0))
        advanced = growth * (cosines[None, :] * current - damping * before)
        before, current = (current, advanced)
        if offset < block_rows:
            rows_list.append(current)
    biggest = jnp.maximum(jnp.abs(before), jnp.abs(current))
    table_rows = jnp.stack(rows_list, axis=1) * jnp.exp(log_scale)[:, None, :]
    return (table_rows, (before / biggest, current / biggest, log_scale + jnp.log(biggest)))

def legendre_sweep(legendre_basis, contract, level_count, trunc_count):
    degree, cosines, start_log = legendre_basis
    slot_count = degree.shape[0]
    lat_used = cosines.shape[0]
    before = jnp.zeros((slot_count, lat_used), jnp.float32)
    current = jnp.ones((slot_count, lat_used), jnp.float32)
    result_init = jnp.zeros((level_count, slot_count, 2, trunc_count), jnp.float32)

    def advance(block_index, loop_carry):
        recurrence, result_now = loop_carry
        first_order = block_index * block_rows
        table_rows, recurrence = legendre_rows(recurrence, degree, cosines, first_order)
        orders = (first_order + jnp.arange(block_rows, dtype=jnp.int32)).astype(jnp.float32)
        inside_triangle = (orders[None, :] < trunc_count - degree[:, None]).astype(jnp.float32)
        partial_value = contract(table_rows * inside_triangle[:, :, None])
        result_now = lax.dynamic_update_slice_in_dim(result_now, partial_value, first_order, 3)
        return (recurrence, result_now)
    finished = lax.fori_loop(0, trunc_count // block_rows, advance, ((before, current, start_log), result_init))
    return finished[1]

def reference(tracer, wind_east, wind_north, keep_m, slot_wave):
    fourier_matrix = fourier_table(slot_wave, NLON)

    def one_level(level_args):
        tracer_row, east_row, north_row = level_args
        padded = jnp.pad(tracer_row[None], ((0, 0), (1, 1), (1, 1)), mode='wrap')
        advected = advect(padded, east_row[None], north_row[None], 0, NLAT)[0]
        return jnp.einsum('sck,jk->scj', fourier_matrix, advected, precision=precise)
    fourier = lax.map(one_level, (tracer, wind_east, wind_north))
    kept_mask = (slot_wave[:, None] < keep_m[None, :]).astype(jnp.float32)
    fourier = fourier * kept_mask[None, :, None, :]
    spectral_in = jnp.transpose(fourier, (1, 2, 0, 3))
    sines_all = jnp.sin(math.pi / NLAT * (jnp.arange(NLAT, dtype=jnp.float32) + 0.5))
    weighted = spectral_in * (sines_all * math.sqrt(2.0 / NLAT))[None, None, None, :]
    legendre_basis = legendre_setup(slot_wave, M, NLAT, NLAT)

    def contract(table_rows):
        return jnp.einsum('stj,scij->isct', table_rows, weighted, precision=precise)
    return legendre_sweep(legendre_basis, contract, LEV, M)
```

```python
import math

import jax
import jax.numpy as jnp
import numpy as np
from jax import lax
from jax.experimental import pallas as pl
from jax.experimental.pallas import tpu as pltpu
from jax.sharding import PartitionSpec as P

M = 400
NLAT = 800
NLON = 1600
LANES = 128
BLOCK = 40
CHUNK = 40


def split_bf16(values):
    high = values.astype(jnp.bfloat16)
    low = (values - high.astype(jnp.float32)).astype(jnp.bfloat16)
    return high, low


def table_bf16(table):
    high = table.astype(jnp.bfloat16)
    low = (table - high.astype(np.float64)).astype(jnp.bfloat16)
    return high, low


def fourier_table(pieces):
    phase = np.arange(NLON)[:, None] * np.arange(M)[None, :] % NLON
    angles = 2.0 * math.pi / NLON * phase
    table = np.concatenate([np.cos(angles), -np.sin(angles)], axis=1) / math.sqrt(NLON)
    return table.reshape(pieces, NLON // pieces, 2 * M)


def resample_table():
    half = M // 2
    coarse = math.pi / M * (np.arange(M) + 0.5)
    fine = math.pi / NLAT * (np.arange(NLAT) + 0.5)
    waves = np.arange(M)
    weight = np.where(waves == 0, 1.0, 2.0) / M
    even = (np.cos(np.outer(coarse, waves)) * weight) @ np.cos(np.outer(waves, fine))
    odd = (np.sin(np.outer(coarse, waves)) * weight) @ np.sin(np.outer(waves, fine))
    rows = []
    for full in (even, odd):
        for sign in (1.0, -1.0):
            rows.append(full[:half] + sign * full[::-1][:half])
    return np.concatenate(rows, axis=0)


def latitude_table():
    half = M // 2
    angles = math.pi / M * (np.arange(half) + 0.5)
    log_sine = np.log2(np.sin(angles))
    coarse = np.round(log_sine * 1024.0) / 1024.0
    rows = np.stack([2.0 * np.cos(angles), coarse, log_sine - coarse])
    return np.broadcast_to(rows[:, :, None], (3, half, LANES)).astype(np.float32)


def advect(tracer, east_wind, north_wind):
    rows = tracer.shape[1]
    lat_count = lax.axis_size("lat")
    ring = ("lev", "fld")
    lon_count = lax.axis_size(ring)
    down = [(i, i + 1) for i in range(lat_count - 1)]
    up = [(i + 1, i) for i in range(lat_count - 1)]
    right = [(i, (i + 1) % lon_count) for i in range(lon_count)]
    left = [((i + 1) % lon_count, i) for i in range(lon_count)]
    north = lax.ppermute(tracer[:, rows - 1 :, :], "lat", down)
    south = lax.ppermute(tracer[:, :1, :], "lat", up)
    west = lax.ppermute(tracer[:, :, -1:], ring, right)
    east = lax.ppermute(tracer[:, :, :1], ring, left)
    wide = jnp.concatenate([west, tracer, east], axis=2).astype(jnp.float32)
    tall = jnp.concatenate([north, tracer, south], axis=1).astype(jnp.float32)
    east_diff = wide[:, :, 2:] - wide[:, :, :-2]
    north_diff = tall[:, 2:, :] - tall[:, :-2, :]
    return (
        tracer.astype(jnp.float32)
        - 0.5 * east_wind.astype(jnp.float32) * east_diff
        - 0.5 * north_wind.astype(jnp.float32) * north_diff
    )


def fourier_kernel(grid_ref, high_ref, low_ref, place_ref, wave_ref, keep_ref, sine_ref, out_ref):
    pieces = grid_ref.shape[0]
    total = None
    for piece in range(pieces):
        high, low = split_bf16(grid_ref[piece])
        part = jnp.dot(high, high_ref[piece], preferred_element_type=jnp.float32)
        part += jnp.dot(low, high_ref[piece], preferred_element_type=jnp.float32)
        part += jnp.dot(high, low_ref[piece], preferred_element_type=jnp.float32)
        total = part if total is None else total + part
    high, low = split_bf16(total)
    placed = jnp.dot(high, place_ref[...], preferred_element_type=jnp.float32)
    placed += jnp.dot(low, place_ref[...], preferred_element_type=jnp.float32)
    kept = jnp.where(wave_ref[...] < keep_ref[...], placed * sine_ref[...], 0.0)
    targets, _, width = out_ref.shape
    for target in range(targets):
        out_ref[target] = kept[:, target * width : (target + 1) * width]


def fourier(grid, places, wave_row, keep_col, sine_col, targets):
    pieces, rows, lons = grid.shape
    width = wave_row.shape[1] // targets
    high, low = table_bf16(fourier_table(pieces))
    return pl.pallas_call(
        fourier_kernel,
        out_shape=jax.ShapeDtypeStruct((targets, rows, width), jnp.float32),
        in_specs=[pl.BlockSpec(memory_space=pltpu.VMEM)] * 7,
        out_specs=pl.BlockSpec(memory_space=pltpu.VMEM),
        compiler_params=pltpu.CompilerParams(vmem_limit_bytes=48 * 2**20),
        cost_estimate=pl.CostEstimate(
            flops=6 * rows * NLON * 2 * M, bytes_accessed=12 * 2**20, transcendentals=0
        ),
    )(grid, high, low, places, wave_row, keep_col, sine_col)


def legendre_kernel(
    fields_ref, high_ref, low_ref, lat_ref, wave_ref, norm_ref, beta_ref, scale_ref, growth_ref,
    out_ref, weight, before, current, level, sums, result,
):
    half = lat_ref.shape[1]
    lanes = wave_ref.shape[1]
    slots = out_ref.shape[0]
    groups = lanes // LANES
    wave = wave_ref[...]
    odd = wave - 2.0 * jnp.floor(wave * 0.5) > 0.5

    for comp in range(2):
        high, low = split_bf16(fields_ref[:, comp * lanes : (comp + 1) * lanes])
        for parity in range(2):
            both = []
            for wave_parity in range(2):
                rows = pl.ds((2 * wave_parity + parity) * half, half)
                value = jnp.dot(high_ref[rows], high, preferred_element_type=jnp.float32)
                value += jnp.dot(high_ref[rows], low, preferred_element_type=jnp.float32)
                value += jnp.dot(low_ref[rows], high, preferred_element_type=jnp.float32)
                both.append(value)
            weight[2 * parity + comp] = jnp.where(odd, both[1], both[0])

    for group in range(groups):
        cols = slice(group * LANES, (group + 1) * LANES)
        coarse = lat_ref[1] * wave[:, cols]
        whole = jnp.floor(coarse)
        level[:, cols] = whole
        current[:, cols] = jnp.exp2(
            (coarse - whole) + lat_ref[2] * wave[:, cols] + norm_ref[:, cols]
        )
        before[:, cols] = jnp.zeros((half, LANES), jnp.float32)

    def step(block, carry):
        first = pl.multiple_of(block * BLOCK, 8)
        for group in range(groups):
            cols = slice(group * LANES, (group + 1) * LANES)
            grow = growth_ref[pl.ds(block, 1), cols]
            for chunk in range(half // CHUNK):
                rows = slice(chunk * CHUNK, (chunk + 1) * CHUNK)
                height = level[rows, cols]
                factor = jnp.exp2(height)
                weights = [weight[k, rows, cols] * factor for k in range(4)]
                cosine = lat_ref[0, rows]
                old = before[rows, cols]
                new = current[rows, cols]
                for order in range(BLOCK):
                    for comp in range(2):
                        product = new * weights[2 * (order % 2) + comp]
                        partial = product.reshape(CHUNK // 8, 8, LANES).sum(axis=0)
                        place = pl.ds((order * 2 + comp) * 8, 8)
                        if chunk == 0:
                            sums[place] = partial
                        else:
                            sums[place] += partial
                    beta = beta_ref[pl.ds(first + order, 1), cols]
                    old, new = new, cosine * new - beta * old
                biggest = jnp.maximum(jnp.abs(old), jnp.abs(new)) * grow
                shift = jnp.floor(jnp.log(biggest) * (1.0 / math.log(2.0)))
                factor = grow * jnp.exp2(-shift)
                before[rows, cols] = old * factor
                current[rows, cols] = new * factor
                level[rows, cols] = height + shift
            for comp in range(2):
                total = sums[pl.ds(comp * 8, BLOCK, stride=16)]
                for lane in range(1, 8):
                    total += sums[pl.ds(comp * 8 + lane, BLOCK, stride=16)]
                result[comp, pl.ds(first, BLOCK), cols] = (
                    total * scale_ref[pl.ds(first, BLOCK), cols]
                )
        return carry

    lax.fori_loop(0, M // BLOCK, step, 0)
    for comp in range(2):
        out_ref[:, comp, :] = result[comp].T[:slots]


def legendre(fields, slot_wave):
    slots = slot_wave.shape[0]
    lanes = fields.shape[1] // 2
    half = M // 2
    wave_row = jnp.pad(slot_wave, (0, lanes - slots), constant_values=2 * M)
    inside_wave = jnp.minimum(wave_row, M - 1).astype(jnp.float32)[None, :]
    counter = np.arange(1, M)
    log_terms = np.log1p(0.5 / counter) / math.log(2.0)
    log_norm = jnp.sum(
        jnp.where(
            counter.astype(np.float32)[:, None] <= inside_wave, log_terms.astype(np.float32)[:, None], 0.0
        ),
        axis=0,
        keepdims=True,
    )
    norm = 0.5 * (log_norm - 1.0)
    order = jnp.arange(M + 1, dtype=jnp.float32)[:, None]
    degree = inside_wave + order
    square = 4.0 * degree * degree - 1.0
    beta = 4.0 * order * (degree + inside_wave) / jnp.maximum(square, 1.0)
    ratio = jnp.sqrt(square[1:] / (4.0 * order[1:] * (degree[1:] + inside_wave)))
    ratio = ratio.reshape(M // BLOCK, BLOCK, lanes)
    scales = [jnp.ones_like(ratio[:, 0])]
    for index in range(BLOCK):
        scales.append(scales[-1] * ratio[:, index])
    growth = scales[-1]
    scale = jnp.stack(scales[:-1], axis=1).reshape(M, lanes)
    scale = jnp.where(order[:-1] < (M - wave_row).astype(jnp.float32)[None, :], scale, 0.0)
    high, low = table_bf16(resample_table())
    vector = pltpu.VMEM((half, lanes), jnp.float32)
    return pl.pallas_call(
        legendre_kernel,
        out_shape=jax.ShapeDtypeStruct((slots, 2, M), jnp.float32),
        in_specs=[pl.BlockSpec(memory_space=pltpu.VMEM)] * 9,
        out_specs=pl.BlockSpec(memory_space=pltpu.VMEM),
        scratch_shapes=[
            pltpu.VMEM((4, half, lanes), jnp.float32),
            vector,
            vector,
            vector,
            pltpu.VMEM((BLOCK * 16, LANES), jnp.float32),
            pltpu.VMEM((2, M, lanes), jnp.float32),
        ],
        compiler_params=pltpu.CompilerParams(vmem_limit_bytes=48 * 2**20),
        cost_estimate=pl.CostEstimate(
            flops=7 * half * lanes * M, bytes_accessed=6 * 2**20, transcendentals=0
        ),
    )(fields, high, low, latitude_table(), inside_wave, norm, beta[:-1], scale, growth)


def shards(tracer, wind_east, wind_north, keep_m, slot_wave):
    rows = tracer.shape[1]
    lat_count = lax.axis_size("lat")
    slots = slot_wave.shape[0] // lat_count
    lanes = -(-slots // LANES) * LANES
    lat_index = lax.axis_index("lat")

    advected = advect(tracer, wind_east, wind_north)
    grid = lax.all_to_all(advected, ("lev", "fld"), split_axis=0, concat_axis=0, tiled=True)

    waves = jnp.pad(
        slot_wave.reshape(lat_count, 1, slots), ((0, 0), (0, 0), (0, lanes - slots)),
        constant_values=2 * NLON,
    )
    waves = jnp.broadcast_to(waves, (lat_count, 2, lanes))
    offsets = jnp.array([0, M], jnp.int32)[None, :, None]
    columns = jnp.where(waves < M, waves + offsets, -1).reshape(1, -1)
    places = (jnp.arange(2 * M, dtype=jnp.int32)[:, None] == columns).astype(jnp.bfloat16)
    row_ids = (lat_index * rows + jnp.arange(rows, dtype=jnp.int32)).astype(jnp.float32)
    sines = jnp.sin(math.pi / NLAT * (row_ids + 0.5)) * math.sqrt(2.0 / NLAT)
    waved = fourier(
        grid, places, waves.reshape(1, -1), keep_m[:, None], sines[:, None], lat_count
    )
    fields = lax.all_to_all(waved, "lat", split_axis=0, concat_axis=0, tiled=True)
    fields = fields.reshape(lat_count * rows, 2 * lanes)
    my_waves = lax.dynamic_slice_in_dim(slot_wave, lat_index * slots, slots)
    return legendre(fields, my_waves)[None]


def solution(mesh):
    return jax.shard_map(
        shards,
        mesh=mesh,
        in_specs=(
            P("member", "lat", ("lev", "fld")),
            P("member", "lat", ("lev", "fld")),
            P("member", "lat", ("lev", "fld")),
            P("lat"),
            P(),
        ),
        out_specs=P(("member", "lev", "fld"), "lat", None, None),
        check_vma=False,
    )
```

```python
import math

import jax
import jax.numpy as jnp
import numpy as np
from jax import lax
from jax.experimental import pallas as pl
from jax.experimental.pallas import tpu as pltpu
from jax.sharding import PartitionSpec as P

M = 400
NLAT = 800
NLON = 1600
LANES = 128
BLOCK = 40
CHUNK = 40
TOP = 32767.0
VMEM_BYTES = 24 * 2**20


def split_bf16(values):
    high = values.astype(jnp.bfloat16)
    low = (values - high.astype(jnp.float32)).astype(jnp.bfloat16)
    return high, low


def table_bf16(table):
    high = table.astype(jnp.bfloat16)
    low = (table - high.astype(np.float64)).astype(jnp.bfloat16)
    return high, low


def fourier_tables(pieces):
    quarter = NLON // 4
    spots = np.arange(quarter)[:, None]
    factor = 1.0 / math.sqrt(NLON)

    def parts(waves):
        angles = 2.0 * math.pi / NLON * (spots * waves[None, :] % NLON)
        return factor * np.cos(angles), factor * np.sin(angles)

    tables = []
    for first in (0, 2):
        cosine, sine = parts(np.arange(first, M, 4))
        tables.append([cosine, -sine])
    waves = np.arange(1, M, 2)
    sign = np.where(waves % 4 == 1, 1.0, -1.0)[None, :]
    cosine, sine = parts(waves)
    tables.append([cosine, -sine])
    tables.append([-sign * sine, -sign * cosine])
    share = pieces // 4
    result = []
    for columns in tables:
        table = np.concatenate(columns, axis=1)
        table = np.pad(table, ((0, 0), (0, -table.shape[1] % (2 * LANES))))
        result.append(table.reshape(share, quarter // share, table.shape[1]))
    return result


def wave_rows():
    quarter_width = -(-M // 2 // (2 * LANES)) * 2 * LANES
    waves = np.arange(M)
    quarter_count, half_count = M // 4, M // 2
    rows = []
    for part in range(2):
        even = np.where(waves % 4 == 0, 0, quarter_width) + part * quarter_count + waves // 4
        odd = 2 * quarter_width + part * half_count + waves // 2
        rows.append(np.where(waves % 2 == 0, even, odd))
    return np.stack(rows).astype(np.int32)


def resample_table():
    half = M // 2
    coarse = math.pi / M * (np.arange(M) + 0.5)
    fine = math.pi / NLAT * (np.arange(NLAT) + 0.5)
    waves = np.arange(M)
    weight = np.where(waves == 0, 1.0, 2.0) / M
    even = (np.cos(np.outer(coarse, waves)) * weight) @ np.cos(np.outer(waves, fine))
    odd = (np.sin(np.outer(coarse, waves)) * weight) @ np.sin(np.outer(waves, fine))
    rows = []
    for full in (even, odd):
        for sign in (1.0, -1.0):
            rows.append(full[:half] + sign * full[::-1][:half])
    return np.concatenate(rows, axis=0)


def latitude_table():
    half = M // 2
    angles = math.pi / M * (np.arange(half) + 0.5)
    log_sine = np.log2(np.sin(angles))
    coarse = np.round(log_sine * 1024.0) / 1024.0
    rows = np.stack([2.0 * np.cos(angles), coarse, log_sine - coarse])
    return np.broadcast_to(rows[:, :, None], (3, half, LANES)).astype(np.float32)


def scale_code(biggest):
    wanted = jnp.maximum(biggest, 1e-30) * (1.0 / TOP)
    exponent = jnp.floor(jnp.log(wanted) * (1.0 / math.log(2.0)))
    return exponent * 128.0 + jnp.ceil((wanted * jnp.exp2(-exponent) - 1.0) * 128.0)


def scale_of(code):
    exponent = jnp.floor(code * (1.0 / 128.0))
    rest = code - 128.0 * exponent
    return jnp.exp2(exponent) * (1.0 + rest * (1.0 / 128.0))


def coded(values, scale):
    steps = jnp.floor(values * (1.0 / scale) + 0.5)
    return jnp.clip(steps, -TOP, TOP)


def as_int16(values):
    return values.astype(jnp.int32).astype(jnp.int16)


def from_int16(codes):
    return codes.astype(jnp.int32).astype(jnp.float32)


def advect_kernel(tracer_ref, east_ref, north_ref, above_ref, below_ref, west_ref, east_edge_ref, out_ref):
    levels, rows, lons = tracer_ref.shape
    for level in range(levels):
        field = tracer_ref[level].astype(jnp.float32)
        west = jnp.concatenate([west_ref[level].astype(jnp.float32), field[:, :-1]], axis=1)
        east = jnp.concatenate([field[:, 1:], east_edge_ref[level].astype(jnp.float32)], axis=1)
        north = jnp.concatenate([above_ref[level].astype(jnp.float32), field[:-1]], axis=0)
        south = jnp.concatenate([field[1:], below_ref[level].astype(jnp.float32)], axis=0)
        moved = (
            field
            - 0.5 * east_ref[level].astype(jnp.float32) * (east - west)
            - 0.5 * north_ref[level].astype(jnp.float32) * (south - north)
        )
        code = scale_code(jnp.max(jnp.abs(moved), axis=1, keepdims=True))
        steps = coded(moved, scale_of(code))
        out_ref[level] = as_int16(jnp.concatenate([steps, code], axis=1))


def advect(tracer, east_wind, north_wind):
    levels, rows, lons = tracer.shape
    lat_count = lax.axis_size("lat")
    ring = ("lev", "fld")
    lon_count = lax.axis_size(ring)
    down = [(i, i + 1) for i in range(lat_count - 1)]
    up = [(i + 1, i) for i in range(lat_count - 1)]
    right = [(i, (i + 1) % lon_count) for i in range(lon_count)]
    left = [((i + 1) % lon_count, i) for i in range(lon_count)]
    above = lax.ppermute(tracer[:, rows - 1 :, :], "lat", down)
    below = lax.ppermute(tracer[:, :1, :], "lat", up)
    west = lax.ppermute(tracer[:, :, -1:], ring, right)
    east = lax.ppermute(tracer[:, :, :1], ring, left)
    return pl.pallas_call(
        advect_kernel,
        out_shape=jax.ShapeDtypeStruct((levels, rows, lons + 1), jnp.int16),
        in_specs=[pl.BlockSpec(memory_space=pltpu.VMEM)] * 7,
        out_specs=pl.BlockSpec(memory_space=pltpu.VMEM),
        compiler_params=pltpu.CompilerParams(vmem_limit_bytes=VMEM_BYTES),
        cost_estimate=pl.CostEstimate(
            flops=20 * levels * rows * lons, bytes_accessed=8 * levels * rows * lons, transcendentals=0
        ),
    )(tracer, east_wind, north_wind, above, below, west, east)


def fourier_kernel(
    grid_ref, t0h, t0l, t2h, t2l, tah, tal, tbh, tbl, place_ref, wave_ref, keep_ref, sine_ref, out_ref
):
    pieces, rows, width = grid_ref.shape
    lons = width - 1
    share = pieces // 4

    def product(value, high_ref, low_ref, spot):
        high, low = split_bf16(value)
        part = jnp.dot(high, high_ref[spot], preferred_element_type=jnp.float32)
        part += jnp.dot(low, high_ref[spot], preferred_element_type=jnp.float32)
        return part + jnp.dot(high, low_ref[spot], preferred_element_type=jnp.float32)

    sums = [None, None, None]
    for spot in range(share):
        quarters = []
        for quarter in range(4):
            values = from_int16(grid_ref[quarter * share + spot])
            quarters.append(values[:, :lons] * scale_of(values[:, lons:]))
        sum02, dif02 = quarters[0] + quarters[2], quarters[0] - quarters[2]
        sum13, dif13 = quarters[1] + quarters[3], quarters[1] - quarters[3]
        parts = [
            product(sum02 + sum13, t0h, t0l, spot),
            product(sum02 - sum13, t2h, t2l, spot),
            product(dif02, tah, tal, spot) + product(dif13, tbh, tbl, spot),
        ]
        sums = [part if total is None else total + part for total, part in zip(sums, parts)]
    placed = None
    first = 0
    for total in sums:
        last = first + total.shape[1]
        high, low = split_bf16(total)
        part = jnp.dot(high, place_ref[first:last], preferred_element_type=jnp.float32)
        part += jnp.dot(low, place_ref[first:last], preferred_element_type=jnp.float32)
        placed = part if placed is None else placed + part
        first = last
    kept = jnp.where(wave_ref[...] < keep_ref[...], placed * sine_ref[...], 0.0)
    code = scale_code(jnp.max(jnp.abs(kept), axis=0, keepdims=True))
    steps = coded(kept, scale_of(code))
    targets, padded_rows, span = out_ref.shape
    codes = jnp.broadcast_to(code, (padded_rows - rows, code.shape[1]))
    result = as_int16(jnp.concatenate([steps, codes], axis=0))
    for target in range(targets):
        out_ref[target] = result[:, target * span : (target + 1) * span]


def fourier(grid, places, wave_row, keep_col, sine_col, targets):
    pieces, rows, _ = grid.shape
    span = wave_row.shape[1] // targets
    padded_rows = -(-(rows + 1) // 16) * 16
    tables = [part for table in fourier_tables(pieces) for part in table_bf16(table)]
    return pl.pallas_call(
        fourier_kernel,
        out_shape=jax.ShapeDtypeStruct((targets, padded_rows, span), jnp.int16),
        in_specs=[pl.BlockSpec(memory_space=pltpu.VMEM)] * 13,
        out_specs=pl.BlockSpec(memory_space=pltpu.VMEM),
        compiler_params=pltpu.CompilerParams(vmem_limit_bytes=VMEM_BYTES),
        cost_estimate=pl.CostEstimate(
            flops=3 * rows * NLON * M, bytes_accessed=6 * 2**20, transcendentals=0
        ),
    )(grid, *tables, places, wave_row, keep_col, sine_col)


def legendre_kernel(
    fields_ref, high_ref, low_ref, lat_ref, wave_ref, limit_ref, norm_ref,
    out_ref, weight, before, current, level, sums, result, beta_ref, scale_ref, growth_ref,
):
    half = lat_ref.shape[1]
    lanes = wave_ref.shape[1]
    slots = out_ref.shape[0]
    groups = lanes // LANES
    wave = wave_ref[...]
    odd = wave - 2.0 * jnp.floor(wave * 0.5) > 0.5

    def squares(order):
        degree = wave + order
        return 4.0 * degree * degree - 1.0, 4.0 * order * (degree + wave)

    square, spread = squares(
        lax.broadcasted_iota(jnp.int32, (M, lanes), 0).astype(jnp.float32)
    )
    beta_ref[...] = spread / jnp.maximum(square, 1.0)
    blocks = M // BLOCK
    first_order = lax.broadcasted_iota(jnp.int32, (blocks, lanes), 0).astype(jnp.float32) * BLOCK
    scale = jnp.ones((blocks, lanes), jnp.float32)
    for index in range(BLOCK):
        inside = first_order + index < limit_ref[...]
        scale_ref[pl.ds(index, blocks, stride=BLOCK)] = jnp.where(inside, scale, 0.0)
        square, spread = squares(first_order + (index + 1))
        scale = scale * jnp.sqrt(square / spread)
    growth_ref[...] = scale

    pieces, padded_rows, _ = fields_ref.shape
    totals = [None] * 4
    code_row = padded_rows - 1
    for piece in range(pieces):
        values = from_int16(fields_ref[piece])
        values = values * scale_of(values[code_row:])
        high, low = split_bf16(values)
        for table in range(4):
            rows = pl.ds(table * half, half)
            value = jnp.dot(high_ref[piece, rows], high, preferred_element_type=jnp.float32)
            value += jnp.dot(high_ref[piece, rows], low, preferred_element_type=jnp.float32)
            value += jnp.dot(low_ref[piece, rows], high, preferred_element_type=jnp.float32)
            totals[table] = value if piece == 0 else totals[table] + value
    for parity in range(2):
        for comp in range(2):
            cols = slice(comp * lanes, (comp + 1) * lanes)
            weight[2 * parity + comp] = jnp.where(
                odd, totals[2 + parity][:, cols], totals[parity][:, cols]
            )

    for group in range(groups):
        cols = slice(group * LANES, (group + 1) * LANES)
        coarse = lat_ref[1] * wave[:, cols]
        whole = jnp.floor(coarse)
        level[:, cols] = whole
        current[:, cols] = jnp.exp2(
            (coarse - whole) + lat_ref[2] * wave[:, cols] + norm_ref[:, cols]
        )
        before[:, cols] = jnp.zeros((half, LANES), jnp.float32)

    def step(block, carry):
        first = pl.multiple_of(block * BLOCK, 8)
        for group in range(groups):
            cols = slice(group * LANES, (group + 1) * LANES)
            grow = growth_ref[pl.ds(block, 1), cols]
            for chunk in range(half // CHUNK):
                rows = slice(chunk * CHUNK, (chunk + 1) * CHUNK)
                height = level[rows, cols]
                factor = jnp.exp2(height)
                weights = [weight[k, rows, cols] * factor for k in range(4)]
                cosine = lat_ref[0, rows]
                old = before[rows, cols]
                new = current[rows, cols]
                for order in range(BLOCK):
                    for comp in range(2):
                        product = new * weights[2 * (order % 2) + comp]
                        partial = product.reshape(CHUNK // 8, 8, LANES).sum(axis=0)
                        place = pl.ds((order * 2 + comp) * 8, 8)
                        if chunk == 0:
                            sums[place] = partial
                        else:
                            sums[place] += partial
                    beta = beta_ref[pl.ds(first + order, 1), cols]
                    old, new = new, cosine * new - beta * old
                biggest = jnp.maximum(jnp.abs(old), jnp.abs(new)) * grow
                shift = jnp.floor(jnp.log(biggest) * (1.0 / math.log(2.0)))
                factor = grow * jnp.exp2(-shift)
                before[rows, cols] = old * factor
                current[rows, cols] = new * factor
                level[rows, cols] = height + shift
            for comp in range(2):
                total = sums[pl.ds(comp * 8, BLOCK, stride=16)]
                for lane in range(1, 8):
                    total += sums[pl.ds(comp * 8 + lane, BLOCK, stride=16)]
                result[comp, pl.ds(first, BLOCK), cols] = (
                    total * scale_ref[pl.ds(first, BLOCK), cols]
                )
        return carry

    lax.fori_loop(0, M // BLOCK, step, 0)
    for comp in range(2):
        out_ref[:, comp, :] = result[comp].T[:slots]


def legendre(fields, slot_wave, rows):
    slots = slot_wave.shape[0]
    pieces, padded_rows, span = fields.shape
    lanes = span // 2
    half = M // 2
    wave_row = jnp.pad(slot_wave, (0, lanes - slots), constant_values=2 * M)[None, :]
    inside_wave = jnp.minimum(wave_row, M - 1).astype(jnp.float32)
    limit = (M - wave_row).astype(jnp.float32)
    counter = np.arange(1, M)[:, None]
    log_terms = (np.log1p(0.5 / counter) / math.log(2.0)).astype(np.float32)
    log_norm = jnp.sum(
        jnp.where(counter.astype(np.float32) <= inside_wave, log_terms, 0.0), axis=0, keepdims=True
    )
    norm = 0.5 * (log_norm - 1.0)
    table = resample_table().reshape(2 * M, pieces, rows).transpose(1, 0, 2)
    high, low = table_bf16(np.pad(table, ((0, 0), (0, 0), (0, padded_rows - rows))))
    vector = pltpu.VMEM((half, lanes), jnp.float32)
    orders = pltpu.VMEM((M, lanes), jnp.float32)
    return pl.pallas_call(
        legendre_kernel,
        out_shape=jax.ShapeDtypeStruct((slots, 2, M), jnp.float32),
        in_specs=[pl.BlockSpec(memory_space=pltpu.VMEM)] * 7,
        out_specs=pl.BlockSpec(memory_space=pltpu.VMEM),
        scratch_shapes=[
            pltpu.VMEM((4, half, lanes), jnp.float32),
            vector,
            vector,
            vector,
            pltpu.VMEM((BLOCK * 16, LANES), jnp.float32),
            pltpu.VMEM((2, M, lanes), jnp.float32),
            orders,
            orders,
            pltpu.VMEM((M // BLOCK, lanes), jnp.float32),
        ],
        compiler_params=pltpu.CompilerParams(vmem_limit_bytes=VMEM_BYTES),
        cost_estimate=pl.CostEstimate(
            flops=7 * half * lanes * M, bytes_accessed=6 * 2**20, transcendentals=0
        ),
    )(fields, high, low, latitude_table(), inside_wave, limit, norm)


def shards(tracer, wind_east, wind_north, keep_m, slot_wave):
    rows = tracer.shape[1]
    lat_count = lax.axis_size("lat")
    slots = slot_wave.shape[0] // lat_count
    lanes = -(-slots // LANES) * LANES
    lat_index = lax.axis_index("lat")

    advected = advect(tracer, wind_east, wind_north)
    grid = lax.all_to_all(advected, ("lev", "fld"), split_axis=0, concat_axis=0, tiled=True)

    pad = ((0, 0), (0, 0), (0, lanes - slots))
    waves = jnp.pad(slot_wave.reshape(lat_count, 1, slots), pad, constant_values=2 * M)
    waves = jnp.broadcast_to(waves, (lat_count, 2, lanes))
    table_rows = wave_rows()
    spots = np.full(4 * (-(-M // 2 // (2 * LANES)) * 2 * LANES), 4 * M, np.int32)
    for part in range(2):
        spots[table_rows[part]] = np.arange(M) * 2 + part
    columns = (waves * 2 + jnp.array([0, 1], jnp.int32)[None, :, None]).reshape(1, -1)
    places = ((spots[:, None] == columns) & (columns < 2 * M)).astype(jnp.bfloat16)
    row_ids = (lat_index * rows + jnp.arange(rows, dtype=jnp.int32)).astype(jnp.float32)
    sines = jnp.sin(math.pi / NLAT * (row_ids + 0.5)) * math.sqrt(2.0 / NLAT)
    waved = fourier(
        grid, places, waves.reshape(1, -1), keep_m[:, None], sines[:, None], lat_count
    )
    fields = lax.all_to_all(waved, "lat", split_axis=0, concat_axis=0, tiled=True)
    my_waves = lax.dynamic_slice_in_dim(slot_wave, lat_index * slots, slots)
    return legendre(fields, my_waves, rows)[None]


def solution(mesh):
    return jax.shard_map(
        shards,
        mesh=mesh,
        in_specs=(
            P("member", "lat", ("lev", "fld")),
            P("member", "lat", ("lev", "fld")),
            P("member", "lat", ("lev", "fld")),
            P("lat"),
            P(),
        ),
        out_specs=P(("member", "lev", "fld"), "lat", None, None),
        check_vma=False,
    )
```

```python
import functools
import math

import jax
import jax.numpy as jnp
import numpy as np
from jax import lax
from jax.experimental import pallas as pl
from jax.experimental.pallas import tpu as pltpu
from jax.sharding import PartitionSpec as P

M = 400
NLAT = 800
NLON = 1600
LANES = 128
BLOCK = 40
CHUNK = 40
TOP = 32767.0
WIND_STEP = 1.5 / TOP
VMEM_BYTES = 24 * 2**20
VMEM_SPEC = pl.BlockSpec(memory_space=pltpu.VMEM)
SMEM_SPEC = pl.BlockSpec(memory_space=pltpu.SMEM)
ANY_SPEC = pl.BlockSpec(memory_space=pl.ANY)


def split_bf16(values):
    high = values.astype(jnp.bfloat16)
    low = (values - high.astype(jnp.float32)).astype(jnp.bfloat16)
    return high, low


def table_bf16(table):
    high = table.astype(jnp.bfloat16)
    low = (table - high.astype(np.float64)).astype(jnp.bfloat16)
    return np.concatenate([high, low], axis=-1)


def fourier_tables(pieces):
    quarter = NLON // 4
    spots = np.arange(quarter)[:, None]
    factor = 1.0 / math.sqrt(NLON)

    def parts(waves):
        angles = 2.0 * math.pi / NLON * (spots * waves[None, :] % NLON)
        return factor * np.cos(angles), factor * np.sin(angles)

    tables = []
    for first in (0, 2):
        cosine, sine = parts(np.arange(first, M, 4))
        tables.append([cosine, -sine])
    waves = np.arange(1, M, 2)
    sign = np.where(waves % 4 == 1, 1.0, -1.0)[None, :]
    cosine, sine = parts(waves)
    tables.append([cosine, -sine])
    tables.append([-sign * sine, -sign * cosine])
    share = pieces // 4
    result = []
    for columns in tables:
        table = np.concatenate(columns, axis=1)
        table = np.pad(table, ((0, 0), (0, -table.shape[1] % (2 * LANES))))
        result.append(table.reshape(share, quarter // share, table.shape[1]))
    return result


def wave_rows():
    quarter_width = -(-M // 2 // (2 * LANES)) * 2 * LANES
    waves = np.arange(M)
    quarter_count, half_count = M // 4, M // 2
    rows = []
    for part in range(2):
        even = np.where(waves % 4 == 0, 0, quarter_width) + part * quarter_count + waves // 4
        odd = 2 * quarter_width + part * half_count + waves // 2
        rows.append(np.where(waves % 2 == 0, even, odd))
    return np.stack(rows).astype(np.int32)


def resample_table():
    half = M // 2
    coarse = math.pi / M * (np.arange(M) + 0.5)
    fine = math.pi / NLAT * (np.arange(NLAT) + 0.5)
    waves = np.arange(M)
    weight = np.where(waves == 0, 1.0, 2.0) / M
    even = (np.cos(np.outer(coarse, waves)) * weight) @ np.cos(np.outer(waves, fine))
    odd = (np.sin(np.outer(coarse, waves)) * weight) @ np.sin(np.outer(waves, fine))
    rows = []
    for full in (even, odd):
        for sign in (1.0, -1.0):
            rows.append(full[:half] + sign * full[::-1][:half])
    return np.concatenate(rows, axis=0)


def latitude_table():
    half = M // 2
    angles = math.pi / M * (np.arange(half) + 0.5)
    log_sine = np.log2(np.sin(angles))
    coarse = np.round(log_sine * 1024.0) / 1024.0
    rows = np.stack([2.0 * np.cos(angles), coarse, log_sine - coarse])
    return np.broadcast_to(rows[:, :, None], (3, half, LANES)).astype(np.float32)


def scale_code(biggest):
    wanted = jnp.maximum(biggest, 1e-30) * (1.0 / TOP)
    exponent = jnp.floor(jnp.log(wanted) * (1.0 / math.log(2.0)))
    return exponent * 128.0 + jnp.ceil((wanted * jnp.exp2(-exponent) - 1.0) * 128.0)


def scale_of(code):
    exponent = jnp.floor(code * (1.0 / 128.0))
    rest = code - 128.0 * exponent
    return jnp.exp2(exponent) * (1.0 + rest * (1.0 / 128.0))


def coded(values, scale):
    steps = jnp.floor(values * (1.0 / scale) + 0.5)
    return jnp.clip(steps, -TOP, TOP)


def as_int16(values):
    return values.astype(jnp.int32).astype(jnp.int16)


def from_int16(codes):
    return codes.astype(jnp.int32).astype(jnp.float32)


def partners(axis):
    count = lax.axis_size(axis)
    order = jnp.arange(count, dtype=jnp.int32)
    return lax.axis_index(axis).astype(jnp.int32) ^ order if count == 4 else order


def exchange(blocks, axis):
    count = len(blocks)
    if count != 4:
        return list(lax.all_to_all(jnp.stack(blocks), axis, split_axis=0, concat_axis=0, tiled=True))
    pairs = [[(i, i ^ step) for i in range(count)] for step in range(count)]
    return [blocks[0]] + [lax.ppermute(blocks[step], axis, pairs[step]) for step in range(1, count)]


def advect_kernel(order_ref, tracer_hbm, east_hbm, north_hbm, above_ref, below_ref, *rest):
    levels, rows, lons = tracer_hbm.shape
    outs, (tracer, east_wind, north_wind, sems) = rest[:levels], rest[levels:]
    copies = []
    for step in range(levels):
        level = order_ref[step]
        copies.append(
            [
                pltpu.make_async_copy(source.at[level], target.at[step], sems.at[step, kind])
                for kind, (source, target) in enumerate(
                    ((tracer_hbm, tracer), (east_hbm, east_wind), (north_hbm, north_wind))
                )
            ]
        )
        for copy in copies[-1]:
            copy.start()
    for step in range(levels):
        level = order_ref[step]
        for copy in copies[step]:
            copy.wait()
        field = tracer[step].astype(jnp.float32)
        first, last = field[:, :1], field[:, lons - 1 :]
        blank = jnp.zeros_like(first)
        west = jnp.concatenate([blank, field[:, :-1]], axis=1)
        east = jnp.concatenate([field[:, 1:], blank], axis=1)
        above = above_ref[level].astype(jnp.float32)
        below = below_ref[level].astype(jnp.float32)
        north = jnp.concatenate([above, field[:-1]], axis=0)
        south = jnp.concatenate([field[1:], below], axis=0)
        eastward = 0.5 * east_wind[step].astype(jnp.float32)
        moved = (
            field
            - eastward * (east - west)
            - 0.5 * north_wind[step].astype(jnp.float32) * (south - north)
        )
        biggest = jnp.maximum(jnp.abs(moved), jnp.abs(field))
        code = scale_code(jnp.max(biggest, axis=1, keepdims=True))
        scale = scale_of(code)
        wind = jnp.concatenate([eastward[:, :1], eastward[:, lons - 1 :]], axis=1)
        outs[step][...] = as_int16(
            jnp.concatenate(
                [
                    coded(moved, scale),
                    code,
                    coded(first, scale),
                    coded(last, scale),
                    coded(wind, WIND_STEP),
                ],
                axis=1,
            )
        )


def advect(tracer, east_wind, north_wind, order):
    levels, rows, lons = tracer.shape
    lat_count = lax.axis_size("lat")
    down = [(i, i + 1) for i in range(lat_count - 1)]
    up = [(i + 1, i) for i in range(lat_count - 1)]
    above = lax.ppermute(tracer[:, rows - 1 :, :], "lat", down)
    below = lax.ppermute(tracer[:, :1, :], "lat", up)
    held = pltpu.VMEM((levels, rows, lons), jnp.bfloat16)
    return pl.pallas_call(
        advect_kernel,
        out_shape=[jax.ShapeDtypeStruct((rows, lons + 5), jnp.int16)] * levels,
        in_specs=[SMEM_SPEC] + [ANY_SPEC] * 3 + [VMEM_SPEC] * 2,
        out_specs=[VMEM_SPEC] * levels,
        scratch_shapes=[held, held, held, pltpu.SemaphoreType.DMA((levels, 3))],
        compiler_params=pltpu.CompilerParams(vmem_limit_bytes=VMEM_BYTES),
        cost_estimate=pl.CostEstimate(
            flops=20 * levels * rows * lons, bytes_accessed=8 * levels * rows * lons, transcendentals=0
        ),
    )(order, tracer, east_wind, north_wind, above, below)


def fourier_kernel(pieces, targets, order_ref, *rest):
    grids, rest = rest[:pieces], rest[pieces:]
    tables_hbm, (place_ref, wave_ref, keep_ref, sine_ref), rest = rest[:4], rest[4:8], rest[8:]
    outs, rest = rest[:targets], rest[targets:]
    tables, (field, sems) = rest[:4], rest[4:]
    _, rows, lons = field.shape
    share = pieces // 4
    copies = []
    for kind in range(4):
        copies.append(pltpu.make_async_copy(tables_hbm[kind], tables[kind], sems.at[kind]))
        copies[-1].start()

    edges = []
    for piece in range(pieces):
        values = from_int16(grids[piece][...])
        code = values[:, lons : lons + 1]
        field[order_ref[piece]] = values[:, :lons] * scale_of(code)
        edges.append((scale_of(code), values[:, lons + 1 :]))
    end = (lons - 1) // LANES * LANES
    head = lax.broadcasted_iota(jnp.int32, (rows, LANES), 1) == 0
    tail = lax.broadcasted_iota(jnp.int32, (rows, lons - end), 1) == lons - end - 1
    for piece in range(pieces):
        spot = order_ref[piece]
        scale, ends = edges[piece]
        first = scale * ends[:, 0:1]
        last = scale * ends[:, 1:2]
        for other in range(pieces):
            if other == piece:
                continue
            after = order_ref[other] == lax.rem(spot + 1, pieces)
            ahead = order_ref[other] == lax.rem(spot + pieces - 1, pieces)
            winds = edges[other][1][:, 2:4] * WIND_STEP

            @pl.when(after)
            def _():
                field[order_ref[other], :, :LANES] += jnp.where(head, winds[:, 0:1] * last, 0.0)

            @pl.when(ahead)
            def _():
                field[order_ref[other], :, end:] -= jnp.where(tail, winds[:, 1:2] * first, 0.0)

    def product(value, table, spot):
        high, low = split_bf16(value)
        width = table.shape[2] // 2
        both = jnp.dot(high, table[spot], preferred_element_type=jnp.float32)
        part = jnp.dot(low, table[spot, :, :width], preferred_element_type=jnp.float32)
        return part + both[:, :width] + both[:, width:]

    sums = [None, None, None]
    for spot in range(share):
        quarters = [field[quarter * share + spot] for quarter in range(4)]
        sum02, dif02 = quarters[0] + quarters[2], quarters[0] - quarters[2]
        sum13, dif13 = quarters[1] + quarters[3], quarters[1] - quarters[3]
        parts = []
        for kind, value in enumerate((sum02 + sum13, sum02 - sum13, dif02, dif13)):
            if spot == 0:
                copies[kind].wait()
            parts.append(product(value, tables[kind], spot))
        parts = [parts[0], parts[1], parts[2] + parts[3]]
        sums = [part if total is None else total + part for total, part in zip(sums, parts)]
    placed = None
    first = 0
    for total in sums:
        last = first + total.shape[1]
        high, low = split_bf16(total)
        part = jnp.dot(high, place_ref[first:last], preferred_element_type=jnp.float32)
        part += jnp.dot(low, place_ref[first:last], preferred_element_type=jnp.float32)
        placed = part if placed is None else placed + part
        first = last
    kept = jnp.where(wave_ref[...] < keep_ref[...], placed * sine_ref[...], 0.0)
    code = scale_code(jnp.max(jnp.abs(kept), axis=0, keepdims=True))
    steps = coded(kept, scale_of(code))
    padded_rows, span = outs[0].shape
    codes = jnp.broadcast_to(code, (padded_rows - rows, code.shape[1]))
    result = as_int16(jnp.concatenate([steps, codes], axis=0))
    for target in range(targets):
        outs[target][...] = result[:, target * span : (target + 1) * span]


def fourier(grids, order, places, wave_row, keep_col, sine_col, targets):
    pieces = len(grids)
    rows, width = grids[0].shape
    lons = width - 5
    span = wave_row.shape[1] // targets
    padded_rows = -(-(rows + 1) // 16) * 16
    tables = [table_bf16(table) for table in fourier_tables(pieces)]
    return pl.pallas_call(
        functools.partial(fourier_kernel, pieces, targets),
        out_shape=[jax.ShapeDtypeStruct((padded_rows, span), jnp.int16)] * targets,
        in_specs=[SMEM_SPEC] + [VMEM_SPEC] * pieces + [ANY_SPEC] * 4 + [VMEM_SPEC] * 4,
        out_specs=[VMEM_SPEC] * targets,
        scratch_shapes=[pltpu.VMEM(table.shape, jnp.bfloat16) for table in tables]
        + [pltpu.VMEM((pieces, rows, lons), jnp.float32), pltpu.SemaphoreType.DMA((4,))],
        compiler_params=pltpu.CompilerParams(vmem_limit_bytes=VMEM_BYTES),
        cost_estimate=pl.CostEstimate(
            flops=3 * rows * NLON * M, bytes_accessed=6 * 2**20, transcendentals=0
        ),
    )(order, *grids, *tables, places, wave_row, keep_col, sine_col)


def legendre_kernel(pieces, order_ref, *rest):
    fields, rest = rest[:pieces], rest[pieces:]
    table_hbm, lat_hbm, wave_ref, limit_ref, norm_ref, out_ref = rest[:6]
    weight, before, current, level, sums, result, beta_ref, scale_ref, growth_ref = rest[6:15]
    table, lat_ref, sems = rest[15:]
    copies = [pltpu.make_async_copy(lat_hbm, lat_ref, sems.at[pieces])]
    copies[0].start()
    for piece in range(pieces):
        source = table_hbm.at[order_ref[piece]]
        copies.append(pltpu.make_async_copy(source, table.at[piece], sems.at[piece]))
        copies[-1].start()
    half = lat_ref.shape[1]
    lanes = wave_ref.shape[1]
    slots = out_ref.shape[0]
    groups = lanes // LANES
    wave = wave_ref[...]
    odd = wave - 2.0 * jnp.floor(wave * 0.5) > 0.5

    def squares(order):
        degree = wave + order
        return 4.0 * degree * degree - 1.0, 4.0 * order * (degree + wave)

    square, spread = squares(
        lax.broadcasted_iota(jnp.int32, (M, lanes), 0).astype(jnp.float32)
    )
    beta_ref[...] = spread / jnp.maximum(square, 1.0)
    blocks = M // BLOCK
    first_order = lax.broadcasted_iota(jnp.int32, (blocks, lanes), 0).astype(jnp.float32) * BLOCK
    scale = jnp.ones((blocks, lanes), jnp.float32)
    for index in range(BLOCK):
        inside = first_order + index < limit_ref[...]
        scale_ref[pl.ds(index, blocks, stride=BLOCK)] = jnp.where(inside, scale, 0.0)
        square, spread = squares(first_order + (index + 1))
        scale = scale * jnp.sqrt(square / spread)
    growth_ref[...] = scale

    copies[0].wait()
    for group in range(groups):
        cols = slice(group * LANES, (group + 1) * LANES)
        coarse = lat_ref[1] * wave[:, cols]
        whole = jnp.floor(coarse)
        level[:, cols] = whole
        current[:, cols] = jnp.exp2(
            (coarse - whole) + lat_ref[2] * wave[:, cols] + norm_ref[:, cols]
        )
        before[:, cols] = jnp.zeros((half, LANES), jnp.float32)

    padded_rows = fields[0].shape[0]
    totals = [None] * 4
    for piece in range(pieces):
        values = from_int16(fields[piece][...])
        values = values * scale_of(values[padded_rows - 1 :])
        high, low = split_bf16(values)
        copies[1 + piece].wait()
        for kind in range(4):
            rows = pl.ds(kind * half, half)
            value = jnp.dot(table[piece, 0, rows], high, preferred_element_type=jnp.float32)
            value += jnp.dot(table[piece, 0, rows], low, preferred_element_type=jnp.float32)
            value += jnp.dot(table[piece, 1, rows], high, preferred_element_type=jnp.float32)
            totals[kind] = value if piece == 0 else totals[kind] + value
    for parity in range(2):
        for comp in range(2):
            cols = slice(comp * lanes, (comp + 1) * lanes)
            weight[2 * parity + comp] = jnp.where(
                odd, totals[2 + parity][:, cols], totals[parity][:, cols]
            )

    def step(block, carry):
        first = pl.multiple_of(block * BLOCK, 8)
        for group in range(groups):
            cols = slice(group * LANES, (group + 1) * LANES)
            grow = growth_ref[pl.ds(block, 1), cols]
            for chunk in range(half // CHUNK):
                rows = slice(chunk * CHUNK, (chunk + 1) * CHUNK)
                height = level[rows, cols]
                factor = jnp.exp2(height)
                weights = [weight[k, rows, cols] * factor for k in range(4)]
                cosine = lat_ref[0, rows]
                old = before[rows, cols]
                new = current[rows, cols]
                for order in range(BLOCK):
                    for comp in range(2):
                        product = new * weights[2 * (order % 2) + comp]
                        partial = product.reshape(CHUNK // 8, 8, LANES).sum(axis=0)
                        place = pl.ds((order * 2 + comp) * 8, 8)
                        if chunk == 0:
                            sums[place] = partial
                        else:
                            sums[place] += partial
                    beta = beta_ref[pl.ds(first + order, 1), cols]
                    old, new = new, cosine * new - beta * old
                biggest = jnp.maximum(jnp.abs(old), jnp.abs(new)) * grow
                shift = jnp.floor(jnp.log(biggest) * (1.0 / math.log(2.0)))
                factor = grow * jnp.exp2(-shift)
                before[rows, cols] = old * factor
                current[rows, cols] = new * factor
                level[rows, cols] = height + shift
            for comp in range(2):
                total = sums[pl.ds(comp * 8, BLOCK, stride=16)]
                for lane in range(1, 8):
                    total += sums[pl.ds(comp * 8 + lane, BLOCK, stride=16)]
                result[comp, pl.ds(first, BLOCK), cols] = (
                    total * scale_ref[pl.ds(first, BLOCK), cols]
                )
        return carry

    lax.fori_loop(0, M // BLOCK, step, 0)
    for comp in range(2):
        out_ref[:, comp, :] = result[comp].T[:slots]


def legendre(fields, order, slot_wave, rows):
    slots = slot_wave.shape[0]
    pieces = len(fields)
    padded_rows, span = fields[0].shape
    lanes = span // 2
    half = M // 2
    wave_row = jnp.pad(slot_wave, (0, lanes - slots), constant_values=2 * M)[None, :]
    inside_wave = jnp.minimum(wave_row, M - 1).astype(jnp.float32)
    limit = (M - wave_row).astype(jnp.float32)
    counter = np.arange(1, M)[:, None]
    log_terms = (np.log1p(0.5 / counter) / math.log(2.0)).astype(np.float32)
    log_norm = jnp.sum(
        jnp.where(counter.astype(np.float32) <= inside_wave, log_terms, 0.0), axis=0, keepdims=True
    )
    norm = 0.5 * (log_norm - 1.0)
    table = resample_table().reshape(2 * M, pieces, rows).transpose(1, 0, 2)
    table = table_bf16(np.pad(table, ((0, 0), (0, 0), (0, padded_rows - rows))))
    table = table.reshape(pieces, 2 * M, 2, padded_rows).transpose(0, 2, 1, 3)
    latitudes = latitude_table()
    vector = pltpu.VMEM((half, lanes), jnp.float32)
    orders = pltpu.VMEM((M, lanes), jnp.float32)
    return pl.pallas_call(
        functools.partial(legendre_kernel, pieces),
        out_shape=jax.ShapeDtypeStruct((slots, 2, M), jnp.float32),
        in_specs=[SMEM_SPEC] + [VMEM_SPEC] * pieces + [ANY_SPEC] * 2 + [VMEM_SPEC] * 3,
        out_specs=VMEM_SPEC,
        scratch_shapes=[
            pltpu.VMEM((4, half, lanes), jnp.float32),
            vector,
            vector,
            vector,
            pltpu.VMEM((BLOCK * 16, LANES), jnp.float32),
            pltpu.VMEM((2, M, lanes), jnp.float32),
            orders,
            orders,
            pltpu.VMEM((M // BLOCK, lanes), jnp.float32),
            pltpu.VMEM(table.shape, jnp.bfloat16),
            pltpu.VMEM(latitudes.shape, jnp.float32),
            pltpu.SemaphoreType.DMA((pieces + 1,)),
        ],
        compiler_params=pltpu.CompilerParams(vmem_limit_bytes=VMEM_BYTES),
        cost_estimate=pl.CostEstimate(
            flops=7 * half * lanes * M, bytes_accessed=6 * 2**20, transcendentals=0
        ),
    )(order, *fields, table, latitudes, inside_wave, limit, norm)


def shards(tracer, wind_east, wind_north, keep_m, slot_wave):
    rows = tracer.shape[1]
    lat_count = lax.axis_size("lat")
    slots = slot_wave.shape[0] // lat_count
    lanes = -(-slots // LANES) * LANES
    lat_index = lax.axis_index("lat")

    ring = ("lev", "fld")
    level_order, lat_order = partners(ring), partners("lat")
    grids = exchange(advect(tracer, wind_east, wind_north, level_order), ring)

    pad = ((0, 0), (0, 0), (0, lanes - slots))
    waves = jnp.pad(slot_wave.reshape(lat_count, 1, slots), pad, constant_values=2 * M)
    waves = jnp.broadcast_to(waves[lat_order], (lat_count, 2, lanes))
    table_rows = wave_rows()
    spots = np.full(4 * (-(-M // 2 // (2 * LANES)) * 2 * LANES), 4 * M, np.int32)
    for part in range(2):
        spots[table_rows[part]] = np.arange(M) * 2 + part
    columns = (waves * 2 + jnp.array([0, 1], jnp.int32)[None, :, None]).reshape(1, -1)
    places = ((spots[:, None] == columns) & (columns < 2 * M)).astype(jnp.bfloat16)
    row_ids = (lat_index * rows + jnp.arange(rows, dtype=jnp.int32)).astype(jnp.float32)
    sines = jnp.sin(math.pi / NLAT * (row_ids + 0.5)) * math.sqrt(2.0 / NLAT)
    waved = fourier(
        grids, level_order, places, waves.reshape(1, -1), keep_m[:, None], sines[:, None], lat_count
    )
    fields = exchange(waved, "lat")
    my_waves = lax.dynamic_slice_in_dim(slot_wave, lat_index * slots, slots)
    return legendre(fields, lat_order, my_waves, rows)[None]


def solution(mesh):
    return jax.shard_map(
        shards,
        mesh=mesh,
        in_specs=(
            P("member", "lat", ("lev", "fld")),
            P("member", "lat", ("lev", "fld")),
            P("member", "lat", ("lev", "fld")),
            P("lat"),
            P(),
        ),
        out_specs=P(("member", "lev", "fld"), "lat", None, None),
        check_vma=False,
    )
```

```python
import functools
import math

import jax
import jax.numpy as jnp
import numpy as np
from jax import lax
from jax.experimental import pallas as pl
from jax.experimental.pallas import tpu as pltpu
from jax.sharding import PartitionSpec as P

M = 400
NLAT = 800
NLON = 1600
LANES = 128
BLOCK = 40
CHUNK = 40
TOP = 32767.0
WIND_STEP = 1.5 / TOP
VMEM_BYTES = 24 * 2**20
VMEM_SPEC = pl.BlockSpec(memory_space=pltpu.VMEM)
SMEM_SPEC = pl.BlockSpec(memory_space=pltpu.SMEM)
HBM_SPEC = pl.BlockSpec(memory_space=pltpu.HBM)


def split_bf16(values):
    high = values.astype(jnp.bfloat16)
    low = (values - high.astype(jnp.float32)).astype(jnp.bfloat16)
    return high, low


def table_bf16(table):
    high = table.astype(jnp.bfloat16)
    low = (table - high.astype(np.float64)).astype(jnp.bfloat16)
    return np.concatenate([high, low], axis=-1)


def fourier_tables(pieces):
    quarter = NLON // 4
    spots = np.arange(quarter)[:, None]
    factor = 1.0 / math.sqrt(NLON)

    def parts(waves):
        angles = 2.0 * math.pi / NLON * (spots * waves[None, :] % NLON)
        return factor * np.cos(angles), factor * np.sin(angles)

    tables = []
    for first in (0, 2):
        cosine, sine = parts(np.arange(first, M, 4))
        tables.append([cosine, -sine])
    waves = np.arange(1, M, 2)
    sign = np.where(waves % 4 == 1, 1.0, -1.0)[None, :]
    cosine, sine = parts(waves)
    tables.append([cosine, -sine])
    tables.append([-sign * sine, -sign * cosine])
    share = pieces // 4
    result = []
    for columns in tables:
        table = np.concatenate(columns, axis=1)
        table = np.pad(table, ((0, 0), (0, -table.shape[1] % (2 * LANES))))
        result.append(table.reshape(share, quarter // share, table.shape[1]))
    return result


def wave_rows():
    quarter_width = -(-M // 2 // (2 * LANES)) * 2 * LANES
    waves = np.arange(M)
    quarter_count, half_count = M // 4, M // 2
    rows = []
    for part in range(2):
        even = np.where(waves % 4 == 0, 0, quarter_width) + part * quarter_count + waves // 4
        odd = 2 * quarter_width + part * half_count + waves // 2
        rows.append(np.where(waves % 2 == 0, even, odd))
    return np.stack(rows).astype(np.int32)


def resample_table():
    half = M // 2
    coarse = math.pi / M * (np.arange(M) + 0.5)
    fine = math.pi / NLAT * (np.arange(NLAT) + 0.5)
    waves = np.arange(M)
    weight = np.where(waves == 0, 1.0, 2.0) / M
    even = (np.cos(np.outer(coarse, waves)) * weight) @ np.cos(np.outer(waves, fine))
    odd = (np.sin(np.outer(coarse, waves)) * weight) @ np.sin(np.outer(waves, fine))
    rows = []
    for full in (even, odd):
        for sign in (1.0, -1.0):
            rows.append(full[:half] + sign * full[::-1][:half])
    return np.concatenate(rows, axis=0)


def latitude_table():
    half = M // 2
    angles = math.pi / M * (np.arange(half) + 0.5)
    log_sine = np.log2(np.sin(angles))
    coarse = np.round(log_sine * 1024.0) / 1024.0
    rows = np.stack([2.0 * np.cos(angles), coarse, log_sine - coarse])
    return np.broadcast_to(rows[:, :, None], (3, half, LANES)).astype(np.float32)


def scale_code(biggest):
    wanted = jnp.maximum(biggest, 1e-30) * (1.0 / TOP)
    exponent = jnp.floor(jnp.log(wanted) * (1.0 / math.log(2.0)))
    return exponent * 128.0 + jnp.ceil((wanted * jnp.exp2(-exponent) - 1.0) * 128.0)


def scale_of(code):
    exponent = jnp.floor(code * (1.0 / 128.0))
    rest = code - 128.0 * exponent
    return jnp.exp2(exponent) * (1.0 + rest * (1.0 / 128.0))


def coded(values, inverse):
    return jnp.floor(values * inverse + 0.5)


def as_int16(values):
    return values.astype(jnp.int32).astype(jnp.int16)


def from_int16(codes):
    return codes.astype(jnp.int32).astype(jnp.float32)


def partners(axis):
    count = lax.axis_size(axis)
    order = jnp.arange(count, dtype=jnp.int32)
    return lax.axis_index(axis).astype(jnp.int32) ^ order if count == 4 else order


def exchange(blocks, axis):
    count = len(blocks)
    if count != 4:
        return list(lax.all_to_all(jnp.stack(blocks), axis, split_axis=0, concat_axis=0, tiled=True))
    pairs = [[(i, i ^ step) for i in range(count)] for step in range(count)]
    return [blocks[0]] + [lax.ppermute(blocks[step], axis, pairs[step]) for step in range(1, count)]


def advect_kernel(order_ref, tracer_hbm, east_hbm, north_hbm, *rest):
    levels, rows, lons = tracer_hbm.shape
    outs, rest = rest[:levels], rest[levels:]
    first_row, last_row, row_wind, tracer, east_wind, north_wind, sems = rest
    copies = []
    for step in range(levels):
        level = order_ref[step]
        copies.append(
            [
                pltpu.make_async_copy(source.at[level], target.at[step], sems.at[step, kind])
                for kind, (source, target) in enumerate(
                    ((tracer_hbm, tracer), (east_hbm, east_wind), (north_hbm, north_wind))
                )
            ]
        )
        for copy in copies[-1]:
            copy.start()
    end = (lons - 1) // LANES * LANES
    spare = lons - end
    lane = lax.broadcasted_iota(jnp.int32, (rows, LANES), 1)
    for step in range(levels):
        level = order_ref[step]
        for copy in copies[step]:
            copy.wait()
        field = tracer[step].astype(jnp.float32)
        first_row[level] = field[:1]
        last_row[level] = field[rows - 1 :]
        blank = jnp.zeros((rows, 1), jnp.float32)
        west = jnp.concatenate([blank, field[:, :-1]], axis=1)
        east = jnp.concatenate([field[:, 1:], blank], axis=1)
        blank = jnp.zeros((1, lons), jnp.float32)
        north = jnp.concatenate([blank, field[:-1]], axis=0)
        south = jnp.concatenate([field[1:], blank], axis=0)
        eastward = 0.5 * east_wind[step].astype(jnp.float32)
        northward = 0.5 * north_wind[step].astype(jnp.float32)
        row_wind[step, :1] = northward[:1]
        row_wind[step, 1:2] = -northward[rows - 1 :]
        moved = field - eastward * (east - west) - northward * (south - north)
        first, last = field[:, :1], field[:, lons - 1 :]
        biggest = jnp.max(jnp.abs(moved), axis=1, keepdims=True)
        biggest = jnp.maximum(biggest, jnp.maximum(jnp.abs(first), jnp.abs(last)))
        code = scale_code(biggest)
        inverse = 1.0 / scale_of(code)
        filler = jnp.zeros((rows, LANES - spare), jnp.float32)
        tile = jnp.concatenate([moved[:, end:], filler], axis=1)
        tile = jnp.where(lane == spare + 1, first, jnp.where(lane == spare + 2, last, tile))
        tile = coded(tile, inverse)
        tile = jnp.where(lane == spare, code, tile)
        winds = jnp.where(lane == spare + 3, eastward[:, :1], eastward[:, lons - 1 :])
        winds = coded(winds, 1.0 / WIND_STEP)
        tile = jnp.where((lane == spare + 3) | (lane == spare + 4), winds, tile)
        outs[step][:, :end] = as_int16(coded(moved[:, :end], inverse))
        outs[step][:, end:] = as_int16(tile)


def advect(tracer, east_wind, north_wind, order):
    levels, rows, lons = tracer.shape
    width = (lons - 1) // LANES * LANES + LANES
    held = pltpu.VMEM((levels, rows, lons), jnp.bfloat16)
    row = jax.ShapeDtypeStruct((levels, 1, lons), jnp.float32)
    result = pl.pallas_call(
        advect_kernel,
        out_shape=[jax.ShapeDtypeStruct((rows, width), jnp.int16)] * levels
        + [row, row, jax.ShapeDtypeStruct((levels, 2, lons), jnp.float32)],
        in_specs=[SMEM_SPEC] + [HBM_SPEC] * 3,
        out_specs=[VMEM_SPEC] * (levels + 3),
        scratch_shapes=[held, held, held, pltpu.SemaphoreType.DMA((levels, 3))],
        compiler_params=pltpu.CompilerParams(vmem_limit_bytes=VMEM_BYTES),
        cost_estimate=pl.CostEstimate(
            flops=20 * levels * rows * lons, bytes_accessed=8 * levels * rows * lons, transcendentals=0
        ),
    )(order, tracer, east_wind, north_wind)
    return result[:levels], result[levels:]


def halo_kernel(order_ref, above_ref, below_ref, row_wind, *outs):
    for step, out_ref in enumerate(outs):
        level = order_ref[step]
        out_ref[:1] = row_wind[step, :1] * above_ref[level]
        out_ref[1:] = row_wind[step, 1:2] * below_ref[level]


def halo(order, first_row, last_row, row_wind):
    levels, _, lons = first_row.shape
    count = lax.axis_size("lat")
    above = lax.ppermute(last_row, "lat", [(i, i + 1) for i in range(count - 1)])
    below = lax.ppermute(first_row, "lat", [(i + 1, i) for i in range(count - 1)])
    return pl.pallas_call(
        halo_kernel,
        out_shape=[jax.ShapeDtypeStruct((2, lons), jnp.float32)] * levels,
        in_specs=[SMEM_SPEC] + [VMEM_SPEC] * 3,
        out_specs=[VMEM_SPEC] * levels,
    )(order, above, below, row_wind)


def fourier_kernel(pieces, targets, order_ref, *rest):
    grids, halos, rest = rest[:pieces], rest[pieces : 2 * pieces], rest[2 * pieces :]
    tables_hbm, (place_ref, wave_ref, keep_ref, sine_ref), rest = rest[:4], rest[4:8], rest[8:]
    outs, rest = rest[:targets], rest[targets:]
    tables, (field, sems) = rest[:4], rest[4:]
    _, rows, width = field.shape
    lons = tables[0].shape[1]
    share = pieces // 4
    copies = []
    for kind in range(4):
        copies.append(pltpu.make_async_copy(tables_hbm[kind], tables[kind], sems.at[kind]))
        copies[-1].start()

    end = width - LANES
    spare = lons - end
    lane = lax.broadcasted_iota(jnp.int32, (rows, LANES), 1)
    winds = (lane == spare + 3) | (lane == spare + 4)
    for piece in range(pieces):
        spot = order_ref[piece]
        values = from_int16(grids[piece][...])
        tile = values[:, end:]
        scale = scale_of(tile[:, spare : spare + 1])
        field[spot, :, :end] = values[:, :end] * scale
        field[spot, :, end:] = tile * jnp.where(winds, WIND_STEP, scale)
        field[spot, :1, :lons] += halos[piece][:1]
        field[spot, rows - 1 :, :lons] += halos[piece][1:]
    for spot in range(pieces):
        tile = field[spot, :, end:]
        before = field[(spot - 1) % pieces, :, end:]
        after = field[(spot + 1) % pieces, :, end:]
        shift = LANES - spare
        gain = pltpu.roll(tile, shift - 3, 1) * pltpu.roll(before, shift - 2, 1)
        loss = pltpu.roll(tile, LANES - 5, 1) * pltpu.roll(after, LANES - 2, 1)
        field[spot, :, end:] = tile - jnp.where(lane == spare - 1, loss, 0.0)
        field[spot, :, :LANES] += jnp.where(lane == 0, gain, 0.0)

    def product(value, table, spot):
        high, low = split_bf16(value)
        width = table.shape[2] // 2
        both = jnp.dot(high, table[spot], preferred_element_type=jnp.float32)
        part = jnp.dot(low, table[spot, :, :width], preferred_element_type=jnp.float32)
        return part + both[:, :width] + both[:, width:]

    sums = [None, None, None]
    for spot in range(share):
        quarters = [field[quarter * share + spot, :, :lons] for quarter in range(4)]
        sum02, dif02 = quarters[0] + quarters[2], quarters[0] - quarters[2]
        sum13, dif13 = quarters[1] + quarters[3], quarters[1] - quarters[3]
        parts = []
        for kind, value in enumerate((sum02 + sum13, sum02 - sum13, dif02, dif13)):
            if spot == 0:
                copies[kind].wait()
            parts.append(product(value, tables[kind], spot))
        parts = [parts[0], parts[1], parts[2] + parts[3]]
        sums = [part if total is None else total + part for total, part in zip(sums, parts)]
    placed = None
    first = 0
    for total in sums:
        last = first + total.shape[1]
        high, low = split_bf16(total)
        part = jnp.dot(high, place_ref[first:last], preferred_element_type=jnp.float32)
        part += jnp.dot(low, place_ref[first:last], preferred_element_type=jnp.float32)
        placed = part if placed is None else placed + part
        first = last
    kept = jnp.where(wave_ref[...] < keep_ref[...], placed * sine_ref[...], 0.0)
    code = scale_code(jnp.max(jnp.abs(kept), axis=0, keepdims=True))
    steps = coded(kept, 1.0 / scale_of(code))
    padded_rows, span = outs[0].shape
    codes = jnp.broadcast_to(code, (padded_rows - rows, code.shape[1]))
    result = as_int16(jnp.concatenate([steps, codes], axis=0))
    for target in range(targets):
        outs[target][...] = result[:, target * span : (target + 1) * span]


def fourier(grids, halos, order, places, wave_row, keep_col, sine_col, targets):
    pieces = len(grids)
    rows, width = grids[0].shape
    lons = NLON // pieces
    span = wave_row.shape[1] // targets
    padded_rows = -(-(rows + 1) // 16) * 16
    tables = [table_bf16(table) for table in fourier_tables(pieces)]
    return pl.pallas_call(
        functools.partial(fourier_kernel, pieces, targets),
        out_shape=[jax.ShapeDtypeStruct((padded_rows, span), jnp.int16)] * targets,
        in_specs=[SMEM_SPEC] + [VMEM_SPEC] * (2 * pieces) + [HBM_SPEC] * 4 + [VMEM_SPEC] * 4,
        out_specs=[VMEM_SPEC] * targets,
        scratch_shapes=[pltpu.VMEM(table.shape, jnp.bfloat16) for table in tables]
        + [pltpu.VMEM((pieces, rows, width), jnp.float32), pltpu.SemaphoreType.DMA((4,))],
        compiler_params=pltpu.CompilerParams(vmem_limit_bytes=VMEM_BYTES),
        cost_estimate=pl.CostEstimate(
            flops=3 * rows * NLON * M, bytes_accessed=6 * 2**20, transcendentals=0
        ),
    )(order, *grids, *halos, *tables, places, wave_row, keep_col, sine_col)


def legendre_kernel(pieces, order_ref, *rest):
    fields, rest = rest[:pieces], rest[pieces:]
    table_hbm, lat_hbm, wave_ref, limit_ref, norm_ref, out_ref = rest[:6]
    weight, before, current, level, sums, result, beta_ref, scale_ref, growth_ref = rest[6:15]
    table, lat_ref, sems = rest[15:]
    copies = [pltpu.make_async_copy(lat_hbm, lat_ref, sems.at[pieces])]
    copies[0].start()
    for piece in range(pieces):
        source = table_hbm.at[order_ref[piece]]
        copies.append(pltpu.make_async_copy(source, table.at[piece], sems.at[piece]))
        copies[-1].start()
    half = lat_ref.shape[1]
    lanes = wave_ref.shape[1]
    slots = out_ref.shape[0]
    groups = lanes // LANES
    wave = wave_ref[...]
    odd = wave - 2.0 * jnp.floor(wave * 0.5) > 0.5

    def squares(order):
        degree = wave + order
        return 4.0 * degree * degree - 1.0, 4.0 * order * (degree + wave)

    square, spread = squares(
        lax.broadcasted_iota(jnp.int32, (M, lanes), 0).astype(jnp.float32)
    )
    beta_ref[...] = spread / jnp.maximum(square, 1.0)
    blocks = M // BLOCK
    first_order = lax.broadcasted_iota(jnp.int32, (blocks, lanes), 0).astype(jnp.float32) * BLOCK
    scale = jnp.ones((blocks, lanes), jnp.float32)
    for index in range(BLOCK):
        inside = first_order + index < limit_ref[...]
        scale_ref[pl.ds(index, blocks, stride=BLOCK)] = jnp.where(inside, scale, 0.0)
        square, spread = squares(first_order + (index + 1))
        scale = scale * jnp.sqrt(square / spread)
    growth_ref[...] = scale

    copies[0].wait()
    for group in range(groups):
        cols = slice(group * LANES, (group + 1) * LANES)
        coarse = lat_ref[1] * wave[:, cols]
        whole = jnp.floor(coarse)
        level[:, cols] = whole
        current[:, cols] = jnp.exp2(
            (coarse - whole) + lat_ref[2] * wave[:, cols] + norm_ref[:, cols]
        )
        before[:, cols] = jnp.zeros((half, LANES), jnp.float32)

    padded_rows = fields[0].shape[0]
    totals = [None] * 4
    for piece in range(pieces):
        values = from_int16(fields[piece][...])
        values = values * scale_of(values[padded_rows - 1 :])
        high, low = split_bf16(values)
        copies[1 + piece].wait()
        for kind in range(4):
            rows = pl.ds(kind * half, half)
            value = jnp.dot(table[piece, 0, rows], high, preferred_element_type=jnp.float32)
            value += jnp.dot(table[piece, 0, rows], low, preferred_element_type=jnp.float32)
            value += jnp.dot(table[piece, 1, rows], high, preferred_element_type=jnp.float32)
            totals[kind] = value if piece == 0 else totals[kind] + value
    for parity in range(2):
        for comp in range(2):
            cols = slice(comp * lanes, (comp + 1) * lanes)
            weight[2 * parity + comp] = jnp.where(
                odd, totals[2 + parity][:, cols], totals[parity][:, cols]
            )

    def step(block, carry):
        first = pl.multiple_of(block * BLOCK, 8)
        for group in range(groups):
            cols = slice(group * LANES, (group + 1) * LANES)
            grow = growth_ref[pl.ds(block, 1), cols]
            for chunk in range(half // CHUNK):
                rows = slice(chunk * CHUNK, (chunk + 1) * CHUNK)
                height = level[rows, cols]
                factor = jnp.exp2(height)
                weights = [weight[k, rows, cols] * factor for k in range(4)]
                cosine = lat_ref[0, rows]
                old = before[rows, cols]
                new = current[rows, cols]
                for order in range(BLOCK):
                    for comp in range(2):
                        product = new * weights[2 * (order % 2) + comp]
                        partial = product.reshape(CHUNK // 8, 8, LANES).sum(axis=0)
                        place = pl.ds((order * 2 + comp) * 8, 8)
                        if chunk == 0:
                            sums[place] = partial
                        else:
                            sums[place] += partial
                    beta = beta_ref[pl.ds(first + order, 1), cols]
                    old, new = new, cosine * new - beta * old
                biggest = jnp.maximum(jnp.abs(old), jnp.abs(new)) * grow
                shift = jnp.floor(jnp.log(biggest) * (1.0 / math.log(2.0)))
                factor = grow * jnp.exp2(-shift)
                before[rows, cols] = old * factor
                current[rows, cols] = new * factor
                level[rows, cols] = height + shift
            for comp in range(2):
                total = sums[pl.ds(comp * 8, BLOCK, stride=16)]
                for lane in range(1, 8):
                    total += sums[pl.ds(comp * 8 + lane, BLOCK, stride=16)]
                result[comp, pl.ds(first, BLOCK), cols] = (
                    total * scale_ref[pl.ds(first, BLOCK), cols]
                )
        return carry

    lax.fori_loop(0, M // BLOCK, step, 0)
    for comp in range(2):
        out_ref[:, comp, :] = result[comp].T[:slots]


def legendre(fields, order, slot_wave, rows):
    slots = slot_wave.shape[0]
    pieces = len(fields)
    padded_rows, span = fields[0].shape
    lanes = span // 2
    half = M // 2
    wave_row = jnp.pad(slot_wave, (0, lanes - slots), constant_values=2 * M)[None, :]
    inside_wave = jnp.minimum(wave_row, M - 1).astype(jnp.float32)
    limit = (M - wave_row).astype(jnp.float32)
    counter = np.arange(1, M)[:, None]
    log_terms = (np.log1p(0.5 / counter) / math.log(2.0)).astype(np.float32)
    log_norm = jnp.sum(
        jnp.where(counter.astype(np.float32) <= inside_wave, log_terms, 0.0), axis=0, keepdims=True
    )
    norm = 0.5 * (log_norm - 1.0)
    table = resample_table().reshape(2 * M, pieces, rows).transpose(1, 0, 2)
    table = table_bf16(np.pad(table, ((0, 0), (0, 0), (0, padded_rows - rows))))
    table = table.reshape(pieces, 2 * M, 2, padded_rows).transpose(0, 2, 1, 3)
    latitudes = latitude_table()
    vector = pltpu.VMEM((half, lanes), jnp.float32)
    orders = pltpu.VMEM((M, lanes), jnp.float32)
    return pl.pallas_call(
        functools.partial(legendre_kernel, pieces),
        out_shape=jax.ShapeDtypeStruct((slots, 2, M), jnp.float32),
        in_specs=[SMEM_SPEC] + [VMEM_SPEC] * pieces + [HBM_SPEC] * 2 + [VMEM_SPEC] * 3,
        out_specs=VMEM_SPEC,
        scratch_shapes=[
            pltpu.VMEM((4, half, lanes), jnp.float32),
            vector,
            vector,
            vector,
            pltpu.VMEM((BLOCK * 16, LANES), jnp.float32),
            pltpu.VMEM((2, M, lanes), jnp.float32),
            orders,
            orders,
            pltpu.VMEM((M // BLOCK, lanes), jnp.float32),
            pltpu.VMEM(table.shape, jnp.bfloat16),
            pltpu.VMEM(latitudes.shape, jnp.float32),
            pltpu.SemaphoreType.DMA((pieces + 1,)),
        ],
        compiler_params=pltpu.CompilerParams(vmem_limit_bytes=VMEM_BYTES),
        cost_estimate=pl.CostEstimate(
            flops=7 * half * lanes * M, bytes_accessed=6 * 2**20, transcendentals=0
        ),
    )(order, *fields, table, latitudes, inside_wave, limit, norm)


def shards(tracer, wind_east, wind_north, keep_m, slot_wave):
    rows = tracer.shape[1]
    lat_count = lax.axis_size("lat")
    slots = slot_wave.shape[0] // lat_count
    lanes = -(-slots // LANES) * LANES
    lat_index = lax.axis_index("lat")

    ring = ("lev", "fld")
    level_order, lat_order = partners(ring), partners("lat")
    blocks, edges = advect(tracer, wind_east, wind_north, level_order)
    blocks, slot_wave, keep_m = lax.optimization_barrier((blocks, slot_wave, keep_m))
    grids = exchange(blocks, ring)
    halos = exchange(halo(level_order, *edges), ring)

    pad = ((0, 0), (0, 0), (0, lanes - slots))
    waves = jnp.pad(slot_wave.reshape(lat_count, 1, slots), pad, constant_values=2 * M)
    waves = jnp.broadcast_to(waves[lat_order], (lat_count, 2, lanes))
    table_rows = wave_rows()
    spots = np.full(4 * (-(-M // 2 // (2 * LANES)) * 2 * LANES), 4 * M, np.int32)
    for part in range(2):
        spots[table_rows[part]] = np.arange(M) * 2 + part
    columns = (waves * 2 + jnp.array([0, 1], jnp.int32)[None, :, None]).reshape(1, -1)
    places = ((spots[:, None] == columns) & (columns < 2 * M)).astype(jnp.bfloat16)
    row_ids = (lat_index * rows + jnp.arange(rows, dtype=jnp.int32)).astype(jnp.float32)
    sines = jnp.sin(math.pi / NLAT * (row_ids + 0.5)) * math.sqrt(2.0 / NLAT)
    waved = fourier(
        grids, halos, level_order, places, waves.reshape(1, -1), keep_m[:, None], sines[:, None], lat_count
    )
    fields = exchange(waved, "lat")
    my_waves = lax.dynamic_slice_in_dim(slot_wave, lat_index * slots, slots)
    return legendre(fields, lat_order, my_waves, rows)[None]


def solution(mesh):
    return jax.shard_map(
        shards,
        mesh=mesh,
        in_specs=(
            P("member", "lat", ("lev", "fld")),
            P("member", "lat", ("lev", "fld")),
            P("member", "lat", ("lev", "fld")),
            P("lat"),
            P(),
        ),
        out_specs=P(("member", "lev", "fld"), "lat", None, None),
        check_vma=False,
    )
```

```python
import functools
import math

import jax
import jax.numpy as jnp
import numpy as np
from jax import lax
from jax.experimental import pallas as pl
from jax.experimental.pallas import tpu as pltpu
from jax.sharding import PartitionSpec as P

M = 400
NLAT = 800
NLON = 1600
LANES = 128
BLOCK = 40
CHUNK = 40
TOP = 32767.0
WIND_STEP = 1.5 / TOP
VMEM_BYTES = 60 * 2**20
VMEM_SPEC = pl.BlockSpec(memory_space=pltpu.VMEM)
SMEM_SPEC = pl.BlockSpec(memory_space=pltpu.SMEM)
HBM_SPEC = pl.BlockSpec(memory_space=pltpu.HBM)


def split_bf16(values):
    high = values.astype(jnp.bfloat16)
    low = (values - high.astype(jnp.float32)).astype(jnp.bfloat16)
    return high, low


def table_bf16(table):
    high = table.astype(jnp.bfloat16)
    low = (table - high.astype(np.float64)).astype(jnp.bfloat16)
    return np.concatenate([high, low], axis=-1)


def fourier_tables(pieces):
    quarter = NLON // 4
    spots = np.arange(quarter)[:, None]
    factor = 1.0 / math.sqrt(NLON)

    def parts(waves):
        angles = 2.0 * math.pi / NLON * (spots * waves[None, :] % NLON)
        return factor * np.cos(angles), factor * np.sin(angles)

    tables = []
    for first in (0, 2):
        cosine, sine = parts(np.arange(first, M, 4))
        tables.append([cosine, -sine])
    waves = np.arange(1, M, 2)
    sign = np.where(waves % 4 == 1, 1.0, -1.0)[None, :]
    cosine, sine = parts(waves)
    tables.append([cosine, -sine])
    tables.append([-sign * sine, -sign * cosine])
    share = pieces // 4
    result = []
    for columns in tables:
        table = np.concatenate(columns, axis=1)
        table = np.pad(table, ((0, 0), (0, -table.shape[1] % (2 * LANES))))
        result.append(table.reshape(share, quarter // share, table.shape[1]))
    return result


def wave_rows():
    quarter_width = -(-M // 2 // (2 * LANES)) * 2 * LANES
    waves = np.arange(M)
    quarter_count, half_count = M // 4, M // 2
    rows = []
    for part in range(2):
        even = np.where(waves % 4 == 0, 0, quarter_width) + part * quarter_count + waves // 4
        odd = 2 * quarter_width + part * half_count + waves // 2
        rows.append(np.where(waves % 2 == 0, even, odd))
    return np.stack(rows).astype(np.int32)


def resample_table():
    half = M // 2
    coarse = math.pi / M * (np.arange(M) + 0.5)
    fine = math.pi / NLAT * (np.arange(NLAT) + 0.5)
    waves = np.arange(M)
    weight = np.where(waves == 0, 1.0, 2.0) / M
    even = (np.cos(np.outer(coarse, waves)) * weight) @ np.cos(np.outer(waves, fine))
    odd = (np.sin(np.outer(coarse, waves)) * weight) @ np.sin(np.outer(waves, fine))
    rows = []
    for full in (even, odd):
        for sign in (1.0, -1.0):
            rows.append(full[:half] + sign * full[::-1][:half])
    return np.concatenate(rows, axis=0)


def latitude_table():
    half = M // 2
    angles = math.pi / M * (np.arange(half) + 0.5)
    log_sine = np.log2(np.sin(angles))
    coarse = np.round(log_sine * 1024.0) / 1024.0
    rows = np.stack([2.0 * np.cos(angles), coarse, log_sine - coarse])
    return np.broadcast_to(rows[:, :, None], (3, half, LANES)).astype(np.float32)


def scale_code(biggest):
    wanted = jnp.maximum(biggest, 1e-30) * (1.0 / TOP)
    exponent = jnp.floor(jnp.log(wanted) * (1.0 / math.log(2.0)))
    return exponent * 128.0 + jnp.ceil((wanted * jnp.exp2(-exponent) - 1.0) * 128.0)


def scale_of(code):
    exponent = jnp.floor(code * (1.0 / 128.0))
    rest = code - 128.0 * exponent
    return jnp.exp2(exponent) * (1.0 + rest * (1.0 / 128.0))


def coded(values, inverse):
    return jnp.floor(values * inverse + 0.5)


def as_int16(values):
    return values.astype(jnp.int32).astype(jnp.int16)


def from_int16(codes):
    return codes.astype(jnp.int32).astype(jnp.float32)


def partners(axis):
    count = lax.axis_size(axis)
    order = jnp.arange(count, dtype=jnp.int32)
    return lax.axis_index(axis).astype(jnp.int32) ^ order if count == 4 else order


def exchange(blocks, axis):
    count = len(blocks)
    if count != 4:
        return list(lax.all_to_all(jnp.stack(blocks), axis, split_axis=0, concat_axis=0, tiled=True))
    pairs = [[(i, i ^ step) for i in range(count)] for step in range(count)]
    return [blocks[0]] + [lax.ppermute(blocks[step], axis, pairs[step]) for step in range(1, count)]


def advect_kernel(order_ref, tracer_hbm, east_hbm, north_hbm, *rest):
    levels, rows, lons = tracer_hbm.shape
    outs, rest = rest[:levels], rest[levels:]
    first_row, last_row, row_wind, tracer, east_wind, north_wind, sems = rest
    copies = []
    for step in range(levels):
        level = order_ref[step]
        copies.append(
            [
                pltpu.make_async_copy(source.at[level], target.at[step], sems.at[step, kind])
                for kind, (source, target) in enumerate(
                    ((tracer_hbm, tracer), (east_hbm, east_wind), (north_hbm, north_wind))
                )
            ]
        )
        for copy in copies[-1]:
            copy.start()
    end = (lons - 1) // LANES * LANES
    spare = lons - end
    lane = lax.broadcasted_iota(jnp.int32, (rows, LANES), 1)
    for step in range(levels):
        level = order_ref[step]
        for copy in copies[step]:
            copy.wait()
        field = tracer[step].astype(jnp.float32)
        first_row[level] = field[:1]
        last_row[level] = field[rows - 1 :]
        blank = jnp.zeros((rows, 1), jnp.float32)
        west = jnp.concatenate([blank, field[:, :-1]], axis=1)
        east = jnp.concatenate([field[:, 1:], blank], axis=1)
        blank = jnp.zeros((1, lons), jnp.float32)
        north = jnp.concatenate([blank, field[:-1]], axis=0)
        south = jnp.concatenate([field[1:], blank], axis=0)
        eastward = 0.5 * east_wind[step].astype(jnp.float32)
        northward = 0.5 * north_wind[step].astype(jnp.float32)
        row_wind[step, :1] = northward[:1]
        row_wind[step, 1:2] = -northward[rows - 1 :]
        moved = field - eastward * (east - west) - northward * (south - north)
        first, last = field[:, :1], field[:, lons - 1 :]
        biggest = jnp.max(jnp.abs(moved), axis=1, keepdims=True)
        biggest = jnp.maximum(biggest, jnp.maximum(jnp.abs(first), jnp.abs(last)))
        code = scale_code(biggest)
        inverse = 1.0 / scale_of(code)
        filler = jnp.zeros((rows, LANES - spare), jnp.float32)
        tile = jnp.concatenate([moved[:, end:], filler], axis=1)
        tile = jnp.where(lane == spare + 1, first, jnp.where(lane == spare + 2, last, tile))
        tile = coded(tile, inverse)
        tile = jnp.where(lane == spare, code, tile)
        winds = jnp.where(lane == spare + 3, eastward[:, :1], eastward[:, lons - 1 :])
        winds = coded(winds, 1.0 / WIND_STEP)
        tile = jnp.where((lane == spare + 3) | (lane == spare + 4), winds, tile)
        outs[step][:, :end] = as_int16(coded(moved[:, :end], inverse))
        outs[step][:, end:] = as_int16(tile)


def advect(tracer, east_wind, north_wind, order):
    levels, rows, lons = tracer.shape
    width = (lons - 1) // LANES * LANES + LANES
    held = pltpu.VMEM((levels, rows, lons), jnp.bfloat16)
    row = jax.ShapeDtypeStruct((levels, 1, lons), jnp.float32)
    result = pl.pallas_call(
        advect_kernel,
        out_shape=[jax.ShapeDtypeStruct((rows, width), jnp.int16)] * levels
        + [row, row, jax.ShapeDtypeStruct((levels, 2, lons), jnp.float32)],
        in_specs=[SMEM_SPEC] + [HBM_SPEC] * 3,
        out_specs=[VMEM_SPEC] * (levels + 3),
        scratch_shapes=[held, held, held, pltpu.SemaphoreType.DMA((levels, 3))],
        compiler_params=pltpu.CompilerParams(vmem_limit_bytes=VMEM_BYTES),
        cost_estimate=pl.CostEstimate(
            flops=20 * levels * rows * lons, bytes_accessed=8 * levels * rows * lons, transcendentals=0
        ),
    )(order, tracer, east_wind, north_wind)
    return result[:levels], result[levels:]


def halo_kernel(order_ref, above_ref, below_ref, row_wind, *outs):
    for step, out_ref in enumerate(outs):
        level = order_ref[step]
        out_ref[:1] = row_wind[step, :1] * above_ref[level]
        out_ref[1:] = row_wind[step, 1:2] * below_ref[level]


def halo(order, first_row, last_row, row_wind):
    levels, _, lons = first_row.shape
    count = lax.axis_size("lat")
    above = lax.ppermute(last_row, "lat", [(i, i + 1) for i in range(count - 1)])
    below = lax.ppermute(first_row, "lat", [(i + 1, i) for i in range(count - 1)])
    return pl.pallas_call(
        halo_kernel,
        out_shape=[jax.ShapeDtypeStruct((2, lons), jnp.float32)] * levels,
        in_specs=[SMEM_SPEC] + [VMEM_SPEC] * 3,
        out_specs=[VMEM_SPEC] * levels,
    )(order, above, below, row_wind)


def fourier_kernel(pieces, targets, order_ref, *rest):
    grids, halos, rest = rest[:pieces], rest[pieces : 2 * pieces], rest[2 * pieces :]
    tables_hbm, (place_ref, wave_ref, keep_ref, sine_ref), rest = rest[:4], rest[4:8], rest[8:]
    outs, rest = rest[:targets], rest[targets:]
    tables, (field, sems) = rest[:4], rest[4:]
    _, rows, width = field.shape
    lons = tables[0].shape[1]
    share = pieces // 4
    copies = []
    for kind in range(4):
        copies.append(pltpu.make_async_copy(tables_hbm[kind], tables[kind], sems.at[kind]))
        copies[-1].start()

    end = width - LANES
    spare = lons - end
    lane = lax.broadcasted_iota(jnp.int32, (rows, LANES), 1)
    winds = (lane == spare + 3) | (lane == spare + 4)
    for piece in range(pieces):
        spot = order_ref[piece]
        values = from_int16(grids[piece][...])
        tile = values[:, end:]
        scale = scale_of(tile[:, spare : spare + 1])
        field[spot, :, :end] = values[:, :end] * scale
        field[spot, :, end:] = tile * jnp.where(winds, WIND_STEP, scale)
        field[spot, :1, :lons] += halos[piece][:1]
        field[spot, rows - 1 :, :lons] += halos[piece][1:]
    for spot in range(pieces):
        tile = field[spot, :, end:]
        before = field[(spot - 1) % pieces, :, end:]
        after = field[(spot + 1) % pieces, :, end:]
        shift = LANES - spare
        gain = pltpu.roll(tile, shift - 3, 1) * pltpu.roll(before, shift - 2, 1)
        loss = pltpu.roll(tile, LANES - 5, 1) * pltpu.roll(after, LANES - 2, 1)
        field[spot, :, end:] = tile - jnp.where(lane == spare - 1, loss, 0.0)
        field[spot, :, :LANES] += jnp.where(lane == 0, gain, 0.0)

    def product(value, table, spot):
        high, low = split_bf16(value)
        width = table.shape[2] // 2
        both = jnp.dot(high, table[spot], preferred_element_type=jnp.float32)
        part = jnp.dot(low, table[spot, :, :width], preferred_element_type=jnp.float32)
        return part + both[:, :width] + both[:, width:]

    sums = [None, None, None]
    for spot in range(share):
        quarters = [field[quarter * share + spot, :, :lons] for quarter in range(4)]
        sum02, dif02 = quarters[0] + quarters[2], quarters[0] - quarters[2]
        sum13, dif13 = quarters[1] + quarters[3], quarters[1] - quarters[3]
        parts = []
        for kind, value in enumerate((sum02 + sum13, sum02 - sum13, dif02, dif13)):
            if spot == 0:
                copies[kind].wait()
            parts.append(product(value, tables[kind], spot))
        parts = [parts[0], parts[1], parts[2] + parts[3]]
        sums = [part if total is None else total + part for total, part in zip(sums, parts)]
    placed = None
    first = 0
    for total in sums:
        last = first + total.shape[1]
        high, low = split_bf16(total)
        part = jnp.dot(high, place_ref[first:last], preferred_element_type=jnp.float32)
        part += jnp.dot(low, place_ref[first:last], preferred_element_type=jnp.float32)
        placed = part if placed is None else placed + part
        first = last
    kept = jnp.where(wave_ref[...] < keep_ref[...], placed * sine_ref[...], 0.0)
    code = scale_code(jnp.max(jnp.abs(kept), axis=0, keepdims=True))
    steps = coded(kept, 1.0 / scale_of(code))
    padded_rows, span = outs[0].shape
    codes = jnp.broadcast_to(code, (padded_rows - rows, code.shape[1]))
    result = as_int16(jnp.concatenate([steps, codes], axis=0))
    for target in range(targets):
        outs[target][...] = result[:, target * span : (target + 1) * span]


def fourier(grids, halos, order, places, wave_row, keep_col, sine_col, targets):
    pieces = len(grids)
    rows, width = grids[0].shape
    lons = NLON // pieces
    span = wave_row.shape[1] // targets
    padded_rows = -(-(rows + 1) // 16) * 16
    tables = [table_bf16(table) for table in fourier_tables(pieces)]
    return pl.pallas_call(
        functools.partial(fourier_kernel, pieces, targets),
        out_shape=[jax.ShapeDtypeStruct((padded_rows, span), jnp.int16)] * targets,
        in_specs=[SMEM_SPEC] + [VMEM_SPEC] * (2 * pieces) + [HBM_SPEC] * 4 + [VMEM_SPEC] * 4,
        out_specs=[VMEM_SPEC] * targets,
        scratch_shapes=[pltpu.VMEM(table.shape, jnp.bfloat16) for table in tables]
        + [pltpu.VMEM((pieces, rows, width), jnp.float32), pltpu.SemaphoreType.DMA((4,))],
        compiler_params=pltpu.CompilerParams(vmem_limit_bytes=VMEM_BYTES),
        cost_estimate=pl.CostEstimate(
            flops=3 * rows * NLON * M, bytes_accessed=6 * 2**20, transcendentals=0
        ),
    )(order, *grids, *halos, *tables, places, wave_row, keep_col, sine_col)


def legendre_kernel(pieces, order_ref, *rest):
    fields, rest = rest[:pieces], rest[pieces:]
    table_hbm, lat_hbm, wave_ref, limit_ref, norm_ref, out_ref = rest[:6]
    weight, before, current, level, sums, result, beta_ref, scale_ref, growth_ref = rest[6:15]
    table, lat_ref, sems = rest[15:]
    copies = [pltpu.make_async_copy(lat_hbm, lat_ref, sems.at[pieces])]
    copies[0].start()
    for piece in range(pieces):
        source = table_hbm.at[order_ref[piece]]
        copies.append(pltpu.make_async_copy(source, table.at[piece], sems.at[piece]))
        copies[-1].start()
    half = lat_ref.shape[1]
    lanes = wave_ref.shape[1]
    slots = out_ref.shape[0]
    groups = lanes // LANES
    wave = wave_ref[...]
    odd = wave - 2.0 * jnp.floor(wave * 0.5) > 0.5

    def squares(order):
        degree = wave + order
        return 4.0 * degree * degree - 1.0, 4.0 * order * (degree + wave)

    square, spread = squares(
        lax.broadcasted_iota(jnp.int32, (M, lanes), 0).astype(jnp.float32)
    )
    beta_ref[...] = spread / jnp.maximum(square, 1.0)
    blocks = M // BLOCK
    first_order = lax.broadcasted_iota(jnp.int32, (blocks, lanes), 0).astype(jnp.float32) * BLOCK
    scale = jnp.ones((blocks, lanes), jnp.float32)
    for index in range(BLOCK):
        inside = first_order + index < limit_ref[...]
        scale_ref[pl.ds(index, blocks, stride=BLOCK)] = jnp.where(inside, scale, 0.0)
        square, spread = squares(first_order + (index + 1))
        scale = scale * jnp.sqrt(square / spread)
    growth_ref[...] = scale

    copies[0].wait()
    for group in range(groups):
        cols = slice(group * LANES, (group + 1) * LANES)
        coarse = lat_ref[1] * wave[:, cols]
        whole = jnp.floor(coarse)
        level[:, cols] = whole
        current[:, cols] = jnp.exp2(
            (coarse - whole) + lat_ref[2] * wave[:, cols] + norm_ref[:, cols]
        )
        before[:, cols] = jnp.zeros((half, LANES), jnp.float32)

    padded_rows = fields[0].shape[0]
    totals = [None] * 4
    for piece in range(pieces):
        values = from_int16(fields[piece][...])
        values = values * scale_of(values[padded_rows - 1 :])
        high, low = split_bf16(values)
        copies[1 + piece].wait()
        for kind in range(4):
            rows = pl.ds(kind * half, half)
            value = jnp.dot(table[piece, 0, rows], high, preferred_element_type=jnp.float32)
            value += jnp.dot(table[piece, 0, rows], low, preferred_element_type=jnp.float32)
            value += jnp.dot(table[piece, 1, rows], high, preferred_element_type=jnp.float32)
            totals[kind] = value if piece == 0 else totals[kind] + value
    for parity in range(2):
        for comp in range(2):
            cols = slice(comp * lanes, (comp + 1) * lanes)
            weight[2 * parity + comp] = jnp.where(
                odd, totals[2 + parity][:, cols], totals[parity][:, cols]
            )

    def step(block, carry):
        first = pl.multiple_of(block * BLOCK, 8)
        for group in range(groups):
            cols = slice(group * LANES, (group + 1) * LANES)
            grow = growth_ref[pl.ds(block, 1), cols]
            for chunk in range(half // CHUNK):
                rows = slice(chunk * CHUNK, (chunk + 1) * CHUNK)
                height = level[rows, cols]
                factor = jnp.exp2(height)
                weights = [weight[k, rows, cols] * factor for k in range(4)]
                cosine = lat_ref[0, rows]
                old = before[rows, cols]
                new = current[rows, cols]
                for order in range(BLOCK):
                    for comp in range(2):
                        product = new * weights[2 * (order % 2) + comp]
                        partial = product.reshape(CHUNK // 8, 8, LANES).sum(axis=0)
                        place = pl.ds((order * 2 + comp) * 8, 8)
                        if chunk == 0:
                            sums[place] = partial
                        else:
                            sums[place] += partial
                    beta = beta_ref[pl.ds(first + order, 1), cols]
                    old, new = new, cosine * new - beta * old
                biggest = jnp.maximum(jnp.abs(old), jnp.abs(new)) * grow
                shift = jnp.floor(jnp.log(biggest) * (1.0 / math.log(2.0)))
                factor = grow * jnp.exp2(-shift)
                before[rows, cols] = old * factor
                current[rows, cols] = new * factor
                level[rows, cols] = height + shift
            for comp in range(2):
                total = sums[pl.ds(comp * 8, BLOCK, stride=16)]
                for lane in range(1, 8):
                    total += sums[pl.ds(comp * 8 + lane, BLOCK, stride=16)]
                result[comp, pl.ds(first, BLOCK), cols] = (
                    total * scale_ref[pl.ds(first, BLOCK), cols]
                )
        return carry

    lax.fori_loop(0, M // BLOCK, step, 0)
    for comp in range(2):
        out_ref[:, comp, :] = result[comp].T[:slots]


def legendre(fields, order, slot_wave, rows):
    slots = slot_wave.shape[0]
    pieces = len(fields)
    padded_rows, span = fields[0].shape
    lanes = span // 2
    half = M // 2
    wave_row = jnp.pad(slot_wave, (0, lanes - slots), constant_values=2 * M)[None, :]
    inside_wave = jnp.minimum(wave_row, M - 1).astype(jnp.float32)
    limit = (M - wave_row).astype(jnp.float32)
    counter = np.arange(1, M)[:, None]
    log_terms = (np.log1p(0.5 / counter) / math.log(2.0)).astype(np.float32)
    log_norm = jnp.sum(
        jnp.where(counter.astype(np.float32) <= inside_wave, log_terms, 0.0), axis=0, keepdims=True
    )
    norm = 0.5 * (log_norm - 1.0)
    table = resample_table().reshape(2 * M, pieces, rows).transpose(1, 0, 2)
    table = table_bf16(np.pad(table, ((0, 0), (0, 0), (0, padded_rows - rows))))
    table = table.reshape(pieces, 2 * M, 2, padded_rows).transpose(0, 2, 1, 3)
    latitudes = latitude_table()
    vector = pltpu.VMEM((half, lanes), jnp.float32)
    orders = pltpu.VMEM((M, lanes), jnp.float32)
    return pl.pallas_call(
        functools.partial(legendre_kernel, pieces),
        out_shape=jax.ShapeDtypeStruct((slots, 2, M), jnp.float32),
        in_specs=[SMEM_SPEC] + [VMEM_SPEC] * pieces + [HBM_SPEC] * 2 + [VMEM_SPEC] * 3,
        out_specs=VMEM_SPEC,
        scratch_shapes=[
            pltpu.VMEM((4, half, lanes), jnp.float32),
            vector,
            vector,
            vector,
            pltpu.VMEM((BLOCK * 16, LANES), jnp.float32),
            pltpu.VMEM((2, M, lanes), jnp.float32),
            orders,
            orders,
            pltpu.VMEM((M // BLOCK, lanes), jnp.float32),
            pltpu.VMEM(table.shape, jnp.bfloat16),
            pltpu.VMEM(latitudes.shape, jnp.float32),
            pltpu.SemaphoreType.DMA((pieces + 1,)),
        ],
        compiler_params=pltpu.CompilerParams(vmem_limit_bytes=VMEM_BYTES),
        cost_estimate=pl.CostEstimate(
            flops=7 * half * lanes * M, bytes_accessed=6 * 2**20, transcendentals=0
        ),
    )(order, *fields, table, latitudes, inside_wave, limit, norm)


def shards(tracer, wind_east, wind_north, keep_m, slot_wave):
    rows = tracer.shape[1]
    lat_count = lax.axis_size("lat")
    slots = slot_wave.shape[0] // lat_count
    lanes = -(-slots // LANES) * LANES
    lat_index = lax.axis_index("lat")

    ring = ("lev", "fld")
    level_order, lat_order = partners(ring), partners("lat")
    blocks, edges = advect(tracer, wind_east, wind_north, level_order)
    blocks, slot_wave, keep_m = lax.optimization_barrier((blocks, slot_wave, keep_m))
    grids = exchange(blocks, ring)
    halos = exchange(halo(level_order, *edges), ring)

    pad = ((0, 0), (0, 0), (0, lanes - slots))
    waves = jnp.pad(slot_wave.reshape(lat_count, 1, slots), pad, constant_values=2 * M)
    waves = jnp.broadcast_to(waves[lat_order], (lat_count, 2, lanes))
    table_rows = wave_rows()
    spots = np.full(4 * (-(-M // 2 // (2 * LANES)) * 2 * LANES), 4 * M, np.int32)
    for part in range(2):
        spots[table_rows[part]] = np.arange(M) * 2 + part
    columns = (waves * 2 + jnp.array([0, 1], jnp.int32)[None, :, None]).reshape(1, -1)
    places = ((spots[:, None] == columns) & (columns < 2 * M)).astype(jnp.bfloat16)
    row_ids = (lat_index * rows + jnp.arange(rows, dtype=jnp.int32)).astype(jnp.float32)
    sines = jnp.sin(math.pi / NLAT * (row_ids + 0.5)) * math.sqrt(2.0 / NLAT)
    waved = fourier(
        grids, halos, level_order, places, waves.reshape(1, -1), keep_m[:, None], sines[:, None], lat_count
    )
    fields = exchange(waved, "lat")
    my_waves = lax.dynamic_slice_in_dim(slot_wave, lat_index * slots, slots)
    return legendre(fields, lat_order, my_waves, rows)[None]


def solution(mesh):
    return jax.shard_map(
        shards,
        mesh=mesh,
        in_specs=(
            P("member", "lat", ("lev", "fld")),
            P("member", "lat", ("lev", "fld")),
            P("member", "lat", ("lev", "fld")),
            P("lat"),
            P(),
        ),
        out_specs=P(("member", "lev", "fld"), "lat", None, None),
        check_vma=False,
    )
```

```python
import functools
import math

import jax
import jax.numpy as jnp
import numpy as np
from jax import lax
from jax.experimental import pallas as pl
from jax.experimental.pallas import tpu as pltpu
from jax.sharding import PartitionSpec as P

M = 400
NLAT = 800
NLON = 1600
LANES = 128
BLOCK = 40
CHUNK = 40
TOP = 32767.0
WIND_STEP = 1.5 / TOP
VMEM_BYTES = 60 * 2**20
VMEM_SPEC = pl.BlockSpec(memory_space=pltpu.VMEM)
SMEM_SPEC = pl.BlockSpec(memory_space=pltpu.SMEM)
HBM_SPEC = pl.BlockSpec(memory_space=pltpu.HBM)


def split_bf16(values):
    high = values.astype(jnp.bfloat16)
    low = (values - high.astype(jnp.float32)).astype(jnp.bfloat16)
    return high, low


def table_bf16(table):
    high = table.astype(jnp.bfloat16)
    low = (table - high.astype(np.float64)).astype(jnp.bfloat16)
    return np.concatenate([high, low], axis=-1)


def fourier_tables(pieces):
    quarter = NLON // 4
    spots = np.arange(quarter)[:, None]
    factor = 1.0 / math.sqrt(NLON)

    def parts(waves):
        angles = 2.0 * math.pi / NLON * (spots * waves[None, :] % NLON)
        return factor * np.cos(angles), factor * np.sin(angles)

    tables = []
    for first in (0, 2):
        cosine, sine = parts(np.arange(first, M, 4))
        tables.append([cosine, -sine])
    waves = np.arange(1, M, 2)
    sign = np.where(waves % 4 == 1, 1.0, -1.0)[None, :]
    cosine, sine = parts(waves)
    tables.append([cosine, -sine])
    tables.append([-sign * sine, -sign * cosine])
    share = pieces // 4
    result = []
    for columns in tables:
        table = np.concatenate(columns, axis=1)
        table = np.pad(table, ((0, 0), (0, -table.shape[1] % (2 * LANES))))
        result.append(table.reshape(share, quarter // share, table.shape[1]))
    return result


def wave_rows():
    quarter_width = -(-M // 2 // (2 * LANES)) * 2 * LANES
    waves = np.arange(M)
    quarter_count, half_count = M // 4, M // 2
    rows = []
    for part in range(2):
        even = np.where(waves % 4 == 0, 0, quarter_width) + part * quarter_count + waves // 4
        odd = 2 * quarter_width + part * half_count + waves // 2
        rows.append(np.where(waves % 2 == 0, even, odd))
    return np.stack(rows).astype(np.int32)


def resample_table():
    half = M // 2
    coarse = math.pi / M * (np.arange(M) + 0.5)
    fine = math.pi / NLAT * (np.arange(NLAT) + 0.5)
    waves = np.arange(M)
    weight = np.where(waves == 0, 1.0, 2.0) / M
    even = (np.cos(np.outer(coarse, waves)) * weight) @ np.cos(np.outer(waves, fine))
    odd = (np.sin(np.outer(coarse, waves)) * weight) @ np.sin(np.outer(waves, fine))
    rows = []
    for full in (even, odd):
        for sign in (1.0, -1.0):
            rows.append(full[:half] + sign * full[::-1][:half])
    return np.concatenate(rows, axis=0)


def latitude_table():
    half = M // 2
    angles = math.pi / M * (np.arange(half) + 0.5)
    log_sine = np.log2(np.sin(angles))
    coarse = np.round(log_sine * 1024.0) / 1024.0
    rows = np.stack([2.0 * np.cos(angles), coarse, log_sine - coarse])
    return np.broadcast_to(rows[:, :, None], (3, half, LANES)).astype(np.float32)


def scale_code(biggest):
    wanted = jnp.maximum(biggest, 1e-30) * (1.0 / TOP)
    exponent = jnp.floor(jnp.log(wanted) * (1.0 / math.log(2.0)))
    return exponent * 128.0 + jnp.ceil((wanted * jnp.exp2(-exponent) - 1.0) * 128.0)


def scale_of(code):
    exponent = jnp.floor(code * (1.0 / 128.0))
    rest = code - 128.0 * exponent
    return jnp.exp2(exponent) * (1.0 + rest * (1.0 / 128.0))


def coded(values, inverse):
    return jnp.floor(values * inverse + 0.5)


def as_int16(values):
    return values.astype(jnp.int32).astype(jnp.int16)


def from_int16(codes):
    return codes.astype(jnp.int32).astype(jnp.float32)


def partners(axis):
    count = lax.axis_size(axis)
    order = jnp.arange(count, dtype=jnp.int32)
    return lax.axis_index(axis).astype(jnp.int32) ^ order if count == 4 else order


def exchange(blocks, axis):
    count = len(blocks)
    if count != 4:
        return list(lax.all_to_all(jnp.stack(blocks), axis, split_axis=0, concat_axis=0, tiled=True))
    pairs = [[(i, i ^ step) for i in range(count)] for step in range(count)]
    return [blocks[0]] + [lax.ppermute(blocks[step], axis, pairs[step]) for step in range(1, count)]


def advect_kernel(order_ref, tracer_hbm, east_hbm, north_hbm, *rest):
    levels, rows, lons = tracer_hbm.shape
    outs, rest = rest[:levels], rest[levels:]
    first_row, last_row, row_wind, tracer, east_wind, north_wind, sems = rest
    copies = []
    for step in range(levels):
        level = order_ref[step]
        copies.append(
            [
                pltpu.make_async_copy(source.at[level], target.at[step], sems.at[step, kind])
                for kind, (source, target) in enumerate(
                    ((tracer_hbm, tracer), (east_hbm, east_wind), (north_hbm, north_wind))
                )
            ]
        )
        for copy in copies[-1]:
            copy.start()
    end = (lons - 1) // LANES * LANES
    spare = lons - end
    lane = lax.broadcasted_iota(jnp.int32, (rows, LANES), 1)
    for step in range(levels):
        level = order_ref[step]
        for copy in copies[step]:
            copy.wait()
        field = tracer[step].astype(jnp.float32)
        first_row[level] = field[:1]
        last_row[level] = field[rows - 1 :]
        blank = jnp.zeros((rows, 1), jnp.float32)
        west = jnp.concatenate([blank, field[:, :-1]], axis=1)
        east = jnp.concatenate([field[:, 1:], blank], axis=1)
        blank = jnp.zeros((1, lons), jnp.float32)
        north = jnp.concatenate([blank, field[:-1]], axis=0)
        south = jnp.concatenate([field[1:], blank], axis=0)
        eastward = 0.5 * east_wind[step].astype(jnp.float32)
        northward = 0.5 * north_wind[step].astype(jnp.float32)
        row_wind[step, :1] = northward[:1]
        row_wind[step, 1:2] = -northward[rows - 1 :]
        moved = field - eastward * (east - west) - northward * (south - north)
        first, last = field[:, :1], field[:, lons - 1 :]
        biggest = jnp.max(jnp.abs(moved), axis=1, keepdims=True)
        biggest = jnp.maximum(biggest, jnp.maximum(jnp.abs(first), jnp.abs(last)))
        code = scale_code(biggest)
        inverse = 1.0 / scale_of(code)
        filler = jnp.zeros((rows, LANES - spare), jnp.float32)
        tile = jnp.concatenate([moved[:, end:], filler], axis=1)
        tile = jnp.where(lane == spare + 1, first, jnp.where(lane == spare + 2, last, tile))
        tile = coded(tile, inverse)
        tile = jnp.where(lane == spare, code, tile)
        winds = jnp.where(lane == spare + 3, eastward[:, :1], eastward[:, lons - 1 :])
        winds = coded(winds, 1.0 / WIND_STEP)
        tile = jnp.where((lane == spare + 3) | (lane == spare + 4), winds, tile)
        outs[step][:, :end] = as_int16(coded(moved[:, :end], inverse))
        outs[step][:, end:] = as_int16(tile)


def advect(tracer, east_wind, north_wind, order):
    levels, rows, lons = tracer.shape
    width = (lons - 1) // LANES * LANES + LANES
    held = pltpu.VMEM((levels, rows, lons), jnp.bfloat16)
    row = jax.ShapeDtypeStruct((levels, 1, lons), jnp.float32)
    result = pl.pallas_call(
        advect_kernel,
        out_shape=[jax.ShapeDtypeStruct((rows, width), jnp.int16)] * levels
        + [row, row, jax.ShapeDtypeStruct((levels, 2, lons), jnp.float32)],
        in_specs=[SMEM_SPEC] + [HBM_SPEC] * 3,
        out_specs=[VMEM_SPEC] * (levels + 3),
        scratch_shapes=[held, held, held, pltpu.SemaphoreType.DMA((levels, 3))],
        compiler_params=pltpu.CompilerParams(vmem_limit_bytes=VMEM_BYTES),
        cost_estimate=pl.CostEstimate(
            flops=20 * levels * rows * lons, bytes_accessed=8 * levels * rows * lons, transcendentals=0
        ),
    )(order, tracer, east_wind, north_wind)
    return result[:levels], result[levels:]


def halo_kernel(order_ref, above_ref, below_ref, row_wind, *outs):
    for step, out_ref in enumerate(outs):
        level = order_ref[step]
        out_ref[:1] = row_wind[step, :1] * above_ref[level]
        out_ref[1:] = row_wind[step, 1:2] * below_ref[level]


def halo(order, first_row, last_row, row_wind):
    levels, _, lons = first_row.shape
    count = lax.axis_size("lat")
    above = lax.ppermute(last_row, "lat", [(i, i + 1) for i in range(count - 1)])
    below = lax.ppermute(first_row, "lat", [(i + 1, i) for i in range(count - 1)])
    return pl.pallas_call(
        halo_kernel,
        out_shape=[jax.ShapeDtypeStruct((2, lons), jnp.float32)] * levels,
        in_specs=[SMEM_SPEC] + [VMEM_SPEC] * 3,
        out_specs=[VMEM_SPEC] * levels,
    )(order, above, below, row_wind)


def fourier_kernel(pieces, targets, order_ref, *rest):
    grids, halos, rest = rest[:pieces], rest[pieces : 2 * pieces], rest[2 * pieces :]
    tables_hbm, (place_ref, wave_ref, keep_ref, sine_ref), rest = rest[:4], rest[4:8], rest[8:]
    outs, rest = rest[:targets], rest[targets:]
    tables, (field, sems) = rest[:4], rest[4:]
    _, rows, width = field.shape
    lons = tables[0].shape[1]
    share = pieces // 4
    copies = []
    for kind in range(4):
        copies.append(pltpu.make_async_copy(tables_hbm[kind], tables[kind], sems.at[kind]))
        copies[-1].start()

    end = width - LANES
    spare = lons - end
    lane = lax.broadcasted_iota(jnp.int32, (rows, LANES), 1)
    winds = (lane == spare + 3) | (lane == spare + 4)
    for piece in range(pieces):
        spot = order_ref[piece]
        values = from_int16(grids[piece][...])
        tile = values[:, end:]
        scale = scale_of(tile[:, spare : spare + 1])
        field[spot, :, :end] = values[:, :end] * scale
        field[spot, :, end:] = tile * jnp.where(winds, WIND_STEP, scale)
        field[spot, :1, :lons] += halos[piece][:1]
        field[spot, rows - 1 :, :lons] += halos[piece][1:]
    for spot in range(pieces):
        tile = field[spot, :, end:]
        before = field[(spot - 1) % pieces, :, end:]
        after = field[(spot + 1) % pieces, :, end:]
        shift = LANES - spare
        gain = pltpu.roll(tile, shift - 3, 1) * pltpu.roll(before, shift - 2, 1)
        loss = pltpu.roll(tile, LANES - 5, 1) * pltpu.roll(after, LANES - 2, 1)
        field[spot, :, end:] = tile - jnp.where(lane == spare - 1, loss, 0.0)
        field[spot, :, :LANES] += jnp.where(lane == 0, gain, 0.0)

    def product(value, table, spot):
        high, low = split_bf16(value)
        width = table.shape[2] // 2
        both = jnp.dot(high, table[spot], preferred_element_type=jnp.float32)
        part = jnp.dot(low, table[spot, :, :width], preferred_element_type=jnp.float32)
        return part + both[:, :width] + both[:, width:]

    sums = [None, None, None]
    for spot in range(share):
        quarters = [field[quarter * share + spot, :, :lons] for quarter in range(4)]
        sum02, dif02 = quarters[0] + quarters[2], quarters[0] - quarters[2]
        sum13, dif13 = quarters[1] + quarters[3], quarters[1] - quarters[3]
        parts = []
        for kind, value in enumerate((sum02 + sum13, sum02 - sum13, dif02, dif13)):
            if spot == 0:
                copies[kind].wait()
            parts.append(product(value, tables[kind], spot))
        parts = [parts[0], parts[1], parts[2] + parts[3]]
        sums = [part if total is None else total + part for total, part in zip(sums, parts)]
    placed = None
    first = 0
    for total in sums:
        last = first + total.shape[1]
        high, low = split_bf16(total)
        part = jnp.dot(high, place_ref[first:last], preferred_element_type=jnp.float32)
        part += jnp.dot(low, place_ref[first:last], preferred_element_type=jnp.float32)
        placed = part if placed is None else placed + part
        first = last
    kept = jnp.where(wave_ref[...] < keep_ref[...], placed * sine_ref[...], 0.0)
    code = scale_code(jnp.max(jnp.abs(kept), axis=0, keepdims=True))
    steps = coded(kept, 1.0 / scale_of(code))
    padded_rows, span = outs[0].shape
    codes = jnp.broadcast_to(code, (padded_rows - rows, code.shape[1]))
    result = as_int16(jnp.concatenate([steps, codes], axis=0))
    for target in range(targets):
        outs[target][...] = result[:, target * span : (target + 1) * span]


def fourier(grids, halos, order, places, wave_row, keep_col, sine_col, targets):
    pieces = len(grids)
    rows, width = grids[0].shape
    lons = NLON // pieces
    span = wave_row.shape[1] // targets
    padded_rows = -(-(rows + 1) // 16) * 16
    tables = [table_bf16(table) for table in fourier_tables(pieces)]
    return pl.pallas_call(
        functools.partial(fourier_kernel, pieces, targets),
        out_shape=[jax.ShapeDtypeStruct((padded_rows, span), jnp.int16)] * targets,
        in_specs=[SMEM_SPEC] + [VMEM_SPEC] * (2 * pieces) + [HBM_SPEC] * 4 + [VMEM_SPEC] * 4,
        out_specs=[VMEM_SPEC] * targets,
        scratch_shapes=[pltpu.VMEM(table.shape, jnp.bfloat16) for table in tables]
        + [pltpu.VMEM((pieces, rows, width), jnp.float32), pltpu.SemaphoreType.DMA((4,))],
        compiler_params=pltpu.CompilerParams(vmem_limit_bytes=VMEM_BYTES),
        cost_estimate=pl.CostEstimate(
            flops=3 * rows * NLON * M, bytes_accessed=6 * 2**20, transcendentals=0
        ),
    )(order, *grids, *halos, *tables, places, wave_row, keep_col, sine_col)


def legendre_kernel(pieces, order_ref, *rest):
    fields, rest = rest[:pieces], rest[pieces:]
    table_hbm, lat_hbm, wave_ref, limit_ref, norm_ref, out_ref = rest[:6]
    weight, before, current, level, sums, result, beta_ref, scale_ref, growth_ref = rest[6:15]
    table, lat_ref, sems = rest[15:]
    copies = [pltpu.make_async_copy(lat_hbm, lat_ref, sems.at[pieces])]
    copies[0].start()
    for piece in range(pieces):
        source = table_hbm.at[order_ref[piece]]
        copies.append(pltpu.make_async_copy(source, table.at[piece], sems.at[piece]))
        copies[-1].start()
    half = lat_ref.shape[1]
    lanes = wave_ref.shape[1]
    slots = out_ref.shape[0]
    groups = lanes // LANES
    wave = wave_ref[...]
    odd = wave - 2.0 * jnp.floor(wave * 0.5) > 0.5

    def squares(order):
        degree = wave + order
        return 4.0 * degree * degree - 1.0, 4.0 * order * (degree + wave)

    square, spread = squares(
        lax.broadcasted_iota(jnp.int32, (M, lanes), 0).astype(jnp.float32)
    )
    beta_ref[...] = spread / jnp.maximum(square, 1.0)
    blocks = M // BLOCK
    first_order = lax.broadcasted_iota(jnp.int32, (blocks, lanes), 0).astype(jnp.float32) * BLOCK
    scale = jnp.ones((blocks, lanes), jnp.float32)
    for index in range(BLOCK):
        inside = first_order + index < limit_ref[...]
        scale_ref[pl.ds(index, blocks, stride=BLOCK)] = jnp.where(inside, scale, 0.0)
        square, spread = squares(first_order + (index + 1))
        scale = scale * jnp.sqrt(square / spread)
    growth_ref[...] = scale

    copies[0].wait()
    for group in range(groups):
        cols = slice(group * LANES, (group + 1) * LANES)
        coarse = lat_ref[1] * wave[:, cols]
        whole = jnp.floor(coarse)
        level[:, cols] = whole
        current[:, cols] = jnp.exp2(
            (coarse - whole) + lat_ref[2] * wave[:, cols] + norm_ref[:, cols]
        )
        before[:, cols] = jnp.zeros((half, LANES), jnp.float32)

    padded_rows = fields[0].shape[0]
    totals = [None] * 4
    for piece in range(pieces):
        values = from_int16(fields[piece][...])
        values = values * scale_of(values[padded_rows - 1 :])
        high, low = split_bf16(values)
        copies[1 + piece].wait()
        for kind in range(4):
            rows = pl.ds(kind * half, half)
            value = jnp.dot(table[piece, 0, rows], high, preferred_element_type=jnp.float32)
            value += jnp.dot(table[piece, 0, rows], low, preferred_element_type=jnp.float32)
            value += jnp.dot(table[piece, 1, rows], high, preferred_element_type=jnp.float32)
            totals[kind] = value if piece == 0 else totals[kind] + value
    for parity in range(2):
        for comp in range(2):
            cols = slice(comp * lanes, (comp + 1) * lanes)
            weight[2 * parity + comp] = jnp.where(
                odd, totals[2 + parity][:, cols], totals[parity][:, cols]
            )

    def step(block, carry):
        first = pl.multiple_of(block * BLOCK, 8)
        for group in range(groups):
            cols = slice(group * LANES, (group + 1) * LANES)
            grow = growth_ref[pl.ds(block, 1), cols]
            for chunk in range(half // CHUNK):
                rows = slice(chunk * CHUNK, (chunk + 1) * CHUNK)
                height = level[rows, cols]
                factor = jnp.exp2(height)
                weights = [weight[k, rows, cols] * factor for k in range(4)]
                cosine = lat_ref[0, rows]
                old = before[rows, cols]
                new = current[rows, cols]
                for order in range(BLOCK):
                    for comp in range(2):
                        product = new * weights[2 * (order % 2) + comp]
                        partial = product.reshape(CHUNK // 8, 8, LANES).sum(axis=0)
                        place = pl.ds((order * 2 + comp) * 8, 8)
                        if chunk == 0:
                            sums[place] = partial
                        else:
                            sums[place] += partial
                    beta = beta_ref[pl.ds(first + order, 1), cols]
                    old, new = new, cosine * new - beta * old
                biggest = jnp.maximum(jnp.abs(old), jnp.abs(new)) * grow
                shift = jnp.floor(jnp.log(biggest) * (1.0 / math.log(2.0)))
                factor = grow * jnp.exp2(-shift)
                before[rows, cols] = old * factor
                current[rows, cols] = new * factor
                level[rows, cols] = height + shift
            for comp in range(2):
                total = sums[pl.ds(comp * 8, BLOCK, stride=16)]
                for lane in range(1, 8):
                    total += sums[pl.ds(comp * 8 + lane, BLOCK, stride=16)]
                result[comp, pl.ds(first, BLOCK), cols] = (
                    total * scale_ref[pl.ds(first, BLOCK), cols]
                )
        return carry

    lax.fori_loop(0, M // BLOCK, step, 0)
    for comp in range(2):
        out_ref[:, comp, :] = result[comp].T[:slots]


def legendre(fields, order, slot_wave, rows):
    slots = slot_wave.shape[0]
    pieces = len(fields)
    padded_rows, span = fields[0].shape
    lanes = span // 2
    half = M // 2
    wave_row = jnp.pad(slot_wave, (0, lanes - slots), constant_values=2 * M)[None, :]
    inside_wave = jnp.minimum(wave_row, M - 1).astype(jnp.float32)
    limit = (M - wave_row).astype(jnp.float32)
    counter = np.arange(1, M)[:, None]
    log_terms = (np.log1p(0.5 / counter) / math.log(2.0)).astype(np.float32)
    log_norm = jnp.sum(
        jnp.where(counter.astype(np.float32) <= inside_wave, log_terms, 0.0), axis=0, keepdims=True
    )
    norm = 0.5 * (log_norm - 1.0)
    table = resample_table().reshape(2 * M, pieces, rows).transpose(1, 0, 2)
    table = table_bf16(np.pad(table, ((0, 0), (0, 0), (0, padded_rows - rows))))
    table = table.reshape(pieces, 2 * M, 2, padded_rows).transpose(0, 2, 1, 3)
    latitudes = latitude_table()
    vector = pltpu.VMEM((half, lanes), jnp.float32)
    orders = pltpu.VMEM((M, lanes), jnp.float32)
    return pl.pallas_call(
        functools.partial(legendre_kernel, pieces),
        out_shape=jax.ShapeDtypeStruct((slots, 2, M), jnp.float32),
        in_specs=[SMEM_SPEC] + [VMEM_SPEC] * pieces + [HBM_SPEC] * 2 + [VMEM_SPEC] * 3,
        out_specs=VMEM_SPEC,
        scratch_shapes=[
            pltpu.VMEM((4, half, lanes), jnp.float32),
            vector,
            vector,
            vector,
            pltpu.VMEM((BLOCK * 16, LANES), jnp.float32),
            pltpu.VMEM((2, M, lanes), jnp.float32),
            orders,
            orders,
            pltpu.VMEM((M // BLOCK, lanes), jnp.float32),
            pltpu.VMEM(table.shape, jnp.bfloat16),
            pltpu.VMEM(latitudes.shape, jnp.float32),
            pltpu.SemaphoreType.DMA((pieces + 1,)),
        ],
        compiler_params=pltpu.CompilerParams(vmem_limit_bytes=VMEM_BYTES),
        cost_estimate=pl.CostEstimate(
            flops=7 * half * lanes * M, bytes_accessed=6 * 2**20, transcendentals=0
        ),
    )(order, *fields, table, latitudes, inside_wave, limit, norm)


def shards(tracer, wind_east, wind_north, keep_m, slot_wave):
    rows = tracer.shape[1]
    lat_count = lax.axis_size("lat")
    slots = slot_wave.shape[0] // lat_count
    lanes = -(-slots // LANES) * LANES
    lat_index = lax.axis_index("lat")

    ring = ("lev", "fld")
    level_order, lat_order = partners(ring), partners("lat")
    blocks, edges = advect(tracer, wind_east, wind_north, level_order)
    grids = exchange(blocks, ring)
    ends, slot_wave, keep_m = lax.optimization_barrier(
        (halo(level_order, *edges), slot_wave, keep_m)
    )
    halos = exchange(ends, ring)

    pad = ((0, 0), (0, 0), (0, lanes - slots))
    waves = jnp.pad(slot_wave.reshape(lat_count, 1, slots), pad, constant_values=2 * M)
    waves = jnp.broadcast_to(waves[lat_order], (lat_count, 2, lanes))
    table_rows = wave_rows()
    spots = np.full(4 * (-(-M // 2 // (2 * LANES)) * 2 * LANES), 4 * M, np.int32)
    for part in range(2):
        spots[table_rows[part]] = np.arange(M) * 2 + part
    columns = (waves * 2 + jnp.array([0, 1], jnp.int32)[None, :, None]).reshape(1, -1)
    places = ((spots[:, None] == columns) & (columns < 2 * M)).astype(jnp.bfloat16)
    row_ids = (lat_index * rows + jnp.arange(rows, dtype=jnp.int32)).astype(jnp.float32)
    sines = jnp.sin(math.pi / NLAT * (row_ids + 0.5)) * math.sqrt(2.0 / NLAT)
    waved = fourier(
        grids, halos, level_order, places, waves.reshape(1, -1), keep_m[:, None], sines[:, None], lat_count
    )
    fields = exchange(waved, "lat")
    my_waves = lax.dynamic_slice_in_dim(slot_wave, lat_index * slots, slots)
    return legendre(fields, lat_order, my_waves, rows)[None]


def solution(mesh):
    return jax.shard_map(
        shards,
        mesh=mesh,
        in_specs=(
            P("member", "lat", ("lev", "fld")),
            P("member", "lat", ("lev", "fld")),
            P("member", "lat", ("lev", "fld")),
            P("lat"),
            P(),
        ),
        out_specs=P(("member", "lev", "fld"), "lat", None, None),
        check_vma=False,
    )
```

```python
import functools
import math

import jax
import jax.numpy as jnp
import numpy as np
from jax import lax
from jax.experimental import pallas as pl
from jax.experimental.pallas import tpu as pltpu
from jax.sharding import PartitionSpec as P

M = 400
NLAT = 800
NLON = 1600
LANES = 128
BLOCK = 32
CHUNKS = (40, 32, 32)
SIDE = LANES // 2
TOP = 32767.0
WIND_STEP = 1.5 / TOP
VMEM_BYTES = 60 * 2**20
VMEM_SPEC = pl.BlockSpec(memory_space=pltpu.VMEM)
SMEM_SPEC = pl.BlockSpec(memory_space=pltpu.SMEM)
HBM_SPEC = pl.BlockSpec(memory_space=pltpu.HBM)


def split_bf16(values):
    high = values.astype(jnp.bfloat16)
    low = (values - high.astype(jnp.float32)).astype(jnp.bfloat16)
    return high, low


def table_bf16(table):
    high = table.astype(jnp.bfloat16)
    low = (table - high.astype(np.float64)).astype(jnp.bfloat16)
    return np.concatenate([high, low], axis=-1)


def fourier_tables(pieces):
    quarter = NLON // 4
    spots = np.arange(quarter)[:, None]
    factor = 1.0 / math.sqrt(NLON)

    def parts(waves):
        angles = 2.0 * math.pi / NLON * (spots * waves[None, :] % NLON)
        return factor * np.cos(angles), factor * np.sin(angles)

    tables = []
    for first in (0, 2):
        cosine, sine = parts(np.arange(first, M, 4))
        tables.append([cosine, -sine])
    waves = np.arange(1, M, 2)
    sign = np.where(waves % 4 == 1, 1.0, -1.0)[None, :]
    cosine, sine = parts(waves)
    tables.append([cosine, -sine])
    tables.append([-sign * sine, -sign * cosine])
    share = pieces // 4
    result = []
    for columns in tables:
        table = np.concatenate(columns, axis=1)
        table = np.pad(table, ((0, 0), (0, -table.shape[1] % (2 * LANES))))
        result.append(table.reshape(share, quarter // share, table.shape[1]))
    return result


def column_waves():
    width = -(-M // 2 // (2 * LANES)) * 2 * LANES
    spots = np.full(4 * width, -1.0, np.float32)
    waves = np.arange(M)
    for part in range(2):
        even = np.where(waves % 4 == 0, 0, width) + part * (M // 4) + waves // 4
        odd = 2 * width + part * (M // 2) + waves // 2
        spots[np.where(waves % 2 == 0, even, odd)] = 2 * waves + part
    return spots[:, None]


def resample_table():
    half = M // 2
    coarse = math.pi / M * (np.arange(M) + 0.5)
    fine = math.pi / NLAT * (np.arange(NLAT) + 0.5)
    waves = np.arange(M)
    weight = np.where(waves == 0, 1.0, 2.0) / M
    even = (np.cos(np.outer(coarse, waves)) * weight) @ np.cos(np.outer(waves, fine))
    odd = (np.sin(np.outer(coarse, waves)) * weight) @ np.sin(np.outer(waves, fine))
    rows = []
    for full in (even, odd):
        for sign in (1.0, -1.0):
            folded = (full[:half] + sign * full[::-1][:half]).reshape(2, half // 2, NLAT)
            rows.append(np.pad(folded, ((0, 0), (0, -half // 2 % 8), (0, 0))).reshape(-1, NLAT))
    return np.concatenate(rows, axis=0)


def latitude_table():
    half = M // 2
    angles = math.pi / M * (np.arange(half) + 0.5)
    log_sine = np.log2(np.sin(angles))
    coarse = np.round(log_sine * 1024.0) / 1024.0
    rows = np.stack([2.0 * np.cos(angles), coarse, log_sine - coarse]).reshape(3, 2, half // 2)
    rows = np.pad(rows, ((0, 0), (0, 0), (0, -half // 2 % 8)))
    return np.repeat(rows.transpose(0, 2, 1), SIDE, axis=2).astype(np.float32)


def scale_code(biggest):
    wanted = jnp.maximum(biggest, 1e-30) * (1.0 / TOP)
    exponent = jnp.floor(jnp.log(wanted) * (1.0 / math.log(2.0)))
    return exponent * 128.0 + jnp.ceil((wanted * jnp.exp2(-exponent) - 1.0) * 128.0)


def scale_of(code):
    exponent = jnp.floor(code * (1.0 / 128.0))
    rest = code - 128.0 * exponent
    return jnp.exp2(exponent) * (1.0 + rest * (1.0 / 128.0))


def coded(values, inverse):
    return jnp.floor(values * inverse + 0.5)


def as_int16(values):
    return values.astype(jnp.int32).astype(jnp.int16)


def from_int16(codes):
    return codes.astype(jnp.int32).astype(jnp.float32)


def partners(axis):
    count = lax.axis_size(axis)
    order = jnp.arange(count, dtype=jnp.int32)
    return lax.axis_index(axis).astype(jnp.int32) ^ order if count == 4 else order


def exchange(blocks, axis):
    count = len(blocks)
    if count != 4:
        return list(lax.all_to_all(jnp.stack(blocks), axis, split_axis=0, concat_axis=0, tiled=True))
    pairs = [[(i, i ^ step) for i in range(count)] for step in range(count)]
    return [blocks[0]] + [lax.ppermute(blocks[step], axis, pairs[step]) for step in range(1, count)]


def advect_kernel(order_ref, tracer_hbm, east_hbm, north_hbm, *rest):
    levels, rows, lons = tracer_hbm.shape
    outs, rest = rest[:levels], rest[levels:]
    first_row, last_row, row_wind, tracer, east_wind, north_wind, sems = rest
    copies = []
    for step in range(levels):
        level = order_ref[step]
        copies.append(
            [
                pltpu.make_async_copy(source.at[level], target.at[step], sems.at[step, kind])
                for kind, (source, target) in enumerate(
                    ((tracer_hbm, tracer), (east_hbm, east_wind), (north_hbm, north_wind))
                )
            ]
        )
        for copy in copies[-1]:
            copy.start()
    end = (lons - 1) // LANES * LANES
    spare = lons - end
    lane = lax.broadcasted_iota(jnp.int32, (rows, LANES), 1)
    for step in range(levels):
        level = order_ref[step]
        for copy in copies[step]:
            copy.wait()
        field = tracer[step].astype(jnp.float32)
        first_row[level] = field[:1]
        last_row[level] = field[rows - 1 :]
        blank = jnp.zeros((rows, 1), jnp.float32)
        west = jnp.concatenate([blank, field[:, :-1]], axis=1)
        east = jnp.concatenate([field[:, 1:], blank], axis=1)
        blank = jnp.zeros((1, lons), jnp.float32)
        north = jnp.concatenate([blank, field[:-1]], axis=0)
        south = jnp.concatenate([field[1:], blank], axis=0)
        eastward = 0.5 * east_wind[step].astype(jnp.float32)
        northward = 0.5 * north_wind[step].astype(jnp.float32)
        row_wind[step, :1] = northward[:1]
        row_wind[step, 1:2] = -northward[rows - 1 :]
        moved = field - eastward * (east - west) - northward * (south - north)
        first, last = field[:, :1], field[:, lons - 1 :]
        biggest = jnp.max(jnp.abs(moved), axis=1, keepdims=True)
        biggest = jnp.maximum(biggest, jnp.maximum(jnp.abs(first), jnp.abs(last)))
        code = scale_code(biggest)
        inverse = 1.0 / scale_of(code)
        filler = jnp.zeros((rows, LANES - spare), jnp.float32)
        tile = jnp.concatenate([moved[:, end:], filler], axis=1)
        tile = jnp.where(lane == spare + 1, first, jnp.where(lane == spare + 2, last, tile))
        tile = coded(tile, inverse)
        tile = jnp.where(lane == spare, code, tile)
        winds = jnp.where(lane == spare + 3, eastward[:, :1], eastward[:, lons - 1 :])
        winds = coded(winds, 1.0 / WIND_STEP)
        tile = jnp.where((lane == spare + 3) | (lane == spare + 4), winds, tile)
        outs[step][:, :end] = as_int16(coded(moved[:, :end], inverse))
        outs[step][:, end:] = as_int16(tile)


def advect(tracer, east_wind, north_wind, order):
    levels, rows, lons = tracer.shape
    width = (lons - 1) // LANES * LANES + LANES
    held = pltpu.VMEM((levels, rows, lons), jnp.bfloat16)
    row = jax.ShapeDtypeStruct((levels, 1, lons), jnp.float32)
    result = pl.pallas_call(
        advect_kernel,
        out_shape=[jax.ShapeDtypeStruct((rows, width), jnp.int16)] * levels
        + [row, row, jax.ShapeDtypeStruct((levels, 2, lons), jnp.float32)],
        in_specs=[SMEM_SPEC] + [HBM_SPEC] * 3,
        out_specs=[VMEM_SPEC] * (levels + 3),
        scratch_shapes=[held, held, held, pltpu.SemaphoreType.DMA((levels, 3))],
        compiler_params=pltpu.CompilerParams(vmem_limit_bytes=VMEM_BYTES),
        cost_estimate=pl.CostEstimate(
            flops=20 * levels * rows * lons, bytes_accessed=8 * levels * rows * lons, transcendentals=0
        ),
    )(order, tracer, east_wind, north_wind)
    return result[:levels], result[levels:]


def halo_kernel(order_ref, above_ref, below_ref, row_wind, *outs):
    for step, out_ref in enumerate(outs):
        level = order_ref[step]
        out_ref[:1] = row_wind[step, :1] * above_ref[level]
        out_ref[1:] = row_wind[step, 1:2] * below_ref[level]


def halo(order, first_row, last_row, row_wind):
    levels, _, lons = first_row.shape
    count = lax.axis_size("lat")
    above = lax.ppermute(last_row, "lat", [(i, i + 1) for i in range(count - 1)])
    below = lax.ppermute(first_row, "lat", [(i + 1, i) for i in range(count - 1)])
    return pl.pallas_call(
        halo_kernel,
        out_shape=[jax.ShapeDtypeStruct((2, lons), jnp.float32)] * levels,
        in_specs=[SMEM_SPEC] + [VMEM_SPEC] * 3,
        out_specs=[VMEM_SPEC] * levels,
    )(order, above, below, row_wind)


def fourier_kernel(pieces, targets, order_ref, *rest):
    grids, halos, rest = rest[:pieces], rest[pieces : 2 * pieces], rest[2 * pieces :]
    tables_hbm, (wave_ref, keep_ref, sine_ref), rest = rest[:5], rest[5:8], rest[8:]
    outs, rest = rest[:targets], rest[targets:]
    tables, place_ref, (field, sems) = rest[:4], rest[4], rest[5:]
    _, rows, width = field.shape
    lons = tables[0].shape[1]
    share = pieces // 4
    copies = []
    for kind, target in enumerate((*tables, place_ref)):
        copies.append(pltpu.make_async_copy(tables_hbm[kind], target, sems.at[kind]))
        copies[-1].start()

    end = width - LANES
    spare = lons - end
    lane = lax.broadcasted_iota(jnp.int32, (rows, LANES), 1)
    winds = (lane == spare + 3) | (lane == spare + 4)
    for piece in range(pieces):
        spot = order_ref[piece]
        values = from_int16(grids[piece][...])
        tile = values[:, end:]
        scale = scale_of(tile[:, spare : spare + 1])
        field[spot, :, :end] = values[:, :end] * scale
        field[spot, :, end:] = tile * jnp.where(winds, WIND_STEP, scale)
        field[spot, :1, :lons] += halos[piece][:1]
        field[spot, rows - 1 :, :lons] += halos[piece][1:]
    for spot in range(pieces):
        tile = field[spot, :, end:]
        before = field[(spot - 1) % pieces, :, end:]
        after = field[(spot + 1) % pieces, :, end:]
        shift = LANES - spare
        gain = pltpu.roll(tile, shift - 3, 1) * pltpu.roll(before, shift - 2, 1)
        loss = pltpu.roll(tile, LANES - 5, 1) * pltpu.roll(after, LANES - 2, 1)
        field[spot, :, end:] = tile - jnp.where(lane == spare - 1, loss, 0.0)
        field[spot, :, :LANES] += jnp.where(lane == 0, gain, 0.0)

    def product(value, table, spot):
        high, low = split_bf16(value)
        width = table.shape[2] // 2
        both = jnp.dot(high, table[spot], preferred_element_type=jnp.float32)
        part = jnp.dot(low, table[spot, :, :width], preferred_element_type=jnp.float32)
        return part + both[:, :width] + both[:, width:]

    sums = [None, None, None]
    for spot in range(share):
        quarters = [field[quarter * share + spot, :, :lons] for quarter in range(4)]
        sum02, dif02 = quarters[0] + quarters[2], quarters[0] - quarters[2]
        sum13, dif13 = quarters[1] + quarters[3], quarters[1] - quarters[3]
        parts = []
        for kind, value in enumerate((sum02 + sum13, sum02 - sum13, dif02, dif13)):
            if spot == 0:
                copies[kind].wait()
            parts.append(product(value, tables[kind], spot))
        parts = [parts[0], parts[1], parts[2] + parts[3]]
        sums = [part if total is None else total + part for total, part in zip(sums, parts)]
    placed = None
    first = 0
    copies[4].wait()
    for total in sums:
        last = first + total.shape[1]
        high, low = split_bf16(total)
        part = jnp.dot(high, place_ref[first:last], preferred_element_type=jnp.float32)
        part += jnp.dot(low, place_ref[first:last], preferred_element_type=jnp.float32)
        placed = part if placed is None else placed + part
        first = last
    kept = jnp.where(wave_ref[...] < keep_ref[...], placed * sine_ref[...], 0.0)
    code = scale_code(jnp.max(jnp.abs(kept), axis=0, keepdims=True))
    steps = coded(kept, 1.0 / scale_of(code))
    padded_rows, span = outs[0].shape
    codes = jnp.broadcast_to(code, (padded_rows - rows, code.shape[1]))
    result = as_int16(jnp.concatenate([steps, codes], axis=0))
    for target in range(targets):
        outs[target][...] = result[:, target * span : (target + 1) * span]


def fourier(grids, halos, order, places, wave_row, keep_col, sine_col, targets):
    pieces = len(grids)
    rows, width = grids[0].shape
    lons = NLON // pieces
    span = wave_row.shape[1] // targets
    padded_rows = -(-(rows + 1) // 16) * 16
    tables = [table_bf16(table) for table in fourier_tables(pieces)]
    return pl.pallas_call(
        functools.partial(fourier_kernel, pieces, targets),
        out_shape=[jax.ShapeDtypeStruct((padded_rows, span), jnp.int16)] * targets,
        in_specs=[SMEM_SPEC] + [VMEM_SPEC] * (2 * pieces) + [HBM_SPEC] * 5 + [VMEM_SPEC] * 3,
        out_specs=[VMEM_SPEC] * targets,
        scratch_shapes=[pltpu.VMEM(table.shape, jnp.bfloat16) for table in tables]
        + [pltpu.VMEM(places.shape, jnp.bfloat16)]
        + [pltpu.VMEM((pieces, rows, width), jnp.float32), pltpu.SemaphoreType.DMA((5,))],
        compiler_params=pltpu.CompilerParams(vmem_limit_bytes=VMEM_BYTES),
        cost_estimate=pl.CostEstimate(
            flops=3 * rows * NLON * M, bytes_accessed=6 * 2**20, transcendentals=0
        ),
    )(order, *grids, *halos, *tables, places, wave_row, keep_col, sine_col)


def places_kernel(
    order_ref, lat_ref, slot_ref, keep_ref, sine_ref, spot_ref,
    place_ref, wave_ref, mine_ref, back_ref, keep_col, sine_col, sorted_rows,
):
    groups, _, rows = sine_ref.shape
    slots = slot_ref.shape[1] // groups
    paired = (slots + 1) // 2
    shape = (LANES, LANES)
    down = lax.broadcasted_iota(jnp.int32, shape, 0)
    across = lax.broadcasted_iota(jnp.int32, shape, 1)
    filler = jnp.full((1, LANES - slots), 2.0 * M, jnp.float32)
    for group in range(groups):
        row = slot_ref[:, group * slots : (group + 1) * slots].astype(jnp.float32)
        row = jnp.broadcast_to(jnp.concatenate([row, filler], axis=1), shape)
        column = jnp.sum(jnp.where(down == across, row, 0.0), axis=1, keepdims=True)
        ahead = (row < column) | ((row == column) & (across < down))
        rank = jnp.sum(jnp.where(ahead, 1.0, 0.0), axis=1, keepdims=True)
        place = jnp.where(rank < paired, rank, SIDE + slots - 1.0 - rank)
        place = jnp.where(rank < slots, place, -1.0)
        hot = jnp.where(place == across.astype(jnp.float32), 1.0, 0.0)
        filled = jnp.sum(hot, axis=0, keepdims=True)
        values = jnp.sum(hot * column, axis=0, keepdims=True)
        values = jnp.where(filled > 0.5, values, 2.0 * M)
        sorted_rows[group] = jnp.broadcast_to(values, sorted_rows.shape[1:])

        @pl.when(group == lat_ref[0])
        def _():
            mine_ref[...] = values
            back_ref[...] = hot.astype(jnp.bfloat16)

    spots = spot_ref[...]
    for step in range(groups):
        row = sorted_rows[order_ref[step], :1]
        for part in range(2):
            cols = slice((2 * step + part) * LANES, (2 * step + part + 1) * LANES)
            wave_ref[:, cols] = row
            hit = spots == 2.0 * row + part
            place_ref[:, cols] = jnp.where(hit, 1.0, 0.0).astype(jnp.bfloat16)

    shape = (rows, rows)
    same = lax.broadcasted_iota(jnp.int32, shape, 0) == lax.broadcasted_iota(jnp.int32, shape, 1)
    kept = jnp.broadcast_to(keep_ref[...].astype(jnp.float32), shape)
    keep_col[...] = jnp.sum(jnp.where(same, kept, 0.0), axis=1, keepdims=True)
    sine = jnp.broadcast_to(sine_ref[lat_ref[0]], shape)
    sine_col[...] = jnp.sum(jnp.where(same, sine, 0.0), axis=1, keepdims=True)


def prepare_places(order, lat_index, slot_wave, keep_m, groups):
    rows = keep_m.shape[0]
    sines = np.sin(math.pi / NLAT * (np.arange(NLAT) + 0.5)) * math.sqrt(2.0 / NLAT)
    spots = column_waves()
    width = 2 * groups * LANES
    return pl.pallas_call(
        places_kernel,
        out_shape=[
            jax.ShapeDtypeStruct((spots.shape[0], width), jnp.bfloat16),
            jax.ShapeDtypeStruct((1, width), jnp.float32),
            jax.ShapeDtypeStruct((1, LANES), jnp.float32),
            jax.ShapeDtypeStruct((LANES, LANES), jnp.bfloat16),
            jax.ShapeDtypeStruct((rows, 1), jnp.float32),
            jax.ShapeDtypeStruct((rows, 1), jnp.float32),
        ],
        in_specs=[SMEM_SPEC] * 2 + [VMEM_SPEC] * 4,
        out_specs=[VMEM_SPEC] * 6,
        scratch_shapes=[pltpu.VMEM((groups, 8, LANES), jnp.float32)],
        compiler_params=pltpu.CompilerParams(vmem_limit_bytes=VMEM_BYTES),
    )(
        order, lat_index[None], slot_wave[None], keep_m[None],
        sines.reshape(groups, 1, rows).astype(np.float32), spots,
    )


def lane_pairs(row):
    lane = lax.broadcasted_iota(jnp.int32, row.shape, 1)
    other = pltpu.roll(row, SIDE, 1)
    return jnp.where(lane < SIDE, row, other), jnp.where(lane < SIDE, other, row)


def block_count(wave):
    return jnp.floor((jnp.maximum(M - wave, 0.0) + (BLOCK - 1)) * (1.0 / BLOCK))


def recurrence_kernel(mine_ref, lat_ref, term_ref, beta_ref, scale_ref, growth_ref, start_ref):
    pair = lane_pairs(jnp.broadcast_to(mine_ref[...], (8, LANES)))
    one, two = pair[0][:1], pair[1][:1]
    blocks = growth_ref.shape[0]
    turn = block_count(one)
    block = lax.broadcasted_iota(jnp.int32, (blocks, LANES), 0).astype(jnp.float32)
    second = block >= turn
    wave = jnp.where(second, two, one)
    limit = M - wave
    wave = jnp.minimum(wave, M - 1.0)
    first = (block - jnp.where(second, turn, 0.0)) * BLOCK

    scale = jnp.ones((blocks, LANES), jnp.float32)
    for index in range(BLOCK + 1):
        order = first + index
        degree = wave + order
        square = 4.0 * degree * degree - 1.0
        spread = 4.0 * order * (degree + wave)
        if index > 0:
            scale = scale * jnp.sqrt(square / spread)
        if index < BLOCK:
            beta_ref[pl.ds(index, blocks, stride=BLOCK)] = spread / jnp.maximum(square, 1.0)
            scale_ref[pl.ds(index, blocks, stride=BLOCK)] = jnp.where(order < limit, scale, 0.0)
    growth_ref[...] = scale

    for kind, wave in enumerate((one, two)):
        wave = jnp.minimum(wave, M - 1.0)
        counter = lax.broadcasted_iota(jnp.int32, term_ref.shape, 0).astype(jnp.float32)
        norm = jnp.sum(jnp.where(counter <= wave, term_ref[...], 0.0), axis=0, keepdims=True)
        coarse = lat_ref[1] * wave
        whole = jnp.floor(coarse)
        start_ref[2 * kind] = jnp.exp2(
            (coarse - whole) + lat_ref[2] * wave + 0.5 * (norm - 1.0)
        )
        start_ref[2 * kind + 1] = whole


def prepare_recurrence(mine):
    latitudes = latitude_table()
    points = latitudes.shape[1]
    blocks = 2 * -(-M // BLOCK)
    counter = np.arange(M)
    terms = np.log1p(0.5 / np.maximum(counter, 1)) * (counter > 0) / math.log(2.0)
    terms = np.broadcast_to(terms[:, None], (M, LANES)).astype(np.float32)
    orders = jax.ShapeDtypeStruct((blocks * BLOCK, LANES), jnp.float32)
    return pl.pallas_call(
        recurrence_kernel,
        out_shape=[
            orders,
            orders,
            jax.ShapeDtypeStruct((blocks, LANES), jnp.float32),
            jax.ShapeDtypeStruct((4, points, LANES), jnp.float32),
        ],
        in_specs=[VMEM_SPEC] * 3,
        out_specs=[VMEM_SPEC] * 4,
        compiler_params=pltpu.CompilerParams(vmem_limit_bytes=VMEM_BYTES),
    )(mine, latitudes, terms)


def legendre_kernel(pieces, order_ref, *rest):
    fields, rest = rest[:pieces], rest[pieces:]
    hbm, (mine_ref, back_ref, out_ref), rest = rest[:6], rest[6:9], rest[9:]
    held, (weights, before, current, level, sums, result, final, sems) = rest[:6], rest[6:]
    table, lat_ref, beta_ref, scale_ref, growth_ref, start_ref = held
    copies = []
    for piece in range(pieces):
        source = hbm[0].at[order_ref[piece]]
        copies.append(pltpu.make_async_copy(source, table.at[piece], sems.at[piece]))
        copies[-1].start()
    for kind in range(1, 6):
        copies.append(pltpu.make_async_copy(hbm[kind], held[kind], sems.at[pieces + kind - 1]))
        copies[-1].start()
    points = lat_ref.shape[1]
    slots = out_ref.shape[0]
    mine = mine_ref[...]
    odd = mine - 2.0 * jnp.floor(mine * 0.5) > 0.5
    pair = lane_pairs(jnp.broadcast_to(mine, (8, LANES)))
    turn = block_count(pair[0][:1])
    block_total = jnp.max(turn + block_count(pair[1][:1])).astype(jnp.int32)

    padded_rows = fields[0].shape[0]
    totals = [None] * 4
    for piece in range(pieces):
        values = from_int16(fields[piece][...])
        values = values * scale_of(values[padded_rows - 1 :])
        high, low = split_bf16(values)
        copies[piece].wait()
        for kind in range(4):
            rows = pl.ds(kind * 2 * points, 2 * points)
            value = jnp.dot(table[piece, 0, rows], high, preferred_element_type=jnp.float32)
            value += jnp.dot(table[piece, 0, rows], low, preferred_element_type=jnp.float32)
            value += jnp.dot(table[piece, 1, rows], high, preferred_element_type=jnp.float32)
            totals[kind] = value if piece == 0 else totals[kind] + value
    left = lax.broadcasted_iota(jnp.int32, (points, LANES), 1) < SIDE
    for parity in range(2):
        for comp in range(2):
            cols = slice(comp * LANES, (comp + 1) * LANES)
            value = jnp.where(odd, totals[2 + parity][:, cols], totals[parity][:, cols])
            top, bottom = value[:points], value[points:]
            kind = 2 * parity + comp
            weights[0, kind] = jnp.where(left, top, pltpu.roll(bottom, SIDE, 1))
            weights[1, kind] = jnp.where(left, pltpu.roll(top, SIDE, 1), bottom)
    for copy in copies[pieces:]:
        copy.wait()
    current[...] = start_ref[0]
    level[...] = start_ref[1]
    before[...] = jnp.zeros_like(before)

    def step(block, carry):
        base = pl.multiple_of(block * BLOCK, BLOCK)
        now = block.astype(jnp.float32)
        second, begins = now >= turn, now == turn
        grow = growth_ref[pl.ds(block, 1)]
        first = 0
        for chunk in CHUNKS:
            rows = slice(first, first + chunk)
            height = jnp.where(begins, start_ref[3, rows], level[rows])
            factor = jnp.exp2(height)
            scaled = [
                jnp.where(second, weights[1, k, rows], weights[0, k, rows]) * factor for k in range(4)
            ]
            cosine = lat_ref[0, rows]
            old = jnp.where(begins, 0.0, before[rows])
            new = jnp.where(begins, start_ref[2, rows], current[rows])
            for order in range(BLOCK):
                for comp in range(2):
                    product = new * scaled[2 * (order % 2) + comp]
                    partial = product.reshape(chunk // 8, 8, LANES).sum(axis=0)
                    place = pl.ds((order * 2 + comp) * 8, 8)
                    if first == 0:
                        sums[place] = partial
                    else:
                        sums[place] += partial
                beta = beta_ref[pl.ds(base + order, 1)]
                old, new = new, cosine * new - beta * old
            biggest = jnp.maximum(jnp.abs(old), jnp.abs(new)) * grow
            shift = jnp.floor(jnp.log(biggest) * (1.0 / math.log(2.0)))
            factor = grow * jnp.exp2(-shift)
            before[rows] = old * factor
            current[rows] = new * factor
            level[rows] = height + shift
            first += chunk
        for comp in range(2):
            total = sums[pl.ds(comp * 8, BLOCK, stride=16)]
            for lane in range(1, 8):
                total += sums[pl.ds(comp * 8 + lane, BLOCK, stride=16)]
            total = total * scale_ref[pl.ds(base, BLOCK)]
            result[comp, pl.ds(base, BLOCK)] = total + pltpu.roll(total, SIDE, 1)
        return carry

    lax.fori_loop(0, block_total, step, 0)

    left = lax.broadcasted_iota(jnp.int32, (BLOCK, LANES), 1) < SIDE
    for place in range(-(-M // BLOCK)):
        rows = pl.ds(place * BLOCK, BLOCK)

        def pick(block, found):
            chosen = block.astype(jnp.float32) - place == turn
            base = pl.multiple_of(block * BLOCK, BLOCK)
            return tuple(
                jnp.where(chosen, result[comp, pl.ds(base, BLOCK)], found[comp]) for comp in range(2)
            )

        blank = jnp.zeros((BLOCK, LANES), jnp.float32)
        later = lax.fori_loop(place, block_total, pick, (blank, blank))
        for comp in range(2):
            early = jnp.where(turn > place, result[comp, rows], 0.0)
            final[comp, rows] = jnp.where(left, early, later[comp])
    back = back_ref[...]
    dims = (((1,), (1,)), ((), ()))
    for comp in range(2):
        high, low = split_bf16(final[comp])
        value = lax.dot_general(back, high, dims, preferred_element_type=jnp.float32)
        value += lax.dot_general(back, low, dims, preferred_element_type=jnp.float32)
        out_ref[:, comp, :] = value[:slots, :M]


def legendre(fields, order, mine, back, prepared, rows, slots):
    pieces = len(fields)
    padded_rows = fields[0].shape[0]
    latitudes = latitude_table()
    points = latitudes.shape[1]
    table = resample_table().reshape(8 * points, pieces, rows).transpose(1, 0, 2)
    table = table_bf16(np.pad(table, ((0, 0), (0, 0), (0, padded_rows - rows))))
    table = table.reshape(pieces, 8 * points, 2, padded_rows).transpose(0, 2, 1, 3)
    tables = (table, latitudes, *prepared)
    vector = pltpu.VMEM((points, LANES), jnp.float32)
    block_rows = -(-M // BLOCK) * BLOCK
    return pl.pallas_call(
        functools.partial(legendre_kernel, pieces),
        out_shape=jax.ShapeDtypeStruct((slots, 2, M), jnp.float32),
        in_specs=[SMEM_SPEC] + [VMEM_SPEC] * pieces + [HBM_SPEC] * 6 + [VMEM_SPEC] * 2,
        out_specs=VMEM_SPEC,
        scratch_shapes=[pltpu.VMEM(array.shape, array.dtype) for array in tables]
        + [
            pltpu.VMEM((2, 4, points, LANES), jnp.float32),
            vector,
            vector,
            vector,
            pltpu.VMEM((BLOCK * 16, LANES), jnp.float32),
            pltpu.VMEM((2, 2 * block_rows, LANES), jnp.float32),
            pltpu.VMEM((2, block_rows, LANES), jnp.float32),
            pltpu.SemaphoreType.DMA((pieces + 5,)),
        ],
        compiler_params=pltpu.CompilerParams(vmem_limit_bytes=VMEM_BYTES),
        cost_estimate=pl.CostEstimate(
            flops=7 * points * LANES * M, bytes_accessed=6 * 2**20, transcendentals=0
        ),
    )(order, *fields, *tables, mine, back)


def shards(tracer, wind_east, wind_north, keep_m, slot_wave):
    rows = tracer.shape[1]
    lat_count = lax.axis_size("lat")
    slots = slot_wave.shape[0] // lat_count
    lat_index = lax.axis_index("lat").astype(jnp.int32)
    ring = ("lev", "fld")
    level_order, lat_order = partners(ring), partners("lat")

    blocks, edges = advect(tracer, wind_east, wind_north, level_order)
    grids = exchange(blocks, ring)
    ends, slot_wave, keep_m = lax.optimization_barrier(
        (halo(level_order, *edges), slot_wave, keep_m)
    )
    halos = exchange(ends, ring)
    places, wave_row, mine, back, keep_col, sine_col = prepare_places(
        lat_order, lat_index, slot_wave, keep_m, lat_count
    )
    waved = fourier(
        grids, halos, level_order, places, wave_row, keep_col, sine_col, lat_count
    )
    waved, mine = lax.optimization_barrier((list(waved), mine))
    fields = exchange(waved, "lat")
    prepared = prepare_recurrence(mine)
    return legendre(fields, lat_order, mine, back, prepared, rows, slots)[None]


def solution(mesh):
    return jax.shard_map(
        shards,
        mesh=mesh,
        in_specs=(
            P("member", "lat", ("lev", "fld")),
            P("member", "lat", ("lev", "fld")),
            P("member", "lat", ("lev", "fld")),
            P("lat"),
            P(),
        ),
        out_specs=P(("member", "lev", "fld"), "lat", None, None),
        check_vma=False,
    )
```

```python
import functools
import math

import jax
import jax.numpy as jnp
import numpy as np
from jax import lax
from jax.experimental import pallas as pl
from jax.experimental.pallas import tpu as pltpu
from jax.sharding import PartitionSpec as P

M = 400
NLAT = 800
NLON = 1600
LANES = 128
BLOCK = 32
CHUNKS = (40, 32, 32)
SIDE = LANES // 2
TOP = 32767.0
WIND_STEP = 1.5 / TOP
VMEM_BYTES = 60 * 2**20
LATE_BYTES = 24 * 2**20
VMEM_SPEC = pl.BlockSpec(memory_space=pltpu.VMEM)
SMEM_SPEC = pl.BlockSpec(memory_space=pltpu.SMEM)
HBM_SPEC = pl.BlockSpec(memory_space=pltpu.HBM)


def split_bf16(values):
    high = values.astype(jnp.bfloat16)
    low = (values - high.astype(jnp.float32)).astype(jnp.bfloat16)
    return high, low


def table_bf16(table):
    high = table.astype(jnp.bfloat16)
    low = (table - high.astype(np.float64)).astype(jnp.bfloat16)
    return np.concatenate([high, low], axis=-1)


def fourier_tables(pieces):
    quarter = NLON // 4
    spots = np.arange(quarter)[:, None]
    factor = 1.0 / math.sqrt(NLON)

    def parts(waves):
        angles = 2.0 * math.pi / NLON * (spots * waves[None, :] % NLON)
        return factor * np.cos(angles), factor * np.sin(angles)

    tables = []
    for first in (0, 2):
        cosine, sine = parts(np.arange(first, M, 4))
        tables.append([cosine, -sine])
    waves = np.arange(1, M, 2)
    sign = np.where(waves % 4 == 1, 1.0, -1.0)[None, :]
    cosine, sine = parts(waves)
    tables.append([cosine, -sine])
    tables.append([-sign * sine, -sign * cosine])
    share = pieces // 4
    result = []
    for columns in tables:
        table = np.concatenate(columns, axis=1)
        table = np.pad(table, ((0, 0), (0, -table.shape[1] % (2 * LANES))))
        result.append(table.reshape(share, quarter // share, table.shape[1]))
    return result


def column_waves():
    width = -(-M // 2 // (2 * LANES)) * 2 * LANES
    spots = np.full(4 * width, -1.0, np.float32)
    waves = np.arange(M)
    for part in range(2):
        even = np.where(waves % 4 == 0, 0, width) + part * (M // 4) + waves // 4
        odd = 2 * width + part * (M // 2) + waves // 2
        spots[np.where(waves % 2 == 0, even, odd)] = 2 * waves + part
    return spots[:, None]


def resample_table():
    half = M // 2
    coarse = math.pi / M * (np.arange(M) + 0.5)
    fine = math.pi / NLAT * (np.arange(NLAT) + 0.5)
    waves = np.arange(M)
    weight = np.where(waves == 0, 1.0, 2.0) / M
    even = (np.cos(np.outer(coarse, waves)) * weight) @ np.cos(np.outer(waves, fine))
    odd = (np.sin(np.outer(coarse, waves)) * weight) @ np.sin(np.outer(waves, fine))
    rows = []
    for full in (even, odd):
        for sign in (1.0, -1.0):
            folded = (full[:half] + sign * full[::-1][:half]).reshape(2, half // 2, NLAT)
            rows.append(np.pad(folded, ((0, 0), (0, -half // 2 % 8), (0, 0))).reshape(-1, NLAT))
    return np.concatenate(rows, axis=0)


def latitude_table():
    half = M // 2
    angles = math.pi / M * (np.arange(half) + 0.5)
    log_sine = np.log2(np.sin(angles))
    coarse = np.round(log_sine * 1024.0) / 1024.0
    rows = np.stack([2.0 * np.cos(angles), coarse, log_sine - coarse]).reshape(3, 2, half // 2)
    rows = np.pad(rows, ((0, 0), (0, 0), (0, -half // 2 % 8)))
    return np.repeat(rows.transpose(0, 2, 1), SIDE, axis=2).astype(np.float32)


def scale_code(biggest):
    wanted = jnp.maximum(biggest, 1e-30) * (1.0 / TOP)
    exponent = jnp.floor(jnp.log(wanted) * (1.0 / math.log(2.0)))
    return exponent * 128.0 + jnp.ceil((wanted * jnp.exp2(-exponent) - 1.0) * 128.0)


def scale_of(code):
    exponent = jnp.floor(code * (1.0 / 128.0))
    rest = code - 128.0 * exponent
    return jnp.exp2(exponent) * (1.0 + rest * (1.0 / 128.0))


def coded(values, inverse):
    return jnp.floor(values * inverse + 0.5)


def as_int16(values):
    return values.astype(jnp.int32).astype(jnp.int16)


def from_int16(codes):
    return codes.astype(jnp.int32).astype(jnp.float32)


def partners(axis):
    count = lax.axis_size(axis)
    order = jnp.arange(count, dtype=jnp.int32)
    return lax.axis_index(axis).astype(jnp.int32) ^ order if count == 4 else order


def exchange(blocks, axis):
    count = len(blocks)
    if count != 4:
        return list(lax.all_to_all(jnp.stack(blocks), axis, split_axis=0, concat_axis=0, tiled=True))
    pairs = [[(i, i ^ step) for i in range(count)] for step in range(count)]
    return [blocks[0]] + [lax.ppermute(blocks[step], axis, pairs[step]) for step in range(1, count)]


def advect_kernel(steps, order_ref, tracer_hbm, east_hbm, north_hbm, above_ref, below_ref, *rest):
    _, rows, lons = tracer_hbm.shape
    outs, (tracer, east_wind, north_wind, sems) = rest[: len(steps)], rest[len(steps) :]
    copies = []
    for spot, step in enumerate(steps):
        level = order_ref[step]
        copies.append(
            [
                pltpu.make_async_copy(source.at[level], target.at[spot], sems.at[spot, kind])
                for kind, (source, target) in enumerate(
                    ((tracer_hbm, tracer), (east_hbm, east_wind), (north_hbm, north_wind))
                )
            ]
        )
        for copy in copies[-1]:
            copy.start()
    end = (lons - 1) // LANES * LANES
    spare = lons - end
    lane = lax.broadcasted_iota(jnp.int32, (rows, LANES), 1)
    for spot, step in enumerate(steps):
        level = order_ref[step]
        for copy in copies[spot]:
            copy.wait()
        field = tracer[spot].astype(jnp.float32)
        blank = jnp.zeros((rows, 1), jnp.float32)
        west = jnp.concatenate([blank, field[:, :-1]], axis=1)
        east = jnp.concatenate([field[:, 1:], blank], axis=1)
        north = jnp.concatenate([above_ref[level].astype(jnp.float32), field[:-1]], axis=0)
        south = jnp.concatenate([field[1:], below_ref[level].astype(jnp.float32)], axis=0)
        eastward = 0.5 * east_wind[spot].astype(jnp.float32)
        northward = 0.5 * north_wind[spot].astype(jnp.float32)
        moved = field - eastward * (east - west) - northward * (south - north)
        first, last = field[:, :1], field[:, lons - 1 :]
        biggest = jnp.max(jnp.abs(moved), axis=1, keepdims=True)
        biggest = jnp.maximum(biggest, jnp.maximum(jnp.abs(first), jnp.abs(last)))
        code = scale_code(biggest)
        inverse = 1.0 / scale_of(code)
        filler = jnp.zeros((rows, LANES - spare), jnp.float32)
        tile = jnp.concatenate([moved[:, end:], filler], axis=1)
        tile = jnp.where(lane == spare + 1, first, jnp.where(lane == spare + 2, last, tile))
        tile = coded(tile, inverse)
        tile = jnp.where(lane == spare, code, tile)
        winds = jnp.where(lane == spare + 3, eastward[:, :1], eastward[:, lons - 1 :])
        winds = coded(winds, 1.0 / WIND_STEP)
        tile = jnp.where((lane == spare + 3) | (lane == spare + 4), winds, tile)
        outs[spot][:, :end] = as_int16(coded(moved[:, :end], inverse))
        outs[spot][:, end:] = as_int16(tile)


def advect(tracer, east_wind, north_wind, above, below, order, steps):
    levels, rows, lons = tracer.shape
    width = (lons - 1) // LANES * LANES + LANES
    count = len(steps)
    held = pltpu.VMEM((count, rows, lons), jnp.bfloat16)
    return pl.pallas_call(
        functools.partial(advect_kernel, steps),
        out_shape=[jax.ShapeDtypeStruct((rows, width), jnp.int16)] * count,
        in_specs=[SMEM_SPEC] + [HBM_SPEC] * 3 + [VMEM_SPEC] * 2,
        out_specs=[VMEM_SPEC] * count,
        scratch_shapes=[held, held, held, pltpu.SemaphoreType.DMA((count, 3))],
        compiler_params=pltpu.CompilerParams(vmem_limit_bytes=VMEM_BYTES),
        cost_estimate=pl.CostEstimate(
            flops=20 * count * rows * lons, bytes_accessed=8 * count * rows * lons, transcendentals=0
        ),
    )(order, tracer, east_wind, north_wind, above, below)


def fourier_kernel(pieces, targets, order_ref, *rest):
    grids, rest = rest[:pieces], rest[pieces:]
    tables_hbm, (wave_ref, keep_ref, sine_ref), rest = rest[:5], rest[5:8], rest[8:]
    outs, rest = rest[:targets], rest[targets:]
    tables, place_ref, (field, sems) = rest[:4], rest[4], rest[5:]
    _, rows, width = field.shape
    lons = tables[0].shape[1]
    share = pieces // 4
    copies = []
    for kind, target in enumerate((*tables, place_ref)):
        copies.append(pltpu.make_async_copy(tables_hbm[kind], target, sems.at[kind]))
        copies[-1].start()

    end = width - LANES
    spare = lons - end
    lane = lax.broadcasted_iota(jnp.int32, (rows, LANES), 1)
    winds = (lane == spare + 3) | (lane == spare + 4)
    for piece in range(pieces):
        spot = order_ref[piece]
        values = from_int16(grids[piece][...])
        tile = values[:, end:]
        scale = scale_of(tile[:, spare : spare + 1])
        field[spot, :, :end] = values[:, :end] * scale
        field[spot, :, end:] = tile * jnp.where(winds, WIND_STEP, scale)
    for spot in range(pieces):
        tile = field[spot, :, end:]
        before = field[(spot - 1) % pieces, :, end:]
        after = field[(spot + 1) % pieces, :, end:]
        shift = LANES - spare
        gain = pltpu.roll(tile, shift - 3, 1) * pltpu.roll(before, shift - 2, 1)
        loss = pltpu.roll(tile, LANES - 5, 1) * pltpu.roll(after, LANES - 2, 1)
        field[spot, :, end:] = tile - jnp.where(lane == spare - 1, loss, 0.0)
        field[spot, :, :LANES] += jnp.where(lane == 0, gain, 0.0)

    def product(value, table, spot):
        high, low = split_bf16(value)
        width = table.shape[2] // 2
        both = jnp.dot(high, table[spot], preferred_element_type=jnp.float32)
        part = jnp.dot(low, table[spot, :, :width], preferred_element_type=jnp.float32)
        return part + both[:, :width] + both[:, width:]

    sums = [None, None, None]
    for spot in range(share):
        quarters = [field[quarter * share + spot, :, :lons] for quarter in range(4)]
        sum02, dif02 = quarters[0] + quarters[2], quarters[0] - quarters[2]
        sum13, dif13 = quarters[1] + quarters[3], quarters[1] - quarters[3]
        parts = []
        for kind, value in enumerate((sum02 + sum13, sum02 - sum13, dif02, dif13)):
            if spot == 0:
                copies[kind].wait()
            parts.append(product(value, tables[kind], spot))
        parts = [parts[0], parts[1], parts[2] + parts[3]]
        sums = [part if total is None else total + part for total, part in zip(sums, parts)]
    placed = None
    first = 0
    copies[4].wait()
    for total in sums:
        last = first + total.shape[1]
        high, low = split_bf16(total)
        part = jnp.dot(high, place_ref[first:last], preferred_element_type=jnp.float32)
        part += jnp.dot(low, place_ref[first:last], preferred_element_type=jnp.float32)
        placed = part if placed is None else placed + part
        first = last
    kept = jnp.where(wave_ref[...] < keep_ref[...], placed * sine_ref[...], 0.0)
    code = scale_code(jnp.max(jnp.abs(kept), axis=0, keepdims=True))
    steps = coded(kept, 1.0 / scale_of(code))
    padded_rows, span = outs[0].shape
    codes = jnp.broadcast_to(code, (padded_rows - rows, code.shape[1]))
    result = as_int16(jnp.concatenate([steps, codes], axis=0))
    for target in range(targets):
        outs[target][...] = result[:, target * span : (target + 1) * span]


def fourier(grids, order, places, wave_row, keep_col, sine_col, targets):
    pieces = len(grids)
    rows, width = grids[0].shape
    lons = NLON // pieces
    span = wave_row.shape[1] // targets
    padded_rows = -(-(rows + 1) // 16) * 16
    tables = [table_bf16(table) for table in fourier_tables(pieces)]
    return pl.pallas_call(
        functools.partial(fourier_kernel, pieces, targets),
        out_shape=[jax.ShapeDtypeStruct((padded_rows, span), jnp.int16)] * targets,
        in_specs=[SMEM_SPEC] + [VMEM_SPEC] * pieces + [HBM_SPEC] * 5 + [VMEM_SPEC] * 3,
        out_specs=[VMEM_SPEC] * targets,
        scratch_shapes=[pltpu.VMEM(table.shape, jnp.bfloat16) for table in tables]
        + [pltpu.VMEM(places.shape, jnp.bfloat16)]
        + [pltpu.VMEM((pieces, rows, width), jnp.float32), pltpu.SemaphoreType.DMA((5,))],
        compiler_params=pltpu.CompilerParams(vmem_limit_bytes=VMEM_BYTES),
        cost_estimate=pl.CostEstimate(
            flops=3 * rows * NLON * M, bytes_accessed=6 * 2**20, transcendentals=0
        ),
    )(order, *grids, *tables, places, wave_row, keep_col, sine_col)


def places_kernel(
    order_ref, lat_ref, slot_ref, keep_ref, sine_ref, spot_ref,
    place_ref, wave_ref, mine_ref, back_ref, keep_col, sine_col, sorted_rows,
):
    groups, _, rows = sine_ref.shape
    slots = slot_ref.shape[1] // groups
    paired = (slots + 1) // 2
    shape = (LANES, LANES)
    down = lax.broadcasted_iota(jnp.int32, shape, 0)
    across = lax.broadcasted_iota(jnp.int32, shape, 1)
    filler = jnp.full((1, LANES - slots), 2.0 * M, jnp.float32)
    for group in range(groups):
        row = slot_ref[:, group * slots : (group + 1) * slots].astype(jnp.float32)
        row = jnp.broadcast_to(jnp.concatenate([row, filler], axis=1), shape)
        column = jnp.sum(jnp.where(down == across, row, 0.0), axis=1, keepdims=True)
        ahead = (row < column) | ((row == column) & (across < down))
        rank = jnp.sum(jnp.where(ahead, 1.0, 0.0), axis=1, keepdims=True)
        place = jnp.where(rank < paired, rank, SIDE + slots - 1.0 - rank)
        place = jnp.where(rank < slots, place, -1.0)
        hot = jnp.where(place == across.astype(jnp.float32), 1.0, 0.0)
        filled = jnp.sum(hot, axis=0, keepdims=True)
        values = jnp.sum(hot * column, axis=0, keepdims=True)
        values = jnp.where(filled > 0.5, values, 2.0 * M)
        sorted_rows[group] = jnp.broadcast_to(values, sorted_rows.shape[1:])

        @pl.when(group == lat_ref[0])
        def _():
            mine_ref[...] = values
            back_ref[...] = hot.astype(jnp.bfloat16)

    spots = spot_ref[...]
    for step in range(groups):
        row = sorted_rows[order_ref[step], :1]
        for part in range(2):
            cols = slice((2 * step + part) * LANES, (2 * step + part + 1) * LANES)
            wave_ref[:, cols] = row
            hit = spots == 2.0 * row + part
            place_ref[:, cols] = jnp.where(hit, 1.0, 0.0).astype(jnp.bfloat16)

    shape = (rows, rows)
    same = lax.broadcasted_iota(jnp.int32, shape, 0) == lax.broadcasted_iota(jnp.int32, shape, 1)
    kept = jnp.broadcast_to(keep_ref[...].astype(jnp.float32), shape)
    keep_col[...] = jnp.sum(jnp.where(same, kept, 0.0), axis=1, keepdims=True)
    sine = jnp.broadcast_to(sine_ref[lat_ref[0]], shape)
    sine_col[...] = jnp.sum(jnp.where(same, sine, 0.0), axis=1, keepdims=True)


def prepare_places(order, lat_index, slot_wave, keep_m, groups):
    rows = keep_m.shape[0]
    sines = np.sin(math.pi / NLAT * (np.arange(NLAT) + 0.5)) * math.sqrt(2.0 / NLAT)
    spots = column_waves()
    width = 2 * groups * LANES
    return pl.pallas_call(
        places_kernel,
        out_shape=[
            jax.ShapeDtypeStruct((spots.shape[0], width), jnp.bfloat16),
            jax.ShapeDtypeStruct((1, width), jnp.float32),
            jax.ShapeDtypeStruct((1, LANES), jnp.float32),
            jax.ShapeDtypeStruct((LANES, LANES), jnp.bfloat16),
            jax.ShapeDtypeStruct((rows, 1), jnp.float32),
            jax.ShapeDtypeStruct((rows, 1), jnp.float32),
        ],
        in_specs=[SMEM_SPEC] * 2 + [VMEM_SPEC] * 4,
        out_specs=[VMEM_SPEC] * 6,
        scratch_shapes=[pltpu.VMEM((groups, 8, LANES), jnp.float32)],
        compiler_params=pltpu.CompilerParams(vmem_limit_bytes=VMEM_BYTES),
    )(
        order, lat_index[None], slot_wave[None], keep_m[None],
        sines.reshape(groups, 1, rows).astype(np.float32), spots,
    )


def lane_pairs(row):
    lane = lax.broadcasted_iota(jnp.int32, row.shape, 1)
    other = pltpu.roll(row, SIDE, 1)
    return jnp.where(lane < SIDE, row, other), jnp.where(lane < SIDE, other, row)


def block_count(wave):
    return jnp.floor((jnp.maximum(M - wave, 0.0) + (BLOCK - 1)) * (1.0 / BLOCK))


def recurrence_kernel(mine_ref, lat_ref, term_ref, beta_ref, scale_ref, growth_ref, start_ref):
    pair = lane_pairs(jnp.broadcast_to(mine_ref[...], (8, LANES)))
    one, two = pair[0][:1], pair[1][:1]
    blocks = growth_ref.shape[0]
    turn = block_count(one)
    block = lax.broadcasted_iota(jnp.int32, (blocks, LANES), 0).astype(jnp.float32)
    second = block >= turn
    wave = jnp.where(second, two, one)
    limit = M - wave
    wave = jnp.minimum(wave, M - 1.0)
    first = (block - jnp.where(second, turn, 0.0)) * BLOCK

    scale = jnp.ones((blocks, LANES), jnp.float32)
    for index in range(BLOCK + 1):
        order = first + index
        degree = wave + order
        square = 4.0 * degree * degree - 1.0
        spread = 4.0 * order * (degree + wave)
        if index > 0:
            scale = scale * jnp.sqrt(square / spread)
        if index < BLOCK:
            beta_ref[pl.ds(index, blocks, stride=BLOCK)] = spread / jnp.maximum(square, 1.0)
            scale_ref[pl.ds(index, blocks, stride=BLOCK)] = jnp.where(order < limit, scale, 0.0)
    growth_ref[...] = scale

    for kind, wave in enumerate((one, two)):
        wave = jnp.minimum(wave, M - 1.0)
        counter = lax.broadcasted_iota(jnp.int32, term_ref.shape, 0).astype(jnp.float32)
        norm = jnp.sum(jnp.where(counter <= wave, term_ref[...], 0.0), axis=0, keepdims=True)
        coarse = lat_ref[1] * wave
        whole = jnp.floor(coarse)
        start_ref[2 * kind] = jnp.exp2(
            (coarse - whole) + lat_ref[2] * wave + 0.5 * (norm - 1.0)
        )
        start_ref[2 * kind + 1] = whole


def prepare_recurrence(mine):
    latitudes = latitude_table()
    points = latitudes.shape[1]
    blocks = 2 * -(-M // BLOCK)
    counter = np.arange(M)
    terms = np.log1p(0.5 / np.maximum(counter, 1)) * (counter > 0) / math.log(2.0)
    terms = np.broadcast_to(terms[:, None], (M, LANES)).astype(np.float32)
    orders = jax.ShapeDtypeStruct((blocks * BLOCK, LANES), jnp.float32)
    return pl.pallas_call(
        recurrence_kernel,
        out_shape=[
            orders,
            orders,
            jax.ShapeDtypeStruct((blocks, LANES), jnp.float32),
            jax.ShapeDtypeStruct((4, points, LANES), jnp.float32),
        ],
        in_specs=[VMEM_SPEC] * 3,
        out_specs=[VMEM_SPEC] * 4,
        compiler_params=pltpu.CompilerParams(vmem_limit_bytes=LATE_BYTES),
    )(mine, latitudes, terms)


def resampled(first, order_ref, fields, table, total):
    for piece, field in enumerate(fields):
        values = from_int16(field[...])
        values = values * scale_of(values[field.shape[0] - 1 :])
        high, low = split_bf16(values)
        spot = order_ref[first + piece]
        both = jnp.concatenate([high, low], axis=1)
        part = jnp.dot(table[spot, 0], both, preferred_element_type=jnp.float32)
        part = part[:, : high.shape[1]] + part[:, high.shape[1] :]
        part += jnp.dot(table[spot, 1], high, preferred_element_type=jnp.float32)
        total = part if total is None else total + part
    return total


def resample_kernel(order_ref, table_ref, *rest):
    rest[-1][...] = resampled(0, order_ref, rest[:-1], table_ref, None)


def resample(fields, order, table):
    count, _, height, _ = table.shape
    span = fields[0].shape[1]
    return pl.pallas_call(
        resample_kernel,
        out_shape=jax.ShapeDtypeStruct((height, span), jnp.float32),
        in_specs=[SMEM_SPEC] + [VMEM_SPEC] * (1 + len(fields)),
        out_specs=VMEM_SPEC,
        compiler_params=pltpu.CompilerParams(vmem_limit_bytes=LATE_BYTES),
        cost_estimate=pl.CostEstimate(
            flops=6 * height * span * NLAT // count * len(fields), bytes_accessed=4 * 2**20, transcendentals=0
        ),
    )(order, table, *fields)


def legendre_kernel(early, order_ref, *rest):
    table, lat_ref, beta_ref, scale_ref, growth_ref, start_ref, total_ref, mine_ref, back_ref = rest[:9]
    fields, rest = rest[9:-8], rest[-8:]
    out_ref, weights, before, current, level, sums, result, final = rest
    points = lat_ref.shape[1]
    slots = out_ref.shape[0]
    mine = mine_ref[...]
    odd = mine - 2.0 * jnp.floor(mine * 0.5) > 0.5
    pair = lane_pairs(jnp.broadcast_to(mine, (8, LANES)))
    turn = block_count(pair[0][:1])
    block_total = jnp.max(turn + block_count(pair[1][:1])).astype(jnp.int32)

    total = resampled(early, order_ref, fields, table, total_ref[...])
    totals = [total[2 * points * kind : 2 * points * (kind + 1)] for kind in range(4)]
    left = lax.broadcasted_iota(jnp.int32, (points, LANES), 1) < SIDE
    for parity in range(2):
        for comp in range(2):
            cols = slice(comp * LANES, (comp + 1) * LANES)
            value = jnp.where(odd, totals[2 + parity][:, cols], totals[parity][:, cols])
            top, bottom = value[:points], value[points:]
            kind = 2 * parity + comp
            weights[0, kind] = jnp.where(left, top, pltpu.roll(bottom, SIDE, 1))
            weights[1, kind] = jnp.where(left, pltpu.roll(top, SIDE, 1), bottom)
    result[...] = jnp.zeros_like(result)
    current[...] = start_ref[0]
    level[...] = start_ref[1]
    before[...] = jnp.zeros_like(before)

    def step(block, carry):
        base = pl.multiple_of(block * BLOCK, BLOCK)
        now = block.astype(jnp.float32)
        second, begins = now >= turn, now == turn
        grow = growth_ref[pl.ds(block, 1)]
        first = 0
        for chunk in CHUNKS:
            rows = slice(first, first + chunk)
            height = jnp.where(begins, start_ref[3, rows], level[rows])
            factor = jnp.exp2(height)
            scaled = [
                jnp.where(second, weights[1, k, rows], weights[0, k, rows]) * factor for k in range(4)
            ]
            cosine = lat_ref[0, rows]
            old = jnp.where(begins, 0.0, before[rows])
            new = jnp.where(begins, start_ref[2, rows], current[rows])
            for order in range(BLOCK):
                for comp in range(2):
                    product = new * scaled[2 * (order % 2) + comp]
                    partial = product.reshape(chunk // 8, 8, LANES).sum(axis=0)
                    place = pl.ds((order * 2 + comp) * 8, 8)
                    if first == 0:
                        sums[place] = partial
                    else:
                        sums[place] += partial
                beta = beta_ref[pl.ds(base + order, 1)]
                old, new = new, cosine * new - beta * old
            biggest = jnp.maximum(jnp.abs(old), jnp.abs(new)) * grow
            shift = jnp.floor(jnp.log(biggest) * (1.0 / math.log(2.0)))
            factor = grow * jnp.exp2(-shift)
            before[rows] = old * factor
            current[rows] = new * factor
            level[rows] = height + shift
            first += chunk
        for comp in range(2):
            total = sums[pl.ds(comp * 8, BLOCK, stride=16)]
            for lane in range(1, 8):
                total += sums[pl.ds(comp * 8 + lane, BLOCK, stride=16)]
            total = total * scale_ref[pl.ds(base, BLOCK)]
            result[comp, pl.ds(base, BLOCK)] = total + pltpu.roll(total, SIDE, 1)
        return carry

    lax.fori_loop(0, block_total, step, 0)

    left = lax.broadcasted_iota(jnp.int32, (BLOCK, LANES), 1) < SIDE
    spots = -(-M // BLOCK)
    chosen = [jnp.broadcast_to(turn, (8, LANES)) == value for value in range(spots + 1)]
    chosen = [jnp.concatenate([mask] * (BLOCK // 8), axis=0) for mask in chosen]
    for place in range(spots):
        rows = slice(place * BLOCK, (place + 1) * BLOCK)
        for comp in range(2):
            early_part = jnp.where(turn > place, result[comp, rows], 0.0)
            later = jnp.zeros((BLOCK, LANES), jnp.float32)
            for value in range(spots + 1):
                base = (place + value) * BLOCK
                if base < result.shape[1]:
                    later = jnp.where(chosen[value], result[comp, base : base + BLOCK], later)
            final[comp, rows] = jnp.where(left, early_part, later)
    back = back_ref[...]
    dims = (((1,), (1,)), ((), ()))
    for comp in range(2):
        high, low = split_bf16(final[comp])
        value = lax.dot_general(back, high, dims, preferred_element_type=jnp.float32)
        value += lax.dot_general(back, low, dims, preferred_element_type=jnp.float32)
        out_ref[:, comp, :] = value[:slots, :M]


def resample_pieces(pieces, rows, padded_rows):
    full = resample_table()
    table = full.reshape(full.shape[0], pieces, rows).transpose(1, 0, 2)
    table = table_bf16(np.pad(table, ((0, 0), (0, 0), (0, padded_rows - rows))))
    return table.reshape(pieces, full.shape[0], 2, padded_rows).transpose(0, 2, 1, 3)


def legendre(fields, order, mine, back, prepared, rows, slots):
    pieces = len(fields)
    early = pieces // 2
    latitudes = latitude_table()
    points = latitudes.shape[1]
    table = jnp.asarray(resample_pieces(pieces, rows, fields[0].shape[0]))
    total = resample(fields[:early], order, table)
    vector = pltpu.VMEM((points, LANES), jnp.float32)
    block_rows = -(-M // BLOCK) * BLOCK
    return pl.pallas_call(
        functools.partial(legendre_kernel, early),
        out_shape=jax.ShapeDtypeStruct((slots, 2, M), jnp.float32),
        in_specs=[SMEM_SPEC] + [VMEM_SPEC] * (9 + pieces - early),
        out_specs=VMEM_SPEC,
        scratch_shapes=[
            pltpu.VMEM((2, 4, points, LANES), jnp.float32),
            vector,
            vector,
            vector,
            pltpu.VMEM((BLOCK * 16, LANES), jnp.float32),
            pltpu.VMEM((2, 2 * block_rows, LANES), jnp.float32),
            pltpu.VMEM((2, block_rows, LANES), jnp.float32),
        ],
        compiler_params=pltpu.CompilerParams(vmem_limit_bytes=LATE_BYTES),
        cost_estimate=pl.CostEstimate(
            flops=7 * points * LANES * M, bytes_accessed=6 * 2**20, transcendentals=0
        ),
    )(order, table, latitudes, *prepared, total, mine, back, *fields[early:])


def shards(tracer, wind_east, wind_north, keep_m, slot_wave):
    rows = tracer.shape[1]
    lat_count = lax.axis_size("lat")
    slots = slot_wave.shape[0] // lat_count
    lat_index = lax.axis_index("lat").astype(jnp.int32)
    ring = ("lev", "fld")
    level_order, lat_order = partners(ring), partners("lat")

    count = lax.axis_size("lat")
    above = lax.ppermute(tracer[:, rows - 1 :], "lat", [(i, i + 1) for i in range(count - 1)])
    below = lax.ppermute(tracer[:, :1], "lat", [(i + 1, i) for i in range(count - 1)])
    fields = (tracer, wind_east, wind_north, above, below, level_order)
    levels = tracer.shape[0]
    far = advect(*fields, tuple(range(levels // 2, levels)))
    near = advect(*fields, tuple(range(levels // 2)))
    near, slot_wave, keep_m = lax.optimization_barrier((list(near), slot_wave, keep_m))
    grids = exchange([*near, *far], ring)
    places, wave_row, mine, back, keep_col, sine_col = prepare_places(
        lat_order, lat_index, slot_wave, keep_m, lat_count
    )
    waved = fourier(
        grids, level_order, places, wave_row, keep_col, sine_col, lat_count
    )
    waved, mine = lax.optimization_barrier((list(waved), mine))
    fields = exchange(waved, "lat")
    prepared = prepare_recurrence(mine)
    return legendre(fields, lat_order, mine, back, prepared, rows, slots)[None]


def solution(mesh):
    return jax.shard_map(
        shards,
        mesh=mesh,
        in_specs=(
            P("member", "lat", ("lev", "fld")),
            P("member", "lat", ("lev", "fld")),
            P("member", "lat", ("lev", "fld")),
            P("lat"),
            P(),
        ),
        out_specs=P(("member", "lev", "fld"), "lat", None, None),
        check_vma=False,
    )
```

```python
import functools
import math

import jax
import jax.numpy as jnp
import numpy as np
from jax import lax
from jax.experimental import pallas as pl
from jax.experimental.pallas import tpu as pltpu
from jax.sharding import PartitionSpec as P

M = 400
NLAT = 800
NLON = 1600
LANES = 128
BLOCK = 32
CHUNKS = (40, 32, 32)
SIDE = LANES // 2
TOP = 32767.0
WIND_STEP = 1.5 / TOP
VMEM_BYTES = 60 * 2**20
LATE_BYTES = 24 * 2**20
VMEM_SPEC = pl.BlockSpec(memory_space=pltpu.VMEM)
SMEM_SPEC = pl.BlockSpec(memory_space=pltpu.SMEM)
HBM_SPEC = pl.BlockSpec(memory_space=pltpu.HBM)


def split_bf16(values):
    high = values.astype(jnp.bfloat16)
    low = (values - high.astype(jnp.float32)).astype(jnp.bfloat16)
    return high, low


def table_bf16(table):
    high = table.astype(jnp.bfloat16)
    low = (table - high.astype(np.float64)).astype(jnp.bfloat16)
    return np.concatenate([high, low], axis=-1)


def fourier_tables(pieces):
    quarter = NLON // 4
    spots = np.arange(quarter)[:, None]
    factor = 1.0 / math.sqrt(NLON)

    def parts(waves):
        angles = 2.0 * math.pi / NLON * (spots * waves[None, :] % NLON)
        return factor * np.cos(angles), factor * np.sin(angles)

    def shaped(columns):
        pad = [(0, 0), (0, -columns[0].shape[1] % LANES)]
        table = np.concatenate([np.pad(part, pad) for part in columns], axis=1)
        return table.reshape(share, quarter // share, -1)

    share = pieces // 4
    tables = []
    for first in (0, 2):
        cosine, sine = parts(np.arange(first, M, 4))
        tables.append(shaped([cosine, -sine]))
    waves = np.arange(1, M, 2)
    sign = np.where(waves % 4 == 1, 1.0, -1.0)[None, :]
    cosine, sine = parts(waves)
    return [*tables, shaped([cosine, -sine]), shaped([-sign * sine, -sign * cosine])]


def column_waves():
    columns = []
    for waves in (np.arange(0, M, 4), np.arange(2, M, 4), np.arange(1, M, 2)):
        columns.append(np.pad(waves, (0, -len(waves) % LANES), constant_values=-1))
    return np.concatenate(columns).astype(np.float32)[:, None]


def resample_table():
    half = M // 2
    coarse = math.pi / M * (np.arange(M) + 0.5)
    fine = math.pi / NLAT * (np.arange(NLAT) + 0.5)
    waves = np.arange(M)
    weight = np.where(waves == 0, 1.0, 2.0) / M
    even = (np.cos(np.outer(coarse, waves)) * weight) @ np.cos(np.outer(waves, fine))
    odd = (np.sin(np.outer(coarse, waves)) * weight) @ np.sin(np.outer(waves, fine))
    rows = []
    for full in (even, odd):
        for sign in (1.0, -1.0):
            folded = (full[:half] + sign * full[::-1][:half]).reshape(2, half // 2, NLAT)
            rows.append(np.pad(folded, ((0, 0), (0, -half // 2 % 8), (0, 0))).reshape(-1, NLAT))
    return np.concatenate(rows, axis=0)


def latitude_table():
    half = M // 2
    angles = math.pi / M * (np.arange(half) + 0.5)
    log_sine = np.log2(np.sin(angles))
    coarse = np.round(log_sine * 1024.0) / 1024.0
    rows = np.stack([2.0 * np.cos(angles), coarse, log_sine - coarse]).reshape(3, 2, half // 2)
    rows = np.pad(rows, ((0, 0), (0, 0), (0, -half // 2 % 8)))
    return np.repeat(rows.transpose(0, 2, 1), SIDE, axis=2).astype(np.float32)


def scale_code(biggest):
    wanted = jnp.maximum(biggest, 1e-30) * (1.0 / TOP)
    exponent = jnp.floor(jnp.log(wanted) * (1.0 / math.log(2.0)))
    return exponent * 128.0 + jnp.ceil((wanted * jnp.exp2(-exponent) - 1.0) * 128.0)


def scale_of(code):
    exponent = jnp.floor(code * (1.0 / 128.0))
    rest = code - 128.0 * exponent
    return jnp.exp2(exponent) * (1.0 + rest * (1.0 / 128.0))


def coded(values, inverse):
    return jnp.floor(values * inverse + 0.5)


def as_int16(values):
    return values.astype(jnp.int32).astype(jnp.int16)


def from_int16(codes):
    return codes.astype(jnp.int32).astype(jnp.float32)


def partner(axes, sizes, step):
    count = math.prod(sizes)
    if count != 4:
        return step
    index = lax.axis_index(axes[0])
    for axis, size in zip(axes[1:], sizes[1:]):
        index = index * size + lax.axis_index(axis)
    return index ^ step


def exchange(blocks, axis):
    count = len(blocks)
    if count != 4:
        return list(lax.all_to_all(jnp.stack(blocks), axis, split_axis=0, concat_axis=0, tiled=True))
    pairs = [[(i, i ^ step) for i in range(count)] for step in range(count)]
    return [blocks[0]] + [lax.ppermute(blocks[step], axis, pairs[step]) for step in range(1, count)]


def advect_kernel(ring, lat_count, tracer_hbm, east_hbm, north_hbm, *rest):
    levels, rows, lons = tracer_hbm.shape
    outs, (edge_ref, tracer, east_wind, north_wind, sems) = rest[:levels], rest[levels:]
    chosen = [partner(*ring, step) for step in range(levels)]
    copies = []
    for step, level in enumerate(chosen):
        copies.append(
            [
                pltpu.make_async_copy(source.at[level], target.at[step], sems.at[step, kind])
                for kind, (source, target) in enumerate(
                    ((tracer_hbm, tracer), (east_hbm, east_wind), (north_hbm, north_wind))
                )
            ]
        )
        for copy in copies[-1]:
            copy.start()
    padded_rows = outs[0].shape[0]
    end = (lons - 1) // LANES * LANES
    spare = lons - end
    lane = lax.broadcasted_iota(jnp.int32, (rows, LANES), 1)
    lat_index = lax.axis_index("lat")
    edge_ref[...] = jnp.zeros_like(edge_ref)
    for step, level in enumerate(chosen):
        for copy in copies[step]:
            copy.wait()
        field = tracer[step].astype(jnp.float32)

        @pl.when(lat_index < lat_count - 1)
        def _():
            edge_ref[(lat_index + 1) * levels + level] = field[rows - 1 :]

        @pl.when(lat_index > 0)
        def _():
            edge_ref[(lat_index - 1) * levels + level] = field[:1]

        blank = jnp.zeros((rows, 1), jnp.float32)
        west = jnp.concatenate([blank, field[:, :-1]], axis=1)
        east = jnp.concatenate([field[:, 1:], blank], axis=1)
        blank = jnp.zeros((1, lons), jnp.float32)
        north = jnp.concatenate([blank, field[:-1]], axis=0)
        south = jnp.concatenate([field[1:], blank], axis=0)
        eastward = 0.5 * east_wind[step].astype(jnp.float32)
        northward = 0.5 * north_wind[step].astype(jnp.float32)
        moved = field - eastward * (east - west) - northward * (south - north)
        first, last = field[:, :1], field[:, lons - 1 :]
        biggest = jnp.max(jnp.abs(moved), axis=1, keepdims=True)
        biggest = jnp.maximum(biggest, jnp.maximum(jnp.abs(first), jnp.abs(last)))
        code = scale_code(biggest)
        inverse = 1.0 / scale_of(code)
        filler = jnp.zeros((rows, LANES - spare), jnp.float32)
        tile = jnp.concatenate([moved[:, end:], filler], axis=1)
        tile = jnp.where(lane == spare + 1, first, jnp.where(lane == spare + 2, last, tile))
        tile = coded(tile, inverse)
        tile = jnp.where(lane == spare, code, tile)
        winds = jnp.where(lane == spare + 3, eastward[:, :1], eastward[:, lons - 1 :])
        winds = coded(winds, 1.0 / WIND_STEP)
        tile = jnp.where((lane == spare + 3) | (lane == spare + 4), winds, tile)
        wind_rows = jnp.concatenate([northward[:1], northward[rows - 1 :]], axis=0)
        wind_rows = coded(wind_rows, 1.0 / WIND_STEP)
        blank = jnp.zeros((padded_rows - rows - 2, lons), jnp.float32)
        wind_rows = jnp.concatenate([wind_rows, blank], axis=0)
        filler = jnp.zeros((padded_rows - rows, LANES - spare), jnp.float32)
        wind_tile = jnp.concatenate([wind_rows[:, end:], filler], axis=1)
        steps = jnp.concatenate([coded(moved[:, :end], inverse), wind_rows[:, :end]], axis=0)
        outs[step][:, :end] = as_int16(steps)
        outs[step][:, end:] = as_int16(jnp.concatenate([tile, wind_tile], axis=0))


def advect(tracer, east_wind, north_wind, ring):
    levels, rows, lons = tracer.shape
    lat_count = lax.axis_size("lat")
    width = (lons - 1) // LANES * LANES + LANES
    padded_rows = -(-(rows + 2) // 16) * 16
    held = pltpu.VMEM((levels, rows, lons), jnp.bfloat16)
    result = pl.pallas_call(
        functools.partial(advect_kernel, ring, lat_count),
        out_shape=[jax.ShapeDtypeStruct((padded_rows, width), jnp.int16)] * levels
        + [jax.ShapeDtypeStruct((lat_count * levels, 1, lons), jnp.float32)],
        in_specs=[HBM_SPEC] * 3,
        out_specs=[VMEM_SPEC] * (levels + 1),
        scratch_shapes=[held, held, held, pltpu.SemaphoreType.DMA((levels, 3))],
        compiler_params=pltpu.CompilerParams(vmem_limit_bytes=VMEM_BYTES),
        cost_estimate=pl.CostEstimate(
            flops=20 * levels * rows * lons, bytes_accessed=8 * levels * rows * lons, transcendentals=0
        ),
    )(tracer, east_wind, north_wind)
    return list(result[:levels]), result[levels]


def fourier_kernel(ring, lat_count, pieces, *rest):
    grids, (edge_ref, *tables_hbm, wave_ref, keep_ref, sine_ref) = rest[:pieces], rest[pieces : pieces + 9]
    outs, rest = rest[pieces + 9 :][:lat_count], rest[pieces + 9 + lat_count :]
    tables, place_ref, (field, sems) = rest[:4], rest[4], rest[5:]
    _, rows, width = field.shape
    lons = tables[0].shape[1]
    share = pieces // 4
    copies = []
    for kind, target in enumerate((*tables, place_ref)):
        copies.append(pltpu.make_async_copy(tables_hbm[kind], target, sems.at[kind]))
        copies[-1].start()

    end = width - LANES
    spare = lons - end
    lane = lax.broadcasted_iota(jnp.int32, (rows, LANES), 1)
    winds = (lane == spare + 3) | (lane == spare + 4)
    lat_index = lax.axis_index("lat")
    for piece in range(pieces):
        spot = partner(*ring, piece)
        values = from_int16(grids[piece][...])
        tile = values[:rows, end:]
        scale = scale_of(tile[:, spare : spare + 1])
        field[spot, :, :end] = values[:rows, :end] * scale
        field[spot, :, end:] = tile * jnp.where(winds, WIND_STEP, scale)
        wind_rows = values[rows : rows + 2, :lons] * WIND_STEP

        @pl.when(lat_index > 0)
        def _():
            above = edge_ref[(lat_index - 1) * pieces + spot]
            field[spot, :1, :lons] += wind_rows[:1] * above

        @pl.when(lat_index < lat_count - 1)
        def _():
            below = edge_ref[(lat_index + 1) * pieces + spot]
            field[spot, rows - 1 :, :lons] -= wind_rows[1:] * below

    for spot in range(pieces):
        tile = field[spot, :, end:]
        before = field[(spot - 1) % pieces, :, end:]
        after = field[(spot + 1) % pieces, :, end:]
        shift = LANES - spare
        gain = pltpu.roll(tile, shift - 3, 1) * pltpu.roll(before, shift - 2, 1)
        loss = pltpu.roll(tile, LANES - 5, 1) * pltpu.roll(after, LANES - 2, 1)
        field[spot, :, end:] = tile - jnp.where(lane == spare - 1, loss, 0.0)
        field[spot, :, :LANES] += jnp.where(lane == 0, gain, 0.0)

    def product(value, table, spot):
        high, low = split_bf16(value)
        width = table.shape[2] // 2
        both = jnp.dot(high, table[spot], preferred_element_type=jnp.float32)
        part = jnp.dot(low, table[spot, :, :width], preferred_element_type=jnp.float32)
        return part + both[:, :width] + both[:, width:]

    sums = [None, None, None]
    for spot in range(share):
        quarters = [field[quarter * share + spot, :, :lons] for quarter in range(4)]
        sum02, dif02 = quarters[0] + quarters[2], quarters[0] - quarters[2]
        sum13, dif13 = quarters[1] + quarters[3], quarters[1] - quarters[3]
        parts = []
        for kind, value in enumerate((sum02 + sum13, sum02 - sum13, dif02, dif13)):
            if spot == 0:
                copies[kind].wait()
            parts.append(product(value, tables[kind], spot))
        parts = [parts[0], parts[1], parts[2] + parts[3]]
        sums = [part if total is None else total + part for total, part in zip(sums, parts)]
    copies[4].wait()
    placed = []
    for part in range(2):
        columns = []
        for total in sums:
            half = total.shape[1] // 2
            columns.append(total[:, part * half : (part + 1) * half])
        high, low = split_bf16(jnp.concatenate(columns, axis=1))
        value = jnp.dot(high, place_ref[...], preferred_element_type=jnp.float32)
        value += jnp.dot(low, place_ref[...], preferred_element_type=jnp.float32)
        kept = jnp.where(wave_ref[...] < keep_ref[...], value * sine_ref[...], 0.0)
        code = scale_code(jnp.max(jnp.abs(kept), axis=0, keepdims=True))
        steps = coded(kept, 1.0 / scale_of(code))
        codes = jnp.broadcast_to(code, (outs[0].shape[0] - rows, code.shape[1]))
        placed.append(as_int16(jnp.concatenate([steps, codes], axis=0)))
    for target in range(lat_count):
        for part in range(2):
            cols = slice(target * LANES, (target + 1) * LANES)
            outs[target][:, part * LANES : (part + 1) * LANES] = placed[part][:, cols]


def fourier(grids, edges, ring, places, wave_row, keep_col, sine_col, lat_count):
    pieces = len(grids)
    rows = keep_col.shape[0]
    width = grids[0].shape[1]
    padded_rows = -(-(rows + 1) // 16) * 16
    tables = [table_bf16(table) for table in fourier_tables(pieces)]
    return pl.pallas_call(
        functools.partial(fourier_kernel, ring, lat_count, pieces),
        out_shape=[jax.ShapeDtypeStruct((padded_rows, 2 * LANES), jnp.int16)] * lat_count,
        in_specs=[VMEM_SPEC] * (pieces + 1) + [HBM_SPEC] * 5 + [VMEM_SPEC] * 3,
        out_specs=[VMEM_SPEC] * lat_count,
        scratch_shapes=[pltpu.VMEM(table.shape, jnp.bfloat16) for table in tables]
        + [pltpu.VMEM(places.shape, jnp.bfloat16)]
        + [pltpu.VMEM((pieces, rows, width), jnp.float32), pltpu.SemaphoreType.DMA((5,))],
        compiler_params=pltpu.CompilerParams(vmem_limit_bytes=VMEM_BYTES),
        cost_estimate=pl.CostEstimate(
            flops=3 * rows * NLON * M, bytes_accessed=6 * 2**20, transcendentals=0
        ),
    )(*grids, edges, *tables, places, wave_row, keep_col, sine_col)


def places_kernel(
    slot_ref, keep_ref, sine_ref, spot_ref,
    place_ref, wave_ref, mine_ref, back_ref, keep_col, sine_col, sorted_rows,
):
    groups, _, rows = sine_ref.shape
    lat_index = lax.axis_index("lat")
    slots = slot_ref.shape[1] // groups
    paired = (slots + 1) // 2
    shape = (LANES, LANES)
    down = lax.broadcasted_iota(jnp.int32, shape, 0)
    across = lax.broadcasted_iota(jnp.int32, shape, 1)
    filler = jnp.full((1, LANES - slots), 2.0 * M, jnp.float32)
    for group in range(groups):
        row = slot_ref[:, group * slots : (group + 1) * slots].astype(jnp.float32)
        row = jnp.broadcast_to(jnp.concatenate([row, filler], axis=1), shape)
        column = jnp.sum(jnp.where(down == across, row, 0.0), axis=1, keepdims=True)
        ahead = (row < column) | ((row == column) & (across < down))
        rank = jnp.sum(jnp.where(ahead, 1.0, 0.0), axis=1, keepdims=True)
        place = jnp.where(rank < paired, rank, SIDE + slots - 1.0 - rank)
        place = jnp.where(rank < slots, place, -1.0)
        hot = jnp.where(place == across.astype(jnp.float32), 1.0, 0.0)
        filled = jnp.sum(hot, axis=0, keepdims=True)
        values = jnp.sum(hot * column, axis=0, keepdims=True)
        values = jnp.where(filled > 0.5, values, 2.0 * M)
        sorted_rows[group] = jnp.broadcast_to(values, sorted_rows.shape[1:])

        @pl.when(group == lat_index)
        def _():
            mine_ref[...] = values
            back_ref[...] = hot.astype(jnp.bfloat16)

    spots = jnp.broadcast_to(spot_ref[...], (spot_ref.shape[0], LANES))
    for step in range(groups):
        row = sorted_rows[partner(("lat",), (groups,), step), :1]
        cols = slice(step * LANES, (step + 1) * LANES)
        wave_ref[:, cols] = row
        place_ref[:, cols] = jnp.where(spots == row, 1.0, 0.0).astype(jnp.bfloat16)

    shape = (rows, rows)
    same = lax.broadcasted_iota(jnp.int32, shape, 0) == lax.broadcasted_iota(jnp.int32, shape, 1)
    kept = jnp.broadcast_to(keep_ref[...].astype(jnp.float32), shape)
    keep_col[...] = jnp.sum(jnp.where(same, kept, 0.0), axis=1, keepdims=True)
    sine = jnp.broadcast_to(sine_ref[lat_index], shape)
    sine_col[...] = jnp.sum(jnp.where(same, sine, 0.0), axis=1, keepdims=True)


def prepare_places(slot_wave, keep_m, groups):
    rows = keep_m.shape[0]
    sines = np.sin(math.pi / NLAT * (np.arange(NLAT) + 0.5)) * math.sqrt(2.0 / NLAT)
    spots = column_waves()
    width = groups * LANES
    return pl.pallas_call(
        places_kernel,
        out_shape=[
            jax.ShapeDtypeStruct((spots.shape[0], width), jnp.bfloat16),
            jax.ShapeDtypeStruct((1, width), jnp.float32),
            jax.ShapeDtypeStruct((1, LANES), jnp.float32),
            jax.ShapeDtypeStruct((LANES, LANES), jnp.bfloat16),
            jax.ShapeDtypeStruct((rows, 1), jnp.float32),
            jax.ShapeDtypeStruct((rows, 1), jnp.float32),
        ],
        in_specs=[VMEM_SPEC] * 4,
        out_specs=[VMEM_SPEC] * 6,
        scratch_shapes=[pltpu.VMEM((groups, 8, LANES), jnp.float32)],
        compiler_params=pltpu.CompilerParams(vmem_limit_bytes=VMEM_BYTES),
    )(
        slot_wave[None], keep_m[None],
        sines.reshape(groups, 1, rows).astype(np.float32), spots,
    )


def lane_pairs(row):
    lane = lax.broadcasted_iota(jnp.int32, row.shape, 1)
    other = pltpu.roll(row, SIDE, 1)
    return jnp.where(lane < SIDE, row, other), jnp.where(lane < SIDE, other, row)


def block_count(wave):
    return jnp.floor((jnp.maximum(M - wave, 0.0) + (BLOCK - 1)) * (1.0 / BLOCK))


def recurrence_kernel(mine_ref, lat_ref, term_ref, beta_ref, scale_ref, growth_ref, start_ref):
    pair = lane_pairs(jnp.broadcast_to(mine_ref[...], (8, LANES)))
    one, two = pair[0][:1], pair[1][:1]
    blocks = growth_ref.shape[0]
    turn = block_count(one)
    block = lax.broadcasted_iota(jnp.int32, (blocks, LANES), 0).astype(jnp.float32)
    second = block >= turn
    wave = jnp.where(second, two, one)
    limit = M - wave
    wave = jnp.minimum(wave, M - 1.0)
    first = (block - jnp.where(second, turn, 0.0)) * BLOCK

    scale = jnp.ones((blocks, LANES), jnp.float32)
    for index in range(BLOCK + 1):
        order = first + index
        degree = wave + order
        square = 4.0 * degree * degree - 1.0
        spread = 4.0 * order * (degree + wave)
        if index > 0:
            scale = scale * jnp.sqrt(square / spread)
        if index < BLOCK:
            beta_ref[pl.ds(index, blocks, stride=BLOCK)] = spread / jnp.maximum(square, 1.0)
            scale_ref[pl.ds(index, blocks, stride=BLOCK)] = jnp.where(order < limit, scale, 0.0)
    growth_ref[...] = scale

    for kind, wave in enumerate((one, two)):
        wave = jnp.minimum(wave, M - 1.0)
        counter = lax.broadcasted_iota(jnp.int32, term_ref.shape, 0).astype(jnp.float32)
        norm = jnp.sum(jnp.where(counter <= wave, term_ref[...], 0.0), axis=0, keepdims=True)
        coarse = lat_ref[1] * wave
        whole = jnp.floor(coarse)
        start_ref[2 * kind] = jnp.exp2(
            (coarse - whole) + lat_ref[2] * wave + 0.5 * (norm - 1.0)
        )
        start_ref[2 * kind + 1] = whole


def prepare_recurrence(mine):
    latitudes = latitude_table()
    points = latitudes.shape[1]
    blocks = 2 * -(-M // BLOCK)
    counter = np.arange(M)
    terms = np.log1p(0.5 / np.maximum(counter, 1)) * (counter > 0) / math.log(2.0)
    terms = np.broadcast_to(terms[:, None], (M, LANES)).astype(np.float32)
    orders = jax.ShapeDtypeStruct((blocks * BLOCK, LANES), jnp.float32)
    return pl.pallas_call(
        recurrence_kernel,
        out_shape=[
            orders,
            orders,
            jax.ShapeDtypeStruct((blocks, LANES), jnp.float32),
            jax.ShapeDtypeStruct((4, points, LANES), jnp.float32),
        ],
        in_specs=[VMEM_SPEC] * 3,
        out_specs=[VMEM_SPEC] * 4,
        compiler_params=pltpu.CompilerParams(vmem_limit_bytes=LATE_BYTES),
    )(mine, latitudes, terms)


def resampled(first, fields, table, total):
    for piece, field in enumerate(fields):
        values = from_int16(field[...])
        values = values * scale_of(values[field.shape[0] - 1 :])
        high, low = split_bf16(values)
        spot = partner(("lat",), table.shape[:1], first + piece)
        both = jnp.concatenate([high, low], axis=1)
        part = jnp.dot(table[spot, 0], both, preferred_element_type=jnp.float32)
        part = part[:, : high.shape[1]] + part[:, high.shape[1] :]
        part += jnp.dot(table[spot, 1], high, preferred_element_type=jnp.float32)
        total = part if total is None else total + part
    return total


def resample_kernel(table_ref, *rest):
    rest[-1][...] = resampled(0, rest[:-1], table_ref, None)


def resample(fields, table):
    count, _, height, _ = table.shape
    span = fields[0].shape[1]
    return pl.pallas_call(
        resample_kernel,
        out_shape=jax.ShapeDtypeStruct((height, span), jnp.float32),
        in_specs=[VMEM_SPEC] * (1 + len(fields)),
        out_specs=VMEM_SPEC,
        compiler_params=pltpu.CompilerParams(vmem_limit_bytes=LATE_BYTES),
        cost_estimate=pl.CostEstimate(
            flops=6 * height * span * NLAT // count * len(fields), bytes_accessed=4 * 2**20, transcendentals=0
        ),
    )(table, *fields)


def legendre_kernel(early, *rest):
    table, lat_ref, beta_ref, scale_ref, growth_ref, start_ref, total_ref, mine_ref, back_ref = rest[:9]
    fields, rest = rest[9:-8], rest[-8:]
    out_ref, weights, before, current, level, sums, result, final = rest
    points = lat_ref.shape[1]
    slots = out_ref.shape[0]
    mine = mine_ref[...]
    odd = mine - 2.0 * jnp.floor(mine * 0.5) > 0.5
    pair = lane_pairs(jnp.broadcast_to(mine, (8, LANES)))
    turn = block_count(pair[0][:1])
    block_total = jnp.max(turn + block_count(pair[1][:1])).astype(jnp.int32)

    total = resampled(early, fields, table, total_ref[...])
    totals = [total[2 * points * kind : 2 * points * (kind + 1)] for kind in range(4)]
    left = lax.broadcasted_iota(jnp.int32, (points, LANES), 1) < SIDE
    for parity in range(2):
        for comp in range(2):
            cols = slice(comp * LANES, (comp + 1) * LANES)
            value = jnp.where(odd, totals[2 + parity][:, cols], totals[parity][:, cols])
            top, bottom = value[:points], value[points:]
            kind = 2 * parity + comp
            weights[0, kind] = jnp.where(left, top, pltpu.roll(bottom, SIDE, 1))
            weights[1, kind] = jnp.where(left, pltpu.roll(top, SIDE, 1), bottom)
    result[...] = jnp.zeros_like(result)
    current[...] = start_ref[0]
    level[...] = start_ref[1]
    before[...] = jnp.zeros_like(before)

    def step(block, carry):
        base = pl.multiple_of(block * BLOCK, BLOCK)
        now = block.astype(jnp.float32)
        second, begins = now >= turn, now == turn
        grow = growth_ref[pl.ds(block, 1)]
        first = 0
        for chunk in CHUNKS:
            rows = slice(first, first + chunk)
            height = jnp.where(begins, start_ref[3, rows], level[rows])
            factor = jnp.exp2(height)
            scaled = [
                jnp.where(second, weights[1, k, rows], weights[0, k, rows]) * factor for k in range(4)
            ]
            cosine = lat_ref[0, rows]
            old = jnp.where(begins, 0.0, before[rows])
            new = jnp.where(begins, start_ref[2, rows], current[rows])
            for order in range(BLOCK):
                for comp in range(2):
                    product = new * scaled[2 * (order % 2) + comp]
                    partial = product.reshape(chunk // 8, 8, LANES).sum(axis=0)
                    place = pl.ds((order * 2 + comp) * 8, 8)
                    if first == 0:
                        sums[place] = partial
                    else:
                        sums[place] += partial
                beta = beta_ref[pl.ds(base + order, 1)]
                old, new = new, cosine * new - beta * old
            biggest = jnp.maximum(jnp.abs(old), jnp.abs(new)) * grow
            shift = jnp.floor(jnp.log(biggest) * (1.0 / math.log(2.0)))
            factor = grow * jnp.exp2(-shift)
            before[rows] = old * factor
            current[rows] = new * factor
            level[rows] = height + shift
            first += chunk
        for comp in range(2):
            total = sums[pl.ds(comp * 8, BLOCK, stride=16)]
            for lane in range(1, 8):
                total += sums[pl.ds(comp * 8 + lane, BLOCK, stride=16)]
            total = total * scale_ref[pl.ds(base, BLOCK)]
            result[comp, pl.ds(base, BLOCK)] = total + pltpu.roll(total, SIDE, 1)
        return carry

    lax.fori_loop(0, block_total, step, 0)

    left = lax.broadcasted_iota(jnp.int32, (BLOCK, LANES), 1) < SIDE
    spots = -(-M // BLOCK)
    chosen = [jnp.broadcast_to(turn, (8, LANES)) == value for value in range(spots + 1)]
    chosen = [jnp.concatenate([mask] * (BLOCK // 8), axis=0) for mask in chosen]
    for place in range(spots):
        rows = slice(place * BLOCK, (place + 1) * BLOCK)
        for comp in range(2):
            early_part = jnp.where(turn > place, result[comp, rows], 0.0)
            later = jnp.zeros((BLOCK, LANES), jnp.float32)
            for value in range(spots + 1):
                base = (place + value) * BLOCK
                if base < result.shape[1]:
                    later = jnp.where(chosen[value], result[comp, base : base + BLOCK], later)
            final[comp, rows] = jnp.where(left, early_part, later)
    back = back_ref[...]
    dims = (((1,), (1,)), ((), ()))
    for comp in range(2):
        high, low = split_bf16(final[comp])
        value = lax.dot_general(back, high, dims, preferred_element_type=jnp.float32)
        value += lax.dot_general(back, low, dims, preferred_element_type=jnp.float32)
        out_ref[:, comp, :] = value[:slots, :M]


def resample_pieces(pieces, rows, padded_rows):
    full = resample_table()
    table = full.reshape(full.shape[0], pieces, rows).transpose(1, 0, 2)
    table = table_bf16(np.pad(table, ((0, 0), (0, 0), (0, padded_rows - rows))))
    return table.reshape(pieces, full.shape[0], 2, padded_rows).transpose(0, 2, 1, 3)


def legendre(fields, mine, back, prepared, rows, slots):
    pieces = len(fields)
    early = pieces // 2
    latitudes = latitude_table()
    points = latitudes.shape[1]
    table = jnp.asarray(resample_pieces(pieces, rows, fields[0].shape[0]))
    total = resample(fields[:early], table)
    vector = pltpu.VMEM((points, LANES), jnp.float32)
    block_rows = -(-M // BLOCK) * BLOCK
    return pl.pallas_call(
        functools.partial(legendre_kernel, early),
        out_shape=jax.ShapeDtypeStruct((slots, 2, M), jnp.float32),
        in_specs=[VMEM_SPEC] * (9 + pieces - early),
        out_specs=VMEM_SPEC,
        scratch_shapes=[
            pltpu.VMEM((2, 4, points, LANES), jnp.float32),
            vector,
            vector,
            vector,
            pltpu.VMEM((BLOCK * 16, LANES), jnp.float32),
            pltpu.VMEM((2, 2 * block_rows, LANES), jnp.float32),
            pltpu.VMEM((2, block_rows, LANES), jnp.float32),
        ],
        compiler_params=pltpu.CompilerParams(vmem_limit_bytes=LATE_BYTES),
        cost_estimate=pl.CostEstimate(
            flops=7 * points * LANES * M, bytes_accessed=6 * 2**20, transcendentals=0
        ),
    )(table, latitudes, *prepared, total, mine, back, *fields[early:])


def shards(tracer, wind_east, wind_north, keep_m, slot_wave):
    rows = tracer.shape[1]
    lat_count = lax.axis_size("lat")
    slots = slot_wave.shape[0] // lat_count
    axes = ("lev", "fld")
    ring = (axes, tuple(lax.axis_size(axis) for axis in axes))

    blocks, edges = advect(tracer, wind_east, wind_north, ring)
    blocks, slot_wave, keep_m = lax.optimization_barrier((blocks, slot_wave, keep_m))
    grids = exchange(blocks, axes)
    edges = lax.all_to_all(edges, ("lat", *axes), split_axis=0, concat_axis=0, tiled=True)
    places, wave_row, mine, back, keep_col, sine_col = prepare_places(slot_wave, keep_m, lat_count)
    waved = fourier(grids, edges, ring, places, wave_row, keep_col, sine_col, lat_count)
    waved, mine = lax.optimization_barrier((list(waved), mine))
    fields = exchange(waved, "lat")
    prepared = prepare_recurrence(mine)
    return legendre(fields, mine, back, prepared, rows, slots)[None]


def solution(mesh):
    return jax.shard_map(
        shards,
        mesh=mesh,
        in_specs=(
            P("member", "lat", ("lev", "fld")),
            P("member", "lat", ("lev", "fld")),
            P("member", "lat", ("lev", "fld")),
            P("lat"),
            P(),
        ),
        out_specs=P(("member", "lev", "fld"), "lat", None, None),
        check_vma=False,
    )
```

```python
import functools
import math

import jax
import jax.numpy as jnp
import numpy as np
from jax import lax
from jax.experimental import pallas as pl
from jax.experimental.pallas import tpu as pltpu
from jax.sharding import PartitionSpec as P

M = 400
NLAT = 800
NLON = 1600
LANES = 128
BLOCK = 32
CHUNKS = (40, 32, 32)
SIDE = LANES // 2
TOP = 32767.0
WIND_STEP = 1.5 / TOP
VMEM_BYTES = 60 * 2**20
LATE_BYTES = 24 * 2**20
VMEM_SPEC = pl.BlockSpec(memory_space=pltpu.VMEM)
SMEM_SPEC = pl.BlockSpec(memory_space=pltpu.SMEM)
HBM_SPEC = pl.BlockSpec(memory_space=pltpu.HBM)


def split_bf16(values):
    high = values.astype(jnp.bfloat16)
    low = (values - high.astype(jnp.float32)).astype(jnp.bfloat16)
    return high, low


def table_bf16(table):
    high = table.astype(jnp.bfloat16)
    low = (table - high.astype(np.float64)).astype(jnp.bfloat16)
    return np.concatenate([high, low], axis=-1)


def fourier_tables(pieces):
    quarter = NLON // 4
    spots = np.arange(quarter)[:, None]
    factor = 1.0 / math.sqrt(NLON)

    def parts(waves):
        angles = 2.0 * math.pi / NLON * (spots * waves[None, :] % NLON)
        return factor * np.cos(angles), factor * np.sin(angles)

    def shaped(columns):
        pad = [(0, 0), (0, -columns[0].shape[1] % LANES)]
        table = np.concatenate([np.pad(part, pad) for part in columns], axis=1)
        return table.reshape(share, quarter // share, -1)

    share = pieces // 4
    tables = []
    for first in (0, 2):
        cosine, sine = parts(np.arange(first, M, 4))
        tables.append(shaped([cosine, -sine]))
    waves = np.arange(1, M, 2)
    sign = np.where(waves % 4 == 1, 1.0, -1.0)[None, :]
    cosine, sine = parts(waves)
    return [*tables, shaped([cosine, -sine]), shaped([-sign * sine, -sign * cosine])]


def column_waves():
    columns = []
    for waves in (np.arange(0, M, 4), np.arange(2, M, 4), np.arange(1, M, 2)):
        columns.append(np.pad(waves, (0, -len(waves) % LANES), constant_values=-1))
    return np.concatenate(columns).astype(np.float32)[:, None]


def resample_table():
    half = M // 2
    coarse = math.pi / M * (np.arange(M) + 0.5)
    fine = math.pi / NLAT * (np.arange(NLAT) + 0.5)
    waves = np.arange(M)
    weight = np.where(waves == 0, 1.0, 2.0) / M
    even = (np.cos(np.outer(coarse, waves)) * weight) @ np.cos(np.outer(waves, fine))
    odd = (np.sin(np.outer(coarse, waves)) * weight) @ np.sin(np.outer(waves, fine))
    rows = []
    for full in (even, odd):
        for sign in (1.0, -1.0):
            folded = (full[:half] + sign * full[::-1][:half]).reshape(2, half // 2, NLAT)
            rows.append(np.pad(folded, ((0, 0), (0, -half // 2 % 8), (0, 0))).reshape(-1, NLAT))
    return np.concatenate(rows, axis=0)


def latitude_table():
    half = M // 2
    angles = math.pi / M * (np.arange(half) + 0.5)
    log_sine = np.log2(np.sin(angles))
    coarse = np.round(log_sine * 1024.0) / 1024.0
    rows = np.stack([2.0 * np.cos(angles), coarse, log_sine - coarse]).reshape(3, 2, half // 2)
    rows = np.pad(rows, ((0, 0), (0, 0), (0, -half // 2 % 8)))
    return np.repeat(rows.transpose(0, 2, 1), SIDE, axis=2).astype(np.float32)


def scale_code(biggest):
    wanted = jnp.maximum(biggest, 1e-30) * (1.0 / TOP)
    exponent = jnp.floor(jnp.log(wanted) * (1.0 / math.log(2.0)))
    return exponent * 128.0 + jnp.ceil((wanted * jnp.exp2(-exponent) - 1.0) * 128.0)


def scale_of(code):
    exponent = jnp.floor(code * (1.0 / 128.0))
    rest = code - 128.0 * exponent
    return jnp.exp2(exponent) * (1.0 + rest * (1.0 / 128.0))


def coded(values, inverse):
    return jnp.floor(values * inverse + 0.5)


def as_int16(values):
    return values.astype(jnp.int32).astype(jnp.int16)


def from_int16(codes):
    return codes.astype(jnp.int32).astype(jnp.float32)


def group_index(axes, sizes):
    index = lax.axis_index(axes[0])
    for axis, size in zip(axes[1:], sizes[1:]):
        index = index * size + lax.axis_index(axis)
    return index


def partner(axes, sizes, step):
    return group_index(axes, sizes) ^ step if math.prod(sizes) == 4 else step


def exchange(blocks, axis):
    count = len(blocks)
    if count != 4:
        return list(lax.all_to_all(jnp.stack(blocks), axis, split_axis=0, concat_axis=0, tiled=True))
    pairs = [[(i, i ^ step) for i in range(count)] for step in range(count)]
    return [blocks[0]] + [lax.ppermute(blocks[step], axis, pairs[step]) for step in range(1, count)]


def advect_kernel(ring, tracer_hbm, east_hbm, north_hbm, *rest):
    levels, rows, lons = tracer_hbm.shape
    outs, (tracer, east_wind, north_wind, sems) = rest[:levels], rest[levels:]
    chosen = [partner(*ring, step) for step in range(levels)]
    copies = []
    for step, level in enumerate(chosen):
        copies.append(
            [
                pltpu.make_async_copy(source.at[level], target.at[step], sems.at[step, kind])
                for kind, (source, target) in enumerate(
                    ((tracer_hbm, tracer), (east_hbm, east_wind), (north_hbm, north_wind))
                )
            ]
        )
        for copy in copies[-1]:
            copy.start()
    padded_rows = outs[0].shape[0]
    end = (lons - 1) // LANES * LANES
    spare = lons - end
    lane = lax.broadcasted_iota(jnp.int32, (rows, LANES), 1)
    for step in range(levels):
        for copy in copies[step]:
            copy.wait()
        field = tracer[step].astype(jnp.float32)
        blank = jnp.zeros((rows, 1), jnp.float32)
        west = jnp.concatenate([blank, field[:, :-1]], axis=1)
        east = jnp.concatenate([field[:, 1:], blank], axis=1)
        blank = jnp.zeros((1, lons), jnp.float32)
        north = jnp.concatenate([blank, field[:-1]], axis=0)
        south = jnp.concatenate([field[1:], blank], axis=0)
        eastward = 0.5 * east_wind[step].astype(jnp.float32)
        northward = 0.5 * north_wind[step].astype(jnp.float32)
        moved = field - eastward * (east - west) - northward * (south - north)
        first, last = field[:, :1], field[:, lons - 1 :]
        biggest = jnp.max(jnp.abs(moved), axis=1, keepdims=True)
        biggest = jnp.maximum(biggest, jnp.maximum(jnp.abs(first), jnp.abs(last)))
        code = scale_code(biggest)
        inverse = 1.0 / scale_of(code)
        filler = jnp.zeros((rows, LANES - spare), jnp.float32)
        tile = jnp.concatenate([moved[:, end:], filler], axis=1)
        tile = jnp.where(lane == spare + 1, first, jnp.where(lane == spare + 2, last, tile))
        tile = coded(tile, inverse)
        tile = jnp.where(lane == spare, code, tile)
        winds = jnp.where(lane == spare + 3, eastward[:, :1], eastward[:, lons - 1 :])
        winds = coded(winds, 1.0 / WIND_STEP)
        tile = jnp.where((lane == spare + 3) | (lane == spare + 4), winds, tile)
        wind_rows = jnp.concatenate([northward[:1], northward[rows - 1 :]], axis=0)
        wind_rows = coded(wind_rows, 1.0 / WIND_STEP)
        blank = jnp.zeros((padded_rows - rows - 2, lons), jnp.float32)
        wind_rows = jnp.concatenate([wind_rows, blank], axis=0)
        filler = jnp.zeros((padded_rows - rows, LANES - spare), jnp.float32)
        wind_tile = jnp.concatenate([wind_rows[:, end:], filler], axis=1)
        steps = jnp.concatenate([coded(moved[:, :end], inverse), wind_rows[:, :end]], axis=0)
        outs[step][:, :end] = as_int16(steps)
        outs[step][:, end:] = as_int16(jnp.concatenate([tile, wind_tile], axis=0))


def advect(tracer, east_wind, north_wind, ring):
    levels, rows, lons = tracer.shape
    width = (lons - 1) // LANES * LANES + LANES
    padded_rows = -(-(rows + 2) // 16) * 16
    held = pltpu.VMEM((levels, rows, lons), jnp.bfloat16)
    return pl.pallas_call(
        functools.partial(advect_kernel, ring),
        out_shape=[jax.ShapeDtypeStruct((padded_rows, width), jnp.int16)] * levels,
        in_specs=[HBM_SPEC] * 3,
        out_specs=[VMEM_SPEC] * levels,
        scratch_shapes=[held, held, held, pltpu.SemaphoreType.DMA((levels, 3))],
        compiler_params=pltpu.CompilerParams(vmem_limit_bytes=VMEM_BYTES),
        cost_estimate=pl.CostEstimate(
            flops=20 * levels * rows * lons, bytes_accessed=8 * levels * rows * lons, transcendentals=0
        ),
    )(tracer, east_wind, north_wind)


def fourier_kernel(ring, lat_count, pieces, *rest):
    grids, (edge_ref, *tables_hbm, wave_ref, keep_ref, sine_ref) = rest[:pieces], rest[pieces : pieces + 9]
    outs, rest = rest[pieces + 9 :][:lat_count], rest[pieces + 9 + lat_count :]
    tables, place_ref, (field, sems) = rest[:4], rest[4], rest[5:]
    _, rows, width = field.shape
    lons = tables[0].shape[1]
    share = pieces // 4
    copies = []
    for kind, target in enumerate((*tables, place_ref)):
        copies.append(pltpu.make_async_copy(tables_hbm[kind], target, sems.at[kind]))
        copies[-1].start()

    end = width - LANES
    spare = lons - end
    lane = lax.broadcasted_iota(jnp.int32, (rows, LANES), 1)
    winds = (lane == spare + 3) | (lane == spare + 4)
    lat_index = lax.axis_index("lat")
    level = group_index(*ring)
    for piece in range(pieces):
        spot = partner(*ring, piece)
        values = from_int16(grids[piece][...])
        tile = values[:rows, end:]
        scale = scale_of(tile[:, spare : spare + 1])
        field[spot, :, :end] = values[:rows, :end] * scale
        field[spot, :, end:] = tile * jnp.where(winds, WIND_STEP, scale)
        wind_rows = values[rows : rows + 2, :lons] * WIND_STEP

        @pl.when(lat_index > 0)
        def _():
            above = edge_ref[(lat_index - 1) * pieces + spot, pl.ds(pieces + level, 1)]
            field[spot, :1, :lons] += wind_rows[:1] * above

        @pl.when(lat_index < lat_count - 1)
        def _():
            below = edge_ref[(lat_index + 1) * pieces + spot, pl.ds(level, 1)]
            field[spot, rows - 1 :, :lons] -= wind_rows[1:] * below

    for spot in range(pieces):
        tile = field[spot, :, end:]
        before = field[(spot - 1) % pieces, :, end:]
        after = field[(spot + 1) % pieces, :, end:]
        shift = LANES - spare
        gain = pltpu.roll(tile, shift - 3, 1) * pltpu.roll(before, shift - 2, 1)
        loss = pltpu.roll(tile, LANES - 5, 1) * pltpu.roll(after, LANES - 2, 1)
        field[spot, :, end:] = tile - jnp.where(lane == spare - 1, loss, 0.0)
        field[spot, :, :LANES] += jnp.where(lane == 0, gain, 0.0)

    def product(value, table, spot):
        high, low = split_bf16(value)
        width = table.shape[2] // 2
        both = jnp.dot(high, table[spot], preferred_element_type=jnp.float32)
        part = jnp.dot(low, table[spot, :, :width], preferred_element_type=jnp.float32)
        return part + both[:, :width] + both[:, width:]

    sums = [None, None, None]
    for spot in range(share):
        quarters = [field[quarter * share + spot, :, :lons] for quarter in range(4)]
        sum02, dif02 = quarters[0] + quarters[2], quarters[0] - quarters[2]
        sum13, dif13 = quarters[1] + quarters[3], quarters[1] - quarters[3]
        parts = []
        for kind, value in enumerate((sum02 + sum13, sum02 - sum13, dif02, dif13)):
            if spot == 0:
                copies[kind].wait()
            parts.append(product(value, tables[kind], spot))
        parts = [parts[0], parts[1], parts[2] + parts[3]]
        sums = [part if total is None else total + part for total, part in zip(sums, parts)]
    copies[4].wait()
    placed = []
    for part in range(2):
        columns = []
        for total in sums:
            half = total.shape[1] // 2
            columns.append(total[:, part * half : (part + 1) * half])
        high, low = split_bf16(jnp.concatenate(columns, axis=1))
        value = jnp.dot(high, place_ref[...], preferred_element_type=jnp.float32)
        value += jnp.dot(low, place_ref[...], preferred_element_type=jnp.float32)
        kept = jnp.where(wave_ref[...] < keep_ref[...], value * sine_ref[...], 0.0)
        code = scale_code(jnp.max(jnp.abs(kept), axis=0, keepdims=True))
        steps = coded(kept, 1.0 / scale_of(code))
        codes = jnp.broadcast_to(code, (outs[0].shape[0] - rows, code.shape[1]))
        placed.append(as_int16(jnp.concatenate([steps, codes], axis=0)))
    for target in range(lat_count):
        for part in range(2):
            cols = slice(target * LANES, (target + 1) * LANES)
            outs[target][:, part * LANES : (part + 1) * LANES] = placed[part][:, cols]


def fourier(grids, edges, ring, places, wave_row, keep_col, sine_col, lat_count):
    pieces = len(grids)
    rows = keep_col.shape[0]
    width = grids[0].shape[1]
    padded_rows = -(-(rows + 1) // 16) * 16
    tables = [table_bf16(table) for table in fourier_tables(pieces)]
    return pl.pallas_call(
        functools.partial(fourier_kernel, ring, lat_count, pieces),
        out_shape=[jax.ShapeDtypeStruct((padded_rows, 2 * LANES), jnp.int16)] * lat_count,
        in_specs=[VMEM_SPEC] * (pieces + 1) + [HBM_SPEC] * 5 + [VMEM_SPEC] * 3,
        out_specs=[VMEM_SPEC] * lat_count,
        scratch_shapes=[pltpu.VMEM(table.shape, jnp.bfloat16) for table in tables]
        + [pltpu.VMEM(places.shape, jnp.bfloat16)]
        + [pltpu.VMEM((pieces, rows, width), jnp.float32), pltpu.SemaphoreType.DMA((5,))],
        compiler_params=pltpu.CompilerParams(vmem_limit_bytes=VMEM_BYTES),
        cost_estimate=pl.CostEstimate(
            flops=3 * rows * NLON * M, bytes_accessed=6 * 2**20, transcendentals=0
        ),
    )(*grids, edges, *tables, places, wave_row, keep_col, sine_col)


def places_kernel(
    slot_ref, keep_ref, sine_ref, spot_ref,
    place_ref, wave_ref, mine_ref, back_ref, keep_col, sine_col, sorted_rows,
):
    groups, _, rows = sine_ref.shape
    lat_index = lax.axis_index("lat")
    slots = slot_ref.shape[1] // groups
    paired = (slots + 1) // 2
    shape = (LANES, LANES)
    down = lax.broadcasted_iota(jnp.int32, shape, 0)
    across = lax.broadcasted_iota(jnp.int32, shape, 1)
    filler = jnp.full((1, LANES - slots), 2.0 * M, jnp.float32)
    for group in range(groups):
        row = slot_ref[:, group * slots : (group + 1) * slots].astype(jnp.float32)
        row = jnp.broadcast_to(jnp.concatenate([row, filler], axis=1), shape)
        column = jnp.sum(jnp.where(down == across, row, 0.0), axis=1, keepdims=True)
        ahead = (row < column) | ((row == column) & (across < down))
        rank = jnp.sum(jnp.where(ahead, 1.0, 0.0), axis=1, keepdims=True)
        place = jnp.where(rank < paired, rank, SIDE + slots - 1.0 - rank)
        place = jnp.where(rank < slots, place, -1.0)
        hot = jnp.where(place == across.astype(jnp.float32), 1.0, 0.0)
        filled = jnp.sum(hot, axis=0, keepdims=True)
        values = jnp.sum(hot * column, axis=0, keepdims=True)
        values = jnp.where(filled > 0.5, values, 2.0 * M)
        sorted_rows[group] = jnp.broadcast_to(values, sorted_rows.shape[1:])

        @pl.when(group == lat_index)
        def _():
            mine_ref[...] = values
            back_ref[...] = hot.astype(jnp.bfloat16)

    spots = jnp.broadcast_to(spot_ref[...], (spot_ref.shape[0], LANES))
    for step in range(groups):
        row = sorted_rows[partner(("lat",), (groups,), step), :1]
        cols = slice(step * LANES, (step + 1) * LANES)
        wave_ref[:, cols] = row
        place_ref[:, cols] = jnp.where(spots == row, 1.0, 0.0).astype(jnp.bfloat16)

    shape = (rows, rows)
    same = lax.broadcasted_iota(jnp.int32, shape, 0) == lax.broadcasted_iota(jnp.int32, shape, 1)
    kept = jnp.broadcast_to(keep_ref[...].astype(jnp.float32), shape)
    keep_col[...] = jnp.sum(jnp.where(same, kept, 0.0), axis=1, keepdims=True)
    sine = jnp.broadcast_to(sine_ref[lat_index], shape)
    sine_col[...] = jnp.sum(jnp.where(same, sine, 0.0), axis=1, keepdims=True)


def prepare_places(slot_wave, keep_m, groups):
    rows = keep_m.shape[0]
    sines = np.sin(math.pi / NLAT * (np.arange(NLAT) + 0.5)) * math.sqrt(2.0 / NLAT)
    spots = column_waves()
    width = groups * LANES
    return pl.pallas_call(
        places_kernel,
        out_shape=[
            jax.ShapeDtypeStruct((spots.shape[0], width), jnp.bfloat16),
            jax.ShapeDtypeStruct((1, width), jnp.float32),
            jax.ShapeDtypeStruct((1, LANES), jnp.float32),
            jax.ShapeDtypeStruct((LANES, LANES), jnp.bfloat16),
            jax.ShapeDtypeStruct((rows, 1), jnp.float32),
            jax.ShapeDtypeStruct((rows, 1), jnp.float32),
        ],
        in_specs=[VMEM_SPEC] * 4,
        out_specs=[VMEM_SPEC] * 6,
        scratch_shapes=[pltpu.VMEM((groups, 8, LANES), jnp.float32)],
        compiler_params=pltpu.CompilerParams(vmem_limit_bytes=VMEM_BYTES),
    )(
        slot_wave[None], keep_m[None],
        sines.reshape(groups, 1, rows).astype(np.float32), spots,
    )


def lane_pairs(row):
    lane = lax.broadcasted_iota(jnp.int32, row.shape, 1)
    other = pltpu.roll(row, SIDE, 1)
    return jnp.where(lane < SIDE, row, other), jnp.where(lane < SIDE, other, row)


def block_count(wave):
    return jnp.floor((jnp.maximum(M - wave, 0.0) + (BLOCK - 1)) * (1.0 / BLOCK))


def recurrence_kernel(mine_ref, lat_ref, term_ref, beta_ref, scale_ref, growth_ref, start_ref):
    pair = lane_pairs(jnp.broadcast_to(mine_ref[...], (8, LANES)))
    one, two = pair[0][:1], pair[1][:1]
    blocks = growth_ref.shape[0]
    turn = block_count(one)
    block = lax.broadcasted_iota(jnp.int32, (blocks, LANES), 0).astype(jnp.float32)
    second = block >= turn
    wave = jnp.where(second, two, one)
    limit = M - wave
    wave = jnp.minimum(wave, M - 1.0)
    first = (block - jnp.where(second, turn, 0.0)) * BLOCK

    scale = jnp.ones((blocks, LANES), jnp.float32)
    for index in range(BLOCK + 1):
        order = first + index
        degree = wave + order
        square = 4.0 * degree * degree - 1.0
        spread = 4.0 * order * (degree + wave)
        if index > 0:
            scale = scale * jnp.sqrt(square / spread)
        if index < BLOCK:
            beta_ref[pl.ds(index, blocks, stride=BLOCK)] = spread / jnp.maximum(square, 1.0)
            scale_ref[pl.ds(index, blocks, stride=BLOCK)] = jnp.where(order < limit, scale, 0.0)
    growth_ref[...] = scale

    for kind, wave in enumerate((one, two)):
        wave = jnp.minimum(wave, M - 1.0)
        counter = lax.broadcasted_iota(jnp.int32, term_ref.shape, 0).astype(jnp.float32)
        norm = jnp.sum(jnp.where(counter <= wave, term_ref[...], 0.0), axis=0, keepdims=True)
        coarse = lat_ref[1] * wave
        whole = jnp.floor(coarse)
        start_ref[2 * kind] = jnp.exp2(
            (coarse - whole) + lat_ref[2] * wave + 0.5 * (norm - 1.0)
        )
        start_ref[2 * kind + 1] = whole


def prepare_recurrence(mine):
    latitudes = latitude_table()
    points = latitudes.shape[1]
    blocks = 2 * -(-M // BLOCK)
    counter = np.arange(M)
    terms = np.log1p(0.5 / np.maximum(counter, 1)) * (counter > 0) / math.log(2.0)
    terms = np.broadcast_to(terms[:, None], (M, LANES)).astype(np.float32)
    orders = jax.ShapeDtypeStruct((blocks * BLOCK, LANES), jnp.float32)
    return pl.pallas_call(
        recurrence_kernel,
        out_shape=[
            orders,
            orders,
            jax.ShapeDtypeStruct((blocks, LANES), jnp.float32),
            jax.ShapeDtypeStruct((4, points, LANES), jnp.float32),
        ],
        in_specs=[VMEM_SPEC] * 3,
        out_specs=[VMEM_SPEC] * 4,
        compiler_params=pltpu.CompilerParams(vmem_limit_bytes=LATE_BYTES),
    )(mine, latitudes, terms)


def resampled(first, fields, table, total):
    for piece, field in enumerate(fields):
        values = from_int16(field[...])
        values = values * scale_of(values[field.shape[0] - 1 :])
        high, low = split_bf16(values)
        spot = partner(("lat",), table.shape[:1], first + piece)
        both = jnp.concatenate([high, low], axis=1)
        part = jnp.dot(table[spot, 0], both, preferred_element_type=jnp.float32)
        part = part[:, : high.shape[1]] + part[:, high.shape[1] :]
        part += jnp.dot(table[spot, 1], high, preferred_element_type=jnp.float32)
        total = part if total is None else total + part
    return total


def resample_kernel(table_ref, *rest):
    rest[-1][...] = resampled(0, rest[:-1], table_ref, None)


def resample(fields, table):
    count, _, height, _ = table.shape
    span = fields[0].shape[1]
    return pl.pallas_call(
        resample_kernel,
        out_shape=jax.ShapeDtypeStruct((height, span), jnp.float32),
        in_specs=[VMEM_SPEC] * (1 + len(fields)),
        out_specs=VMEM_SPEC,
        compiler_params=pltpu.CompilerParams(vmem_limit_bytes=LATE_BYTES),
        cost_estimate=pl.CostEstimate(
            flops=6 * height * span * NLAT // count * len(fields), bytes_accessed=4 * 2**20, transcendentals=0
        ),
    )(table, *fields)


def legendre_kernel(early, *rest):
    table, lat_ref, beta_ref, scale_ref, growth_ref, start_ref, total_ref, mine_ref, back_ref = rest[:9]
    fields, rest = rest[9:-8], rest[-8:]
    out_ref, weights, before, current, level, sums, result, final = rest
    points = lat_ref.shape[1]
    slots = out_ref.shape[0]
    mine = mine_ref[...]
    odd = mine - 2.0 * jnp.floor(mine * 0.5) > 0.5
    pair = lane_pairs(jnp.broadcast_to(mine, (8, LANES)))
    turn = block_count(pair[0][:1])
    block_total = jnp.max(turn + block_count(pair[1][:1])).astype(jnp.int32)

    total = resampled(early, fields, table, total_ref[...])
    totals = [total[2 * points * kind : 2 * points * (kind + 1)] for kind in range(4)]
    left = lax.broadcasted_iota(jnp.int32, (points, LANES), 1) < SIDE
    for parity in range(2):
        for comp in range(2):
            cols = slice(comp * LANES, (comp + 1) * LANES)
            value = jnp.where(odd, totals[2 + parity][:, cols], totals[parity][:, cols])
            top, bottom = value[:points], value[points:]
            kind = 2 * parity + comp
            weights[0, kind] = jnp.where(left, top, pltpu.roll(bottom, SIDE, 1))
            weights[1, kind] = jnp.where(left, pltpu.roll(top, SIDE, 1), bottom)
    result[...] = jnp.zeros_like(result)
    current[...] = start_ref[0]
    level[...] = start_ref[1]
    before[...] = jnp.zeros_like(before)

    def step(block, carry):
        base = pl.multiple_of(block * BLOCK, BLOCK)
        now = block.astype(jnp.float32)
        second, begins = now >= turn, now == turn
        grow = growth_ref[pl.ds(block, 1)]
        first = 0
        for chunk in CHUNKS:
            rows = slice(first, first + chunk)
            height = jnp.where(begins, start_ref[3, rows], level[rows])
            factor = jnp.exp2(height)
            scaled = [
                jnp.where(second, weights[1, k, rows], weights[0, k, rows]) * factor for k in range(4)
            ]
            cosine = lat_ref[0, rows]
            old = jnp.where(begins, 0.0, before[rows])
            new = jnp.where(begins, start_ref[2, rows], current[rows])
            for order in range(BLOCK):
                for comp in range(2):
                    product = new * scaled[2 * (order % 2) + comp]
                    partial = product.reshape(chunk // 8, 8, LANES).sum(axis=0)
                    place = pl.ds((order * 2 + comp) * 8, 8)
                    if first == 0:
                        sums[place] = partial
                    else:
                        sums[place] += partial
                beta = beta_ref[pl.ds(base + order, 1)]
                old, new = new, cosine * new - beta * old
            biggest = jnp.maximum(jnp.abs(old), jnp.abs(new)) * grow
            shift = jnp.floor(jnp.log(biggest) * (1.0 / math.log(2.0)))
            factor = grow * jnp.exp2(-shift)
            before[rows] = old * factor
            current[rows] = new * factor
            level[rows] = height + shift
            first += chunk
        for comp in range(2):
            total = sums[pl.ds(comp * 8, BLOCK, stride=16)]
            for lane in range(1, 8):
                total += sums[pl.ds(comp * 8 + lane, BLOCK, stride=16)]
            total = total * scale_ref[pl.ds(base, BLOCK)]
            result[comp, pl.ds(base, BLOCK)] = total + pltpu.roll(total, SIDE, 1)
        return carry

    lax.fori_loop(0, block_total, step, 0)

    left = lax.broadcasted_iota(jnp.int32, (BLOCK, LANES), 1) < SIDE
    spots = -(-M // BLOCK)
    chosen = [jnp.broadcast_to(turn, (8, LANES)) == value for value in range(spots + 1)]
    chosen = [jnp.concatenate([mask] * (BLOCK // 8), axis=0) for mask in chosen]
    for place in range(spots):
        rows = slice(place * BLOCK, (place + 1) * BLOCK)
        for comp in range(2):
            early_part = jnp.where(turn > place, result[comp, rows], 0.0)
            later = jnp.zeros((BLOCK, LANES), jnp.float32)
            for value in range(spots + 1):
                base = (place + value) * BLOCK
                if base < result.shape[1]:
                    later = jnp.where(chosen[value], result[comp, base : base + BLOCK], later)
            final[comp, rows] = jnp.where(left, early_part, later)
    back = back_ref[...]
    dims = (((1,), (1,)), ((), ()))
    for comp in range(2):
        high, low = split_bf16(final[comp])
        value = lax.dot_general(back, high, dims, preferred_element_type=jnp.float32)
        value += lax.dot_general(back, low, dims, preferred_element_type=jnp.float32)
        out_ref[:, comp, :] = value[:slots, :M]


def resample_pieces(pieces, rows, padded_rows):
    full = resample_table()
    table = full.reshape(full.shape[0], pieces, rows).transpose(1, 0, 2)
    table = table_bf16(np.pad(table, ((0, 0), (0, 0), (0, padded_rows - rows))))
    return table.reshape(pieces, full.shape[0], 2, padded_rows).transpose(0, 2, 1, 3)


def legendre(fields, mine, back, prepared, rows, slots):
    pieces = len(fields)
    early = pieces // 2
    latitudes = latitude_table()
    points = latitudes.shape[1]
    table = jnp.asarray(resample_pieces(pieces, rows, fields[0].shape[0]))
    total = resample(fields[:early], table)
    vector = pltpu.VMEM((points, LANES), jnp.float32)
    block_rows = -(-M // BLOCK) * BLOCK
    return pl.pallas_call(
        functools.partial(legendre_kernel, early),
        out_shape=jax.ShapeDtypeStruct((slots, 2, M), jnp.float32),
        in_specs=[VMEM_SPEC] * (9 + pieces - early),
        out_specs=VMEM_SPEC,
        scratch_shapes=[
            pltpu.VMEM((2, 4, points, LANES), jnp.float32),
            vector,
            vector,
            vector,
            pltpu.VMEM((BLOCK * 16, LANES), jnp.float32),
            pltpu.VMEM((2, 2 * block_rows, LANES), jnp.float32),
            pltpu.VMEM((2, block_rows, LANES), jnp.float32),
        ],
        compiler_params=pltpu.CompilerParams(vmem_limit_bytes=LATE_BYTES),
        cost_estimate=pl.CostEstimate(
            flops=7 * points * LANES * M, bytes_accessed=6 * 2**20, transcendentals=0
        ),
    )(table, latitudes, *prepared, total, mine, back, *fields[early:])


def shards(tracer, wind_east, wind_north, keep_m, slot_wave):
    rows = tracer.shape[1]
    lat_count = lax.axis_size("lat")
    slots = slot_wave.shape[0] // lat_count
    axes = ("lev", "fld")
    ring = (axes, tuple(lax.axis_size(axis) for axis in axes))

    edges = jnp.concatenate([tracer[:, 0], tracer[:, rows - 1]], axis=0).astype(jnp.float32)
    edges = lax.all_gather(edges, ("lat", *axes))
    blocks = advect(tracer, wind_east, wind_north, ring)
    blocks, slot_wave, keep_m = lax.optimization_barrier((list(blocks), slot_wave, keep_m))
    grids = exchange(blocks, axes)
    places, wave_row, mine, back, keep_col, sine_col = prepare_places(slot_wave, keep_m, lat_count)
    waved = fourier(grids, edges, ring, places, wave_row, keep_col, sine_col, lat_count)
    waved, mine = lax.optimization_barrier((list(waved), mine))
    fields = exchange(waved, "lat")
    prepared = prepare_recurrence(mine)
    return legendre(fields, mine, back, prepared, rows, slots)[None]


def solution(mesh):
    return jax.shard_map(
        shards,
        mesh=mesh,
        in_specs=(
            P("member", "lat", ("lev", "fld")),
            P("member", "lat", ("lev", "fld")),
            P("member", "lat", ("lev", "fld")),
            P("lat"),
            P(),
        ),
        out_specs=P(("member", "lev", "fld"), "lat", None, None),
        check_vma=False,
    )
```

```python
import functools
import math

import jax
import jax.numpy as jnp
import numpy as np
from jax import lax
from jax.experimental import pallas as pl
from jax.experimental.pallas import tpu as pltpu
from jax.sharding import PartitionSpec as P

M = 400
NLAT = 800
NLON = 1600
LANES = 128
BLOCK = 32
CHUNKS = (40, 32, 32)
HELD = -(-M // BLOCK)
SIDE = LANES // 2
TOP = 32767.0
WIND_STEP = 1.5 / TOP
VMEM_BYTES = 60 * 2**20
LATE_BYTES = 30 * 2**20
VMEM_SPEC = pl.BlockSpec(memory_space=pltpu.VMEM)
SMEM_SPEC = pl.BlockSpec(memory_space=pltpu.SMEM)
HBM_SPEC = pl.BlockSpec(memory_space=pltpu.HBM)


def split_bf16(values):
    high = values.astype(jnp.bfloat16)
    low = (values - high.astype(jnp.float32)).astype(jnp.bfloat16)
    return high, low


def table_bf16(table):
    high = table.astype(jnp.bfloat16)
    low = (table - high.astype(np.float64)).astype(jnp.bfloat16)
    return np.concatenate([high, low], axis=-1)


def fourier_tables(pieces):
    quarter = NLON // 4
    spots = np.arange(quarter)[:, None]
    factor = 1.0 / math.sqrt(NLON)

    def parts(waves):
        angles = 2.0 * math.pi / NLON * (spots * waves[None, :] % NLON)
        return factor * np.cos(angles), factor * np.sin(angles)

    def shaped(columns):
        pad = [(0, 0), (0, -columns[0].shape[1] % LANES)]
        table = np.concatenate([np.pad(part, pad) for part in columns], axis=1)
        return table.reshape(share, quarter // share, -1)

    share = pieces // 4
    tables = []
    for first in (0, 2):
        cosine, sine = parts(np.arange(first, M, 4))
        tables.append(shaped([cosine, -sine]))
    waves = np.arange(1, M, 2)
    sign = np.where(waves % 4 == 1, 1.0, -1.0)[None, :]
    cosine, sine = parts(waves)
    return [*tables, shaped([cosine, -sine]), shaped([-sign * sine, -sign * cosine])]


def column_waves():
    columns = []
    for waves in (np.arange(0, M, 4), np.arange(2, M, 4), np.arange(1, M, 2)):
        columns.append(np.pad(waves, (0, -len(waves) % LANES), constant_values=-1))
    return np.concatenate(columns).astype(np.float32)[:, None]


def resample_table():
    half = M // 2
    coarse = math.pi / M * (np.arange(M) + 0.5)
    fine = math.pi / NLAT * (np.arange(NLAT) + 0.5)
    waves = np.arange(M)
    weight = np.where(waves == 0, 1.0, 2.0) / M
    even = (np.cos(np.outer(coarse, waves)) * weight) @ np.cos(np.outer(waves, fine))
    odd = (np.sin(np.outer(coarse, waves)) * weight) @ np.sin(np.outer(waves, fine))
    rows = []
    for full in (even, odd):
        for sign in (1.0, -1.0):
            folded = (full[:half] + sign * full[::-1][:half]).reshape(2, half // 2, NLAT)
            rows.append(np.pad(folded, ((0, 0), (0, -half // 2 % 8), (0, 0))).reshape(-1, NLAT))
    return np.concatenate(rows, axis=0)


def latitude_table():
    half = M // 2
    angles = math.pi / M * (np.arange(half) + 0.5)
    log_sine = np.log2(np.sin(angles))
    coarse = np.round(log_sine * 1024.0) / 1024.0
    rows = np.stack([2.0 * np.cos(angles), coarse, log_sine - coarse]).reshape(3, 2, half // 2)
    rows = np.pad(rows, ((0, 0), (0, 0), (0, -half // 2 % 8)))
    return np.repeat(rows.transpose(0, 2, 1), SIDE, axis=2).astype(np.float32)


def scale_code(biggest):
    wanted = jnp.maximum(biggest, 1e-30) * (1.0 / TOP)
    exponent = jnp.floor(jnp.log(wanted) * (1.0 / math.log(2.0)))
    return exponent * 128.0 + jnp.ceil((wanted * jnp.exp2(-exponent) - 1.0) * 128.0)


def scale_of(code):
    exponent = jnp.floor(code * (1.0 / 128.0))
    rest = code - 128.0 * exponent
    return jnp.exp2(exponent) * (1.0 + rest * (1.0 / 128.0))


def coded(values, inverse):
    return jnp.floor(values * inverse + 0.5)


def as_int16(values):
    return values.astype(jnp.int32).astype(jnp.int16)


def from_int16(codes):
    return codes.astype(jnp.int32).astype(jnp.float32)


def partner(axes, sizes, step):
    count = math.prod(sizes)
    if count != 4:
        return step
    index = lax.axis_index(axes[0])
    for axis, size in zip(axes[1:], sizes[1:]):
        index = index * size + lax.axis_index(axis)
    return index ^ step


def exchange(blocks, axis):
    count = len(blocks)
    if count != 4:
        return list(lax.all_to_all(jnp.stack(blocks), axis, split_axis=0, concat_axis=0, tiled=True))
    pairs = [[(i, i ^ step) for i in range(count)] for step in range(count)]
    return [blocks[0]] + [lax.ppermute(blocks[step], axis, pairs[step]) for step in range(1, count)]


def advect_kernel(ring, lat_count, tracer_hbm, east_hbm, north_hbm, *rest):
    levels, rows, lons = tracer_hbm.shape
    outs, (edge_ref, tracer, east_wind, north_wind, sems) = rest[:levels], rest[levels:]
    chosen = [partner(*ring, step) for step in range(levels)]
    copies = []
    for step, level in enumerate(chosen):
        copies.append(
            [
                pltpu.make_async_copy(source.at[level], target.at[step], sems.at[step, kind])
                for kind, (source, target) in enumerate(
                    ((tracer_hbm, tracer), (east_hbm, east_wind), (north_hbm, north_wind))
                )
            ]
        )
        for copy in copies[-1]:
            copy.start()
    padded_rows = outs[0].shape[0]
    end = (lons - 1) // LANES * LANES
    spare = lons - end
    lane = lax.broadcasted_iota(jnp.int32, (rows, LANES), 1)
    lat_index = lax.axis_index("lat")
    edge_ref[...] = jnp.zeros_like(edge_ref)
    for step, level in enumerate(chosen):
        for copy in copies[step]:
            copy.wait()
        field = tracer[step].astype(jnp.float32)

        @pl.when(lat_index < lat_count - 1)
        def _():
            edge_ref[(lat_index + 1) * levels + level] = field[rows - 1 :]

        @pl.when(lat_index > 0)
        def _():
            edge_ref[(lat_index - 1) * levels + level] = field[:1]

        blank = jnp.zeros((rows, 1), jnp.float32)
        west = jnp.concatenate([blank, field[:, :-1]], axis=1)
        east = jnp.concatenate([field[:, 1:], blank], axis=1)
        blank = jnp.zeros((1, lons), jnp.float32)
        north = jnp.concatenate([blank, field[:-1]], axis=0)
        south = jnp.concatenate([field[1:], blank], axis=0)
        eastward = 0.5 * east_wind[step].astype(jnp.float32)
        northward = 0.5 * north_wind[step].astype(jnp.float32)
        moved = field - eastward * (east - west) - northward * (south - north)
        first, last = field[:, :1], field[:, lons - 1 :]
        biggest = jnp.max(jnp.abs(moved), axis=1, keepdims=True)
        biggest = jnp.maximum(biggest, jnp.maximum(jnp.abs(first), jnp.abs(last)))
        code = scale_code(biggest)
        inverse = 1.0 / scale_of(code)
        filler = jnp.zeros((rows, LANES - spare), jnp.float32)
        tile = jnp.concatenate([moved[:, end:], filler], axis=1)
        tile = jnp.where(lane == spare + 1, first, jnp.where(lane == spare + 2, last, tile))
        tile = coded(tile, inverse)
        tile = jnp.where(lane == spare, code, tile)
        winds = jnp.where(lane == spare + 3, eastward[:, :1], eastward[:, lons - 1 :])
        winds = coded(winds, 1.0 / WIND_STEP)
        tile = jnp.where((lane == spare + 3) | (lane == spare + 4), winds, tile)
        wind_rows = jnp.concatenate([northward[:1], northward[rows - 1 :]], axis=0)
        wind_rows = coded(wind_rows, 1.0 / WIND_STEP)
        blank = jnp.zeros((padded_rows - rows - 2, lons), jnp.float32)
        wind_rows = jnp.concatenate([wind_rows, blank], axis=0)
        filler = jnp.zeros((padded_rows - rows, LANES - spare), jnp.float32)
        wind_tile = jnp.concatenate([wind_rows[:, end:], filler], axis=1)
        steps = jnp.concatenate([coded(moved[:, :end], inverse), wind_rows[:, :end]], axis=0)
        outs[step][:, :end] = as_int16(steps)
        outs[step][:, end:] = as_int16(jnp.concatenate([tile, wind_tile], axis=0))


def advect(tracer, east_wind, north_wind, ring):
    levels, rows, lons = tracer.shape
    lat_count = lax.axis_size("lat")
    width = (lons - 1) // LANES * LANES + LANES
    padded_rows = -(-(rows + 2) // 16) * 16
    held = pltpu.VMEM((levels, rows, lons), jnp.bfloat16)
    result = pl.pallas_call(
        functools.partial(advect_kernel, ring, lat_count),
        out_shape=[jax.ShapeDtypeStruct((padded_rows, width), jnp.int16)] * levels
        + [jax.ShapeDtypeStruct((lat_count * levels, 1, lons), jnp.float32)],
        in_specs=[HBM_SPEC] * 3,
        out_specs=[VMEM_SPEC] * (levels + 1),
        scratch_shapes=[held, held, held, pltpu.SemaphoreType.DMA((levels, 3))],
        compiler_params=pltpu.CompilerParams(vmem_limit_bytes=VMEM_BYTES),
        cost_estimate=pl.CostEstimate(
            flops=20 * levels * rows * lons, bytes_accessed=8 * levels * rows * lons, transcendentals=0
        ),
    )(tracer, east_wind, north_wind)
    return list(result[:levels]), result[levels]


def fourier_kernel(ring, lat_count, pieces, *rest):
    grids, (edge_ref, *tables_hbm, wave_ref, keep_ref, sine_ref) = rest[:pieces], rest[pieces : pieces + 9]
    outs, rest = rest[pieces + 9 :][:lat_count], rest[pieces + 9 + lat_count :]
    tables, place_ref, (field, sems) = rest[:4], rest[4], rest[5:]
    _, rows, width = field.shape
    lons = tables[0].shape[1]
    share = pieces // 4
    copies = []
    for kind, target in enumerate((*tables, place_ref)):
        copies.append(pltpu.make_async_copy(tables_hbm[kind], target, sems.at[kind]))
        copies[-1].start()

    end = width - LANES
    spare = lons - end
    lane = lax.broadcasted_iota(jnp.int32, (rows, LANES), 1)
    winds = (lane == spare + 3) | (lane == spare + 4)
    lat_index = lax.axis_index("lat")
    for piece in range(pieces):
        spot = partner(*ring, piece)
        values = from_int16(grids[piece][...])
        tile = values[:rows, end:]
        scale = scale_of(tile[:, spare : spare + 1])
        field[spot, :, :end] = values[:rows, :end] * scale
        field[spot, :, end:] = tile * jnp.where(winds, WIND_STEP, scale)
        wind_rows = values[rows : rows + 2, :lons] * WIND_STEP

        @pl.when(lat_index > 0)
        def _():
            above = edge_ref[(lat_index - 1) * pieces + spot]
            field[spot, :1, :lons] += wind_rows[:1] * above

        @pl.when(lat_index < lat_count - 1)
        def _():
            below = edge_ref[(lat_index + 1) * pieces + spot]
            field[spot, rows - 1 :, :lons] -= wind_rows[1:] * below

    for spot in range(pieces):
        tile = field[spot, :, end:]
        before = field[(spot - 1) % pieces, :, end:]
        after = field[(spot + 1) % pieces, :, end:]
        shift = LANES - spare
        gain = pltpu.roll(tile, shift - 3, 1) * pltpu.roll(before, shift - 2, 1)
        loss = pltpu.roll(tile, LANES - 5, 1) * pltpu.roll(after, LANES - 2, 1)
        field[spot, :, end:] = tile - jnp.where(lane == spare - 1, loss, 0.0)
        field[spot, :, :LANES] += jnp.where(lane == 0, gain, 0.0)

    def product(value, table, spot):
        high, low = split_bf16(value)
        width = table.shape[2] // 2
        both = jnp.dot(high, table[spot], preferred_element_type=jnp.float32)
        part = jnp.dot(low, table[spot, :, :width], preferred_element_type=jnp.float32)
        return part + both[:, :width] + both[:, width:]

    sums = [None, None, None]
    for spot in range(share):
        quarters = [field[quarter * share + spot, :, :lons] for quarter in range(4)]
        sum02, dif02 = quarters[0] + quarters[2], quarters[0] - quarters[2]
        sum13, dif13 = quarters[1] + quarters[3], quarters[1] - quarters[3]
        parts = []
        for kind, value in enumerate((sum02 + sum13, sum02 - sum13, dif02, dif13)):
            if spot == 0:
                copies[kind].wait()
            parts.append(product(value, tables[kind], spot))
        parts = [parts[0], parts[1], parts[2] + parts[3]]
        sums = [part if total is None else total + part for total, part in zip(sums, parts)]
    copies[4].wait()
    placed = []
    for part in range(2):
        columns = []
        for total in sums:
            half = total.shape[1] // 2
            columns.append(total[:, part * half : (part + 1) * half])
        high, low = split_bf16(jnp.concatenate(columns, axis=1))
        value = jnp.dot(high, place_ref[...], preferred_element_type=jnp.float32)
        value += jnp.dot(low, place_ref[...], preferred_element_type=jnp.float32)
        kept = jnp.where(wave_ref[...] < keep_ref[...], value * sine_ref[...], 0.0)
        code = scale_code(jnp.max(jnp.abs(kept), axis=0, keepdims=True))
        steps = coded(kept, 1.0 / scale_of(code))
        codes = jnp.broadcast_to(code, (outs[0].shape[0] - rows, code.shape[1]))
        placed.append(as_int16(jnp.concatenate([steps, codes], axis=0)))
    for target in range(lat_count):
        for part in range(2):
            cols = slice(target * LANES, (target + 1) * LANES)
            outs[target][:, part * LANES : (part + 1) * LANES] = placed[part][:, cols]


def fourier(grids, edges, ring, places, wave_row, keep_col, sine_col, lat_count):
    pieces = len(grids)
    rows = keep_col.shape[0]
    width = grids[0].shape[1]
    padded_rows = -(-(rows + 1) // 16) * 16
    tables = [table_bf16(table) for table in fourier_tables(pieces)]
    return pl.pallas_call(
        functools.partial(fourier_kernel, ring, lat_count, pieces),
        out_shape=[jax.ShapeDtypeStruct((padded_rows, 2 * LANES), jnp.int16)] * lat_count,
        in_specs=[VMEM_SPEC] * (pieces + 1) + [HBM_SPEC] * 5 + [VMEM_SPEC] * 3,
        out_specs=[VMEM_SPEC] * lat_count,
        scratch_shapes=[pltpu.VMEM(table.shape, jnp.bfloat16) for table in tables]
        + [pltpu.VMEM(places.shape, jnp.bfloat16)]
        + [pltpu.VMEM((pieces, rows, width), jnp.float32), pltpu.SemaphoreType.DMA((5,))],
        compiler_params=pltpu.CompilerParams(vmem_limit_bytes=VMEM_BYTES),
        cost_estimate=pl.CostEstimate(
            flops=3 * rows * NLON * M, bytes_accessed=6 * 2**20, transcendentals=0
        ),
    )(*grids, edges, *tables, places, wave_row, keep_col, sine_col)


def places_kernel(
    slot_ref, keep_ref, sine_ref, spot_ref,
    place_ref, wave_ref, mine_ref, back_ref, keep_col, sine_col, sorted_rows,
):
    groups, _, rows = sine_ref.shape
    lat_index = lax.axis_index("lat")
    slots = slot_ref.shape[1] // groups
    paired = (slots + 1) // 2
    shape = (LANES, LANES)
    down = lax.broadcasted_iota(jnp.int32, shape, 0)
    across = lax.broadcasted_iota(jnp.int32, shape, 1)
    filler = jnp.full((1, LANES - slots), 2.0 * M, jnp.float32)
    for group in range(groups):
        row = slot_ref[:, group * slots : (group + 1) * slots].astype(jnp.float32)
        row = jnp.broadcast_to(jnp.concatenate([row, filler], axis=1), shape)
        column = jnp.sum(jnp.where(down == across, row, 0.0), axis=1, keepdims=True)
        ahead = (row < column) | ((row == column) & (across < down))
        rank = jnp.sum(jnp.where(ahead, 1.0, 0.0), axis=1, keepdims=True)
        place = jnp.where(rank < paired, rank, SIDE + slots - 1.0 - rank)
        place = jnp.where(rank < slots, place, -1.0)
        hot = jnp.where(place == across.astype(jnp.float32), 1.0, 0.0)
        filled = jnp.sum(hot, axis=0, keepdims=True)
        values = jnp.sum(hot * column, axis=0, keepdims=True)
        values = jnp.where(filled > 0.5, values, 2.0 * M)
        sorted_rows[group] = jnp.broadcast_to(values, sorted_rows.shape[1:])

        @pl.when(group == lat_index)
        def _():
            mine_ref[...] = values
            back_ref[...] = hot.astype(jnp.bfloat16)

    spots = jnp.broadcast_to(spot_ref[...], (spot_ref.shape[0], LANES))
    for step in range(groups):
        row = sorted_rows[partner(("lat",), (groups,), step), :1]
        cols = slice(step * LANES, (step + 1) * LANES)
        wave_ref[:, cols] = row
        place_ref[:, cols] = jnp.where(spots == row, 1.0, 0.0).astype(jnp.bfloat16)

    shape = (rows, rows)
    same = lax.broadcasted_iota(jnp.int32, shape, 0) == lax.broadcasted_iota(jnp.int32, shape, 1)
    kept = jnp.broadcast_to(keep_ref[...].astype(jnp.float32), shape)
    keep_col[...] = jnp.sum(jnp.where(same, kept, 0.0), axis=1, keepdims=True)
    sine = jnp.broadcast_to(sine_ref[lat_index], shape)
    sine_col[...] = jnp.sum(jnp.where(same, sine, 0.0), axis=1, keepdims=True)


def prepare_places(slot_wave, keep_m, groups):
    rows = keep_m.shape[0]
    sines = np.sin(math.pi / NLAT * (np.arange(NLAT) + 0.5)) * math.sqrt(2.0 / NLAT)
    spots = column_waves()
    width = groups * LANES
    return pl.pallas_call(
        places_kernel,
        out_shape=[
            jax.ShapeDtypeStruct((spots.shape[0], width), jnp.bfloat16),
            jax.ShapeDtypeStruct((1, width), jnp.float32),
            jax.ShapeDtypeStruct((1, LANES), jnp.float32),
            jax.ShapeDtypeStruct((LANES, LANES), jnp.bfloat16),
            jax.ShapeDtypeStruct((rows, 1), jnp.float32),
            jax.ShapeDtypeStruct((rows, 1), jnp.float32),
        ],
        in_specs=[VMEM_SPEC] * 4,
        out_specs=[VMEM_SPEC] * 6,
        scratch_shapes=[pltpu.VMEM((groups, 8, LANES), jnp.float32)],
        compiler_params=pltpu.CompilerParams(vmem_limit_bytes=VMEM_BYTES),
    )(
        slot_wave[None], keep_m[None],
        sines.reshape(groups, 1, rows).astype(np.float32), spots,
    )


def lane_pairs(row):
    lane = lax.broadcasted_iota(jnp.int32, row.shape, 1)
    other = pltpu.roll(row, SIDE, 1)
    return jnp.where(lane < SIDE, row, other), jnp.where(lane < SIDE, other, row)


def block_count(wave):
    return jnp.floor((jnp.maximum(M - wave, 0.0) + (BLOCK - 1)) * (1.0 / BLOCK))


def sweep_kernel(
    mine_ref, lat_ref, term_ref, beta_ref, scale_ref, growth_ref, start_ref, state_ref, values_ref
):
    pair = lane_pairs(jnp.broadcast_to(mine_ref[...], (8, LANES)))
    one, two = pair[0][:1], pair[1][:1]
    blocks = growth_ref.shape[0]
    turn = block_count(one)
    block = lax.broadcasted_iota(jnp.int32, (blocks, LANES), 0).astype(jnp.float32)
    second = block >= turn
    wave = jnp.where(second, two, one)
    limit = M - wave
    wave = jnp.minimum(wave, M - 1.0)
    first = (block - jnp.where(second, turn, 0.0)) * BLOCK

    scale = jnp.ones((blocks, LANES), jnp.float32)
    for index in range(BLOCK + 1):
        order = first + index
        degree = wave + order
        square = 4.0 * degree * degree - 1.0
        spread = 4.0 * order * (degree + wave)
        if index > 0:
            scale = scale * jnp.sqrt(square / spread)
        if index < BLOCK:
            beta_ref[pl.ds(index, blocks, stride=BLOCK)] = spread / jnp.maximum(square, 1.0)
            scale_ref[pl.ds(index, blocks, stride=BLOCK)] = jnp.where(order < limit, scale, 0.0)
    growth_ref[...] = scale

    for kind, wave in enumerate((one, two)):
        wave = jnp.minimum(wave, M - 1.0)
        counter = lax.broadcasted_iota(jnp.int32, term_ref.shape, 0).astype(jnp.float32)
        norm = jnp.sum(jnp.where(counter <= wave, term_ref[...], 0.0), axis=0, keepdims=True)
        coarse = lat_ref[1] * wave
        whole = jnp.floor(coarse)
        start_ref[2 * kind] = jnp.exp2(
            (coarse - whole) + lat_ref[2] * wave + 0.5 * (norm - 1.0)
        )
        start_ref[2 * kind + 1] = whole

    state_ref[0] = jnp.zeros_like(state_ref[0])
    state_ref[1] = start_ref[0]
    state_ref[2] = start_ref[1]
    points = lat_ref.shape[1]

    def step(block, carry):
        first = 0
        for chunk in (points // 16 * 8, points - points // 16 * 8):
            rows = slice(first, first + chunk)

            def keep(order, value):
                values_ref[block, order, rows] = value

            sweep_block(block, turn, rows, lat_ref, beta_ref, growth_ref, start_ref, state_ref, keep)
            first += chunk
        return carry

    total = jnp.max(turn + block_count(two)).astype(jnp.int32)
    lax.fori_loop(0, jnp.minimum(total, HELD), step, 0)


def sweep_block(block, turn, rows, lat_ref, beta_ref, growth_ref, start_ref, state_ref, use):
    base = pl.multiple_of(block * BLOCK, BLOCK)
    begins = block.astype(jnp.float32) == turn
    grow = growth_ref[pl.ds(block, 1)]
    cosine = lat_ref[0, rows]
    height = jnp.where(begins, start_ref[3, rows], state_ref[2, rows])
    factor = jnp.exp2(height)
    old = jnp.where(begins, 0.0, state_ref[0, rows])
    new = jnp.where(begins, start_ref[2, rows], state_ref[1, rows])
    for order in range(BLOCK):
        use(order, new * factor)
        beta = beta_ref[pl.ds(base + order, 1)]
        old, new = new, cosine * new - beta * old
    biggest = jnp.maximum(jnp.abs(old), jnp.abs(new)) * grow
    shift = jnp.floor(jnp.log(biggest) * (1.0 / math.log(2.0)))
    factor = grow * jnp.exp2(-shift)
    state_ref[0, rows] = old * factor
    state_ref[1, rows] = new * factor
    state_ref[2, rows] = height + shift


def prepare_recurrence(mine):
    latitudes = latitude_table()
    points = latitudes.shape[1]
    blocks = 2 * -(-M // BLOCK)
    counter = np.arange(M)
    terms = np.log1p(0.5 / np.maximum(counter, 1)) * (counter > 0) / math.log(2.0)
    terms = np.broadcast_to(terms[:, None], (M, LANES)).astype(np.float32)
    orders = jax.ShapeDtypeStruct((blocks * BLOCK, LANES), jnp.float32)
    return pl.pallas_call(
        sweep_kernel,
        out_shape=[
            orders,
            orders,
            jax.ShapeDtypeStruct((blocks, LANES), jnp.float32),
            jax.ShapeDtypeStruct((4, points, LANES), jnp.float32),
            jax.ShapeDtypeStruct((3, points, LANES), jnp.float32),
            jax.ShapeDtypeStruct((HELD, BLOCK, points, LANES), jnp.float32),
        ],
        in_specs=[VMEM_SPEC] * 3,
        out_specs=[VMEM_SPEC] * 6,
        compiler_params=pltpu.CompilerParams(vmem_limit_bytes=LATE_BYTES),
    )(mine, latitudes, terms)


def resampled(first, fields, table, total):
    for piece, field in enumerate(fields):
        values = from_int16(field[...])
        values = values * scale_of(values[field.shape[0] - 1 :])
        high, low = split_bf16(values)
        spot = partner(("lat",), table.shape[:1], first + piece)
        both = jnp.concatenate([high, low], axis=1)
        part = jnp.dot(table[spot, 0], both, preferred_element_type=jnp.float32)
        part = part[:, : high.shape[1]] + part[:, high.shape[1] :]
        part += jnp.dot(table[spot, 1], high, preferred_element_type=jnp.float32)
        total = part if total is None else total + part
    return total


def resample_kernel(table_ref, *rest):
    rest[-1][...] = resampled(0, rest[:-1], table_ref, None)


def resample(fields, table):
    count, _, height, _ = table.shape
    span = fields[0].shape[1]
    return pl.pallas_call(
        resample_kernel,
        out_shape=jax.ShapeDtypeStruct((height, span), jnp.float32),
        in_specs=[VMEM_SPEC] * (1 + len(fields)),
        out_specs=VMEM_SPEC,
        compiler_params=pltpu.CompilerParams(vmem_limit_bytes=LATE_BYTES),
        cost_estimate=pl.CostEstimate(
            flops=6 * height * span * NLAT // count * len(fields), bytes_accessed=4 * 2**20, transcendentals=0
        ),
    )(table, *fields)


def legendre_kernel(early, *rest):
    table, lat_ref, beta_ref, scale_ref, growth_ref, start_ref, left_ref, values_ref = rest[:8]
    total_ref, mine_ref, back_ref = rest[8:11]
    fields, (out_ref, weights, state_ref, sums, result, final) = rest[11:-6], rest[-6:]
    points = lat_ref.shape[1]
    slots = out_ref.shape[0]
    mine = mine_ref[...]
    odd = mine - 2.0 * jnp.floor(mine * 0.5) > 0.5
    pair = lane_pairs(jnp.broadcast_to(mine, (8, LANES)))
    turn = block_count(pair[0][:1])
    block_total = jnp.max(turn + block_count(pair[1][:1])).astype(jnp.int32)

    total = resampled(early, fields, table, total_ref[...])
    totals = [total[2 * points * kind : 2 * points * (kind + 1)] for kind in range(4)]
    left = lax.broadcasted_iota(jnp.int32, (points, LANES), 1) < SIDE
    for parity in range(2):
        for comp in range(2):
            cols = slice(comp * LANES, (comp + 1) * LANES)
            value = jnp.where(odd, totals[2 + parity][:, cols], totals[parity][:, cols])
            top, bottom = value[:points], value[points:]
            kind = 2 * parity + comp
            weights[0, kind] = jnp.where(left, top, pltpu.roll(bottom, SIDE, 1))
            weights[1, kind] = jnp.where(left, pltpu.roll(top, SIDE, 1), bottom)
    result[...] = jnp.zeros_like(result)
    state_ref[...] = left_ref[...]

    def reduced(block):
        base = pl.multiple_of(block * BLOCK, BLOCK)
        for comp in range(2):
            total = sums[pl.ds(comp * 8, BLOCK, stride=16)]
            for lane in range(1, 8):
                total += sums[pl.ds(comp * 8 + lane, BLOCK, stride=16)]
            total = total * scale_ref[pl.ds(base, BLOCK)]
            result[comp, pl.ds(base, BLOCK)] = total + pltpu.roll(total, SIDE, 1)

    def held_step(block, carry):
        second = block.astype(jnp.float32) >= turn
        for parity in range(2):
            scaled = [
                jnp.where(second, weights[1, 2 * parity + comp], weights[0, 2 * parity + comp])
                for comp in range(2)
            ]
            for order in range(parity, BLOCK, 2):
                value = values_ref[block, order]
                for comp in range(2):
                    product = (value * scaled[comp]).reshape(points // 8, 8, LANES)
                    sums[pl.ds((order * 2 + comp) * 8, 8)] = product.sum(axis=0)
        reduced(block)
        return carry

    def step(block, carry):
        second = block.astype(jnp.float32) >= turn
        first = 0
        for chunk in CHUNKS:
            rows = slice(first, first + chunk)
            scaled = [jnp.where(second, weights[1, k, rows], weights[0, k, rows]) for k in range(4)]

            def add(order, value):
                for comp in range(2):
                    product = value * scaled[2 * (order % 2) + comp]
                    partial = product.reshape(chunk // 8, 8, LANES).sum(axis=0)
                    place = pl.ds((order * 2 + comp) * 8, 8)
                    if first == 0:
                        sums[place] = partial
                    else:
                        sums[place] += partial

            sweep_block(block, turn, rows, lat_ref, beta_ref, growth_ref, start_ref, state_ref, add)
            first += chunk
        reduced(block)
        return carry

    lax.fori_loop(0, jnp.minimum(block_total, HELD), held_step, 0)
    lax.fori_loop(HELD, block_total, step, 0)

    left = lax.broadcasted_iota(jnp.int32, (BLOCK, LANES), 1) < SIDE
    spots = -(-M // BLOCK)
    chosen = [jnp.broadcast_to(turn, (8, LANES)) == value for value in range(spots + 1)]
    chosen = [jnp.concatenate([mask] * (BLOCK // 8), axis=0) for mask in chosen]
    for place in range(spots):
        rows = slice(place * BLOCK, (place + 1) * BLOCK)
        for comp in range(2):
            early_part = jnp.where(turn > place, result[comp, rows], 0.0)
            later = jnp.zeros((BLOCK, LANES), jnp.float32)
            for value in range(spots + 1):
                base = (place + value) * BLOCK
                if base < result.shape[1]:
                    later = jnp.where(chosen[value], result[comp, base : base + BLOCK], later)
            final[comp, rows] = jnp.where(left, early_part, later)
    back = back_ref[...]
    dims = (((1,), (1,)), ((), ()))
    for comp in range(2):
        high, low = split_bf16(final[comp])
        value = lax.dot_general(back, high, dims, preferred_element_type=jnp.float32)
        value += lax.dot_general(back, low, dims, preferred_element_type=jnp.float32)
        out_ref[:, comp, :] = value[:slots, :M]


def resample_pieces(pieces, rows, padded_rows):
    full = resample_table()
    table = full.reshape(full.shape[0], pieces, rows).transpose(1, 0, 2)
    table = table_bf16(np.pad(table, ((0, 0), (0, 0), (0, padded_rows - rows))))
    return table.reshape(pieces, full.shape[0], 2, padded_rows).transpose(0, 2, 1, 3)


def legendre(fields, mine, back, prepared, rows, slots):
    pieces = len(fields)
    early = pieces // 2
    latitudes = latitude_table()
    points = latitudes.shape[1]
    table = jnp.asarray(resample_pieces(pieces, rows, fields[0].shape[0]))
    total = resample(fields[:early], table)
    block_rows = -(-M // BLOCK) * BLOCK
    return pl.pallas_call(
        functools.partial(legendre_kernel, early),
        out_shape=jax.ShapeDtypeStruct((slots, 2, M), jnp.float32),
        in_specs=[VMEM_SPEC] * (11 + pieces - early),
        out_specs=VMEM_SPEC,
        scratch_shapes=[
            pltpu.VMEM((2, 4, points, LANES), jnp.float32),
            pltpu.VMEM((3, points, LANES), jnp.float32),
            pltpu.VMEM((BLOCK * 16, LANES), jnp.float32),
            pltpu.VMEM((2, 2 * block_rows, LANES), jnp.float32),
            pltpu.VMEM((2, block_rows, LANES), jnp.float32),
        ],
        compiler_params=pltpu.CompilerParams(vmem_limit_bytes=LATE_BYTES),
        cost_estimate=pl.CostEstimate(
            flops=7 * points * LANES * M, bytes_accessed=6 * 2**20, transcendentals=0
        ),
    )(table, latitudes, *prepared, total, mine, back, *fields[early:])


def shards(tracer, wind_east, wind_north, keep_m, slot_wave):
    rows = tracer.shape[1]
    lat_count = lax.axis_size("lat")
    slots = slot_wave.shape[0] // lat_count
    axes = ("lev", "fld")
    ring = (axes, tuple(lax.axis_size(axis) for axis in axes))

    blocks, edges = advect(tracer, wind_east, wind_north, ring)
    blocks, slot_wave, keep_m = lax.optimization_barrier((blocks, slot_wave, keep_m))
    grids = exchange(blocks, axes)
    edges = lax.all_to_all(edges, ("lat", *axes), split_axis=0, concat_axis=0, tiled=True)
    places, wave_row, mine, back, keep_col, sine_col = prepare_places(slot_wave, keep_m, lat_count)
    waved = fourier(grids, edges, ring, places, wave_row, keep_col, sine_col, lat_count)
    waved, mine = lax.optimization_barrier((list(waved), mine))
    fields = exchange(waved, "lat")
    prepared = prepare_recurrence(mine)
    return legendre(fields, mine, back, prepared, rows, slots)[None]


def solution(mesh):
    return jax.shard_map(
        shards,
        mesh=mesh,
        in_specs=(
            P("member", "lat", ("lev", "fld")),
            P("member", "lat", ("lev", "fld")),
            P("member", "lat", ("lev", "fld")),
            P("lat"),
            P(),
        ),
        out_specs=P(("member", "lev", "fld"), "lat", None, None),
        check_vma=False,
    )
```

```python
import functools
import math

import jax
import jax.numpy as jnp
import numpy as np
from jax import lax
from jax.experimental import pallas as pl
from jax.experimental.pallas import tpu as pltpu
from jax.sharding import PartitionSpec as P

M = 400
NLAT = 800
NLON = 1600
LANES = 128
BLOCK = 32
CHUNKS = (40, 32, 32)
HELD = -(-M // BLOCK)
SIDE = LANES // 2
TOP = 32767.0
WIND_STEP = 1.5 / TOP
VMEM_BYTES = 60 * 2**20
LATE_BYTES = 20 * 2**20
VMEM_SPEC = pl.BlockSpec(memory_space=pltpu.VMEM)
SMEM_SPEC = pl.BlockSpec(memory_space=pltpu.SMEM)
HBM_SPEC = pl.BlockSpec(memory_space=pltpu.HBM)


def split_bf16(values):
    high = values.astype(jnp.bfloat16)
    low = (values - high.astype(jnp.float32)).astype(jnp.bfloat16)
    return high, low


def table_bf16(table):
    high = table.astype(jnp.bfloat16)
    low = (table - high.astype(np.float64)).astype(jnp.bfloat16)
    return np.concatenate([high, low], axis=-1)


def fourier_tables(pieces):
    quarter = NLON // 4
    spots = np.arange(quarter)[:, None]
    factor = 1.0 / math.sqrt(NLON)

    def parts(waves):
        angles = 2.0 * math.pi / NLON * (spots * waves[None, :] % NLON)
        return factor * np.cos(angles), factor * np.sin(angles)

    def shaped(columns):
        pad = [(0, 0), (0, -columns[0].shape[1] % LANES)]
        table = np.concatenate([np.pad(part, pad) for part in columns], axis=1)
        return table.reshape(share, quarter // share, -1)

    share = pieces // 4
    tables = []
    for first in (0, 2):
        cosine, sine = parts(np.arange(first, M, 4))
        tables.append(shaped([cosine, -sine]))
    waves = np.arange(1, M, 2)
    sign = np.where(waves % 4 == 1, 1.0, -1.0)[None, :]
    cosine, sine = parts(waves)
    return [*tables, shaped([cosine, -sine]), shaped([-sign * sine, -sign * cosine])]


def column_waves():
    columns = []
    for waves in (np.arange(0, M, 4), np.arange(2, M, 4), np.arange(1, M, 2)):
        columns.append(np.pad(waves, (0, -len(waves) % LANES), constant_values=-1))
    return np.concatenate(columns).astype(np.float32)[:, None]


def resample_table():
    half = M // 2
    coarse = math.pi / M * (np.arange(M) + 0.5)
    fine = math.pi / NLAT * (np.arange(NLAT) + 0.5)
    waves = np.arange(M)
    weight = np.where(waves == 0, 1.0, 2.0) / M
    even = (np.cos(np.outer(coarse, waves)) * weight) @ np.cos(np.outer(waves, fine))
    odd = (np.sin(np.outer(coarse, waves)) * weight) @ np.sin(np.outer(waves, fine))
    rows = []
    for full in (even, odd):
        for sign in (1.0, -1.0):
            folded = (full[:half] + sign * full[::-1][:half]).reshape(2, half // 2, NLAT)
            rows.append(np.pad(folded, ((0, 0), (0, -half // 2 % 8), (0, 0))).reshape(-1, NLAT))
    return np.concatenate(rows, axis=0)


def latitude_table():
    half = M // 2
    angles = math.pi / M * (np.arange(half) + 0.5)
    log_sine = np.log2(np.sin(angles))
    coarse = np.round(log_sine * 1024.0) / 1024.0
    rows = np.stack([2.0 * np.cos(angles), coarse, log_sine - coarse]).reshape(3, 2, half // 2)
    rows = np.pad(rows, ((0, 0), (0, 0), (0, -half // 2 % 8)))
    return np.repeat(rows.transpose(0, 2, 1), SIDE, axis=2).astype(np.float32)


def scale_code(biggest):
    wanted = jnp.maximum(biggest, 1e-30) * (1.0 / TOP)
    exponent = jnp.floor(jnp.log(wanted) * (1.0 / math.log(2.0)))
    return exponent * 128.0 + jnp.ceil((wanted * jnp.exp2(-exponent) - 1.0) * 128.0)


def scale_of(code):
    exponent = jnp.floor(code * (1.0 / 128.0))
    rest = code - 128.0 * exponent
    return jnp.exp2(exponent) * (1.0 + rest * (1.0 / 128.0))


def coded(values, inverse):
    return jnp.floor(values * inverse + 0.5)


def as_int16(values):
    return values.astype(jnp.int32).astype(jnp.int16)


def from_int16(codes):
    return codes.astype(jnp.int32).astype(jnp.float32)


def partner(axes, sizes, step):
    count = math.prod(sizes)
    if count != 4:
        return step
    index = lax.axis_index(axes[0])
    for axis, size in zip(axes[1:], sizes[1:]):
        index = index * size + lax.axis_index(axis)
    return index ^ step


def exchange(blocks, axis):
    count = len(blocks)
    if count != 4:
        return list(lax.all_to_all(jnp.stack(blocks), axis, split_axis=0, concat_axis=0, tiled=True))
    pairs = [[(i, i ^ step) for i in range(count)] for step in range(count)]
    return [blocks[0]] + [lax.ppermute(blocks[step], axis, pairs[step]) for step in range(1, count)]


def advect_kernel(ring, lat_count, tracer_hbm, east_hbm, north_hbm, *rest):
    levels, rows, lons = tracer_hbm.shape
    outs, (edge_ref, tracer, east_wind, north_wind, sems) = rest[:levels], rest[levels:]
    chosen = [partner(*ring, step) for step in range(levels)]
    copies = []
    for step, level in enumerate(chosen):
        copies.append(
            [
                pltpu.make_async_copy(source.at[level], target.at[step], sems.at[step, kind])
                for kind, (source, target) in enumerate(
                    ((tracer_hbm, tracer), (east_hbm, east_wind), (north_hbm, north_wind))
                )
            ]
        )
        for copy in copies[-1]:
            copy.start()
    padded_rows = outs[0].shape[0]
    end = (lons - 1) // LANES * LANES
    spare = lons - end
    lane = lax.broadcasted_iota(jnp.int32, (rows, LANES), 1)
    lat_index = lax.axis_index("lat")
    edge_ref[...] = jnp.zeros_like(edge_ref)
    for step, level in enumerate(chosen):
        for copy in copies[step]:
            copy.wait()
        field = tracer[step].astype(jnp.float32)

        @pl.when(lat_index < lat_count - 1)
        def _():
            edge_ref[(lat_index + 1) * levels + level] = field[rows - 1 :]

        @pl.when(lat_index > 0)
        def _():
            edge_ref[(lat_index - 1) * levels + level] = field[:1]

        blank = jnp.zeros((rows, 1), jnp.float32)
        west = jnp.concatenate([blank, field[:, :-1]], axis=1)
        east = jnp.concatenate([field[:, 1:], blank], axis=1)
        blank = jnp.zeros((1, lons), jnp.float32)
        north = jnp.concatenate([blank, field[:-1]], axis=0)
        south = jnp.concatenate([field[1:], blank], axis=0)
        eastward = 0.5 * east_wind[step].astype(jnp.float32)
        northward = 0.5 * north_wind[step].astype(jnp.float32)
        moved = field - eastward * (east - west) - northward * (south - north)
        first, last = field[:, :1], field[:, lons - 1 :]
        biggest = jnp.max(jnp.abs(moved), axis=1, keepdims=True)
        biggest = jnp.maximum(biggest, jnp.maximum(jnp.abs(first), jnp.abs(last)))
        code = scale_code(biggest)
        inverse = 1.0 / scale_of(code)
        filler = jnp.zeros((rows, LANES - spare), jnp.float32)
        tile = jnp.concatenate([moved[:, end:], filler], axis=1)
        tile = jnp.where(lane == spare + 1, first, jnp.where(lane == spare + 2, last, tile))
        tile = coded(tile, inverse)
        tile = jnp.where(lane == spare, code, tile)
        winds = jnp.where(lane == spare + 3, eastward[:, :1], eastward[:, lons - 1 :])
        winds = coded(winds, 1.0 / WIND_STEP)
        tile = jnp.where((lane == spare + 3) | (lane == spare + 4), winds, tile)
        wind_rows = jnp.concatenate([northward[:1], northward[rows - 1 :]], axis=0)
        wind_rows = coded(wind_rows, 1.0 / WIND_STEP)
        blank = jnp.zeros((padded_rows - rows - 2, lons), jnp.float32)
        wind_rows = jnp.concatenate([wind_rows, blank], axis=0)
        filler = jnp.zeros((padded_rows - rows, LANES - spare), jnp.float32)
        wind_tile = jnp.concatenate([wind_rows[:, end:], filler], axis=1)
        steps = jnp.concatenate([coded(moved[:, :end], inverse), wind_rows[:, :end]], axis=0)
        outs[step][:, :end] = as_int16(steps)
        outs[step][:, end:] = as_int16(jnp.concatenate([tile, wind_tile], axis=0))


def advect(tracer, east_wind, north_wind, ring):
    levels, rows, lons = tracer.shape
    lat_count = lax.axis_size("lat")
    width = (lons - 1) // LANES * LANES + LANES
    padded_rows = -(-(rows + 2) // 16) * 16
    held = pltpu.VMEM((levels, rows, lons), jnp.bfloat16)
    result = pl.pallas_call(
        functools.partial(advect_kernel, ring, lat_count),
        out_shape=[jax.ShapeDtypeStruct((padded_rows, width), jnp.int16)] * levels
        + [jax.ShapeDtypeStruct((lat_count * levels, 1, lons), jnp.float32)],
        in_specs=[HBM_SPEC] * 3,
        out_specs=[VMEM_SPEC] * (levels + 1),
        scratch_shapes=[held, held, held, pltpu.SemaphoreType.DMA((levels, 3))],
        compiler_params=pltpu.CompilerParams(vmem_limit_bytes=VMEM_BYTES),
        cost_estimate=pl.CostEstimate(
            flops=20 * levels * rows * lons, bytes_accessed=8 * levels * rows * lons, transcendentals=0
        ),
    )(tracer, east_wind, north_wind)
    return list(result[:levels]), result[levels]


def fourier_kernel(ring, lat_count, pieces, *rest):
    grids, (edge_ref, *tables_hbm, wave_ref, keep_ref, sine_ref) = rest[:pieces], rest[pieces : pieces + 9]
    outs, rest = rest[pieces + 9 :][:lat_count], rest[pieces + 9 + lat_count :]
    tables, place_ref, (field, sems) = rest[:4], rest[4], rest[5:]
    _, rows, width = field.shape
    lons = tables[0].shape[1]
    share = pieces // 4
    copies = []
    for kind, target in enumerate((*tables, place_ref)):
        copies.append(pltpu.make_async_copy(tables_hbm[kind], target, sems.at[kind]))
        copies[-1].start()

    end = width - LANES
    spare = lons - end
    lane = lax.broadcasted_iota(jnp.int32, (rows, LANES), 1)
    winds = (lane == spare + 3) | (lane == spare + 4)
    lat_index = lax.axis_index("lat")
    for piece in range(pieces):
        spot = partner(*ring, piece)
        values = from_int16(grids[piece][...])
        tile = values[:rows, end:]
        scale = scale_of(tile[:, spare : spare + 1])
        field[spot, :, :end] = values[:rows, :end] * scale
        field[spot, :, end:] = tile * jnp.where(winds, WIND_STEP, scale)
        wind_rows = values[rows : rows + 2, :lons] * WIND_STEP

        @pl.when(lat_index > 0)
        def _():
            above = edge_ref[(lat_index - 1) * pieces + spot]
            field[spot, :1, :lons] += wind_rows[:1] * above

        @pl.when(lat_index < lat_count - 1)
        def _():
            below = edge_ref[(lat_index + 1) * pieces + spot]
            field[spot, rows - 1 :, :lons] -= wind_rows[1:] * below

    for spot in range(pieces):
        tile = field[spot, :, end:]
        before = field[(spot - 1) % pieces, :, end:]
        after = field[(spot + 1) % pieces, :, end:]
        shift = LANES - spare
        gain = pltpu.roll(tile, shift - 3, 1) * pltpu.roll(before, shift - 2, 1)
        loss = pltpu.roll(tile, LANES - 5, 1) * pltpu.roll(after, LANES - 2, 1)
        field[spot, :, end:] = tile - jnp.where(lane == spare - 1, loss, 0.0)
        field[spot, :, :LANES] += jnp.where(lane == 0, gain, 0.0)

    def product(value, table, spot):
        high, low = split_bf16(value)
        width = table.shape[2] // 2
        both = jnp.dot(high, table[spot], preferred_element_type=jnp.float32)
        part = jnp.dot(low, table[spot, :, :width], preferred_element_type=jnp.float32)
        return part + both[:, :width] + both[:, width:]

    sums = [None, None, None]
    for spot in range(share):
        quarters = [field[quarter * share + spot, :, :lons] for quarter in range(4)]
        sum02, dif02 = quarters[0] + quarters[2], quarters[0] - quarters[2]
        sum13, dif13 = quarters[1] + quarters[3], quarters[1] - quarters[3]
        parts = []
        for kind, value in enumerate((sum02 + sum13, sum02 - sum13, dif02, dif13)):
            if spot == 0:
                copies[kind].wait()
            parts.append(product(value, tables[kind], spot))
        parts = [parts[0], parts[1], parts[2] + parts[3]]
        sums = [part if total is None else total + part for total, part in zip(sums, parts)]
    copies[4].wait()
    placed = []
    for part in range(2):
        columns = []
        for total in sums:
            half = total.shape[1] // 2
            columns.append(total[:, part * half : (part + 1) * half])
        high, low = split_bf16(jnp.concatenate(columns, axis=1))
        value = jnp.dot(high, place_ref[...], preferred_element_type=jnp.float32)
        value += jnp.dot(low, place_ref[...], preferred_element_type=jnp.float32)
        kept = jnp.where(wave_ref[...] < keep_ref[...], value * sine_ref[...], 0.0)
        code = scale_code(jnp.max(jnp.abs(kept), axis=0, keepdims=True))
        steps = coded(kept, 1.0 / scale_of(code))
        codes = jnp.broadcast_to(code, (outs[0].shape[0] - rows, code.shape[1]))
        placed.append(as_int16(jnp.concatenate([steps, codes], axis=0)))
    for target in range(lat_count):
        for part in range(2):
            cols = slice(target * LANES, (target + 1) * LANES)
            outs[target][:, part * LANES : (part + 1) * LANES] = placed[part][:, cols]


def fourier(grids, edges, ring, places, wave_row, keep_col, sine_col, lat_count):
    pieces = len(grids)
    rows = keep_col.shape[0]
    width = grids[0].shape[1]
    padded_rows = -(-(rows + 1) // 16) * 16
    tables = [table_bf16(table) for table in fourier_tables(pieces)]
    return pl.pallas_call(
        functools.partial(fourier_kernel, ring, lat_count, pieces),
        out_shape=[jax.ShapeDtypeStruct((padded_rows, 2 * LANES), jnp.int16)] * lat_count,
        in_specs=[VMEM_SPEC] * (pieces + 1) + [HBM_SPEC] * 5 + [VMEM_SPEC] * 3,
        out_specs=[VMEM_SPEC] * lat_count,
        scratch_shapes=[pltpu.VMEM(table.shape, jnp.bfloat16) for table in tables]
        + [pltpu.VMEM(places.shape, jnp.bfloat16)]
        + [pltpu.VMEM((pieces, rows, width), jnp.float32), pltpu.SemaphoreType.DMA((5,))],
        compiler_params=pltpu.CompilerParams(vmem_limit_bytes=VMEM_BYTES),
        cost_estimate=pl.CostEstimate(
            flops=3 * rows * NLON * M, bytes_accessed=6 * 2**20, transcendentals=0
        ),
    )(*grids, edges, *tables, places, wave_row, keep_col, sine_col)


def places_kernel(
    slot_ref, keep_ref, sine_ref, spot_ref,
    place_ref, wave_ref, mine_ref, back_ref, keep_col, sine_col, sorted_rows,
):
    groups, _, rows = sine_ref.shape
    lat_index = lax.axis_index("lat")
    slots = slot_ref.shape[1] // groups
    paired = (slots + 1) // 2
    shape = (LANES, LANES)
    down = lax.broadcasted_iota(jnp.int32, shape, 0)
    across = lax.broadcasted_iota(jnp.int32, shape, 1)
    filler = jnp.full((1, LANES - slots), 2.0 * M, jnp.float32)
    for group in range(groups):
        row = slot_ref[:, group * slots : (group + 1) * slots].astype(jnp.float32)
        row = jnp.broadcast_to(jnp.concatenate([row, filler], axis=1), shape)
        column = jnp.sum(jnp.where(down == across, row, 0.0), axis=1, keepdims=True)
        ahead = (row < column) | ((row == column) & (across < down))
        rank = jnp.sum(jnp.where(ahead, 1.0, 0.0), axis=1, keepdims=True)
        place = jnp.where(rank < paired, rank, SIDE + slots - 1.0 - rank)
        place = jnp.where(rank < slots, place, -1.0)
        hot = jnp.where(place == across.astype(jnp.float32), 1.0, 0.0)
        filled = jnp.sum(hot, axis=0, keepdims=True)
        values = jnp.sum(hot * column, axis=0, keepdims=True)
        values = jnp.where(filled > 0.5, values, 2.0 * M)
        sorted_rows[group] = jnp.broadcast_to(values, sorted_rows.shape[1:])

        @pl.when(group == lat_index)
        def _():
            mine_ref[...] = values
            back_ref[...] = hot.astype(jnp.bfloat16)

    spots = jnp.broadcast_to(spot_ref[...], (spot_ref.shape[0], LANES))
    for step in range(groups):
        row = sorted_rows[partner(("lat",), (groups,), step), :1]
        cols = slice(step * LANES, (step + 1) * LANES)
        wave_ref[:, cols] = row
        place_ref[:, cols] = jnp.where(spots == row, 1.0, 0.0).astype(jnp.bfloat16)

    shape = (rows, rows)
    same = lax.broadcasted_iota(jnp.int32, shape, 0) == lax.broadcasted_iota(jnp.int32, shape, 1)
    kept = jnp.broadcast_to(keep_ref[...].astype(jnp.float32), shape)
    keep_col[...] = jnp.sum(jnp.where(same, kept, 0.0), axis=1, keepdims=True)
    sine = jnp.broadcast_to(sine_ref[lat_index], shape)
    sine_col[...] = jnp.sum(jnp.where(same, sine, 0.0), axis=1, keepdims=True)


def prepare_places(slot_wave, keep_m, groups):
    rows = keep_m.shape[0]
    sines = np.sin(math.pi / NLAT * (np.arange(NLAT) + 0.5)) * math.sqrt(2.0 / NLAT)
    spots = column_waves()
    width = groups * LANES
    return pl.pallas_call(
        places_kernel,
        out_shape=[
            jax.ShapeDtypeStruct((spots.shape[0], width), jnp.bfloat16),
            jax.ShapeDtypeStruct((1, width), jnp.float32),
            jax.ShapeDtypeStruct((1, LANES), jnp.float32),
            jax.ShapeDtypeStruct((LANES, LANES), jnp.bfloat16),
            jax.ShapeDtypeStruct((rows, 1), jnp.float32),
            jax.ShapeDtypeStruct((rows, 1), jnp.float32),
        ],
        in_specs=[VMEM_SPEC] * 4,
        out_specs=[VMEM_SPEC] * 6,
        scratch_shapes=[pltpu.VMEM((groups, 8, LANES), jnp.float32)],
        compiler_params=pltpu.CompilerParams(vmem_limit_bytes=VMEM_BYTES),
    )(
        slot_wave[None], keep_m[None],
        sines.reshape(groups, 1, rows).astype(np.float32), spots,
    )


def lane_pairs(row):
    lane = lax.broadcasted_iota(jnp.int32, row.shape, 1)
    other = pltpu.roll(row, SIDE, 1)
    return jnp.where(lane < SIDE, row, other), jnp.where(lane < SIDE, other, row)


def block_count(wave):
    return jnp.floor((jnp.maximum(M - wave, 0.0) + (BLOCK - 1)) * (1.0 / BLOCK))


def sweep_kernel(
    mine_ref, lat_ref, term_ref, beta_ref, scale_ref, growth_ref, start_ref, state_ref, values_ref
):
    pair = lane_pairs(jnp.broadcast_to(mine_ref[...], (8, LANES)))
    one, two = pair[0][:1], pair[1][:1]
    blocks = growth_ref.shape[0]
    turn = block_count(one)
    block = lax.broadcasted_iota(jnp.int32, (blocks, LANES), 0).astype(jnp.float32)
    second = block >= turn
    wave = jnp.where(second, two, one)
    limit = M - wave
    wave = jnp.minimum(wave, M - 1.0)
    first = (block - jnp.where(second, turn, 0.0)) * BLOCK

    scale = jnp.ones((blocks, LANES), jnp.float32)
    for index in range(BLOCK + 1):
        order = first + index
        degree = wave + order
        square = 4.0 * degree * degree - 1.0
        spread = 4.0 * order * (degree + wave)
        if index > 0:
            scale = scale * jnp.sqrt(square / spread)
        if index < BLOCK:
            beta_ref[pl.ds(index, blocks, stride=BLOCK)] = spread / jnp.maximum(square, 1.0)
            scale_ref[pl.ds(index, blocks, stride=BLOCK)] = jnp.where(order < limit, scale, 0.0)
    growth_ref[...] = scale

    for kind, wave in enumerate((one, two)):
        wave = jnp.minimum(wave, M - 1.0)
        counter = lax.broadcasted_iota(jnp.int32, term_ref.shape, 0).astype(jnp.float32)
        norm = jnp.sum(jnp.where(counter <= wave, term_ref[...], 0.0), axis=0, keepdims=True)
        coarse = lat_ref[1] * wave
        whole = jnp.floor(coarse)
        start_ref[2 * kind] = jnp.exp2(
            (coarse - whole) + lat_ref[2] * wave + 0.5 * (norm - 1.0)
        )
        start_ref[2 * kind + 1] = whole

    state_ref[0] = jnp.zeros_like(state_ref[0])
    state_ref[1] = start_ref[0]
    state_ref[2] = start_ref[1]
    points = lat_ref.shape[1]

    def step(block, carry):
        first = 0
        for chunk in (points // 16 * 8, points - points // 16 * 8):
            rows = slice(first, first + chunk)

            def keep(order, value):
                values_ref[block, order, rows] = value

            sweep_block(block, turn, rows, lat_ref, beta_ref, growth_ref, start_ref, state_ref, keep)
            first += chunk
        return carry

    total = jnp.max(turn + block_count(two)).astype(jnp.int32)
    lax.fori_loop(0, jnp.minimum(total, HELD), step, 0)


def sweep_block(block, turn, rows, lat_ref, beta_ref, growth_ref, start_ref, state_ref, use):
    base = pl.multiple_of(block * BLOCK, BLOCK)
    begins = block.astype(jnp.float32) == turn
    grow = growth_ref[pl.ds(block, 1)]
    cosine = lat_ref[0, rows]
    height = jnp.where(begins, start_ref[3, rows], state_ref[2, rows])
    factor = jnp.exp2(height)
    old = jnp.where(begins, 0.0, state_ref[0, rows])
    new = jnp.where(begins, start_ref[2, rows], state_ref[1, rows])
    for order in range(BLOCK):
        use(order, new * factor)
        beta = beta_ref[pl.ds(base + order, 1)]
        old, new = new, cosine * new - beta * old
    biggest = jnp.maximum(jnp.abs(old), jnp.abs(new)) * grow
    shift = jnp.floor(jnp.log(biggest) * (1.0 / math.log(2.0)))
    factor = grow * jnp.exp2(-shift)
    state_ref[0, rows] = old * factor
    state_ref[1, rows] = new * factor
    state_ref[2, rows] = height + shift


def prepare_recurrence(mine, pieces):
    latitudes = latitude_table()
    points = latitudes.shape[1]
    blocks = 2 * -(-M // BLOCK)
    counter = np.arange(M)
    terms = np.log1p(0.5 / np.maximum(counter, 1)) * (counter > 0) / math.log(2.0)
    terms = np.broadcast_to(terms[:, None], (M, LANES)).astype(np.float32)
    orders = jax.ShapeDtypeStruct((blocks * BLOCK, LANES), jnp.float32)
    return pl.pallas_call(
        sweep_kernel,
        out_shape=[
            orders,
            orders,
            jax.ShapeDtypeStruct((blocks, LANES), jnp.float32),
            jax.ShapeDtypeStruct((4, points, LANES), jnp.float32),
            jax.ShapeDtypeStruct((3, points, LANES), jnp.float32),
            jax.ShapeDtypeStruct((HELD, BLOCK, points, LANES), jnp.float32),
        ],
        in_specs=[VMEM_SPEC] * 3,
        out_specs=[VMEM_SPEC] * 6,
        compiler_params=pltpu.CompilerParams(vmem_limit_bytes=late_bytes(pieces)),
    )(mine, latitudes, terms)


def resampled(first, fields, table, total):
    for piece, field in enumerate(fields):
        values = from_int16(field[...])
        values = values * scale_of(values[field.shape[0] - 1 :])
        high, low = split_bf16(values)
        spot = partner(("lat",), table.shape[:1], first + piece)
        both = jnp.concatenate([high, low], axis=1)
        part = jnp.dot(table[spot, 0], both, preferred_element_type=jnp.float32)
        part = part[:, : high.shape[1]] + part[:, high.shape[1] :]
        part += jnp.dot(table[spot, 1], high, preferred_element_type=jnp.float32)
        total = part if total is None else total + part
    return total


def resample_kernel(table_ref, *rest):
    rest[-1][...] = resampled(0, rest[:-1], table_ref, None)


def late_bytes(pieces):
    return LATE_BYTES if pieces <= 4 else VMEM_BYTES


def resample(fields, table):
    count, _, height, _ = table.shape
    span = fields[0].shape[1]
    return pl.pallas_call(
        resample_kernel,
        out_shape=jax.ShapeDtypeStruct((height, span), jnp.float32),
        in_specs=[VMEM_SPEC] * (1 + len(fields)),
        out_specs=VMEM_SPEC,
        compiler_params=pltpu.CompilerParams(vmem_limit_bytes=late_bytes(count)),
        cost_estimate=pl.CostEstimate(
            flops=6 * height * span * NLAT // count * len(fields), bytes_accessed=4 * 2**20, transcendentals=0
        ),
    )(table, *fields)


def legendre_kernel(early, *rest):
    table, lat_ref, beta_ref, scale_ref, growth_ref, start_ref, left_ref, values_ref = rest[:8]
    total_ref, mine_ref, back_ref = rest[8:11]
    fields, (out_ref, weights, state_ref, sums, result, final) = rest[11:-6], rest[-6:]
    points = lat_ref.shape[1]
    slots = out_ref.shape[0]
    mine = mine_ref[...]
    odd = mine - 2.0 * jnp.floor(mine * 0.5) > 0.5
    pair = lane_pairs(jnp.broadcast_to(mine, (8, LANES)))
    turn = block_count(pair[0][:1])
    block_total = jnp.max(turn + block_count(pair[1][:1])).astype(jnp.int32)

    total = resampled(early, fields, table, total_ref[...])
    totals = [total[2 * points * kind : 2 * points * (kind + 1)] for kind in range(4)]
    left = lax.broadcasted_iota(jnp.int32, (points, LANES), 1) < SIDE
    for parity in range(2):
        for comp in range(2):
            cols = slice(comp * LANES, (comp + 1) * LANES)
            value = jnp.where(odd, totals[2 + parity][:, cols], totals[parity][:, cols])
            top, bottom = value[:points], value[points:]
            kind = 2 * parity + comp
            weights[0, kind] = jnp.where(left, top, pltpu.roll(bottom, SIDE, 1))
            weights[1, kind] = jnp.where(left, pltpu.roll(top, SIDE, 1), bottom)
    result[...] = jnp.zeros_like(result)
    state_ref[...] = left_ref[...]

    def reduced(block):
        base = pl.multiple_of(block * BLOCK, BLOCK)
        for comp in range(2):
            total = sums[pl.ds(comp * 8, BLOCK, stride=16)]
            for lane in range(1, 8):
                total += sums[pl.ds(comp * 8 + lane, BLOCK, stride=16)]
            total = total * scale_ref[pl.ds(base, BLOCK)]
            result[comp, pl.ds(base, BLOCK)] = total + pltpu.roll(total, SIDE, 1)

    def held_step(block, carry):
        second = block.astype(jnp.float32) >= turn
        for parity in range(2):
            scaled = [
                jnp.where(second, weights[1, 2 * parity + comp], weights[0, 2 * parity + comp])
                for comp in range(2)
            ]
            for order in range(parity, BLOCK, 2):
                value = values_ref[block, order]
                for comp in range(2):
                    product = (value * scaled[comp]).reshape(points // 8, 8, LANES)
                    sums[pl.ds((order * 2 + comp) * 8, 8)] = product.sum(axis=0)
        reduced(block)
        return carry

    def step(block, carry):
        second = block.astype(jnp.float32) >= turn
        first = 0
        for chunk in CHUNKS:
            rows = slice(first, first + chunk)
            scaled = [jnp.where(second, weights[1, k, rows], weights[0, k, rows]) for k in range(4)]

            def add(order, value):
                for comp in range(2):
                    product = value * scaled[2 * (order % 2) + comp]
                    partial = product.reshape(chunk // 8, 8, LANES).sum(axis=0)
                    place = pl.ds((order * 2 + comp) * 8, 8)
                    if first == 0:
                        sums[place] = partial
                    else:
                        sums[place] += partial

            sweep_block(block, turn, rows, lat_ref, beta_ref, growth_ref, start_ref, state_ref, add)
            first += chunk
        reduced(block)
        return carry

    lax.fori_loop(0, jnp.minimum(block_total, HELD), held_step, 0)
    lax.fori_loop(HELD, block_total, step, 0)

    left = lax.broadcasted_iota(jnp.int32, (BLOCK, LANES), 1) < SIDE
    spots = -(-M // BLOCK)
    chosen = [jnp.broadcast_to(turn, (8, LANES)) == value for value in range(spots + 1)]
    chosen = [jnp.concatenate([mask] * (BLOCK // 8), axis=0) for mask in chosen]
    for place in range(spots):
        rows = slice(place * BLOCK, (place + 1) * BLOCK)
        for comp in range(2):
            early_part = jnp.where(turn > place, result[comp, rows], 0.0)
            later = jnp.zeros((BLOCK, LANES), jnp.float32)
            for value in range(spots + 1):
                base = (place + value) * BLOCK
                if base < result.shape[1]:
                    later = jnp.where(chosen[value], result[comp, base : base + BLOCK], later)
            final[comp, rows] = jnp.where(left, early_part, later)
    back = back_ref[...]
    dims = (((1,), (1,)), ((), ()))
    for comp in range(2):
        high, low = split_bf16(final[comp])
        value = lax.dot_general(back, high, dims, preferred_element_type=jnp.float32)
        value += lax.dot_general(back, low, dims, preferred_element_type=jnp.float32)
        out_ref[:, comp, :] = value[:slots, :M]


def resample_pieces(pieces, rows, padded_rows):
    full = resample_table()
    table = full.reshape(full.shape[0], pieces, rows).transpose(1, 0, 2)
    table = table_bf16(np.pad(table, ((0, 0), (0, 0), (0, padded_rows - rows))))
    return table.reshape(pieces, full.shape[0], 2, padded_rows).transpose(0, 2, 1, 3)


def legendre(fields, mine, back, prepared, rows, slots):
    pieces = len(fields)
    early = pieces // 2
    latitudes = latitude_table()
    points = latitudes.shape[1]
    table = jnp.asarray(resample_pieces(pieces, rows, fields[0].shape[0]))
    total = resample(fields[:early], table)
    block_rows = -(-M // BLOCK) * BLOCK
    return pl.pallas_call(
        functools.partial(legendre_kernel, early),
        out_shape=jax.ShapeDtypeStruct((slots, 2, M), jnp.float32),
        in_specs=[VMEM_SPEC] * (11 + pieces - early),
        out_specs=VMEM_SPEC,
        scratch_shapes=[
            pltpu.VMEM((2, 4, points, LANES), jnp.float32),
            pltpu.VMEM((3, points, LANES), jnp.float32),
            pltpu.VMEM((BLOCK * 16, LANES), jnp.float32),
            pltpu.VMEM((2, 2 * block_rows, LANES), jnp.float32),
            pltpu.VMEM((2, block_rows, LANES), jnp.float32),
        ],
        compiler_params=pltpu.CompilerParams(vmem_limit_bytes=late_bytes(pieces)),
        cost_estimate=pl.CostEstimate(
            flops=7 * points * LANES * M, bytes_accessed=6 * 2**20, transcendentals=0
        ),
    )(table, latitudes, *prepared, total, mine, back, *fields[early:])


def shards(tracer, wind_east, wind_north, keep_m, slot_wave):
    rows = tracer.shape[1]
    lat_count = lax.axis_size("lat")
    slots = slot_wave.shape[0] // lat_count
    axes = ("lev", "fld")
    ring = (axes, tuple(lax.axis_size(axis) for axis in axes))

    blocks, edges = advect(tracer, wind_east, wind_north, ring)
    blocks, slot_wave, keep_m = lax.optimization_barrier((blocks, slot_wave, keep_m))
    grids = exchange(blocks, axes)
    edges = lax.all_to_all(edges, ("lat", *axes), split_axis=0, concat_axis=0, tiled=True)
    places, wave_row, mine, back, keep_col, sine_col = prepare_places(slot_wave, keep_m, lat_count)
    waved = fourier(grids, edges, ring, places, wave_row, keep_col, sine_col, lat_count)
    waved, mine = lax.optimization_barrier((list(waved), mine))
    fields = exchange(waved, "lat")
    prepared = prepare_recurrence(mine, lat_count)
    return legendre(fields, mine, back, prepared, rows, slots)[None]


def solution(mesh):
    return jax.shard_map(
        shards,
        mesh=mesh,
        in_specs=(
            P("member", "lat", ("lev", "fld")),
            P("member", "lat", ("lev", "fld")),
            P("member", "lat", ("lev", "fld")),
            P("lat"),
            P(),
        ),
        out_specs=P(("member", "lev", "fld"), "lat", None, None),
        check_vma=False,
    )
```

```python
import functools
import math

import jax
import jax.numpy as jnp
import numpy as np
from jax import lax
from jax.experimental import pallas as pl
from jax.experimental.pallas import tpu as pltpu
from jax.sharding import PartitionSpec as P

M = 400
NLAT = 800
NLON = 1600
LANES = 128
BLOCK = 32
CHUNKS = (40, 32, 32)
HELD = -(-M // BLOCK)
SIDE = LANES // 2
TOP = 32767.0
WIND_STEP = 1.5 / TOP
VMEM_BYTES = 60 * 2**20
LATE_BYTES = 16 * 2**20
VMEM_SPEC = pl.BlockSpec(memory_space=pltpu.VMEM)
SMEM_SPEC = pl.BlockSpec(memory_space=pltpu.SMEM)
HBM_SPEC = pl.BlockSpec(memory_space=pltpu.HBM)


def split_bf16(values):
    high = values.astype(jnp.bfloat16)
    low = (values - high.astype(jnp.float32)).astype(jnp.bfloat16)
    return high, low


def table_bf16(table):
    high = table.astype(jnp.bfloat16)
    low = (table - high.astype(np.float64)).astype(jnp.bfloat16)
    return np.concatenate([high, low], axis=-1)


def fourier_tables(pieces):
    quarter = NLON // 4
    spots = np.arange(quarter)[:, None]
    factor = 1.0 / math.sqrt(NLON)

    def parts(waves):
        angles = 2.0 * math.pi / NLON * (spots * waves[None, :] % NLON)
        return factor * np.cos(angles), factor * np.sin(angles)

    def shaped(columns):
        pad = [(0, 0), (0, -columns[0].shape[1] % LANES)]
        table = np.concatenate([np.pad(part, pad) for part in columns], axis=1)
        return table.reshape(share, quarter // share, -1)

    share = pieces // 4
    tables = []
    for first in (0, 2):
        cosine, sine = parts(np.arange(first, M, 4))
        tables.append(shaped([cosine, -sine]))
    waves = np.arange(1, M, 2)
    sign = np.where(waves % 4 == 1, 1.0, -1.0)[None, :]
    cosine, sine = parts(waves)
    return [*tables, shaped([cosine, -sine]), shaped([-sign * sine, -sign * cosine])]


def column_waves():
    columns = []
    for waves in (np.arange(0, M, 4), np.arange(2, M, 4), np.arange(1, M, 2)):
        columns.append(np.pad(waves, (0, -len(waves) % LANES), constant_values=-1))
    return np.concatenate(columns).astype(np.float32)[:, None]


def resample_table():
    half = M // 2
    coarse = math.pi / M * (np.arange(M) + 0.5)
    fine = math.pi / NLAT * (np.arange(NLAT) + 0.5)
    waves = np.arange(M)
    weight = np.where(waves == 0, 1.0, 2.0) / M
    even = (np.cos(np.outer(coarse, waves)) * weight) @ np.cos(np.outer(waves, fine))
    odd = (np.sin(np.outer(coarse, waves)) * weight) @ np.sin(np.outer(waves, fine))
    rows = []
    for full in (even, odd):
        for sign in (1.0, -1.0):
            folded = (full[:half] + sign * full[::-1][:half]).reshape(2, half // 2, NLAT)
            rows.append(np.pad(folded, ((0, 0), (0, -half // 2 % 8), (0, 0))).reshape(-1, NLAT))
    return np.concatenate(rows, axis=0)


def latitude_table():
    half = M // 2
    angles = math.pi / M * (np.arange(half) + 0.5)
    log_sine = np.log2(np.sin(angles))
    coarse = np.round(log_sine * 1024.0) / 1024.0
    rows = np.stack([2.0 * np.cos(angles), coarse, log_sine - coarse]).reshape(3, 2, half // 2)
    rows = np.pad(rows, ((0, 0), (0, 0), (0, -half // 2 % 8)))
    return np.repeat(rows.transpose(0, 2, 1), SIDE, axis=2).astype(np.float32)


def scale_code(biggest):
    wanted = jnp.maximum(biggest, 1e-30) * (1.0 / TOP)
    exponent = jnp.floor(jnp.log(wanted) * (1.0 / math.log(2.0)))
    return exponent * 128.0 + jnp.ceil((wanted * jnp.exp2(-exponent) - 1.0) * 128.0)


def scale_of(code):
    exponent = jnp.floor(code * (1.0 / 128.0))
    rest = code - 128.0 * exponent
    return jnp.exp2(exponent) * (1.0 + rest * (1.0 / 128.0))


def coded(values, inverse):
    return jnp.floor(values * inverse + 0.5)


def as_int16(values):
    return values.astype(jnp.int32).astype(jnp.int16)


def from_int16(codes):
    return codes.astype(jnp.int32).astype(jnp.float32)


def partner(axes, sizes, step):
    count = math.prod(sizes)
    if count != 4:
        return step
    index = lax.axis_index(axes[0])
    for axis, size in zip(axes[1:], sizes[1:]):
        index = index * size + lax.axis_index(axis)
    return index ^ step


def exchange(blocks, axis):
    count = len(blocks)
    if count != 4:
        return list(lax.all_to_all(jnp.stack(blocks), axis, split_axis=0, concat_axis=0, tiled=True))
    pairs = [[(i, i ^ step) for i in range(count)] for step in range(count)]
    return [blocks[0]] + [lax.ppermute(blocks[step], axis, pairs[step]) for step in range(1, count)]


def advect_kernel(ring, lat_count, tracer_hbm, east_hbm, north_hbm, *rest):
    levels, rows, lons = tracer_hbm.shape
    outs, (edge_ref, tracer, east_wind, north_wind, sems) = rest[:levels], rest[levels:]
    chosen = [partner(*ring, step) for step in range(levels)]
    copies = []
    for step, level in enumerate(chosen):
        copies.append(
            [
                pltpu.make_async_copy(source.at[level], target.at[step], sems.at[step, kind])
                for kind, (source, target) in enumerate(
                    ((tracer_hbm, tracer), (east_hbm, east_wind), (north_hbm, north_wind))
                )
            ]
        )
        for copy in copies[-1]:
            copy.start()
    padded_rows = outs[0].shape[0]
    end = (lons - 1) // LANES * LANES
    spare = lons - end
    lane = lax.broadcasted_iota(jnp.int32, (rows, LANES), 1)
    lat_index = lax.axis_index("lat")
    edge_ref[...] = jnp.zeros_like(edge_ref)
    for step, level in enumerate(chosen):
        for copy in copies[step]:
            copy.wait()
        field = tracer[step].astype(jnp.float32)

        @pl.when(lat_index < lat_count - 1)
        def _():
            edge_ref[(lat_index + 1) * levels + level] = field[rows - 1 :]

        @pl.when(lat_index > 0)
        def _():
            edge_ref[(lat_index - 1) * levels + level] = field[:1]

        blank = jnp.zeros((rows, 1), jnp.float32)
        west = jnp.concatenate([blank, field[:, :-1]], axis=1)
        east = jnp.concatenate([field[:, 1:], blank], axis=1)
        blank = jnp.zeros((1, lons), jnp.float32)
        north = jnp.concatenate([blank, field[:-1]], axis=0)
        south = jnp.concatenate([field[1:], blank], axis=0)
        eastward = 0.5 * east_wind[step].astype(jnp.float32)
        northward = 0.5 * north_wind[step].astype(jnp.float32)
        moved = field - eastward * (east - west) - northward * (south - north)
        first, last = field[:, :1], field[:, lons - 1 :]
        biggest = jnp.max(jnp.abs(moved), axis=1, keepdims=True)
        biggest = jnp.maximum(biggest, jnp.maximum(jnp.abs(first), jnp.abs(last)))
        code = scale_code(biggest)
        inverse = 1.0 / scale_of(code)
        filler = jnp.zeros((rows, LANES - spare), jnp.float32)
        tile = jnp.concatenate([moved[:, end:], filler], axis=1)
        tile = jnp.where(lane == spare + 1, first, jnp.where(lane == spare + 2, last, tile))
        tile = coded(tile, inverse)
        tile = jnp.where(lane == spare, code, tile)
        winds = jnp.where(lane == spare + 3, eastward[:, :1], eastward[:, lons - 1 :])
        winds = coded(winds, 1.0 / WIND_STEP)
        tile = jnp.where((lane == spare + 3) | (lane == spare + 4), winds, tile)
        wind_rows = jnp.concatenate([northward[:1], northward[rows - 1 :]], axis=0)
        wind_rows = coded(wind_rows, 1.0 / WIND_STEP)
        blank = jnp.zeros((padded_rows - rows - 2, lons), jnp.float32)
        wind_rows = jnp.concatenate([wind_rows, blank], axis=0)
        filler = jnp.zeros((padded_rows - rows, LANES - spare), jnp.float32)
        wind_tile = jnp.concatenate([wind_rows[:, end:], filler], axis=1)
        steps = jnp.concatenate([coded(moved[:, :end], inverse), wind_rows[:, :end]], axis=0)
        outs[step][:, :end] = as_int16(steps)
        outs[step][:, end:] = as_int16(jnp.concatenate([tile, wind_tile], axis=0))


def advect(tracer, east_wind, north_wind, ring):
    levels, rows, lons = tracer.shape
    lat_count = lax.axis_size("lat")
    width = (lons - 1) // LANES * LANES + LANES
    padded_rows = -(-(rows + 2) // 16) * 16
    held = pltpu.VMEM((levels, rows, lons), jnp.bfloat16)
    result = pl.pallas_call(
        functools.partial(advect_kernel, ring, lat_count),
        out_shape=[jax.ShapeDtypeStruct((padded_rows, width), jnp.int16)] * levels
        + [jax.ShapeDtypeStruct((lat_count * levels, 1, lons), jnp.float32)],
        in_specs=[HBM_SPEC] * 3,
        out_specs=[VMEM_SPEC] * (levels + 1),
        scratch_shapes=[held, held, held, pltpu.SemaphoreType.DMA((levels, 3))],
        compiler_params=pltpu.CompilerParams(vmem_limit_bytes=VMEM_BYTES),
        cost_estimate=pl.CostEstimate(
            flops=20 * levels * rows * lons, bytes_accessed=8 * levels * rows * lons, transcendentals=0
        ),
    )(tracer, east_wind, north_wind)
    return list(result[:levels]), result[levels]


def fourier_kernel(ring, lat_count, pieces, *rest):
    grids, (edge_ref, *tables_hbm, wave_ref, keep_ref, sine_ref) = rest[:pieces], rest[pieces : pieces + 9]
    outs, rest = rest[pieces + 9 :][:lat_count], rest[pieces + 9 + lat_count :]
    tables, place_ref, (field, sems) = rest[:4], rest[4], rest[5:]
    _, rows, width = field.shape
    lons = tables[0].shape[1]
    share = pieces // 4
    copies = []
    for kind, target in enumerate((*tables, place_ref)):
        copies.append(pltpu.make_async_copy(tables_hbm[kind], target, sems.at[kind]))
        copies[-1].start()

    end = width - LANES
    spare = lons - end
    lane = lax.broadcasted_iota(jnp.int32, (rows, LANES), 1)
    winds = (lane == spare + 3) | (lane == spare + 4)
    lat_index = lax.axis_index("lat")
    for piece in range(pieces):
        spot = partner(*ring, piece)
        values = from_int16(grids[piece][...])
        tile = values[:rows, end:]
        scale = scale_of(tile[:, spare : spare + 1])
        field[spot, :, :end] = values[:rows, :end] * scale
        field[spot, :, end:] = tile * jnp.where(winds, WIND_STEP, scale)
        wind_rows = values[rows : rows + 2, :lons] * WIND_STEP

        @pl.when(lat_index > 0)
        def _():
            above = edge_ref[(lat_index - 1) * pieces + spot]
            field[spot, :1, :lons] += wind_rows[:1] * above

        @pl.when(lat_index < lat_count - 1)
        def _():
            below = edge_ref[(lat_index + 1) * pieces + spot]
            field[spot, rows - 1 :, :lons] -= wind_rows[1:] * below

    for spot in range(pieces):
        tile = field[spot, :, end:]
        before = field[(spot - 1) % pieces, :, end:]
        after = field[(spot + 1) % pieces, :, end:]
        shift = LANES - spare
        gain = pltpu.roll(tile, shift - 3, 1) * pltpu.roll(before, shift - 2, 1)
        loss = pltpu.roll(tile, LANES - 5, 1) * pltpu.roll(after, LANES - 2, 1)
        field[spot, :, end:] = tile - jnp.where(lane == spare - 1, loss, 0.0)
        field[spot, :, :LANES] += jnp.where(lane == 0, gain, 0.0)

    def product(value, table, spot):
        high, low = split_bf16(value)
        width = table.shape[2] // 2
        both = jnp.dot(high, table[spot], preferred_element_type=jnp.float32)
        part = jnp.dot(low, table[spot, :, :width], preferred_element_type=jnp.float32)
        return part + both[:, :width] + both[:, width:]

    sums = [None, None, None]
    for spot in range(share):
        quarters = [field[quarter * share + spot, :, :lons] for quarter in range(4)]
        sum02, dif02 = quarters[0] + quarters[2], quarters[0] - quarters[2]
        sum13, dif13 = quarters[1] + quarters[3], quarters[1] - quarters[3]
        parts = []
        for kind, value in enumerate((sum02 + sum13, sum02 - sum13, dif02, dif13)):
            if spot == 0:
                copies[kind].wait()
            parts.append(product(value, tables[kind], spot))
        parts = [parts[0], parts[1], parts[2] + parts[3]]
        sums = [part if total is None else total + part for total, part in zip(sums, parts)]
    copies[4].wait()
    placed = []
    for part in range(2):
        columns = []
        for total in sums:
            half = total.shape[1] // 2
            columns.append(total[:, part * half : (part + 1) * half])
        high, low = split_bf16(jnp.concatenate(columns, axis=1))
        value = jnp.dot(high, place_ref[...], preferred_element_type=jnp.float32)
        value += jnp.dot(low, place_ref[...], preferred_element_type=jnp.float32)
        kept = jnp.where(wave_ref[...] < keep_ref[...], value * sine_ref[...], 0.0)
        code = scale_code(jnp.max(jnp.abs(kept), axis=0, keepdims=True))
        steps = coded(kept, 1.0 / scale_of(code))
        codes = jnp.broadcast_to(code, (outs[0].shape[0] - rows, code.shape[1]))
        placed.append(as_int16(jnp.concatenate([steps, codes], axis=0)))
    for target in range(lat_count):
        for part in range(2):
            cols = slice(target * LANES, (target + 1) * LANES)
            outs[target][:, part * LANES : (part + 1) * LANES] = placed[part][:, cols]


def fourier(grids, edges, ring, places, wave_row, keep_col, sine_col, lat_count):
    pieces = len(grids)
    rows = keep_col.shape[0]
    width = grids[0].shape[1]
    padded_rows = -(-(rows + 1) // 16) * 16
    tables = [table_bf16(table) for table in fourier_tables(pieces)]
    return pl.pallas_call(
        functools.partial(fourier_kernel, ring, lat_count, pieces),
        out_shape=[jax.ShapeDtypeStruct((padded_rows, 2 * LANES), jnp.int16)] * lat_count,
        in_specs=[VMEM_SPEC] * (pieces + 1) + [HBM_SPEC] * 5 + [VMEM_SPEC] * 3,
        out_specs=[VMEM_SPEC] * lat_count,
        scratch_shapes=[pltpu.VMEM(table.shape, jnp.bfloat16) for table in tables]
        + [pltpu.VMEM(places.shape, jnp.bfloat16)]
        + [pltpu.VMEM((pieces, rows, width), jnp.float32), pltpu.SemaphoreType.DMA((5,))],
        compiler_params=pltpu.CompilerParams(vmem_limit_bytes=VMEM_BYTES),
        cost_estimate=pl.CostEstimate(
            flops=3 * rows * NLON * M, bytes_accessed=6 * 2**20, transcendentals=0
        ),
    )(*grids, edges, *tables, places, wave_row, keep_col, sine_col)


def places_kernel(
    slot_ref, keep_ref, sine_ref, spot_ref,
    place_ref, wave_ref, mine_ref, back_ref, keep_col, sine_col, sorted_rows,
):
    groups, _, rows = sine_ref.shape
    lat_index = lax.axis_index("lat")
    slots = slot_ref.shape[1] // groups
    paired = (slots + 1) // 2
    shape = (LANES, LANES)
    down = lax.broadcasted_iota(jnp.int32, shape, 0)
    across = lax.broadcasted_iota(jnp.int32, shape, 1)
    filler = jnp.full((1, LANES - slots), 2.0 * M, jnp.float32)
    for group in range(groups):
        row = slot_ref[:, group * slots : (group + 1) * slots].astype(jnp.float32)
        row = jnp.broadcast_to(jnp.concatenate([row, filler], axis=1), shape)
        column = jnp.sum(jnp.where(down == across, row, 0.0), axis=1, keepdims=True)
        ahead = (row < column) | ((row == column) & (across < down))
        rank = jnp.sum(jnp.where(ahead, 1.0, 0.0), axis=1, keepdims=True)
        place = jnp.where(rank < paired, rank, SIDE + slots - 1.0 - rank)
        place = jnp.where(rank < slots, place, -1.0)
        hot = jnp.where(place == across.astype(jnp.float32), 1.0, 0.0)
        filled = jnp.sum(hot, axis=0, keepdims=True)
        values = jnp.sum(hot * column, axis=0, keepdims=True)
        values = jnp.where(filled > 0.5, values, 2.0 * M)
        sorted_rows[group] = jnp.broadcast_to(values, sorted_rows.shape[1:])

        @pl.when(group == lat_index)
        def _():
            mine_ref[...] = values
            back_ref[...] = hot.astype(jnp.bfloat16)

    spots = jnp.broadcast_to(spot_ref[...], (spot_ref.shape[0], LANES))
    for step in range(groups):
        row = sorted_rows[partner(("lat",), (groups,), step), :1]
        cols = slice(step * LANES, (step + 1) * LANES)
        wave_ref[:, cols] = row
        place_ref[:, cols] = jnp.where(spots == row, 1.0, 0.0).astype(jnp.bfloat16)

    shape = (rows, rows)
    same = lax.broadcasted_iota(jnp.int32, shape, 0) == lax.broadcasted_iota(jnp.int32, shape, 1)
    kept = jnp.broadcast_to(keep_ref[...].astype(jnp.float32), shape)
    keep_col[...] = jnp.sum(jnp.where(same, kept, 0.0), axis=1, keepdims=True)
    sine = jnp.broadcast_to(sine_ref[lat_index], shape)
    sine_col[...] = jnp.sum(jnp.where(same, sine, 0.0), axis=1, keepdims=True)


def prepare_places(slot_wave, keep_m, groups):
    rows = keep_m.shape[0]
    sines = np.sin(math.pi / NLAT * (np.arange(NLAT) + 0.5)) * math.sqrt(2.0 / NLAT)
    spots = column_waves()
    width = groups * LANES
    return pl.pallas_call(
        places_kernel,
        out_shape=[
            jax.ShapeDtypeStruct((spots.shape[0], width), jnp.bfloat16),
            jax.ShapeDtypeStruct((1, width), jnp.float32),
            jax.ShapeDtypeStruct((1, LANES), jnp.float32),
            jax.ShapeDtypeStruct((LANES, LANES), jnp.bfloat16),
            jax.ShapeDtypeStruct((rows, 1), jnp.float32),
            jax.ShapeDtypeStruct((rows, 1), jnp.float32),
        ],
        in_specs=[VMEM_SPEC] * 4,
        out_specs=[VMEM_SPEC] * 6,
        scratch_shapes=[pltpu.VMEM((groups, 8, LANES), jnp.float32)],
        compiler_params=pltpu.CompilerParams(vmem_limit_bytes=VMEM_BYTES),
    )(
        slot_wave[None], keep_m[None],
        sines.reshape(groups, 1, rows).astype(np.float32), spots,
    )


def lane_pairs(row):
    lane = lax.broadcasted_iota(jnp.int32, row.shape, 1)
    other = pltpu.roll(row, SIDE, 1)
    return jnp.where(lane < SIDE, row, other), jnp.where(lane < SIDE, other, row)


def block_count(wave):
    return jnp.floor((jnp.maximum(M - wave, 0.0) + (BLOCK - 1)) * (1.0 / BLOCK))


def sweep_kernel(
    mine_ref, lat_ref, term_ref, beta_ref, scale_ref, growth_ref, start_ref, state_ref, values_ref
):
    pair = lane_pairs(jnp.broadcast_to(mine_ref[...], (8, LANES)))
    one, two = pair[0][:1], pair[1][:1]
    blocks = growth_ref.shape[0]
    turn = block_count(one)
    block = lax.broadcasted_iota(jnp.int32, (blocks, LANES), 0).astype(jnp.float32)
    second = block >= turn
    wave = jnp.where(second, two, one)
    limit = M - wave
    wave = jnp.minimum(wave, M - 1.0)
    first = (block - jnp.where(second, turn, 0.0)) * BLOCK

    scale = jnp.ones((blocks, LANES), jnp.float32)
    for index in range(BLOCK + 1):
        order = first + index
        degree = wave + order
        square = 4.0 * degree * degree - 1.0
        spread = 4.0 * order * (degree + wave)
        if index > 0:
            scale = scale * jnp.sqrt(square / spread)
        if index < BLOCK:
            beta_ref[pl.ds(index, blocks, stride=BLOCK)] = spread / jnp.maximum(square, 1.0)
            scale_ref[pl.ds(index, blocks, stride=BLOCK)] = jnp.where(order < limit, scale, 0.0)
    growth_ref[...] = scale

    for kind, wave in enumerate((one, two)):
        wave = jnp.minimum(wave, M - 1.0)
        counter = lax.broadcasted_iota(jnp.int32, term_ref.shape, 0).astype(jnp.float32)
        norm = jnp.sum(jnp.where(counter <= wave, term_ref[...], 0.0), axis=0, keepdims=True)
        coarse = lat_ref[1] * wave
        whole = jnp.floor(coarse)
        start_ref[2 * kind] = jnp.exp2(
            (coarse - whole) + lat_ref[2] * wave + 0.5 * (norm - 1.0)
        )
        start_ref[2 * kind + 1] = whole

    state_ref[0] = jnp.zeros_like(state_ref[0])
    state_ref[1] = start_ref[0]
    state_ref[2] = start_ref[1]
    points = lat_ref.shape[1]

    def step(block, carry):
        first = 0
        for chunk in (points // 16 * 8, points - points // 16 * 8):
            rows = slice(first, first + chunk)

            def keep(order, value):
                values_ref[block, order, rows] = value

            sweep_block(block, turn, rows, lat_ref, beta_ref, growth_ref, start_ref, state_ref, keep)
            first += chunk
        return carry

    total = jnp.max(turn + block_count(two)).astype(jnp.int32)
    lax.fori_loop(0, jnp.minimum(total, HELD), step, 0)


def sweep_block(block, turn, rows, lat_ref, beta_ref, growth_ref, start_ref, state_ref, use):
    base = pl.multiple_of(block * BLOCK, BLOCK)
    begins = block.astype(jnp.float32) == turn
    grow = growth_ref[pl.ds(block, 1)]
    cosine = lat_ref[0, rows]
    height = jnp.where(begins, start_ref[3, rows], state_ref[2, rows])
    factor = jnp.exp2(height)
    old = jnp.where(begins, 0.0, state_ref[0, rows])
    new = jnp.where(begins, start_ref[2, rows], state_ref[1, rows])
    for order in range(BLOCK):
        use(order, new * factor)
        beta = beta_ref[pl.ds(base + order, 1)]
        old, new = new, cosine * new - beta * old
    biggest = jnp.maximum(jnp.abs(old), jnp.abs(new)) * grow
    shift = jnp.floor(jnp.log(biggest) * (1.0 / math.log(2.0)))
    factor = grow * jnp.exp2(-shift)
    state_ref[0, rows] = old * factor
    state_ref[1, rows] = new * factor
    state_ref[2, rows] = height + shift


def prepare_recurrence(mine, pieces):
    latitudes = latitude_table()
    points = latitudes.shape[1]
    blocks = 2 * -(-M // BLOCK)
    counter = np.arange(M)
    terms = np.log1p(0.5 / np.maximum(counter, 1)) * (counter > 0) / math.log(2.0)
    terms = np.broadcast_to(terms[:, None], (M, LANES)).astype(np.float32)
    orders = jax.ShapeDtypeStruct((blocks * BLOCK, LANES), jnp.float32)
    return pl.pallas_call(
        sweep_kernel,
        out_shape=[
            orders,
            orders,
            jax.ShapeDtypeStruct((blocks, LANES), jnp.float32),
            jax.ShapeDtypeStruct((4, points, LANES), jnp.float32),
            jax.ShapeDtypeStruct((3, points, LANES), jnp.float32),
            jax.ShapeDtypeStruct((HELD, BLOCK, points, LANES), jnp.float32),
        ],
        in_specs=[VMEM_SPEC] * 3,
        out_specs=[VMEM_SPEC] * 6,
        compiler_params=pltpu.CompilerParams(vmem_limit_bytes=late_bytes(pieces)),
    )(mine, latitudes, terms)


def resampled(first, fields, table, total):
    for piece, field in enumerate(fields):
        values = from_int16(field[...])
        values = values * scale_of(values[field.shape[0] - 1 :])
        high, low = split_bf16(values)
        spot = partner(("lat",), table.shape[:1], first + piece)
        both = jnp.concatenate([high, low], axis=1)
        part = jnp.dot(table[spot, 0], both, preferred_element_type=jnp.float32)
        part = part[:, : high.shape[1]] + part[:, high.shape[1] :]
        part += jnp.dot(table[spot, 1], high, preferred_element_type=jnp.float32)
        total = part if total is None else total + part
    return total


def resample_kernel(table_ref, *rest):
    rest[-1][...] = resampled(0, rest[:-1], table_ref, None)


def late_bytes(pieces):
    return LATE_BYTES if pieces <= 4 else VMEM_BYTES


def resample(fields, table):
    count, _, height, _ = table.shape
    span = fields[0].shape[1]
    return pl.pallas_call(
        resample_kernel,
        out_shape=jax.ShapeDtypeStruct((height, span), jnp.float32),
        in_specs=[VMEM_SPEC] * (1 + len(fields)),
        out_specs=VMEM_SPEC,
        compiler_params=pltpu.CompilerParams(vmem_limit_bytes=late_bytes(count)),
        cost_estimate=pl.CostEstimate(
            flops=6 * height * span * NLAT // count * len(fields), bytes_accessed=4 * 2**20, transcendentals=0
        ),
    )(table, *fields)


def legendre_kernel(early, *rest):
    table, lat_ref, beta_ref, scale_ref, growth_ref, start_ref, left_ref, values_ref = rest[:8]
    total_ref, mine_ref, back_ref = rest[8:11]
    fields, (out_ref, weights, state_ref, sums, result, final) = rest[11:-6], rest[-6:]
    points = lat_ref.shape[1]
    slots = out_ref.shape[0]
    mine = mine_ref[...]
    odd = mine - 2.0 * jnp.floor(mine * 0.5) > 0.5
    pair = lane_pairs(jnp.broadcast_to(mine, (8, LANES)))
    turn = block_count(pair[0][:1])
    block_total = jnp.max(turn + block_count(pair[1][:1])).astype(jnp.int32)

    total = resampled(early, fields, table, total_ref[...])
    totals = [total[2 * points * kind : 2 * points * (kind + 1)] for kind in range(4)]
    left = lax.broadcasted_iota(jnp.int32, (points, LANES), 1) < SIDE
    for parity in range(2):
        for comp in range(2):
            cols = slice(comp * LANES, (comp + 1) * LANES)
            value = jnp.where(odd, totals[2 + parity][:, cols], totals[parity][:, cols])
            top, bottom = value[:points], value[points:]
            kind = 2 * parity + comp
            weights[0, kind] = jnp.where(left, top, pltpu.roll(bottom, SIDE, 1))
            weights[1, kind] = jnp.where(left, pltpu.roll(top, SIDE, 1), bottom)
    result[...] = jnp.zeros_like(result)
    state_ref[...] = left_ref[...]

    def reduced(block):
        base = pl.multiple_of(block * BLOCK, BLOCK)
        for comp in range(2):
            total = sums[pl.ds(comp * 8, BLOCK, stride=16)]
            for lane in range(1, 8):
                total += sums[pl.ds(comp * 8 + lane, BLOCK, stride=16)]
            total = total * scale_ref[pl.ds(base, BLOCK)]
            result[comp, pl.ds(base, BLOCK)] = total + pltpu.roll(total, SIDE, 1)

    def held_step(block, carry):
        second = block.astype(jnp.float32) >= turn
        for parity in range(2):
            scaled = [
                jnp.where(second, weights[1, 2 * parity + comp], weights[0, 2 * parity + comp])
                for comp in range(2)
            ]
            for order in range(parity, BLOCK, 2):
                value = values_ref[block, order]
                for comp in range(2):
                    product = (value * scaled[comp]).reshape(points // 8, 8, LANES)
                    sums[pl.ds((order * 2 + comp) * 8, 8)] = product.sum(axis=0)
        reduced(block)
        return carry

    def step(block, carry):
        second = block.astype(jnp.float32) >= turn
        first = 0
        for chunk in CHUNKS:
            rows = slice(first, first + chunk)
            scaled = [jnp.where(second, weights[1, k, rows], weights[0, k, rows]) for k in range(4)]

            def add(order, value):
                for comp in range(2):
                    product = value * scaled[2 * (order % 2) + comp]
                    partial = product.reshape(chunk // 8, 8, LANES).sum(axis=0)
                    place = pl.ds((order * 2 + comp) * 8, 8)
                    if first == 0:
                        sums[place] = partial
                    else:
                        sums[place] += partial

            sweep_block(block, turn, rows, lat_ref, beta_ref, growth_ref, start_ref, state_ref, add)
            first += chunk
        reduced(block)
        return carry

    lax.fori_loop(0, jnp.minimum(block_total, HELD), held_step, 0)
    lax.fori_loop(HELD, block_total, step, 0)

    left = lax.broadcasted_iota(jnp.int32, (BLOCK, LANES), 1) < SIDE
    spots = -(-M // BLOCK)
    chosen = [jnp.broadcast_to(turn, (8, LANES)) == value for value in range(spots + 1)]
    chosen = [jnp.concatenate([mask] * (BLOCK // 8), axis=0) for mask in chosen]
    for place in range(spots):
        rows = slice(place * BLOCK, (place + 1) * BLOCK)
        for comp in range(2):
            early_part = jnp.where(turn > place, result[comp, rows], 0.0)
            later = jnp.zeros((BLOCK, LANES), jnp.float32)
            for value in range(spots + 1):
                base = (place + value) * BLOCK
                if base < result.shape[1]:
                    later = jnp.where(chosen[value], result[comp, base : base + BLOCK], later)
            final[comp, rows] = jnp.where(left, early_part, later)
    back = back_ref[...]
    dims = (((1,), (1,)), ((), ()))
    for comp in range(2):
        high, low = split_bf16(final[comp])
        value = lax.dot_general(back, high, dims, preferred_element_type=jnp.float32)
        value += lax.dot_general(back, low, dims, preferred_element_type=jnp.float32)
        out_ref[:, comp, :] = value[:slots, :M]


def resample_pieces(pieces, rows, padded_rows):
    full = resample_table()
    table = full.reshape(full.shape[0], pieces, rows).transpose(1, 0, 2)
    table = table_bf16(np.pad(table, ((0, 0), (0, 0), (0, padded_rows - rows))))
    return table.reshape(pieces, full.shape[0], 2, padded_rows).transpose(0, 2, 1, 3)


def legendre(fields, mine, back, prepared, rows, slots):
    pieces = len(fields)
    early = pieces // 2
    latitudes = latitude_table()
    points = latitudes.shape[1]
    table = jnp.asarray(resample_pieces(pieces, rows, fields[0].shape[0]))
    total = resample(fields[:early], table)
    block_rows = -(-M // BLOCK) * BLOCK
    return pl.pallas_call(
        functools.partial(legendre_kernel, early),
        out_shape=jax.ShapeDtypeStruct((slots, 2, M), jnp.float32),
        in_specs=[VMEM_SPEC] * (11 + pieces - early),
        out_specs=VMEM_SPEC,
        scratch_shapes=[
            pltpu.VMEM((2, 4, points, LANES), jnp.float32),
            pltpu.VMEM((3, points, LANES), jnp.float32),
            pltpu.VMEM((BLOCK * 16, LANES), jnp.float32),
            pltpu.VMEM((2, 2 * block_rows, LANES), jnp.float32),
            pltpu.VMEM((2, block_rows, LANES), jnp.float32),
        ],
        compiler_params=pltpu.CompilerParams(vmem_limit_bytes=late_bytes(pieces)),
        cost_estimate=pl.CostEstimate(
            flops=7 * points * LANES * M, bytes_accessed=6 * 2**20, transcendentals=0
        ),
    )(table, latitudes, *prepared, total, mine, back, *fields[early:])


def shards(tracer, wind_east, wind_north, keep_m, slot_wave):
    rows = tracer.shape[1]
    lat_count = lax.axis_size("lat")
    slots = slot_wave.shape[0] // lat_count
    axes = ("lev", "fld")
    ring = (axes, tuple(lax.axis_size(axis) for axis in axes))

    blocks, edges = advect(tracer, wind_east, wind_north, ring)
    blocks, slot_wave, keep_m = lax.optimization_barrier((blocks, slot_wave, keep_m))
    grids = exchange(blocks, axes)
    edges = lax.all_to_all(edges, ("lat", *axes), split_axis=0, concat_axis=0, tiled=True)
    places, wave_row, mine, back, keep_col, sine_col = prepare_places(slot_wave, keep_m, lat_count)
    waved = fourier(grids, edges, ring, places, wave_row, keep_col, sine_col, lat_count)
    waved, mine = lax.optimization_barrier((list(waved), mine))
    fields = exchange(waved, "lat")
    prepared = prepare_recurrence(mine, lat_count)
    return legendre(fields, mine, back, prepared, rows, slots)[None]


def solution(mesh):
    return jax.shard_map(
        shards,
        mesh=mesh,
        in_specs=(
            P("member", "lat", ("lev", "fld")),
            P("member", "lat", ("lev", "fld")),
            P("member", "lat", ("lev", "fld")),
            P("lat"),
            P(),
        ),
        out_specs=P(("member", "lev", "fld"), "lat", None, None),
        check_vma=False,
    )
```

```python
import functools
import math

import jax
import jax.numpy as jnp
import numpy as np
from jax import lax
from jax.experimental import pallas as pl
from jax.experimental.pallas import tpu as pltpu
from jax.sharding import PartitionSpec as P

M = 400
NLAT = 800
NLON = 1600
LANES = 128
BLOCK = 32
CHUNKS = (40, 32, 32)
HELD = -(-M // BLOCK)
SIDE = LANES // 2
TOP = 32767.0
WIND_STEP = 1.5 / TOP
VMEM_BYTES = 60 * 2**20
LATE_BYTES = 16 * 2**20
MIDDLE_BYTES = 16 * 2**20
VMEM_SPEC = pl.BlockSpec(memory_space=pltpu.VMEM)
SMEM_SPEC = pl.BlockSpec(memory_space=pltpu.SMEM)
HBM_SPEC = pl.BlockSpec(memory_space=pltpu.HBM)


def split_bf16(values):
    high = values.astype(jnp.bfloat16)
    low = (values - high.astype(jnp.float32)).astype(jnp.bfloat16)
    return high, low


def table_bf16(table):
    high = table.astype(jnp.bfloat16)
    low = (table - high.astype(np.float64)).astype(jnp.bfloat16)
    return np.concatenate([high, low], axis=-1)


def fourier_tables(pieces):
    quarter = NLON // 4
    spots = np.arange(quarter)[:, None]
    factor = 1.0 / math.sqrt(NLON)

    def parts(waves):
        angles = 2.0 * math.pi / NLON * (spots * waves[None, :] % NLON)
        return factor * np.cos(angles), factor * np.sin(angles)

    def shaped(columns):
        pad = [(0, 0), (0, -columns[0].shape[1] % LANES)]
        table = np.concatenate([np.pad(part, pad) for part in columns], axis=1)
        return table.reshape(share, quarter // share, -1)

    share = pieces // 4
    tables = []
    for first in (0, 2):
        cosine, sine = parts(np.arange(first, M, 4))
        tables.append(shaped([cosine, -sine]))
    waves = np.arange(1, M, 2)
    sign = np.where(waves % 4 == 1, 1.0, -1.0)[None, :]
    cosine, sine = parts(waves)
    return [*tables, shaped([cosine, -sine]), shaped([-sign * sine, -sign * cosine])]


def column_waves():
    columns = []
    for waves in (np.arange(0, M, 4), np.arange(2, M, 4), np.arange(1, M, 2)):
        columns.append(np.pad(waves, (0, -len(waves) % LANES), constant_values=-1))
    return np.concatenate(columns).astype(np.float32)[:, None]


def resample_table():
    half = M // 2
    coarse = math.pi / M * (np.arange(M) + 0.5)
    fine = math.pi / NLAT * (np.arange(NLAT) + 0.5)
    waves = np.arange(M)
    weight = np.where(waves == 0, 1.0, 2.0) / M
    even = (np.cos(np.outer(coarse, waves)) * weight) @ np.cos(np.outer(waves, fine))
    odd = (np.sin(np.outer(coarse, waves)) * weight) @ np.sin(np.outer(waves, fine))
    rows = []
    for full in (even, odd):
        for sign in (1.0, -1.0):
            folded = (full[:half] + sign * full[::-1][:half]).reshape(2, half // 2, NLAT)
            rows.append(np.pad(folded, ((0, 0), (0, -half // 2 % 8), (0, 0))).reshape(-1, NLAT))
    return np.concatenate(rows, axis=0)


def latitude_table():
    half = M // 2
    angles = math.pi / M * (np.arange(half) + 0.5)
    log_sine = np.log2(np.sin(angles))
    coarse = np.round(log_sine * 1024.0) / 1024.0
    rows = np.stack([2.0 * np.cos(angles), coarse, log_sine - coarse]).reshape(3, 2, half // 2)
    rows = np.pad(rows, ((0, 0), (0, 0), (0, -half // 2 % 8)))
    return np.repeat(rows.transpose(0, 2, 1), SIDE, axis=2).astype(np.float32)


def scale_code(biggest):
    wanted = jnp.maximum(biggest, 1e-30) * (1.0 / TOP)
    exponent = jnp.floor(jnp.log(wanted) * (1.0 / math.log(2.0)))
    return exponent * 128.0 + jnp.ceil((wanted * jnp.exp2(-exponent) - 1.0) * 128.0)


def scale_of(code):
    exponent = jnp.floor(code * (1.0 / 128.0))
    rest = code - 128.0 * exponent
    return jnp.exp2(exponent) * (1.0 + rest * (1.0 / 128.0))


def coded(values, inverse):
    return jnp.floor(values * inverse + 0.5)


def as_int16(values):
    return values.astype(jnp.int32).astype(jnp.int16)


def from_int16(codes):
    return codes.astype(jnp.int32).astype(jnp.float32)


def partner(axes, sizes, step):
    count = math.prod(sizes)
    if count != 4:
        return step
    index = lax.axis_index(axes[0])
    for axis, size in zip(axes[1:], sizes[1:]):
        index = index * size + lax.axis_index(axis)
    return index ^ step


def exchange(blocks, axis):
    count = len(blocks)
    if count != 4:
        return list(lax.all_to_all(jnp.stack(blocks), axis, split_axis=0, concat_axis=0, tiled=True))
    pairs = [[(i, i ^ step) for i in range(count)] for step in range(count)]
    return [blocks[0]] + [lax.ppermute(blocks[step], axis, pairs[step]) for step in range(1, count)]


def advect_kernel(ring, lat_count, tracer_hbm, east_hbm, north_hbm, *rest):
    levels, rows, lons = tracer_hbm.shape
    outs, (edge_ref, tracer, east_wind, north_wind, sems) = rest[:levels], rest[levels:]
    chosen = [partner(*ring, step) for step in range(levels)]
    copies = []
    for step, level in enumerate(chosen):
        copies.append(
            [
                pltpu.make_async_copy(source.at[level], target.at[step], sems.at[step, kind])
                for kind, (source, target) in enumerate(
                    ((tracer_hbm, tracer), (east_hbm, east_wind), (north_hbm, north_wind))
                )
            ]
        )
        for copy in copies[-1]:
            copy.start()
    padded_rows = outs[0].shape[0]
    end = (lons - 1) // LANES * LANES
    spare = lons - end
    lane = lax.broadcasted_iota(jnp.int32, (rows, LANES), 1)
    lat_index = lax.axis_index("lat")
    edge_ref[...] = jnp.zeros_like(edge_ref)
    for step, level in enumerate(chosen):
        for copy in copies[step]:
            copy.wait()
        field = tracer[step].astype(jnp.float32)

        @pl.when(lat_index < lat_count - 1)
        def _():
            edge_ref[(lat_index + 1) * levels + level] = field[rows - 1 :]

        @pl.when(lat_index > 0)
        def _():
            edge_ref[(lat_index - 1) * levels + level] = field[:1]

        blank = jnp.zeros((rows, 1), jnp.float32)
        west = jnp.concatenate([blank, field[:, :-1]], axis=1)
        east = jnp.concatenate([field[:, 1:], blank], axis=1)
        blank = jnp.zeros((1, lons), jnp.float32)
        north = jnp.concatenate([blank, field[:-1]], axis=0)
        south = jnp.concatenate([field[1:], blank], axis=0)
        eastward = 0.5 * east_wind[step].astype(jnp.float32)
        northward = 0.5 * north_wind[step].astype(jnp.float32)
        moved = field - eastward * (east - west) - northward * (south - north)
        first, last = field[:, :1], field[:, lons - 1 :]
        biggest = jnp.max(jnp.abs(moved), axis=1, keepdims=True)
        biggest = jnp.maximum(biggest, jnp.maximum(jnp.abs(first), jnp.abs(last)))
        code = scale_code(biggest)
        inverse = 1.0 / scale_of(code)
        filler = jnp.zeros((rows, LANES - spare), jnp.float32)
        tile = jnp.concatenate([moved[:, end:], filler], axis=1)
        tile = jnp.where(lane == spare + 1, first, jnp.where(lane == spare + 2, last, tile))
        tile = coded(tile, inverse)
        tile = jnp.where(lane == spare, code, tile)
        winds = jnp.where(lane == spare + 3, eastward[:, :1], eastward[:, lons - 1 :])
        winds = coded(winds, 1.0 / WIND_STEP)
        tile = jnp.where((lane == spare + 3) | (lane == spare + 4), winds, tile)
        wind_rows = jnp.concatenate([northward[:1], northward[rows - 1 :]], axis=0)
        wind_rows = coded(wind_rows, 1.0 / WIND_STEP)
        blank = jnp.zeros((padded_rows - rows - 2, lons), jnp.float32)
        wind_rows = jnp.concatenate([wind_rows, blank], axis=0)
        filler = jnp.zeros((padded_rows - rows, LANES - spare), jnp.float32)
        wind_tile = jnp.concatenate([wind_rows[:, end:], filler], axis=1)
        steps = jnp.concatenate([coded(moved[:, :end], inverse), wind_rows[:, :end]], axis=0)
        outs[step][:, :end] = as_int16(steps)
        outs[step][:, end:] = as_int16(jnp.concatenate([tile, wind_tile], axis=0))


def advect(tracer, east_wind, north_wind, ring):
    levels, rows, lons = tracer.shape
    lat_count = lax.axis_size("lat")
    width = (lons - 1) // LANES * LANES + LANES
    padded_rows = -(-(rows + 2) // 16) * 16
    held = pltpu.VMEM((levels, rows, lons), jnp.bfloat16)
    result = pl.pallas_call(
        functools.partial(advect_kernel, ring, lat_count),
        out_shape=[jax.ShapeDtypeStruct((padded_rows, width), jnp.int16)] * levels
        + [jax.ShapeDtypeStruct((lat_count * levels, 1, lons), jnp.float32)],
        in_specs=[HBM_SPEC] * 3,
        out_specs=[VMEM_SPEC] * (levels + 1),
        scratch_shapes=[held, held, held, pltpu.SemaphoreType.DMA((levels, 3))],
        compiler_params=pltpu.CompilerParams(vmem_limit_bytes=VMEM_BYTES),
        cost_estimate=pl.CostEstimate(
            flops=20 * levels * rows * lons, bytes_accessed=8 * levels * rows * lons, transcendentals=0
        ),
    )(tracer, east_wind, north_wind)
    return list(result[:levels]), result[levels]


def fourier_kernel(ring, lat_count, pieces, *rest):
    grids, (edge_ref, table_ref, place_ref, wave_ref, keep_ref, sine_ref) = rest[:pieces], rest[pieces : pieces + 6]
    outs, field = rest[pieces + 6 : -1], rest[-1]
    _, rows, width = field.shape
    lons = table_ref.shape[1]
    share = pieces // 4

    end = width - LANES
    spare = lons - end
    lane = lax.broadcasted_iota(jnp.int32, (rows, LANES), 1)
    winds = (lane == spare + 3) | (lane == spare + 4)
    lat_index = lax.axis_index("lat")
    for piece in range(pieces):
        spot = partner(*ring, piece)
        values = from_int16(grids[piece][...])
        tile = values[:rows, end:]
        scale = scale_of(tile[:, spare : spare + 1])
        field[spot, :, :end] = values[:rows, :end] * scale
        field[spot, :, end:] = tile * jnp.where(winds, WIND_STEP, scale)
        wind_rows = values[rows : rows + 2, :lons] * WIND_STEP

        @pl.when(lat_index > 0)
        def _():
            above = edge_ref[(lat_index - 1) * pieces + spot]
            field[spot, :1, :lons] += wind_rows[:1] * above

        @pl.when(lat_index < lat_count - 1)
        def _():
            below = edge_ref[(lat_index + 1) * pieces + spot]
            field[spot, rows - 1 :, :lons] -= wind_rows[1:] * below

    for spot in range(pieces):
        tile = field[spot, :, end:]
        before = field[(spot - 1) % pieces, :, end:]
        after = field[(spot + 1) % pieces, :, end:]
        shift = LANES - spare
        gain = pltpu.roll(tile, shift - 3, 1) * pltpu.roll(before, shift - 2, 1)
        loss = pltpu.roll(tile, LANES - 5, 1) * pltpu.roll(after, LANES - 2, 1)
        field[spot, :, end:] = tile - jnp.where(lane == spare - 1, loss, 0.0)
        field[spot, :, :LANES] += jnp.where(lane == 0, gain, 0.0)

    spans = [2 * LANES, 2 * LANES, 4 * LANES, 4 * LANES]

    def product(kind, value, spot):
        high, low = split_bf16(value)
        first, span = 2 * sum(spans[:kind]), spans[kind]
        both = jnp.dot(high, table_ref[spot, :, first : first + 2 * span], preferred_element_type=jnp.float32)
        part = jnp.dot(low, table_ref[spot, :, first : first + span], preferred_element_type=jnp.float32)
        return part + both[:, :span] + both[:, span:]

    sums = [None, None, None]
    for spot in range(share):
        quarters = [field[quarter * share + spot, :, :lons] for quarter in range(4)]
        sum02, dif02 = quarters[0] + quarters[2], quarters[0] - quarters[2]
        sum13, dif13 = quarters[1] + quarters[3], quarters[1] - quarters[3]
        parts = []
        for kind, value in enumerate((sum02 + sum13, sum02 - sum13, dif02, dif13)):
            parts.append(product(kind, value, spot))
        parts = [parts[0], parts[1], parts[2] + parts[3]]
        sums = [part if total is None else total + part for total, part in zip(sums, parts)]
    placed = []
    for part in range(2):
        columns = []
        for total in sums:
            half = total.shape[1] // 2
            columns.append(total[:, part * half : (part + 1) * half])
        high, low = split_bf16(jnp.concatenate(columns, axis=1))
        value = jnp.dot(high, place_ref[...], preferred_element_type=jnp.float32)
        value += jnp.dot(low, place_ref[...], preferred_element_type=jnp.float32)
        kept = jnp.where(wave_ref[...] < keep_ref[...], value * sine_ref[...], 0.0)
        code = scale_code(jnp.max(jnp.abs(kept), axis=0, keepdims=True))
        steps = coded(kept, 1.0 / scale_of(code))
        codes = jnp.broadcast_to(code, (outs[0].shape[0] - rows, code.shape[1]))
        placed.append(as_int16(jnp.concatenate([steps, codes], axis=0)))
    for target in range(lat_count):
        for part in range(2):
            cols = slice(target * LANES, (target + 1) * LANES)
            outs[target][:, part * LANES : (part + 1) * LANES] = placed[part][:, cols]


def fourier(grids, edges, ring, places, wave_row, keep_col, sine_col, lat_count):
    pieces = len(grids)
    rows = keep_col.shape[0]
    width = grids[0].shape[1]
    padded_rows = -(-(rows + 1) // 16) * 16
    tables = [table_bf16(table) for table in fourier_tables(pieces)]
    return pl.pallas_call(
        functools.partial(fourier_kernel, ring, lat_count, pieces),
        out_shape=[jax.ShapeDtypeStruct((padded_rows, 2 * LANES), jnp.int16)] * lat_count,
        in_specs=[VMEM_SPEC] * (pieces + 6),
        out_specs=[VMEM_SPEC] * lat_count,
        scratch_shapes=[pltpu.VMEM((pieces, rows, width), jnp.float32)],
        compiler_params=pltpu.CompilerParams(vmem_limit_bytes=MIDDLE_BYTES),
        cost_estimate=pl.CostEstimate(
            flops=3 * rows * NLON * M, bytes_accessed=6 * 2**20, transcendentals=0
        ),
    )(*grids, edges, np.concatenate(tables, axis=-1), places, wave_row, keep_col, sine_col)


def places_kernel(
    slot_ref, keep_ref, sine_ref, spot_ref,
    place_ref, wave_ref, mine_ref, back_ref, keep_col, sine_col, sorted_rows,
):
    groups, _, rows = sine_ref.shape
    lat_index = lax.axis_index("lat")
    slots = slot_ref.shape[1] // groups
    paired = (slots + 1) // 2
    shape = (LANES, LANES)
    down = lax.broadcasted_iota(jnp.int32, shape, 0)
    across = lax.broadcasted_iota(jnp.int32, shape, 1)
    filler = jnp.full((1, LANES - slots), 2.0 * M, jnp.float32)
    for group in range(groups):
        row = slot_ref[:, group * slots : (group + 1) * slots].astype(jnp.float32)
        row = jnp.broadcast_to(jnp.concatenate([row, filler], axis=1), shape)
        column = jnp.sum(jnp.where(down == across, row, 0.0), axis=1, keepdims=True)
        ahead = (row < column) | ((row == column) & (across < down))
        rank = jnp.sum(jnp.where(ahead, 1.0, 0.0), axis=1, keepdims=True)
        place = jnp.where(rank < paired, rank, SIDE + slots - 1.0 - rank)
        place = jnp.where(rank < slots, place, -1.0)
        hot = jnp.where(place == across.astype(jnp.float32), 1.0, 0.0)
        filled = jnp.sum(hot, axis=0, keepdims=True)
        values = jnp.sum(hot * column, axis=0, keepdims=True)
        values = jnp.where(filled > 0.5, values, 2.0 * M)
        sorted_rows[group] = jnp.broadcast_to(values, sorted_rows.shape[1:])

        @pl.when(group == lat_index)
        def _():
            mine_ref[...] = values
            back_ref[...] = hot.astype(jnp.bfloat16)

    spots = jnp.broadcast_to(spot_ref[...], (spot_ref.shape[0], LANES))
    for step in range(groups):
        row = sorted_rows[partner(("lat",), (groups,), step), :1]
        cols = slice(step * LANES, (step + 1) * LANES)
        wave_ref[:, cols] = row
        place_ref[:, cols] = jnp.where(spots == row, 1.0, 0.0).astype(jnp.bfloat16)

    shape = (rows, rows)
    same = lax.broadcasted_iota(jnp.int32, shape, 0) == lax.broadcasted_iota(jnp.int32, shape, 1)
    kept = jnp.broadcast_to(keep_ref[...].astype(jnp.float32), shape)
    keep_col[...] = jnp.sum(jnp.where(same, kept, 0.0), axis=1, keepdims=True)
    sine = jnp.broadcast_to(sine_ref[lat_index], shape)
    sine_col[...] = jnp.sum(jnp.where(same, sine, 0.0), axis=1, keepdims=True)


def prepare_places(slot_wave, keep_m, groups):
    rows = keep_m.shape[0]
    sines = np.sin(math.pi / NLAT * (np.arange(NLAT) + 0.5)) * math.sqrt(2.0 / NLAT)
    spots = column_waves()
    width = groups * LANES
    return pl.pallas_call(
        places_kernel,
        out_shape=[
            jax.ShapeDtypeStruct((spots.shape[0], width), jnp.bfloat16),
            jax.ShapeDtypeStruct((1, width), jnp.float32),
            jax.ShapeDtypeStruct((1, LANES), jnp.float32),
            jax.ShapeDtypeStruct((LANES, LANES), jnp.bfloat16),
            jax.ShapeDtypeStruct((rows, 1), jnp.float32),
            jax.ShapeDtypeStruct((rows, 1), jnp.float32),
        ],
        in_specs=[VMEM_SPEC] * 4,
        out_specs=[VMEM_SPEC] * 6,
        scratch_shapes=[pltpu.VMEM((groups, 8, LANES), jnp.float32)],
        compiler_params=pltpu.CompilerParams(vmem_limit_bytes=MIDDLE_BYTES),
    )(
        slot_wave[None], keep_m[None],
        sines.reshape(groups, 1, rows).astype(np.float32), spots,
    )


def lane_pairs(row):
    lane = lax.broadcasted_iota(jnp.int32, row.shape, 1)
    other = pltpu.roll(row, SIDE, 1)
    return jnp.where(lane < SIDE, row, other), jnp.where(lane < SIDE, other, row)


def block_count(wave):
    return jnp.floor((jnp.maximum(M - wave, 0.0) + (BLOCK - 1)) * (1.0 / BLOCK))


def sweep_kernel(
    mine_ref, lat_ref, term_ref, beta_ref, scale_ref, growth_ref, start_ref, state_ref, values_ref
):
    pair = lane_pairs(jnp.broadcast_to(mine_ref[...], (8, LANES)))
    one, two = pair[0][:1], pair[1][:1]
    blocks = growth_ref.shape[0]
    turn = block_count(one)
    block = lax.broadcasted_iota(jnp.int32, (blocks, LANES), 0).astype(jnp.float32)
    second = block >= turn
    wave = jnp.where(second, two, one)
    limit = M - wave
    wave = jnp.minimum(wave, M - 1.0)
    first = (block - jnp.where(second, turn, 0.0)) * BLOCK

    scale = jnp.ones((blocks, LANES), jnp.float32)
    for index in range(BLOCK + 1):
        order = first + index
        degree = wave + order
        square = 4.0 * degree * degree - 1.0
        spread = 4.0 * order * (degree + wave)
        if index > 0:
            scale = scale * jnp.sqrt(square / spread)
        if index < BLOCK:
            beta_ref[pl.ds(index, blocks, stride=BLOCK)] = spread / jnp.maximum(square, 1.0)
            scale_ref[pl.ds(index, blocks, stride=BLOCK)] = jnp.where(order < limit, scale, 0.0)
    growth_ref[...] = scale

    for kind, wave in enumerate((one, two)):
        wave = jnp.minimum(wave, M - 1.0)
        counter = lax.broadcasted_iota(jnp.int32, term_ref.shape, 0).astype(jnp.float32)
        norm = jnp.sum(jnp.where(counter <= wave, term_ref[...], 0.0), axis=0, keepdims=True)
        coarse = lat_ref[1] * wave
        whole = jnp.floor(coarse)
        start_ref[2 * kind] = jnp.exp2(
            (coarse - whole) + lat_ref[2] * wave + 0.5 * (norm - 1.0)
        )
        start_ref[2 * kind + 1] = whole

    state_ref[0] = jnp.zeros_like(state_ref[0])
    state_ref[1] = start_ref[0]
    state_ref[2] = start_ref[1]
    points = lat_ref.shape[1]

    def step(block, carry):
        first = 0
        for chunk in (points // 16 * 8, points - points // 16 * 8):
            rows = slice(first, first + chunk)

            def keep(order, value):
                values_ref[block, order, rows] = value

            sweep_block(block, turn, rows, lat_ref, beta_ref, growth_ref, start_ref, state_ref, keep)
            first += chunk
        return carry

    total = jnp.max(turn + block_count(two)).astype(jnp.int32)
    lax.fori_loop(0, jnp.minimum(total, HELD), step, 0)


def sweep_block(block, turn, rows, lat_ref, beta_ref, growth_ref, start_ref, state_ref, use):
    base = pl.multiple_of(block * BLOCK, BLOCK)
    begins = block.astype(jnp.float32) == turn
    grow = growth_ref[pl.ds(block, 1)]
    cosine = lat_ref[0, rows]
    height = jnp.where(begins, start_ref[3, rows], state_ref[2, rows])
    factor = jnp.exp2(height)
    old = jnp.where(begins, 0.0, state_ref[0, rows])
    new = jnp.where(begins, start_ref[2, rows], state_ref[1, rows])
    for order in range(BLOCK):
        use(order, new * factor)
        beta = beta_ref[pl.ds(base + order, 1)]
        old, new = new, cosine * new - beta * old
    biggest = jnp.maximum(jnp.abs(old), jnp.abs(new)) * grow
    shift = jnp.floor(jnp.log(biggest) * (1.0 / math.log(2.0)))
    factor = grow * jnp.exp2(-shift)
    state_ref[0, rows] = old * factor
    state_ref[1, rows] = new * factor
    state_ref[2, rows] = height + shift


def prepare_recurrence(mine, pieces):
    latitudes = latitude_table()
    points = latitudes.shape[1]
    blocks = 2 * -(-M // BLOCK)
    counter = np.arange(M)
    terms = np.log1p(0.5 / np.maximum(counter, 1)) * (counter > 0) / math.log(2.0)
    terms = np.broadcast_to(terms[:, None], (M, LANES)).astype(np.float32)
    orders = jax.ShapeDtypeStruct((blocks * BLOCK, LANES), jnp.float32)
    return pl.pallas_call(
        sweep_kernel,
        out_shape=[
            orders,
            orders,
            jax.ShapeDtypeStruct((blocks, LANES), jnp.float32),
            jax.ShapeDtypeStruct((4, points, LANES), jnp.float32),
            jax.ShapeDtypeStruct((3, points, LANES), jnp.float32),
            jax.ShapeDtypeStruct((HELD, BLOCK, points, LANES), jnp.float32),
        ],
        in_specs=[VMEM_SPEC] * 3,
        out_specs=[VMEM_SPEC] * 6,
        compiler_params=pltpu.CompilerParams(vmem_limit_bytes=late_bytes(pieces)),
    )(mine, latitudes, terms)


def resampled(first, fields, table, total):
    for piece, field in enumerate(fields):
        values = from_int16(field[...])
        values = values * scale_of(values[field.shape[0] - 1 :])
        high, low = split_bf16(values)
        spot = partner(("lat",), table.shape[:1], first + piece)
        both = jnp.concatenate([high, low], axis=1)
        part = jnp.dot(table[spot, 0], both, preferred_element_type=jnp.float32)
        part = part[:, : high.shape[1]] + part[:, high.shape[1] :]
        part += jnp.dot(table[spot, 1], high, preferred_element_type=jnp.float32)
        total = part if total is None else total + part
    return total


def resample_kernel(table_ref, *rest):
    rest[-1][...] = resampled(0, rest[:-1], table_ref, None)


def late_bytes(pieces):
    return LATE_BYTES if pieces <= 4 else VMEM_BYTES


def resample(fields, table):
    count, _, height, _ = table.shape
    span = fields[0].shape[1]
    return pl.pallas_call(
        resample_kernel,
        out_shape=jax.ShapeDtypeStruct((height, span), jnp.float32),
        in_specs=[VMEM_SPEC] * (1 + len(fields)),
        out_specs=VMEM_SPEC,
        compiler_params=pltpu.CompilerParams(vmem_limit_bytes=late_bytes(count)),
        cost_estimate=pl.CostEstimate(
            flops=6 * height * span * NLAT // count * len(fields), bytes_accessed=4 * 2**20, transcendentals=0
        ),
    )(table, *fields)


def legendre_kernel(early, *rest):
    table, lat_ref, beta_ref, scale_ref, growth_ref, start_ref, left_ref, values_ref = rest[:8]
    total_ref, mine_ref, back_ref = rest[8:11]
    fields, (out_ref, weights, state_ref, sums, result, final) = rest[11:-6], rest[-6:]
    points = lat_ref.shape[1]
    slots = out_ref.shape[0]
    mine = mine_ref[...]
    odd = mine - 2.0 * jnp.floor(mine * 0.5) > 0.5
    pair = lane_pairs(jnp.broadcast_to(mine, (8, LANES)))
    turn = block_count(pair[0][:1])
    block_total = jnp.max(turn + block_count(pair[1][:1])).astype(jnp.int32)

    total = resampled(early, fields, table, total_ref[...])
    totals = [total[2 * points * kind : 2 * points * (kind + 1)] for kind in range(4)]
    left = lax.broadcasted_iota(jnp.int32, (points, LANES), 1) < SIDE
    for parity in range(2):
        for comp in range(2):
            cols = slice(comp * LANES, (comp + 1) * LANES)
            value = jnp.where(odd, totals[2 + parity][:, cols], totals[parity][:, cols])
            top, bottom = value[:points], value[points:]
            kind = 2 * parity + comp
            weights[0, kind] = jnp.where(left, top, pltpu.roll(bottom, SIDE, 1))
            weights[1, kind] = jnp.where(left, pltpu.roll(top, SIDE, 1), bottom)
    result[...] = jnp.zeros_like(result)
    state_ref[...] = left_ref[...]

    def reduced(block):
        base = pl.multiple_of(block * BLOCK, BLOCK)
        for comp in range(2):
            total = sums[pl.ds(comp * 8, BLOCK, stride=16)]
            for lane in range(1, 8):
                total += sums[pl.ds(comp * 8 + lane, BLOCK, stride=16)]
            total = total * scale_ref[pl.ds(base, BLOCK)]
            result[comp, pl.ds(base, BLOCK)] = total + pltpu.roll(total, SIDE, 1)

    def held_step(block, carry):
        second = block.astype(jnp.float32) >= turn
        for parity in range(2):
            scaled = [
                jnp.where(second, weights[1, 2 * parity + comp], weights[0, 2 * parity + comp])
                for comp in range(2)
            ]
            for order in range(parity, BLOCK, 2):
                value = values_ref[block, order]
                for comp in range(2):
                    product = (value * scaled[comp]).reshape(points // 8, 8, LANES)
                    sums[pl.ds((order * 2 + comp) * 8, 8)] = product.sum(axis=0)
        reduced(block)
        return carry

    def step(block, carry):
        second = block.astype(jnp.float32) >= turn
        first = 0
        for chunk in CHUNKS:
            rows = slice(first, first + chunk)
            scaled = [jnp.where(second, weights[1, k, rows], weights[0, k, rows]) for k in range(4)]

            def add(order, value):
                for comp in range(2):
                    product = value * scaled[2 * (order % 2) + comp]
                    partial = product.reshape(chunk // 8, 8, LANES).sum(axis=0)
                    place = pl.ds((order * 2 + comp) * 8, 8)
                    if first == 0:
                        sums[place] = partial
                    else:
                        sums[place] += partial

            sweep_block(block, turn, rows, lat_ref, beta_ref, growth_ref, start_ref, state_ref, add)
            first += chunk
        reduced(block)
        return carry

    lax.fori_loop(0, jnp.minimum(block_total, HELD), held_step, 0)
    lax.fori_loop(HELD, block_total, step, 0)

    left = lax.broadcasted_iota(jnp.int32, (BLOCK, LANES), 1) < SIDE
    spots = -(-M // BLOCK)
    chosen = [jnp.broadcast_to(turn, (8, LANES)) == value for value in range(spots + 1)]
    chosen = [jnp.concatenate([mask] * (BLOCK // 8), axis=0) for mask in chosen]
    for place in range(spots):
        rows = slice(place * BLOCK, (place + 1) * BLOCK)
        for comp in range(2):
            early_part = jnp.where(turn > place, result[comp, rows], 0.0)
            later = jnp.zeros((BLOCK, LANES), jnp.float32)
            for value in range(spots + 1):
                base = (place + value) * BLOCK
                if base < result.shape[1]:
                    later = jnp.where(chosen[value], result[comp, base : base + BLOCK], later)
            final[comp, rows] = jnp.where(left, early_part, later)
    back = back_ref[...]
    dims = (((1,), (1,)), ((), ()))
    for comp in range(2):
        high, low = split_bf16(final[comp])
        value = lax.dot_general(back, high, dims, preferred_element_type=jnp.float32)
        value += lax.dot_general(back, low, dims, preferred_element_type=jnp.float32)
        out_ref[:, comp, :] = value[:slots, :M]


def resample_pieces(pieces, rows, padded_rows):
    full = resample_table()
    table = full.reshape(full.shape[0], pieces, rows).transpose(1, 0, 2)
    table = table_bf16(np.pad(table, ((0, 0), (0, 0), (0, padded_rows - rows))))
    return table.reshape(pieces, full.shape[0], 2, padded_rows).transpose(0, 2, 1, 3)


def legendre(fields, mine, back, prepared, rows, slots):
    pieces = len(fields)
    early = pieces // 2
    latitudes = latitude_table()
    points = latitudes.shape[1]
    table = jnp.asarray(resample_pieces(pieces, rows, fields[0].shape[0]))
    total = resample(fields[:early], table)
    block_rows = -(-M // BLOCK) * BLOCK
    return pl.pallas_call(
        functools.partial(legendre_kernel, early),
        out_shape=jax.ShapeDtypeStruct((slots, 2, M), jnp.float32),
        in_specs=[VMEM_SPEC] * (11 + pieces - early),
        out_specs=VMEM_SPEC,
        scratch_shapes=[
            pltpu.VMEM((2, 4, points, LANES), jnp.float32),
            pltpu.VMEM((3, points, LANES), jnp.float32),
            pltpu.VMEM((BLOCK * 16, LANES), jnp.float32),
            pltpu.VMEM((2, 2 * block_rows, LANES), jnp.float32),
            pltpu.VMEM((2, block_rows, LANES), jnp.float32),
        ],
        compiler_params=pltpu.CompilerParams(vmem_limit_bytes=late_bytes(pieces)),
        cost_estimate=pl.CostEstimate(
            flops=7 * points * LANES * M, bytes_accessed=6 * 2**20, transcendentals=0
        ),
    )(table, latitudes, *prepared, total, mine, back, *fields[early:])


def shards(tracer, wind_east, wind_north, keep_m, slot_wave):
    rows = tracer.shape[1]
    lat_count = lax.axis_size("lat")
    slots = slot_wave.shape[0] // lat_count
    axes = ("lev", "fld")
    ring = (axes, tuple(lax.axis_size(axis) for axis in axes))

    blocks, edges = advect(tracer, wind_east, wind_north, ring)
    blocks, slot_wave, keep_m = lax.optimization_barrier((blocks, slot_wave, keep_m))
    grids = exchange(blocks, axes)
    edges = lax.all_to_all(edges, ("lat", *axes), split_axis=0, concat_axis=0, tiled=True)
    places, wave_row, mine, back, keep_col, sine_col = prepare_places(slot_wave, keep_m, lat_count)
    waved = fourier(grids, edges, ring, places, wave_row, keep_col, sine_col, lat_count)
    waved, mine = lax.optimization_barrier((list(waved), mine))
    fields = exchange(waved, "lat")
    prepared = prepare_recurrence(mine, lat_count)
    return legendre(fields, mine, back, prepared, rows, slots)[None]


def solution(mesh):
    return jax.shard_map(
        shards,
        mesh=mesh,
        in_specs=(
            P("member", "lat", ("lev", "fld")),
            P("member", "lat", ("lev", "fld")),
            P("member", "lat", ("lev", "fld")),
            P("lat"),
            P(),
        ),
        out_specs=P(("member", "lev", "fld"), "lat", None, None),
        check_vma=False,
    )
```

```python
import functools
import math

import jax
import jax.numpy as jnp
import numpy as np
from jax import lax
from jax.experimental import pallas as pl
from jax.experimental.pallas import tpu as pltpu
from jax.sharding import PartitionSpec as P

M = 400
NLAT = 800
NLON = 1600
LANES = 128
BLOCK = 32
CHUNKS = (40, 32, 32)
HELD = -(-M // BLOCK)
SIDE = LANES // 2
TOP = 32767.0
WIND_STEP = 1.5 / TOP
VMEM_BYTES = 60 * 2**20
LATE_BYTES = 16 * 2**20
MIDDLE_BYTES = 16 * 2**20
VMEM_SPEC = pl.BlockSpec(memory_space=pltpu.VMEM)
SMEM_SPEC = pl.BlockSpec(memory_space=pltpu.SMEM)
HBM_SPEC = pl.BlockSpec(memory_space=pltpu.HBM)


def split_bf16(values):
    high = values.astype(jnp.bfloat16)
    low = (values - high.astype(jnp.float32)).astype(jnp.bfloat16)
    return high, low


def table_bf16(table):
    high = table.astype(jnp.bfloat16)
    low = (table - high.astype(np.float64)).astype(jnp.bfloat16)
    return np.concatenate([high, low], axis=-1)


def fourier_tables(pieces):
    quarter = NLON // 4
    spots = np.arange(quarter)[:, None]
    factor = 1.0 / math.sqrt(NLON)

    def parts(waves):
        angles = 2.0 * math.pi / NLON * (spots * waves[None, :] % NLON)
        return factor * np.cos(angles), factor * np.sin(angles)

    def shaped(columns):
        pad = [(0, 0), (0, -columns[0].shape[1] % LANES)]
        table = np.concatenate([np.pad(part, pad) for part in columns], axis=1)
        return table.reshape(share, quarter // share, -1)

    share = pieces // 4
    tables = []
    for first in (0, 2):
        cosine, sine = parts(np.arange(first, M, 4))
        tables.append(shaped([cosine, -sine]))
    waves = np.arange(1, M, 2)
    sign = np.where(waves % 4 == 1, 1.0, -1.0)[None, :]
    cosine, sine = parts(waves)
    return [*tables, shaped([cosine, -sine]), shaped([-sign * sine, -sign * cosine])]


def column_waves(shape):
    row = lax.broadcasted_iota(jnp.int32, shape, 0)
    waves, first = jnp.full(shape, -1, jnp.int32), 0
    for start, step in ((0, 4), (2, 4), (1, 2)):
        count = len(range(start, M, step))
        inside = (row >= first) & (row < first + count)
        waves = jnp.where(inside, start + step * (row - first), waves)
        first += -(-count // LANES) * LANES
    return waves.astype(jnp.float32)


def column_count():
    return sum(-(-len(range(start, M, step)) // LANES) * LANES for start, step in ((0, 4), (2, 4), (1, 2)))


def resample_table():
    half = M // 2
    coarse = math.pi / M * (np.arange(M) + 0.5)
    fine = math.pi / NLAT * (np.arange(NLAT) + 0.5)
    waves = np.arange(M)
    weight = np.where(waves == 0, 1.0, 2.0) / M
    even = (np.cos(np.outer(coarse, waves)) * weight) @ np.cos(np.outer(waves, fine))
    odd = (np.sin(np.outer(coarse, waves)) * weight) @ np.sin(np.outer(waves, fine))
    rows = []
    for full in (even, odd):
        for sign in (1.0, -1.0):
            folded = (full[:half] + sign * full[::-1][:half]).reshape(2, half // 2, NLAT)
            rows.append(np.pad(folded, ((0, 0), (0, -half // 2 % 8), (0, 0))).reshape(-1, NLAT))
    return np.concatenate(rows, axis=0) * (np.sin(fine) * math.sqrt(2.0 / NLAT))


def latitude_table():
    half = M // 2
    angles = math.pi / M * (np.arange(half) + 0.5)
    log_sine = np.log2(np.sin(angles))
    coarse = np.round(log_sine * 1024.0) / 1024.0
    rows = np.stack([2.0 * np.cos(angles), coarse, log_sine - coarse]).reshape(3, 2, half // 2)
    rows = np.pad(rows, ((0, 0), (0, 0), (0, -half // 2 % 8)))
    return np.repeat(rows.transpose(0, 2, 1), SIDE, axis=2).astype(np.float32)


def scale_code(biggest):
    wanted = jnp.maximum(biggest, 1e-30) * (1.0 / TOP)
    exponent = jnp.floor(jnp.log(wanted) * (1.0 / math.log(2.0)))
    return exponent * 128.0 + jnp.ceil((wanted * jnp.exp2(-exponent) - 1.0) * 128.0)


def scale_of(code):
    exponent = jnp.floor(code * (1.0 / 128.0))
    rest = code - 128.0 * exponent
    return jnp.exp2(exponent) * (1.0 + rest * (1.0 / 128.0))


def coded(values, inverse):
    return jnp.floor(values * inverse + 0.5)


def as_int16(values):
    return values.astype(jnp.int32).astype(jnp.int16)


def from_int16(codes):
    return codes.astype(jnp.int32).astype(jnp.float32)


def partner(axes, sizes, step):
    count = math.prod(sizes)
    if count != 4:
        return step
    index = lax.axis_index(axes[0])
    for axis, size in zip(axes[1:], sizes[1:]):
        index = index * size + lax.axis_index(axis)
    return index ^ step


def exchange(blocks, axis):
    count = len(blocks)
    if count != 4:
        return list(lax.all_to_all(jnp.stack(blocks), axis, split_axis=0, concat_axis=0, tiled=True))
    pairs = [[(i, i ^ step) for i in range(count)] for step in range(count)]
    return [blocks[0]] + [lax.ppermute(blocks[step], axis, pairs[step]) for step in range(1, count)]


def advect_kernel(ring, lat_count, keep_ref, tracer_hbm, east_hbm, north_hbm, *rest):
    levels, rows, lons = tracer_hbm.shape
    outs, (edge_ref, tracer, east_wind, north_wind, blocks, sems) = rest[:levels], rest[levels:]
    chosen = [partner(*ring, step) for step in range(levels)]
    copies = [None] * levels
    order = (*range(levels // 2, levels), *range(levels // 2))
    for step in order:
        copies[step] = [
            pltpu.make_async_copy(source.at[chosen[step]], target.at[step], sems.at[kind, step])
            for kind, (source, target) in enumerate(
                ((tracer_hbm, tracer), (east_hbm, east_wind), (north_hbm, north_wind))
            )
        ]
        for copy in copies[step]:
            copy.start()
    padded_rows = outs[0].shape[0]
    same = (rows, rows)
    same = lax.broadcasted_iota(jnp.int32, same, 0) == lax.broadcasted_iota(jnp.int32, same, 1)
    keep = jnp.broadcast_to(keep_ref[...].astype(jnp.float32), (rows, rows))
    keep = jnp.sum(jnp.where(same, keep, 0.0), axis=1, keepdims=True)
    end = (lons - 1) // LANES * LANES
    spare = lons - end
    lane = lax.broadcasted_iota(jnp.int32, (rows, LANES), 1)
    lat_index = lax.axis_index("lat")
    edge_ref[...] = jnp.zeros_like(edge_ref)
    written = []
    for step in order:
        level = chosen[step]
        for copy in copies[step]:
            copy.wait()
        field = tracer[step].astype(jnp.float32)

        @pl.when(lat_index < lat_count - 1)
        def _():
            edge_ref[(lat_index + 1) * levels + level] = field[rows - 1 :]

        @pl.when(lat_index > 0)
        def _():
            edge_ref[(lat_index - 1) * levels + level] = field[:1]

        blank = jnp.zeros((rows, 1), jnp.float32)
        west = jnp.concatenate([blank, field[:, :-1]], axis=1)
        east = jnp.concatenate([field[:, 1:], blank], axis=1)
        blank = jnp.zeros((1, lons), jnp.float32)
        north = jnp.concatenate([blank, field[:-1]], axis=0)
        south = jnp.concatenate([field[1:], blank], axis=0)
        eastward = 0.5 * east_wind[step].astype(jnp.float32)
        northward = 0.5 * north_wind[step].astype(jnp.float32)
        moved = field - eastward * (east - west) - northward * (south - north)
        first, last = field[:, :1], field[:, lons - 1 :]
        biggest = jnp.max(jnp.abs(moved), axis=1, keepdims=True)
        biggest = jnp.maximum(biggest, jnp.maximum(jnp.abs(first), jnp.abs(last)))
        code = scale_code(biggest)
        inverse = 1.0 / scale_of(code)
        filler = jnp.zeros((rows, LANES - spare), jnp.float32)
        tile = jnp.concatenate([moved[:, end:], filler], axis=1)
        tile = jnp.where(lane == spare + 1, first, jnp.where(lane == spare + 2, last, tile))
        tile = coded(tile, inverse)
        tile = jnp.where(lane == spare, code, tile)
        winds = jnp.where(lane == spare + 3, eastward[:, :1], eastward[:, lons - 1 :])
        winds = coded(winds, 1.0 / WIND_STEP)
        tile = jnp.where((lane == spare + 3) | (lane == spare + 4), winds, tile)
        tile = jnp.where(lane == spare + 5, keep, tile)
        wind_rows = jnp.concatenate([northward[:1], northward[rows - 1 :]], axis=0)
        wind_rows = coded(wind_rows, 1.0 / WIND_STEP)
        blank = jnp.zeros((padded_rows - rows - 2, lons), jnp.float32)
        wind_rows = jnp.concatenate([wind_rows, blank], axis=0)
        filler = jnp.zeros((padded_rows - rows, LANES - spare), jnp.float32)
        wind_tile = jnp.concatenate([wind_rows[:, end:], filler], axis=1)
        steps = jnp.concatenate([coded(moved[:, :end], inverse), wind_rows[:, :end]], axis=0)
        blocks[step, :, :end] = as_int16(steps)
        blocks[step, :, end:] = as_int16(jnp.concatenate([tile, wind_tile], axis=0))
        written.append(pltpu.make_async_copy(blocks.at[step], outs[step], sems.at[3, step]))
        written[-1].start()
    for copy in written:
        copy.wait()


def advect(tracer, east_wind, north_wind, keep_m, ring):
    levels, rows, lons = tracer.shape
    lat_count = lax.axis_size("lat")
    width = (lons - 1) // LANES * LANES + LANES
    padded_rows = -(-(rows + 2) // 16) * 16
    held = pltpu.VMEM((levels, rows, lons), jnp.bfloat16)
    result = pl.pallas_call(
        functools.partial(advect_kernel, ring, lat_count),
        out_shape=[jax.ShapeDtypeStruct((padded_rows, width), jnp.int16)] * levels
        + [jax.ShapeDtypeStruct((lat_count * levels, 1, lons), jnp.float32)],
        in_specs=[VMEM_SPEC] + [HBM_SPEC] * 3,
        out_specs=[HBM_SPEC] * levels + [VMEM_SPEC],
        scratch_shapes=[held, held, held]
        + [pltpu.VMEM((levels, padded_rows, width), jnp.int16), pltpu.SemaphoreType.DMA((4, levels))],
        compiler_params=pltpu.CompilerParams(vmem_limit_bytes=VMEM_BYTES),
        cost_estimate=pl.CostEstimate(
            flops=5 * 10**9, bytes_accessed=8 * levels * rows * lons, transcendentals=0
        ),
    )(keep_m[None], tracer, east_wind, north_wind)
    return list(result[:levels]), result[levels]


def fourier_kernel(ring, lat_count, pieces, *rest):
    grids, (edge_ref, table_ref, place_ref, wave_ref) = rest[:pieces], rest[pieces : pieces + 4]
    outs, field = rest[pieces + 4 : -1], rest[-1]
    _, rows, width = field.shape
    lons = table_ref.shape[1]
    share = pieces // 4

    end = width - LANES
    spare = lons - end
    lane = lax.broadcasted_iota(jnp.int32, (rows, LANES), 1)
    winds = (lane == spare + 3) | (lane == spare + 4)
    lat_index = lax.axis_index("lat")
    for piece in range(pieces):
        spot = partner(*ring, piece)
        values = from_int16(grids[piece][...])
        tile = values[:rows, end:]
        scale = scale_of(tile[:, spare : spare + 1])
        keep = tile[:, spare + 5 : spare + 6]
        field[spot, :, :end] = values[:rows, :end] * scale
        field[spot, :, end:] = tile * jnp.where(winds, WIND_STEP, scale)
        wind_rows = values[rows : rows + 2, :lons] * WIND_STEP

        @pl.when(lat_index > 0)
        def _():
            above = edge_ref[(lat_index - 1) * pieces + spot]
            field[spot, :1, :lons] += wind_rows[:1] * above

        @pl.when(lat_index < lat_count - 1)
        def _():
            below = edge_ref[(lat_index + 1) * pieces + spot]
            field[spot, rows - 1 :, :lons] -= wind_rows[1:] * below

    for spot in range(pieces):
        tile = field[spot, :, end:]
        before = field[(spot - 1) % pieces, :, end:]
        after = field[(spot + 1) % pieces, :, end:]
        shift = LANES - spare
        gain = pltpu.roll(tile, shift - 3, 1) * pltpu.roll(before, shift - 2, 1)
        loss = pltpu.roll(tile, LANES - 5, 1) * pltpu.roll(after, LANES - 2, 1)
        field[spot, :, end:] = tile - jnp.where(lane == spare - 1, loss, 0.0)
        field[spot, :, :LANES] += jnp.where(lane == 0, gain, 0.0)

    spans = [2 * LANES, 2 * LANES, 4 * LANES, 4 * LANES]

    def product(kind, value, spot):
        high, low = split_bf16(value)
        first, span = 2 * sum(spans[:kind]), spans[kind]
        both = jnp.dot(high, table_ref[spot, :, first : first + 2 * span], preferred_element_type=jnp.float32)
        part = jnp.dot(low, table_ref[spot, :, first : first + span], preferred_element_type=jnp.float32)
        return part + both[:, :span] + both[:, span:]

    sums = [None, None, None]
    for spot in range(share):
        quarters = [field[quarter * share + spot, :, :lons] for quarter in range(4)]
        sum02, dif02 = quarters[0] + quarters[2], quarters[0] - quarters[2]
        sum13, dif13 = quarters[1] + quarters[3], quarters[1] - quarters[3]
        parts = []
        for kind, value in enumerate((sum02 + sum13, sum02 - sum13, dif02, dif13)):
            parts.append(product(kind, value, spot))
        parts = [parts[0], parts[1], parts[2] + parts[3]]
        sums = [part if total is None else total + part for total, part in zip(sums, parts)]
    placed = []
    for part in range(2):
        columns = []
        for total in sums:
            half = total.shape[1] // 2
            columns.append(total[:, part * half : (part + 1) * half])
        high, low = split_bf16(jnp.concatenate(columns, axis=1))
        value = jnp.dot(high, place_ref[...], preferred_element_type=jnp.float32)
        value += jnp.dot(low, place_ref[...], preferred_element_type=jnp.float32)
        kept = jnp.where(wave_ref[...] < keep, value, 0.0)
        code = scale_code(jnp.max(jnp.abs(kept), axis=0, keepdims=True))
        steps = coded(kept, 1.0 / scale_of(code))
        codes = jnp.broadcast_to(code, (outs[0].shape[0] - rows, code.shape[1]))
        placed.append(as_int16(jnp.concatenate([steps, codes], axis=0)))
    for target in range(lat_count):
        for part in range(2):
            cols = slice(target * LANES, (target + 1) * LANES)
            outs[target][:, part * LANES : (part + 1) * LANES] = placed[part][:, cols]


def fourier(grids, edges, ring, places, wave_row, rows, lat_count):
    pieces = len(grids)
    width = grids[0].shape[1]
    padded_rows = -(-(rows + 1) // 16) * 16
    tables = [table_bf16(table) for table in fourier_tables(pieces)]
    return pl.pallas_call(
        functools.partial(fourier_kernel, ring, lat_count, pieces),
        out_shape=[jax.ShapeDtypeStruct((padded_rows, 2 * LANES), jnp.int16)] * lat_count,
        in_specs=[VMEM_SPEC] * (pieces + 4),
        out_specs=[VMEM_SPEC] * lat_count,
        scratch_shapes=[pltpu.VMEM((pieces, rows, width), jnp.float32)],
        compiler_params=pltpu.CompilerParams(vmem_limit_bytes=MIDDLE_BYTES),
        cost_estimate=pl.CostEstimate(
            flops=4 * 10**9, bytes_accessed=6 * 2**20, transcendentals=0
        ),
    )(*grids, edges, np.concatenate(tables, axis=-1), places, wave_row)


def places_kernel(groups, slot_ref, place_ref, wave_ref, mine_ref, sorted_rows):
    lat_index = lax.axis_index("lat")
    slots = slot_ref.shape[1] // groups
    paired = (slots + 1) // 2
    shape = (LANES, LANES)
    down = lax.broadcasted_iota(jnp.int32, shape, 0)
    across = lax.broadcasted_iota(jnp.int32, shape, 1)
    filler = jnp.full((1, LANES - slots), 2.0 * M, jnp.float32)
    for group in range(groups):
        plain = slot_ref[:, group * slots : (group + 1) * slots].astype(jnp.float32)
        plain = jnp.concatenate([plain, filler], axis=1)
        row = jnp.broadcast_to(plain, shape)
        column = jnp.sum(jnp.where(down == across, row, 0.0), axis=1, keepdims=True)
        ahead = (row < column) | ((row == column) & (across < down))
        rank = jnp.sum(jnp.where(ahead, 1.0, 0.0), axis=1, keepdims=True)
        place = jnp.where(rank < paired, rank, SIDE + slots - 1.0 - rank)
        place = jnp.where(rank < slots, place, -1.0)
        hot = jnp.where(place == across.astype(jnp.float32), 1.0, 0.0)
        filled = jnp.sum(hot, axis=0, keepdims=True)
        values = jnp.sum(hot * column, axis=0, keepdims=True)
        values = jnp.where(filled > 0.5, values, 2.0 * M)
        sorted_rows[group] = jnp.broadcast_to(values, sorted_rows.shape[1:])

        @pl.when(group == lat_index)
        def _():
            mine_ref[:1] = values
            mine_ref[1:] = plain

    spots = column_waves((place_ref.shape[0], LANES))
    for step in range(groups):
        row = sorted_rows[partner(("lat",), (groups,), step), :1]
        cols = slice(step * LANES, (step + 1) * LANES)
        wave_ref[:, cols] = row
        place_ref[:, cols] = jnp.where(spots == row, 1.0, 0.0).astype(jnp.bfloat16)


def prepare_places(slot_wave, groups):
    width = groups * LANES
    return pl.pallas_call(
        functools.partial(places_kernel, groups),
        out_shape=[
            jax.ShapeDtypeStruct((column_count(), width), jnp.bfloat16),
            jax.ShapeDtypeStruct((1, width), jnp.float32),
            jax.ShapeDtypeStruct((2, LANES), jnp.float32),
        ],
        in_specs=[VMEM_SPEC],
        out_specs=[VMEM_SPEC] * 3,
        scratch_shapes=[pltpu.VMEM((groups, 8, LANES), jnp.float32)],
        compiler_params=pltpu.CompilerParams(vmem_limit_bytes=MIDDLE_BYTES),
        cost_estimate=pl.CostEstimate(flops=2 * 10**9, bytes_accessed=2**20, transcendentals=0),
    )(slot_wave[None])


def lane_pairs(row):
    lane = lax.broadcasted_iota(jnp.int32, row.shape, 1)
    other = pltpu.roll(row, SIDE, 1)
    return jnp.where(lane < SIDE, row, other), jnp.where(lane < SIDE, other, row)


def block_count(wave):
    return jnp.floor((jnp.maximum(M - wave, 0.0) + (BLOCK - 1)) * (1.0 / BLOCK))


def sweep_kernel(
    mine_ref, lat_ref,
    beta_ref, scale_ref, growth_ref, start_ref, state_ref, values_ref, back_ref,
):
    shape = (LANES, LANES)
    same = lax.broadcasted_iota(jnp.int32, shape, 0) == lax.broadcasted_iota(jnp.int32, shape, 1)
    plain = jnp.broadcast_to(mine_ref[1:], shape)
    plain = jnp.sum(jnp.where(same, plain, 0.0), axis=1, keepdims=True)
    hot = (plain == mine_ref[:1]) & (plain < 2.0 * M)
    back_ref[...] = jnp.where(hot, 1.0, 0.0).astype(jnp.bfloat16)
    pair = lane_pairs(jnp.broadcast_to(mine_ref[:1], (8, LANES)))
    one, two = pair[0][:1], pair[1][:1]
    blocks = growth_ref.shape[0]
    turn = block_count(one)
    block = lax.broadcasted_iota(jnp.int32, (blocks, LANES), 0).astype(jnp.float32)
    second = block >= turn
    wave = jnp.where(second, two, one)
    limit = M - wave
    wave = jnp.minimum(wave, M - 1.0)
    first = (block - jnp.where(second, turn, 0.0)) * BLOCK

    scale = jnp.ones((blocks, LANES), jnp.float32)
    for index in range(BLOCK + 1):
        order = first + index
        degree = wave + order
        square = 4.0 * degree * degree - 1.0
        spread = 4.0 * order * (degree + wave)
        if index > 0:
            scale = scale * jnp.sqrt(square / spread)
        if index < BLOCK:
            beta_ref[pl.ds(index, blocks, stride=BLOCK)] = spread / jnp.maximum(square, 1.0)
            scale_ref[pl.ds(index, blocks, stride=BLOCK)] = jnp.where(order < limit, scale, 0.0)
    growth_ref[...] = scale

    counter = lax.broadcasted_iota(jnp.int32, (M, LANES), 0).astype(jnp.float32) + 1.0
    terms = jnp.log(1.0 + 0.5 / counter) * (1.0 / math.log(2.0))
    for kind, wave in enumerate((one, two)):
        wave = jnp.minimum(wave, M - 1.0)
        norm = jnp.sum(jnp.where(counter <= wave, terms, 0.0), axis=0, keepdims=True)
        coarse = lat_ref[1] * wave
        whole = jnp.floor(coarse)
        start_ref[2 * kind] = jnp.exp2(
            (coarse - whole) + lat_ref[2] * wave + 0.5 * (norm - 1.0)
        )
        start_ref[2 * kind + 1] = whole

    state_ref[0] = jnp.zeros_like(state_ref[0])
    state_ref[1] = start_ref[0]
    state_ref[2] = start_ref[1]
    points = lat_ref.shape[1]

    def step(block, carry):
        first = 0
        for chunk in (points // 16 * 8, points - points // 16 * 8):
            rows = slice(first, first + chunk)

            def keep(order, value):
                values_ref[block, order, rows] = value

            sweep_block(block, turn, rows, lat_ref, beta_ref, growth_ref, start_ref, state_ref, keep)
            first += chunk
        return carry

    total = jnp.max(turn + block_count(two)).astype(jnp.int32)
    lax.fori_loop(0, jnp.minimum(total, HELD), step, 0)


def sweep_block(block, turn, rows, lat_ref, beta_ref, growth_ref, start_ref, state_ref, use):
    base = pl.multiple_of(block * BLOCK, BLOCK)
    begins = block.astype(jnp.float32) == turn
    grow = growth_ref[pl.ds(block, 1)]
    cosine = lat_ref[0, rows]
    height = jnp.where(begins, start_ref[3, rows], state_ref[2, rows])
    factor = jnp.exp2(height)
    old = jnp.where(begins, 0.0, state_ref[0, rows])
    new = jnp.where(begins, start_ref[2, rows], state_ref[1, rows])
    for order in range(BLOCK):
        use(order, new * factor)
        beta = beta_ref[pl.ds(base + order, 1)]
        old, new = new, cosine * new - beta * old
    biggest = jnp.maximum(jnp.abs(old), jnp.abs(new)) * grow
    shift = jnp.floor(jnp.log(biggest) * (1.0 / math.log(2.0)))
    factor = grow * jnp.exp2(-shift)
    state_ref[0, rows] = old * factor
    state_ref[1, rows] = new * factor
    state_ref[2, rows] = height + shift


def prepare_recurrence(mine, pieces):
    latitudes = latitude_table()
    points = latitudes.shape[1]
    blocks = 2 * -(-M // BLOCK)
    orders = jax.ShapeDtypeStruct((blocks * BLOCK, LANES), jnp.float32)
    return pl.pallas_call(
        sweep_kernel,
        out_shape=[
            orders,
            orders,
            jax.ShapeDtypeStruct((blocks, LANES), jnp.float32),
            jax.ShapeDtypeStruct((4, points, LANES), jnp.float32),
            jax.ShapeDtypeStruct((3, points, LANES), jnp.float32),
            jax.ShapeDtypeStruct((HELD, BLOCK, points, LANES), jnp.float32),
            jax.ShapeDtypeStruct((LANES, LANES), jnp.bfloat16),
        ],
        in_specs=[VMEM_SPEC] * 2,
        out_specs=[VMEM_SPEC] * 7,
        compiler_params=pltpu.CompilerParams(vmem_limit_bytes=late_bytes(pieces)),
        cost_estimate=pl.CostEstimate(
            flops=5 * 10**9, bytes_accessed=25 * 2**20, transcendentals=0
        ),
    )(mine, latitudes)


def resampled(first, fields, table, total):
    for piece, field in enumerate(fields):
        values = from_int16(field[...])
        values = values * scale_of(values[field.shape[0] - 1 :])
        high, low = split_bf16(values)
        spot = partner(("lat",), table.shape[:1], first + piece)
        both = jnp.concatenate([high, low], axis=1)
        part = jnp.dot(table[spot, 0], both, preferred_element_type=jnp.float32)
        part = part[:, : high.shape[1]] + part[:, high.shape[1] :]
        part += jnp.dot(table[spot, 1], high, preferred_element_type=jnp.float32)
        total = part if total is None else total + part
    return total


def resample_kernel(table_ref, *rest):
    rest[-1][...] = resampled(0, rest[:-1], table_ref, None)


def late_bytes(pieces):
    return LATE_BYTES if pieces <= 4 else VMEM_BYTES


def resample(fields, table):
    count, _, height, _ = table.shape
    span = fields[0].shape[1]
    return pl.pallas_call(
        resample_kernel,
        out_shape=jax.ShapeDtypeStruct((height, span), jnp.float32),
        in_specs=[VMEM_SPEC] * (1 + len(fields)),
        out_specs=VMEM_SPEC,
        compiler_params=pltpu.CompilerParams(vmem_limit_bytes=late_bytes(count)),
        cost_estimate=pl.CostEstimate(
            flops=10**9, bytes_accessed=4 * 2**20, transcendentals=0
        ),
    )(table, *fields)


def legendre_kernel(early, *rest):
    table, lat_ref, beta_ref, scale_ref, growth_ref, start_ref, left_ref, values_ref, back_ref = rest[:9]
    total_ref, mine_ref = rest[9:11]
    fields, (out_ref, weights, state_ref, sums, result, final) = rest[11:-6], rest[-6:]
    points = lat_ref.shape[1]
    slots = out_ref.shape[0]
    mine = mine_ref[:1]
    odd = mine - 2.0 * jnp.floor(mine * 0.5) > 0.5
    pair = lane_pairs(jnp.broadcast_to(mine, (8, LANES)))
    turn = block_count(pair[0][:1])
    block_total = jnp.max(turn + block_count(pair[1][:1])).astype(jnp.int32)

    total = resampled(early, fields, table, total_ref[...])
    totals = [total[2 * points * kind : 2 * points * (kind + 1)] for kind in range(4)]
    left = lax.broadcasted_iota(jnp.int32, (points, LANES), 1) < SIDE
    for parity in range(2):
        for comp in range(2):
            cols = slice(comp * LANES, (comp + 1) * LANES)
            value = jnp.where(odd, totals[2 + parity][:, cols], totals[parity][:, cols])
            top, bottom = value[:points], value[points:]
            kind = 2 * parity + comp
            weights[0, kind] = jnp.where(left, top, pltpu.roll(bottom, SIDE, 1))
            weights[1, kind] = jnp.where(left, pltpu.roll(top, SIDE, 1), bottom)
    result[...] = jnp.zeros_like(result)
    state_ref[...] = left_ref[...]

    def reduced(block):
        base = pl.multiple_of(block * BLOCK, BLOCK)
        for comp in range(2):
            total = sums[pl.ds(comp * 8, BLOCK, stride=16)]
            for lane in range(1, 8):
                total += sums[pl.ds(comp * 8 + lane, BLOCK, stride=16)]
            total = total * scale_ref[pl.ds(base, BLOCK)]
            result[comp, pl.ds(base, BLOCK)] = total + pltpu.roll(total, SIDE, 1)

    def held_step(block, carry):
        second = block.astype(jnp.float32) >= turn
        for parity in range(2):
            scaled = [
                jnp.where(second, weights[1, 2 * parity + comp], weights[0, 2 * parity + comp])
                for comp in range(2)
            ]
            for order in range(parity, BLOCK, 2):
                value = values_ref[block, order]
                for comp in range(2):
                    product = (value * scaled[comp]).reshape(points // 8, 8, LANES)
                    sums[pl.ds((order * 2 + comp) * 8, 8)] = product.sum(axis=0)
        reduced(block)
        return carry

    def step(block, carry):
        second = block.astype(jnp.float32) >= turn
        first = 0
        for chunk in CHUNKS:
            rows = slice(first, first + chunk)
            scaled = [jnp.where(second, weights[1, k, rows], weights[0, k, rows]) for k in range(4)]

            def add(order, value):
                for comp in range(2):
                    product = value * scaled[2 * (order % 2) + comp]
                    partial = product.reshape(chunk // 8, 8, LANES).sum(axis=0)
                    place = pl.ds((order * 2 + comp) * 8, 8)
                    if first == 0:
                        sums[place] = partial
                    else:
                        sums[place] += partial

            sweep_block(block, turn, rows, lat_ref, beta_ref, growth_ref, start_ref, state_ref, add)
            first += chunk
        reduced(block)
        return carry

    lax.fori_loop(0, jnp.minimum(block_total, HELD), held_step, 0)
    lax.fori_loop(HELD, block_total, step, 0)

    left = lax.broadcasted_iota(jnp.int32, (BLOCK, LANES), 1) < SIDE
    spots = -(-M // BLOCK)
    chosen = [jnp.broadcast_to(turn, (8, LANES)) == value for value in range(spots + 1)]
    chosen = [jnp.concatenate([mask] * (BLOCK // 8), axis=0) for mask in chosen]
    for place in range(spots):
        rows = slice(place * BLOCK, (place + 1) * BLOCK)
        for comp in range(2):
            early_part = jnp.where(turn > place, result[comp, rows], 0.0)
            later = jnp.zeros((BLOCK, LANES), jnp.float32)
            for value in range(spots + 1):
                base = (place + value) * BLOCK
                if base < result.shape[1]:
                    later = jnp.where(chosen[value], result[comp, base : base + BLOCK], later)
            final[comp, rows] = jnp.where(left, early_part, later)
    back = back_ref[...]
    dims = (((1,), (1,)), ((), ()))
    for comp in range(2):
        high, low = split_bf16(final[comp])
        value = lax.dot_general(back, high, dims, preferred_element_type=jnp.float32)
        value += lax.dot_general(back, low, dims, preferred_element_type=jnp.float32)
        out_ref[:, comp, :] = value[:slots, :M]


def resample_pieces(pieces, rows, padded_rows):
    full = resample_table()
    table = full.reshape(full.shape[0], pieces, rows).transpose(1, 0, 2)
    table = table_bf16(np.pad(table, ((0, 0), (0, 0), (0, padded_rows - rows))))
    return table.reshape(pieces, full.shape[0], 2, padded_rows).transpose(0, 2, 1, 3)


def legendre(fields, mine, prepared, rows, slots):
    pieces = len(fields)
    early = pieces // 2
    latitudes = latitude_table()
    points = latitudes.shape[1]
    table = jnp.asarray(resample_pieces(pieces, rows, fields[0].shape[0]))
    total = resample(fields[:early], table)
    block_rows = -(-M // BLOCK) * BLOCK
    return pl.pallas_call(
        functools.partial(legendre_kernel, early),
        out_shape=jax.ShapeDtypeStruct((slots, 2, M), jnp.float32),
        in_specs=[VMEM_SPEC] * (11 + pieces - early),
        out_specs=VMEM_SPEC,
        scratch_shapes=[
            pltpu.VMEM((2, 4, points, LANES), jnp.float32),
            pltpu.VMEM((3, points, LANES), jnp.float32),
            pltpu.VMEM((BLOCK * 16, LANES), jnp.float32),
            pltpu.VMEM((2, 2 * block_rows, LANES), jnp.float32),
            pltpu.VMEM((2, block_rows, LANES), jnp.float32),
        ],
        compiler_params=pltpu.CompilerParams(vmem_limit_bytes=late_bytes(pieces)),
        cost_estimate=pl.CostEstimate(
            flops=8 * 10**9, bytes_accessed=6 * 2**20, transcendentals=0
        ),
    )(table, latitudes, *prepared, total, mine, *fields[early:])


def shards(tracer, wind_east, wind_north, keep_m, slot_wave):
    rows = tracer.shape[1]
    lat_count = lax.axis_size("lat")
    slots = slot_wave.shape[0] // lat_count
    axes = ("lev", "fld")
    ring = (axes, tuple(lax.axis_size(axis) for axis in axes))

    blocks, edges = advect(tracer, wind_east, wind_north, keep_m, ring)
    blocks, slot_wave = lax.optimization_barrier((blocks, slot_wave))
    grids = exchange(blocks, axes)
    edges = lax.all_to_all(edges, ("lat", *axes), split_axis=0, concat_axis=0, tiled=True)
    places, wave_row, mine = prepare_places(slot_wave, lat_count)
    waved = fourier(grids, edges, ring, places, wave_row, rows, lat_count)
    waved, mine = lax.optimization_barrier((list(waved), mine))
    fields = exchange(waved, "lat")
    prepared = prepare_recurrence(mine, lat_count)
    return legendre(fields, mine, prepared, rows, slots)[None]


def solution(mesh):
    return jax.shard_map(
        shards,
        mesh=mesh,
        in_specs=(
            P("member", "lat", ("lev", "fld")),
            P("member", "lat", ("lev", "fld")),
            P("member", "lat", ("lev", "fld")),
            P("lat"),
            P(),
        ),
        out_specs=P(("member", "lev", "fld"), "lat", None, None),
        check_vma=False,
    )
```

```python
import functools
import math

import jax
import jax.numpy as jnp
import numpy as np
from jax import lax
from jax.experimental import pallas as pl
from jax.experimental.pallas import tpu as pltpu
from jax.sharding import PartitionSpec as P

M = 400
NLAT = 800
NLON = 1600
LANES = 128
BLOCK = 32
CHUNKS = (40, 32, 32)
SPAN = -(-M // BLOCK)
HELD = 13
SIDE = LANES // 2
TOP = 32767.0
WIND_STEP = 1.5 / TOP
EXTRA = 6
VMEM_BYTES = 60 * 2**20
LATE_BYTES = 16 * 2**20
MIDDLE_BYTES = 16 * 2**20
VMEM_SPEC = pl.BlockSpec(memory_space=pltpu.VMEM)
SMEM_SPEC = pl.BlockSpec(memory_space=pltpu.SMEM)
HBM_SPEC = pl.BlockSpec(memory_space=pltpu.HBM)


def split_bf16(values):
    high = values.astype(jnp.bfloat16)
    low = (values - high.astype(jnp.float32)).astype(jnp.bfloat16)
    return high, low


def table_bf16(table):
    high = table.astype(jnp.bfloat16)
    low = (table - high.astype(np.float64)).astype(jnp.bfloat16)
    return np.concatenate([high, low], axis=-1)


def fourier_tables(pieces):
    quarter = NLON // 4
    spots = np.arange(quarter)[:, None]
    factor = 1.0 / math.sqrt(NLON)

    def parts(waves):
        angles = 2.0 * math.pi / NLON * (spots * waves[None, :] % NLON)
        return factor * np.cos(angles), factor * np.sin(angles)

    def shaped(columns):
        pad = [(0, 0), (0, -columns[0].shape[1] % LANES)]
        table = np.concatenate([np.pad(part, pad) for part in columns], axis=1)
        return table.reshape(share, quarter // share, -1)

    share = pieces // 4
    tables = []
    for first in (0, 2):
        cosine, sine = parts(np.arange(first, M, 4))
        tables.append(shaped([cosine, -sine]))
    waves = np.arange(1, M, 2)
    sign = np.where(waves % 4 == 1, 1.0, -1.0)[None, :]
    cosine, sine = parts(waves)
    return [*tables, shaped([cosine, -sine]), shaped([-sign * sine, -sign * cosine])]


def column_waves(shape):
    row = lax.broadcasted_iota(jnp.int32, shape, 0)
    waves, first = jnp.full(shape, -1, jnp.int32), 0
    for start, step in ((0, 4), (2, 4), (1, 2)):
        count = len(range(start, M, step))
        inside = (row >= first) & (row < first + count)
        waves = jnp.where(inside, start + step * (row - first), waves)
        first += -(-count // LANES) * LANES
    return waves.astype(jnp.float32)


def column_count():
    return sum(-(-len(range(start, M, step)) // LANES) * LANES for start, step in ((0, 4), (2, 4), (1, 2)))


def resample_table():
    half = M // 2
    coarse = math.pi / M * (np.arange(M) + 0.5)
    fine = math.pi / NLAT * (np.arange(NLAT) + 0.5)
    waves = np.arange(M)
    weight = np.where(waves == 0, 1.0, 2.0) / M
    even = (np.cos(np.outer(coarse, waves)) * weight) @ np.cos(np.outer(waves, fine))
    odd = (np.sin(np.outer(coarse, waves)) * weight) @ np.sin(np.outer(waves, fine))
    rows = []
    for full in (even, odd):
        for sign in (1.0, -1.0):
            folded = (full[:half] + sign * full[::-1][:half]).reshape(2, half // 2, NLAT)
            rows.append(np.pad(folded, ((0, 0), (0, -half // 2 % 8), (0, 0))).reshape(-1, NLAT))
    return np.concatenate(rows, axis=0) * (np.sin(fine) * math.sqrt(2.0 / NLAT))


def latitude_table():
    half = M // 2
    angles = math.pi / M * (np.arange(half) + 0.5)
    log_sine = np.log2(np.sin(angles))
    coarse = np.round(log_sine * 1024.0) / 1024.0
    rows = np.stack([2.0 * np.cos(angles), coarse, log_sine - coarse]).reshape(3, 2, half // 2)
    rows = np.pad(rows, ((0, 0), (0, 0), (0, -half // 2 % 8)))
    return np.repeat(rows.transpose(0, 2, 1), SIDE, axis=2).astype(np.float32)


def scale_code(biggest):
    wanted = jnp.maximum(biggest, 1e-30) * (1.0 / TOP)
    exponent = jnp.floor(jnp.log(wanted) * (1.0 / math.log(2.0)))
    return exponent * 128.0 + jnp.ceil((wanted * jnp.exp2(-exponent) - 1.0) * 128.0)


def scale_of(code):
    exponent = jnp.floor(code * (1.0 / 128.0))
    rest = code - 128.0 * exponent
    return jnp.exp2(exponent) * (1.0 + rest * (1.0 / 128.0))


def coded(values, inverse):
    return jnp.floor(values * inverse + 0.5)


def as_int16(values):
    return values.astype(jnp.int32).astype(jnp.int16)


def from_int16(codes):
    return codes.astype(jnp.int32).astype(jnp.float32)


def partner(axes, sizes, step):
    count = math.prod(sizes)
    if count != 4:
        return step
    index = lax.axis_index(axes[0])
    for axis, size in zip(axes[1:], sizes[1:]):
        index = index * size + lax.axis_index(axis)
    return index ^ step


def exchange(blocks, axis):
    count = len(blocks)
    if count != 4:
        return list(lax.all_to_all(jnp.stack(blocks), axis, split_axis=0, concat_axis=0, tiled=True))
    pairs = [[(i, i ^ step) for i in range(count)] for step in range(count)]
    return [blocks[0]] + [lax.ppermute(blocks[step], axis, pairs[step]) for step in range(1, count)]


def advect_kernel(ring, lat_count, keep_ref, tracer_hbm, east_hbm, north_hbm, *rest):
    levels, rows, lons = tracer_hbm.shape
    outs, (edge_ref, tracer, east_wind, north_wind, sems) = rest[:levels], rest[levels:]
    chosen = [partner(*ring, step) for step in range(levels)]
    copies = [None] * levels
    order = (*range(levels // 2, levels), *range(levels // 2))
    for step in order:
        copies[step] = [
            pltpu.make_async_copy(source.at[chosen[step]], target.at[step], sems.at[kind, step])
            for kind, (source, target) in enumerate(
                ((tracer_hbm, tracer), (east_hbm, east_wind), (north_hbm, north_wind))
            )
        ]
        for copy in copies[step]:
            copy.start()
    padded_rows, group_rows, packed_rows = block_shape(rows, lons)
    same = (rows, rows)
    same = lax.broadcasted_iota(jnp.int32, same, 0) == lax.broadcasted_iota(jnp.int32, same, 1)
    keep = jnp.broadcast_to(keep_ref[...].astype(jnp.float32), (rows, rows))
    keep = jnp.sum(jnp.where(same, keep, 0.0), axis=1, keepdims=True)
    end = (lons - 1) // LANES * LANES
    spare = lons - end
    lane = lax.broadcasted_iota(jnp.int32, (rows, LANES), 1)
    group_lane = lax.broadcasted_iota(jnp.int32, (group_rows, LANES), 1)
    lat_index = lax.axis_index("lat")
    edge_ref[...] = jnp.zeros_like(edge_ref)
    for step in order:
        level = chosen[step]
        for copy in copies[step]:
            copy.wait()
        field = tracer[step].astype(jnp.float32)

        @pl.when(lat_index < lat_count - 1)
        def _():
            edge_ref[(lat_index + 1) * levels + level] = field[rows - 1 :]

        @pl.when(lat_index > 0)
        def _():
            edge_ref[(lat_index - 1) * levels + level] = field[:1]

        blank = jnp.zeros((rows, 1), jnp.float32)
        west = jnp.concatenate([blank, field[:, :-1]], axis=1)
        east = jnp.concatenate([field[:, 1:], blank], axis=1)
        blank = jnp.zeros((1, lons), jnp.float32)
        north = jnp.concatenate([blank, field[:-1]], axis=0)
        south = jnp.concatenate([field[1:], blank], axis=0)
        eastward = 0.5 * east_wind[step].astype(jnp.float32)
        northward = 0.5 * north_wind[step].astype(jnp.float32)
        moved = field - eastward * (east - west) - northward * (south - north)
        first, last = field[:, :1], field[:, lons - 1 :]
        biggest = jnp.max(jnp.abs(moved), axis=1, keepdims=True)
        biggest = jnp.maximum(biggest, jnp.maximum(jnp.abs(first), jnp.abs(last)))
        code = scale_code(biggest)
        inverse = 1.0 / scale_of(code)
        filler = jnp.zeros((rows, LANES - spare), jnp.float32)
        tile = jnp.concatenate([moved[:, end:], filler], axis=1)
        tile = jnp.where(lane == spare + 1, first, jnp.where(lane == spare + 2, last, tile))
        tile = coded(tile, inverse)
        tile = jnp.where(lane == spare, code, tile)
        winds = jnp.where(lane == spare + 3, eastward[:, :1], eastward[:, lons - 1 :])
        winds = coded(winds, 1.0 / WIND_STEP)
        tile = jnp.where((lane == spare + 3) | (lane == spare + 4), winds, tile)
        tile = jnp.where(lane == spare + 5, keep, tile)
        wind_rows = jnp.concatenate([northward[:1], northward[rows - 1 :]], axis=0)
        wind_rows = coded(wind_rows, 1.0 / WIND_STEP)
        blank = jnp.zeros((padded_rows - rows - 2, lons), jnp.float32)
        wind_rows = jnp.concatenate([wind_rows, blank], axis=0)
        filler = jnp.zeros((padded_rows - rows, LANES - spare), jnp.float32)
        wind_tile = jnp.concatenate([wind_rows[:, end:], filler], axis=1)
        steps = jnp.concatenate([coded(moved[:, :end], inverse), wind_rows[:, :end]], axis=0)
        outs[step][:padded_rows] = as_int16(steps)
        tile = jnp.concatenate([tile, wind_tile], axis=0)
        wide = spare + EXTRA
        folded = tile[:group_rows]
        for group in range(1, -(-padded_rows // group_rows)):
            part = tile[group * group_rows : (group + 1) * group_rows]
            if part.shape[0] < group_rows:
                short = jnp.zeros((group_rows - part.shape[0], LANES), jnp.float32)
                part = jnp.concatenate([part, short], axis=0)
            part = pltpu.roll(part, group * wide, 1)
            folded = jnp.where(group_lane >= group * wide, part, folded)
        share = packed_rows - padded_rows
        for place in range(end // LANES):
            part = folded[place * share : (place + 1) * share]
            outs[step][padded_rows:, place * LANES : (place + 1) * LANES] = as_int16(part)


def block_shape(rows, lons):
    padded_rows = -(-(rows + 2) // 16) * 16
    tiles = (lons - 1) // LANES
    groups = LANES // (lons - tiles * LANES + EXTRA)
    group_rows = -(-padded_rows // groups // (16 * tiles)) * 16 * tiles
    return padded_rows, group_rows, padded_rows + group_rows // tiles


def advect(tracer, east_wind, north_wind, keep_m, ring):
    levels, rows, lons = tracer.shape
    lat_count = lax.axis_size("lat")
    width = (lons - 1) // LANES * LANES
    packed_rows = block_shape(rows, lons)[2]
    held = pltpu.VMEM((levels, rows, lons), jnp.bfloat16)
    result = pl.pallas_call(
        functools.partial(advect_kernel, ring, lat_count),
        out_shape=[jax.ShapeDtypeStruct((packed_rows, width), jnp.int16)] * levels
        + [jax.ShapeDtypeStruct((lat_count * levels, 1, lons), jnp.float32)],
        in_specs=[VMEM_SPEC] + [HBM_SPEC] * 3,
        out_specs=[VMEM_SPEC] * (levels + 1),
        scratch_shapes=[held, held, held, pltpu.SemaphoreType.DMA((3, levels))],
        compiler_params=pltpu.CompilerParams(vmem_limit_bytes=VMEM_BYTES),
        cost_estimate=pl.CostEstimate(
            flops=5 * 10**9, bytes_accessed=8 * levels * rows * lons, transcendentals=0
        ),
    )(keep_m[None], tracer, east_wind, north_wind)
    return list(result[:levels]), result[levels]


def fourier_kernel(ring, lat_count, pieces, *rest):
    grids, (edge_ref, table_ref, place_ref, wave_ref) = rest[:pieces], rest[pieces : pieces + 4]
    outs, field = rest[pieces + 4 : -1], rest[-1]
    _, rows, width = field.shape
    lons = table_ref.shape[1]
    share = pieces // 4

    end = width - LANES
    spare = lons - end
    padded_rows, group_rows, _ = block_shape(rows, lons)
    lane = lax.broadcasted_iota(jnp.int32, (rows, LANES), 1)
    winds = (lane == spare + 3) | (lane == spare + 4)
    lat_index = lax.axis_index("lat")
    for piece in range(pieces):
        spot = partner(*ring, piece)
        values = from_int16(grids[piece][...])
        folded = [
            values[padded_rows:, place * LANES : (place + 1) * LANES] for place in range(end // LANES)
        ]
        folded = jnp.concatenate(folded, axis=0)
        groups = range(-(-padded_rows // group_rows))
        wide = spare + EXTRA
        tile = [folded] + [pltpu.roll(folded, LANES - group * wide, 1) for group in groups[1:]]
        tile = jnp.concatenate(tile, axis=0)
        wind_tile = tile[rows : rows + 2, :spare]
        tile = tile[:rows]
        scale = scale_of(tile[:, spare : spare + 1])
        keep = tile[:, spare + 5 : spare + 6]
        field[spot, :, :end] = values[:rows, :end] * scale
        field[spot, :, end:] = tile * jnp.where(winds, WIND_STEP, scale)
        wind_rows = jnp.concatenate([values[rows : rows + 2], wind_tile], axis=1) * WIND_STEP

        @pl.when(lat_index > 0)
        def _():
            above = edge_ref[(lat_index - 1) * pieces + spot]
            field[spot, :1, :lons] += wind_rows[:1] * above

        @pl.when(lat_index < lat_count - 1)
        def _():
            below = edge_ref[(lat_index + 1) * pieces + spot]
            field[spot, rows - 1 :, :lons] -= wind_rows[1:] * below

    for spot in range(pieces):
        tile = field[spot, :, end:]
        before = field[(spot - 1) % pieces, :, end:]
        after = field[(spot + 1) % pieces, :, end:]
        shift = LANES - spare
        gain = pltpu.roll(tile, shift - 3, 1) * pltpu.roll(before, shift - 2, 1)
        loss = pltpu.roll(tile, LANES - 5, 1) * pltpu.roll(after, LANES - 2, 1)
        field[spot, :, end:] = tile - jnp.where(lane == spare - 1, loss, 0.0)
        field[spot, :, :LANES] += jnp.where(lane == 0, gain, 0.0)

    spans = [2 * LANES, 2 * LANES, 4 * LANES, 4 * LANES]

    def product(kind, value, spot):
        high, low = split_bf16(value)
        first, span = 2 * sum(spans[:kind]), spans[kind]
        both = jnp.dot(high, table_ref[spot, :, first : first + 2 * span], preferred_element_type=jnp.float32)
        part = jnp.dot(low, table_ref[spot, :, first : first + span], preferred_element_type=jnp.float32)
        return part + both[:, :span] + both[:, span:]

    sums = [None, None, None]
    for spot in range(share):
        quarters = [field[quarter * share + spot, :, :lons] for quarter in range(4)]
        sum02, dif02 = quarters[0] + quarters[2], quarters[0] - quarters[2]
        sum13, dif13 = quarters[1] + quarters[3], quarters[1] - quarters[3]
        parts = []
        for kind, value in enumerate((sum02 + sum13, sum02 - sum13, dif02, dif13)):
            parts.append(product(kind, value, spot))
        parts = [parts[0], parts[1], parts[2] + parts[3]]
        sums = [part if total is None else total + part for total, part in zip(sums, parts)]
    placed = []
    for part in range(2):
        columns = []
        for total in sums:
            half = total.shape[1] // 2
            columns.append(total[:, part * half : (part + 1) * half])
        high, low = split_bf16(jnp.concatenate(columns, axis=1))
        value = jnp.dot(high, place_ref[...], preferred_element_type=jnp.float32)
        value += jnp.dot(low, place_ref[...], preferred_element_type=jnp.float32)
        kept = jnp.where(wave_ref[...] < keep, value, 0.0)
        code = scale_code(jnp.max(jnp.abs(kept), axis=0, keepdims=True))
        steps = coded(kept, 1.0 / scale_of(code))
        codes = jnp.broadcast_to(code, (outs[0].shape[0] - rows, code.shape[1]))
        placed.append(as_int16(jnp.concatenate([steps, codes], axis=0)))
    for target in range(lat_count):
        for part in range(2):
            cols = slice(target * LANES, (target + 1) * LANES)
            outs[target][:, part * LANES : (part + 1) * LANES] = placed[part][:, cols]


def fourier(grids, edges, ring, places, wave_row, rows, lat_count):
    pieces = len(grids)
    width = grids[0].shape[1] + LANES
    padded_rows = -(-(rows + 1) // 16) * 16
    tables = [table_bf16(table) for table in fourier_tables(pieces)]
    return pl.pallas_call(
        functools.partial(fourier_kernel, ring, lat_count, pieces),
        out_shape=[jax.ShapeDtypeStruct((padded_rows, 2 * LANES), jnp.int16)] * lat_count,
        in_specs=[VMEM_SPEC] * (pieces + 4),
        out_specs=[VMEM_SPEC] * lat_count,
        scratch_shapes=[pltpu.VMEM((pieces, rows, width), jnp.float32)],
        compiler_params=pltpu.CompilerParams(vmem_limit_bytes=MIDDLE_BYTES),
        cost_estimate=pl.CostEstimate(
            flops=4 * 10**9, bytes_accessed=6 * 2**20, transcendentals=0
        ),
    )(*grids, edges, np.concatenate(tables, axis=-1), places, wave_row)


def places_kernel(groups, slot_ref, place_ref, wave_ref, mine_ref, sorted_rows):
    lat_index = lax.axis_index("lat")
    slots = slot_ref.shape[1] // groups
    paired = (slots + 1) // 2
    shape = (LANES, LANES)
    down = lax.broadcasted_iota(jnp.int32, shape, 0)
    across = lax.broadcasted_iota(jnp.int32, shape, 1)
    filler = jnp.full((1, LANES - slots), 2.0 * M, jnp.float32)
    for group in range(groups):
        plain = slot_ref[:, group * slots : (group + 1) * slots].astype(jnp.float32)
        plain = jnp.concatenate([plain, filler], axis=1)
        row = jnp.broadcast_to(plain, shape)
        column = jnp.sum(jnp.where(down == across, row, 0.0), axis=1, keepdims=True)
        ahead = (row < column) | ((row == column) & (across < down))
        rank = jnp.sum(jnp.where(ahead, 1.0, 0.0), axis=1, keepdims=True)
        place = jnp.where(rank < paired, rank, SIDE + slots - 1.0 - rank)
        place = jnp.where(rank < slots, place, -1.0)
        hot = jnp.where(place == across.astype(jnp.float32), 1.0, 0.0)
        filled = jnp.sum(hot, axis=0, keepdims=True)
        values = jnp.sum(hot * column, axis=0, keepdims=True)
        values = jnp.where(filled > 0.5, values, 2.0 * M)
        sorted_rows[group] = jnp.broadcast_to(values, sorted_rows.shape[1:])

        @pl.when(group == lat_index)
        def _():
            mine_ref[:1] = values
            mine_ref[1:] = plain

    spots = column_waves((place_ref.shape[0], LANES))
    for step in range(groups):
        row = sorted_rows[partner(("lat",), (groups,), step), :1]
        cols = slice(step * LANES, (step + 1) * LANES)
        wave_ref[:, cols] = row
        place_ref[:, cols] = jnp.where(spots == row, 1.0, 0.0).astype(jnp.bfloat16)


def prepare_places(slot_wave, groups):
    width = groups * LANES
    return pl.pallas_call(
        functools.partial(places_kernel, groups),
        out_shape=[
            jax.ShapeDtypeStruct((column_count(), width), jnp.bfloat16),
            jax.ShapeDtypeStruct((1, width), jnp.float32),
            jax.ShapeDtypeStruct((2, LANES), jnp.float32),
        ],
        in_specs=[VMEM_SPEC],
        out_specs=[VMEM_SPEC] * 3,
        scratch_shapes=[pltpu.VMEM((groups, 8, LANES), jnp.float32)],
        compiler_params=pltpu.CompilerParams(vmem_limit_bytes=MIDDLE_BYTES),
        cost_estimate=pl.CostEstimate(flops=2 * 10**9, bytes_accessed=2**20, transcendentals=0),
    )(slot_wave[None])


def lane_pairs(row):
    lane = lax.broadcasted_iota(jnp.int32, row.shape, 1)
    other = pltpu.roll(row, SIDE, 1)
    return jnp.where(lane < SIDE, row, other), jnp.where(lane < SIDE, other, row)


def block_count(wave):
    return jnp.floor((jnp.maximum(M - wave, 0.0) + (BLOCK - 1)) * (1.0 / BLOCK))


def sweep_kernel(
    mine_ref, lat_ref,
    beta_ref, scale_ref, growth_ref, start_ref, state_ref, values_ref, back_ref,
):
    shape = (LANES, LANES)
    same = lax.broadcasted_iota(jnp.int32, shape, 0) == lax.broadcasted_iota(jnp.int32, shape, 1)
    plain = jnp.broadcast_to(mine_ref[1:], shape)
    plain = jnp.sum(jnp.where(same, plain, 0.0), axis=1, keepdims=True)
    hot = (plain == mine_ref[:1]) & (plain < 2.0 * M)
    back_ref[...] = jnp.where(hot, 1.0, 0.0).astype(jnp.bfloat16)
    pair = lane_pairs(jnp.broadcast_to(mine_ref[:1], (8, LANES)))
    one, two = pair[0][:1], pair[1][:1]
    blocks = growth_ref.shape[0]
    turn = block_count(one)
    block = lax.broadcasted_iota(jnp.int32, (blocks, LANES), 0).astype(jnp.float32)
    second = block >= turn
    wave = jnp.where(second, two, one)
    limit = M - wave
    wave = jnp.minimum(wave, M - 1.0)
    first = (block - jnp.where(second, turn, 0.0)) * BLOCK

    scale = jnp.ones((blocks, LANES), jnp.float32)
    for index in range(BLOCK + 1):
        order = first + index
        degree = wave + order
        square = 4.0 * degree * degree - 1.0
        spread = 4.0 * order * (degree + wave)
        if index > 0:
            scale = scale * jnp.sqrt(square / spread)
        if index < BLOCK:
            beta_ref[pl.ds(index, blocks, stride=BLOCK)] = spread / jnp.maximum(square, 1.0)
            scale_ref[pl.ds(index, blocks, stride=BLOCK)] = jnp.where(order < limit, scale, 0.0)
    growth_ref[...] = scale

    counter = lax.broadcasted_iota(jnp.int32, (M, LANES), 0).astype(jnp.float32) + 1.0
    terms = jnp.log(1.0 + 0.5 / counter) * (1.0 / math.log(2.0))
    for kind, wave in enumerate((one, two)):
        wave = jnp.minimum(wave, M - 1.0)
        norm = jnp.sum(jnp.where(counter <= wave, terms, 0.0), axis=0, keepdims=True)
        coarse = lat_ref[1] * wave
        whole = jnp.floor(coarse)
        start_ref[2 * kind] = jnp.exp2(
            (coarse - whole) + lat_ref[2] * wave + 0.5 * (norm - 1.0)
        )
        start_ref[2 * kind + 1] = whole

    state_ref[0] = jnp.zeros_like(state_ref[0])
    state_ref[1] = start_ref[0]
    state_ref[2] = start_ref[1]
    points = lat_ref.shape[1]

    def step(block, carry):
        first = 0
        for chunk in (points // 16 * 8, points - points // 16 * 8):
            rows = slice(first, first + chunk)

            def keep(order, value):
                values_ref[block, order, rows] = value

            sweep_block(block, turn, rows, lat_ref, beta_ref, growth_ref, start_ref, state_ref, keep)
            first += chunk
        return carry

    total = jnp.max(turn + block_count(two)).astype(jnp.int32)
    lax.fori_loop(0, jnp.minimum(total, HELD), step, 0)


def sweep_block(block, turn, rows, lat_ref, beta_ref, growth_ref, start_ref, state_ref, use):
    base = pl.multiple_of(block * BLOCK, BLOCK)
    begins = block.astype(jnp.float32) == turn
    grow = growth_ref[pl.ds(block, 1)]
    cosine = lat_ref[0, rows]
    height = jnp.where(begins, start_ref[3, rows], state_ref[2, rows])
    factor = jnp.exp2(height)
    old = jnp.where(begins, 0.0, state_ref[0, rows])
    new = jnp.where(begins, start_ref[2, rows], state_ref[1, rows])
    for order in range(BLOCK):
        use(order, new * factor)
        beta = beta_ref[pl.ds(base + order, 1)]
        old, new = new, cosine * new - beta * old
    biggest = jnp.maximum(jnp.abs(old), jnp.abs(new)) * grow
    shift = jnp.floor(jnp.log(biggest) * (1.0 / math.log(2.0)))
    factor = grow * jnp.exp2(-shift)
    state_ref[0, rows] = old * factor
    state_ref[1, rows] = new * factor
    state_ref[2, rows] = height + shift


def prepare_recurrence(mine, pieces):
    latitudes = latitude_table()
    points = latitudes.shape[1]
    blocks = 2 * SPAN
    orders = jax.ShapeDtypeStruct((blocks * BLOCK, LANES), jnp.float32)
    return pl.pallas_call(
        sweep_kernel,
        out_shape=[
            orders,
            orders,
            jax.ShapeDtypeStruct((blocks, LANES), jnp.float32),
            jax.ShapeDtypeStruct((4, points, LANES), jnp.float32),
            jax.ShapeDtypeStruct((3, points, LANES), jnp.float32),
            jax.ShapeDtypeStruct((HELD, BLOCK, points, LANES), jnp.float32),
            jax.ShapeDtypeStruct((LANES, LANES), jnp.bfloat16),
        ],
        in_specs=[VMEM_SPEC] * 2,
        out_specs=[VMEM_SPEC] * 7,
        compiler_params=pltpu.CompilerParams(vmem_limit_bytes=late_bytes(pieces)),
        cost_estimate=pl.CostEstimate(
            flops=5 * 10**9, bytes_accessed=25 * 2**20, transcendentals=0
        ),
    )(mine, latitudes)


def resampled(first, fields, table, total):
    for piece, field in enumerate(fields):
        values = from_int16(field[...])
        values = values * scale_of(values[field.shape[0] - 1 :])
        high, low = split_bf16(values)
        spot = partner(("lat",), table.shape[:1], first + piece)
        both = jnp.concatenate([high, low], axis=1)
        part = jnp.dot(table[spot, 0], both, preferred_element_type=jnp.float32)
        part = part[:, : high.shape[1]] + part[:, high.shape[1] :]
        part += jnp.dot(table[spot, 1], high, preferred_element_type=jnp.float32)
        total = part if total is None else total + part
    return total


def resample_kernel(table_ref, *rest):
    rest[-1][...] = resampled(0, rest[:-1], table_ref, None)


def late_bytes(pieces):
    return LATE_BYTES if pieces <= 4 else VMEM_BYTES


def resample(fields, table):
    count, _, height, _ = table.shape
    span = fields[0].shape[1]
    return pl.pallas_call(
        resample_kernel,
        out_shape=jax.ShapeDtypeStruct((height, span), jnp.float32),
        in_specs=[VMEM_SPEC] * (1 + len(fields)),
        out_specs=VMEM_SPEC,
        compiler_params=pltpu.CompilerParams(vmem_limit_bytes=late_bytes(count)),
        cost_estimate=pl.CostEstimate(
            flops=10**9, bytes_accessed=4 * 2**20, transcendentals=0
        ),
    )(table, *fields)


def legendre_kernel(early, *rest):
    table, lat_ref, beta_ref, scale_ref, growth_ref, start_ref, left_ref, values_ref, back_ref = rest[:9]
    total_ref, mine_ref = rest[9:11]
    fields, (out_ref, weights, state_ref, sums, result, final) = rest[11:-6], rest[-6:]
    points = lat_ref.shape[1]
    slots = out_ref.shape[0]
    mine = mine_ref[:1]
    odd = mine - 2.0 * jnp.floor(mine * 0.5) > 0.5
    pair = lane_pairs(jnp.broadcast_to(mine, (8, LANES)))
    turn = block_count(pair[0][:1])
    block_total = jnp.max(turn + block_count(pair[1][:1])).astype(jnp.int32)

    total = resampled(early, fields, table, total_ref[...])
    totals = [total[2 * points * kind : 2 * points * (kind + 1)] for kind in range(4)]
    left = lax.broadcasted_iota(jnp.int32, (points, LANES), 1) < SIDE
    for parity in range(2):
        for comp in range(2):
            cols = slice(comp * LANES, (comp + 1) * LANES)
            value = jnp.where(odd, totals[2 + parity][:, cols], totals[parity][:, cols])
            top, bottom = value[:points], value[points:]
            kind = 2 * parity + comp
            weights[0, kind] = jnp.where(left, top, pltpu.roll(bottom, SIDE, 1))
            weights[1, kind] = jnp.where(left, pltpu.roll(top, SIDE, 1), bottom)
    result[...] = jnp.zeros_like(result)
    state_ref[...] = left_ref[...]

    def reduced(block):
        base = pl.multiple_of(block * BLOCK, BLOCK)
        for comp in range(2):
            total = sums[pl.ds(comp * 8, BLOCK, stride=16)]
            for lane in range(1, 8):
                total += sums[pl.ds(comp * 8 + lane, BLOCK, stride=16)]
            total = total * scale_ref[pl.ds(base, BLOCK)]
            result[comp, pl.ds(base, BLOCK)] = total + pltpu.roll(total, SIDE, 1)

    def held_step(block, carry):
        second = block.astype(jnp.float32) >= turn
        for parity in range(2):
            scaled = [
                jnp.where(second, weights[1, 2 * parity + comp], weights[0, 2 * parity + comp])
                for comp in range(2)
            ]
            for order in range(parity, BLOCK, 2):
                value = values_ref[block, order]
                for comp in range(2):
                    product = (value * scaled[comp]).reshape(points // 8, 8, LANES)
                    sums[pl.ds((order * 2 + comp) * 8, 8)] = product.sum(axis=0)
        reduced(block)
        return carry

    def step(block, carry):
        second = block.astype(jnp.float32) >= turn
        first = 0
        for chunk in CHUNKS:
            rows = slice(first, first + chunk)
            scaled = [jnp.where(second, weights[1, k, rows], weights[0, k, rows]) for k in range(4)]

            def add(order, value):
                for comp in range(2):
                    product = value * scaled[2 * (order % 2) + comp]
                    partial = product.reshape(chunk // 8, 8, LANES).sum(axis=0)
                    place = pl.ds((order * 2 + comp) * 8, 8)
                    if first == 0:
                        sums[place] = partial
                    else:
                        sums[place] += partial

            sweep_block(block, turn, rows, lat_ref, beta_ref, growth_ref, start_ref, state_ref, add)
            first += chunk
        reduced(block)
        return carry

    lax.fori_loop(0, jnp.minimum(block_total, HELD), held_step, 0)
    lax.fori_loop(HELD, block_total, step, 0)

    left = lax.broadcasted_iota(jnp.int32, (BLOCK, LANES), 1) < SIDE
    spots = SPAN
    chosen = [jnp.broadcast_to(turn, (8, LANES)) == value for value in range(spots + 1)]
    chosen = [jnp.concatenate([mask] * (BLOCK // 8), axis=0) for mask in chosen]
    for place in range(spots):
        rows = slice(place * BLOCK, (place + 1) * BLOCK)
        for comp in range(2):
            early_part = jnp.where(turn > place, result[comp, rows], 0.0)
            later = jnp.zeros((BLOCK, LANES), jnp.float32)
            for value in range(spots + 1):
                base = (place + value) * BLOCK
                if base < result.shape[1]:
                    later = jnp.where(chosen[value], result[comp, base : base + BLOCK], later)
            final[comp, rows] = jnp.where(left, early_part, later)
    back = back_ref[...]
    dims = (((1,), (1,)), ((), ()))
    for comp in range(2):
        high, low = split_bf16(final[comp])
        value = lax.dot_general(back, high, dims, preferred_element_type=jnp.float32)
        value += lax.dot_general(back, low, dims, preferred_element_type=jnp.float32)
        out_ref[:, comp, :] = value[:slots, :M]


def resample_pieces(pieces, rows, padded_rows):
    full = resample_table()
    table = full.reshape(full.shape[0], pieces, rows).transpose(1, 0, 2)
    table = table_bf16(np.pad(table, ((0, 0), (0, 0), (0, padded_rows - rows))))
    return table.reshape(pieces, full.shape[0], 2, padded_rows).transpose(0, 2, 1, 3)


def legendre(fields, mine, prepared, rows, slots):
    pieces = len(fields)
    early = pieces // 2
    latitudes = latitude_table()
    points = latitudes.shape[1]
    table = jnp.asarray(resample_pieces(pieces, rows, fields[0].shape[0]))
    total = resample(fields[:early], table)
    block_rows = SPAN * BLOCK
    return pl.pallas_call(
        functools.partial(legendre_kernel, early),
        out_shape=jax.ShapeDtypeStruct((slots, 2, M), jnp.float32),
        in_specs=[VMEM_SPEC] * (11 + pieces - early),
        out_specs=VMEM_SPEC,
        scratch_shapes=[
            pltpu.VMEM((2, 4, points, LANES), jnp.float32),
            pltpu.VMEM((3, points, LANES), jnp.float32),
            pltpu.VMEM((BLOCK * 16, LANES), jnp.float32),
            pltpu.VMEM((2, 2 * block_rows, LANES), jnp.float32),
            pltpu.VMEM((2, block_rows, LANES), jnp.float32),
        ],
        compiler_params=pltpu.CompilerParams(vmem_limit_bytes=late_bytes(pieces)),
        cost_estimate=pl.CostEstimate(
            flops=8 * 10**9, bytes_accessed=6 * 2**20, transcendentals=0
        ),
    )(table, latitudes, *prepared, total, mine, *fields[early:])


def shards(tracer, wind_east, wind_north, keep_m, slot_wave):
    rows = tracer.shape[1]
    lat_count = lax.axis_size("lat")
    slots = slot_wave.shape[0] // lat_count
    axes = ("lev", "fld")
    ring = (axes, tuple(lax.axis_size(axis) for axis in axes))

    blocks, edges = advect(tracer, wind_east, wind_north, keep_m, ring)
    blocks, slot_wave = lax.optimization_barrier((blocks, slot_wave))
    grids = exchange(blocks, axes)
    edges = lax.all_to_all(edges, ("lat", *axes), split_axis=0, concat_axis=0, tiled=True)
    places, wave_row, mine = prepare_places(slot_wave, lat_count)
    waved = fourier(grids, edges, ring, places, wave_row, rows, lat_count)
    waved, mine = lax.optimization_barrier((list(waved), mine))
    fields = exchange(waved, "lat")
    prepared = prepare_recurrence(mine, lat_count)
    return legendre(fields, mine, prepared, rows, slots)[None]


def solution(mesh):
    return jax.shard_map(
        shards,
        mesh=mesh,
        in_specs=(
            P("member", "lat", ("lev", "fld")),
            P("member", "lat", ("lev", "fld")),
            P("member", "lat", ("lev", "fld")),
            P("lat"),
            P(),
        ),
        out_specs=P(("member", "lev", "fld"), "lat", None, None),
        check_vma=False,
    )
```

```python
import functools
import math

import jax
import jax.numpy as jnp
import numpy as np
from jax import lax
from jax.experimental import pallas as pl
from jax.experimental.pallas import tpu as pltpu
from jax.sharding import PartitionSpec as P

M = 400
NLAT = 800
NLON = 1600
LANES = 128
BLOCK = 32
CHUNKS = (40, 32, 32)
SPAN = -(-M // BLOCK)
HELD = 13
SIDE = LANES // 2
TOP = 32767.0
WIND_STEP = 1.5 / TOP
VMEM_BYTES = 60 * 2**20
LATE_BYTES = 16 * 2**20
MIDDLE_BYTES = 16 * 2**20
VMEM_SPEC = pl.BlockSpec(memory_space=pltpu.VMEM)
SMEM_SPEC = pl.BlockSpec(memory_space=pltpu.SMEM)
HBM_SPEC = pl.BlockSpec(memory_space=pltpu.HBM)


def split_bf16(values):
    high = values.astype(jnp.bfloat16)
    low = (values - high.astype(jnp.float32)).astype(jnp.bfloat16)
    return high, low


def table_bf16(table):
    high = table.astype(jnp.bfloat16)
    low = (table - high.astype(np.float64)).astype(jnp.bfloat16)
    return np.concatenate([high, low], axis=-1)


def fourier_tables(pieces):
    quarter = NLON // 4
    spots = np.arange(quarter)[:, None]
    factor = 1.0 / math.sqrt(NLON)

    def parts(waves):
        angles = 2.0 * math.pi / NLON * (spots * waves[None, :] % NLON)
        return factor * np.cos(angles), factor * np.sin(angles)

    def shaped(columns):
        pad = [(0, 0), (0, -columns[0].shape[1] % LANES)]
        table = np.concatenate([np.pad(part, pad) for part in columns], axis=1)
        return table.reshape(share, quarter // share, -1)

    share = pieces // 4
    tables = []
    for first in (0, 2):
        cosine, sine = parts(np.arange(first, M, 4))
        tables.append(shaped([cosine, -sine]))
    waves = np.arange(1, M, 2)
    sign = np.where(waves % 4 == 1, 1.0, -1.0)[None, :]
    cosine, sine = parts(waves)
    return [*tables, shaped([cosine, -sine]), shaped([-sign * sine, -sign * cosine])]


def column_waves(shape):
    row = lax.broadcasted_iota(jnp.int32, shape, 0)
    waves, first = jnp.full(shape, -1, jnp.int32), 0
    for start, step in ((0, 4), (2, 4), (1, 2)):
        count = len(range(start, M, step))
        inside = (row >= first) & (row < first + count)
        waves = jnp.where(inside, start + step * (row - first), waves)
        first += -(-count // LANES) * LANES
    return waves.astype(jnp.float32)


def column_count():
    return sum(-(-len(range(start, M, step)) // LANES) * LANES for start, step in ((0, 4), (2, 4), (1, 2)))


def resample_table():
    half = M // 2
    coarse = math.pi / M * (np.arange(M) + 0.5)
    fine = math.pi / NLAT * (np.arange(NLAT) + 0.5)
    waves = np.arange(M)
    weight = np.where(waves == 0, 1.0, 2.0) / M
    even = (np.cos(np.outer(coarse, waves)) * weight) @ np.cos(np.outer(waves, fine))
    odd = (np.sin(np.outer(coarse, waves)) * weight) @ np.sin(np.outer(waves, fine))
    rows = []
    for full in (even, odd):
        for sign in (1.0, -1.0):
            folded = (full[:half] + sign * full[::-1][:half]).reshape(2, half // 2, NLAT)
            rows.append(np.pad(folded, ((0, 0), (0, -half // 2 % 8), (0, 0))).reshape(-1, NLAT))
    return np.concatenate(rows, axis=0) * (np.sin(fine) * math.sqrt(2.0 / NLAT))


def latitude_table():
    half = M // 2
    angles = math.pi / M * (np.arange(half) + 0.5)
    log_sine = np.log2(np.sin(angles))
    coarse = np.round(log_sine * 1024.0) / 1024.0
    rows = np.stack([2.0 * np.cos(angles), coarse, log_sine - coarse]).reshape(3, 2, half // 2)
    rows = np.pad(rows, ((0, 0), (0, 0), (0, -half // 2 % 8)))
    return np.repeat(rows.transpose(0, 2, 1), SIDE, axis=2).astype(np.float32)


def scale_code(biggest):
    wanted = jnp.maximum(biggest, 1e-30) * (1.0 / TOP)
    exponent = jnp.floor(jnp.log(wanted) * (1.0 / math.log(2.0)))
    return exponent * 128.0 + jnp.ceil((wanted * jnp.exp2(-exponent) - 1.0) * 128.0)


def scale_of(code):
    exponent = jnp.floor(code * (1.0 / 128.0))
    rest = code - 128.0 * exponent
    return jnp.exp2(exponent) * (1.0 + rest * (1.0 / 128.0))


def coded(values, inverse):
    return jnp.floor(values * inverse + 0.5)


def as_int16(values):
    return values.astype(jnp.int32).astype(jnp.int16)


def from_int16(codes):
    return codes.astype(jnp.int32).astype(jnp.float32)


def partner(axes, sizes, step):
    count = math.prod(sizes)
    if count != 4:
        return step
    index = lax.axis_index(axes[0])
    for axis, size in zip(axes[1:], sizes[1:]):
        index = index * size + lax.axis_index(axis)
    return index ^ step


def exchange(blocks, axis):
    count = len(blocks)
    if count != 4:
        return list(lax.all_to_all(jnp.stack(blocks), axis, split_axis=0, concat_axis=0, tiled=True))
    pairs = [[(i, i ^ step) for i in range(count)] for step in range(count)]
    return [blocks[0]] + [lax.ppermute(blocks[step], axis, pairs[step]) for step in range(1, count)]


def advect_kernel(ring, lat_count, keep_ref, tracer_hbm, east_hbm, north_hbm, *rest):
    levels, rows, lons = tracer_hbm.shape
    outs, (edge_ref, tracer, east_wind, north_wind, sems) = rest[:levels], rest[levels:]
    chosen = [partner(*ring, step) for step in range(levels)]
    copies = [None] * levels
    order = (*range(levels // 2, levels), *range(levels // 2))
    for step in order:
        copies[step] = [
            pltpu.make_async_copy(source.at[chosen[step]], target.at[step], sems.at[kind, step])
            for kind, (source, target) in enumerate(
                ((tracer_hbm, tracer), (east_hbm, east_wind), (north_hbm, north_wind))
            )
        ]
        for copy in copies[step]:
            copy.start()
    padded_rows = outs[0].shape[0]
    same = (rows, rows)
    same = lax.broadcasted_iota(jnp.int32, same, 0) == lax.broadcasted_iota(jnp.int32, same, 1)
    keep = jnp.broadcast_to(keep_ref[...].astype(jnp.float32), (rows, rows))
    keep = jnp.sum(jnp.where(same, keep, 0.0), axis=1, keepdims=True)
    end = (lons - 1) // LANES * LANES
    spare = lons - end
    lane = lax.broadcasted_iota(jnp.int32, (rows, LANES), 1)
    lat_index = lax.axis_index("lat")
    edge_ref[...] = jnp.zeros_like(edge_ref)
    for step in order:
        level = chosen[step]
        for copy in copies[step]:
            copy.wait()
        field = tracer[step].astype(jnp.float32)

        @pl.when(lat_index < lat_count - 1)
        def _():
            edge_ref[(lat_index + 1) * levels + level] = field[rows - 1 :]

        @pl.when(lat_index > 0)
        def _():
            edge_ref[(lat_index - 1) * levels + level] = field[:1]

        blank = jnp.zeros((rows, 1), jnp.float32)
        west = jnp.concatenate([blank, field[:, :-1]], axis=1)
        east = jnp.concatenate([field[:, 1:], blank], axis=1)
        blank = jnp.zeros((1, lons), jnp.float32)
        north = jnp.concatenate([blank, field[:-1]], axis=0)
        south = jnp.concatenate([field[1:], blank], axis=0)
        eastward = 0.5 * east_wind[step].astype(jnp.float32)
        northward = 0.5 * north_wind[step].astype(jnp.float32)
        moved = field - eastward * (east - west) - northward * (south - north)
        first, last = field[:, :1], field[:, lons - 1 :]
        biggest = jnp.max(jnp.abs(moved), axis=1, keepdims=True)
        biggest = jnp.maximum(biggest, jnp.maximum(jnp.abs(first), jnp.abs(last)))
        code = scale_code(biggest)
        inverse = 1.0 / scale_of(code)
        filler = jnp.zeros((rows, LANES - spare), jnp.float32)
        tile = jnp.concatenate([moved[:, end:], filler], axis=1)
        tile = jnp.where(lane == spare + 1, first, jnp.where(lane == spare + 2, last, tile))
        tile = coded(tile, inverse)
        tile = jnp.where(lane == spare, code, tile)
        winds = jnp.where(lane == spare + 3, eastward[:, :1], eastward[:, lons - 1 :])
        winds = coded(winds, 1.0 / WIND_STEP)
        tile = jnp.where((lane == spare + 3) | (lane == spare + 4), winds, tile)
        tile = jnp.where(lane == spare + 5, keep, tile)
        wind_rows = jnp.concatenate([northward[:1], northward[rows - 1 :]], axis=0)
        wind_rows = coded(wind_rows, 1.0 / WIND_STEP)
        blank = jnp.zeros((padded_rows - rows - 2, lons), jnp.float32)
        wind_rows = jnp.concatenate([wind_rows, blank], axis=0)
        filler = jnp.zeros((padded_rows - rows, LANES - spare), jnp.float32)
        wind_tile = jnp.concatenate([wind_rows[:, end:], filler], axis=1)
        steps = jnp.concatenate([coded(moved[:, :end], inverse), wind_rows[:, :end]], axis=0)
        outs[step][:, :end] = as_int16(steps)
        outs[step][:, end:] = as_int16(jnp.concatenate([tile, wind_tile], axis=0))


def advect(tracer, east_wind, north_wind, keep_m, ring):
    levels, rows, lons = tracer.shape
    lat_count = lax.axis_size("lat")
    width = (lons - 1) // LANES * LANES + LANES
    padded_rows = -(-(rows + 2) // 16) * 16
    held = pltpu.VMEM((levels, rows, lons), jnp.bfloat16)
    result = pl.pallas_call(
        functools.partial(advect_kernel, ring, lat_count),
        out_shape=[jax.ShapeDtypeStruct((padded_rows, width), jnp.int16)] * levels
        + [jax.ShapeDtypeStruct((lat_count * levels, 1, lons), jnp.float32)],
        in_specs=[VMEM_SPEC] + [HBM_SPEC] * 3,
        out_specs=[VMEM_SPEC] * (levels + 1),
        scratch_shapes=[held, held, held, pltpu.SemaphoreType.DMA((3, levels))],
        compiler_params=pltpu.CompilerParams(vmem_limit_bytes=VMEM_BYTES),
        cost_estimate=pl.CostEstimate(
            flops=5 * 10**9, bytes_accessed=8 * levels * rows * lons, transcendentals=0
        ),
    )(keep_m[None], tracer, east_wind, north_wind)
    return list(result[:levels]), result[levels]


def fourier_kernel(ring, lat_count, pieces, *rest):
    grids, (edge_ref, table_ref, wave_ref) = rest[:pieces], rest[pieces : pieces + 3]
    outs, field = rest[pieces + 3 : -1], rest[-1]
    _, rows, width = field.shape
    lons = table_ref.shape[1]
    share = pieces // 4

    end = width - LANES
    spare = lons - end
    lane = lax.broadcasted_iota(jnp.int32, (rows, LANES), 1)
    winds = (lane == spare + 3) | (lane == spare + 4)
    lat_index = lax.axis_index("lat")
    for piece in range(pieces):
        spot = partner(*ring, piece)
        values = from_int16(grids[piece][...])
        tile = values[:rows, end:]
        scale = scale_of(tile[:, spare : spare + 1])
        keep = tile[:, spare + 5 : spare + 6]
        field[spot, :, :end] = values[:rows, :end] * scale
        field[spot, :, end:] = tile * jnp.where(winds, WIND_STEP, scale)
        wind_rows = values[rows : rows + 2, :lons] * WIND_STEP

        @pl.when(lat_index > 0)
        def _():
            above = edge_ref[(lat_index - 1) * pieces + spot]
            field[spot, :1, :lons] += wind_rows[:1] * above

        @pl.when(lat_index < lat_count - 1)
        def _():
            below = edge_ref[(lat_index + 1) * pieces + spot]
            field[spot, rows - 1 :, :lons] -= wind_rows[1:] * below

    for spot in range(pieces):
        tile = field[spot, :, end:]
        before = field[(spot - 1) % pieces, :, end:]
        after = field[(spot + 1) % pieces, :, end:]
        shift = LANES - spare
        gain = pltpu.roll(tile, shift - 3, 1) * pltpu.roll(before, shift - 2, 1)
        loss = pltpu.roll(tile, LANES - 5, 1) * pltpu.roll(after, LANES - 2, 1)
        field[spot, :, end:] = tile - jnp.where(lane == spare - 1, loss, 0.0)
        field[spot, :, :LANES] += jnp.where(lane == 0, gain, 0.0)

    spans = [2 * LANES, 2 * LANES, 4 * LANES, 4 * LANES]

    def product(kind, value, spot):
        high, low = split_bf16(value)
        first, span = 2 * sum(spans[:kind]), spans[kind]
        both = jnp.dot(high, table_ref[spot, :, first : first + 2 * span], preferred_element_type=jnp.float32)
        part = jnp.dot(low, table_ref[spot, :, first : first + span], preferred_element_type=jnp.float32)
        return part + both[:, :span] + both[:, span:]

    sums = [None, None, None]
    for spot in range(share):
        quarters = [field[quarter * share + spot, :, :lons] for quarter in range(4)]
        sum02, dif02 = quarters[0] + quarters[2], quarters[0] - quarters[2]
        sum13, dif13 = quarters[1] + quarters[3], quarters[1] - quarters[3]
        parts = []
        for kind, value in enumerate((sum02 + sum13, sum02 - sum13, dif02, dif13)):
            parts.append(product(kind, value, spot))
        parts = [parts[0], parts[1], parts[2] + parts[3]]
        sums = [part if total is None else total + part for total, part in zip(sums, parts)]
    slot_waves = wave_ref[...]
    waves = column_waves((column_count(), LANES))
    places = [
        jnp.where(waves == slot_waves[:, first : first + LANES], 1.0, 0.0).astype(jnp.bfloat16)
        for first in range(0, slot_waves.shape[1], LANES)
    ]
    places = jnp.concatenate(places, axis=1)
    placed = []
    for part in range(2):
        columns = []
        for total in sums:
            half = total.shape[1] // 2
            columns.append(total[:, part * half : (part + 1) * half])
        high, low = split_bf16(jnp.concatenate(columns, axis=1))
        value = jnp.dot(high, places, preferred_element_type=jnp.float32)
        value += jnp.dot(low, places, preferred_element_type=jnp.float32)
        kept = jnp.where(slot_waves < keep, value, 0.0)
        code = scale_code(jnp.max(jnp.abs(kept), axis=0, keepdims=True))
        steps = coded(kept, 1.0 / scale_of(code))
        codes = jnp.broadcast_to(code, (outs[0].shape[0] - rows, code.shape[1]))
        placed.append(as_int16(jnp.concatenate([steps, codes], axis=0)))
    for target in range(lat_count):
        for part in range(2):
            cols = slice(target * LANES, (target + 1) * LANES)
            outs[target][:, part * LANES : (part + 1) * LANES] = placed[part][:, cols]


def fourier(grids, edges, ring, wave_row, rows, lat_count):
    pieces = len(grids)
    width = grids[0].shape[1]
    padded_rows = -(-(rows + 1) // 16) * 16
    tables = [table_bf16(table) for table in fourier_tables(pieces)]
    return pl.pallas_call(
        functools.partial(fourier_kernel, ring, lat_count, pieces),
        out_shape=[jax.ShapeDtypeStruct((padded_rows, 2 * LANES), jnp.int16)] * lat_count,
        in_specs=[VMEM_SPEC] * (pieces + 3),
        out_specs=[VMEM_SPEC] * lat_count,
        scratch_shapes=[pltpu.VMEM((pieces, rows, width), jnp.float32)],
        compiler_params=pltpu.CompilerParams(vmem_limit_bytes=MIDDLE_BYTES),
        cost_estimate=pl.CostEstimate(
            flops=4 * 10**9, bytes_accessed=6 * 2**20, transcendentals=0
        ),
    )(*grids, edges, np.concatenate(tables, axis=-1), wave_row)


def places_kernel(groups, slot_ref, wave_ref, mine_ref, sorted_rows):
    lat_index = lax.axis_index("lat")
    slots = slot_ref.shape[1] // groups
    paired = (slots + 1) // 2
    shape = (LANES, LANES)
    down = lax.broadcasted_iota(jnp.int32, shape, 0)
    across = lax.broadcasted_iota(jnp.int32, shape, 1)
    filler = jnp.full((1, LANES - slots), 2.0 * M, jnp.float32)
    for group in range(groups):
        plain = slot_ref[:, group * slots : (group + 1) * slots].astype(jnp.float32)
        plain = jnp.concatenate([plain, filler], axis=1)
        row = jnp.broadcast_to(plain, shape)
        column = jnp.sum(jnp.where(down == across, row, 0.0), axis=1, keepdims=True)
        ahead = (row < column) | ((row == column) & (across < down))
        rank = jnp.sum(jnp.where(ahead, 1.0, 0.0), axis=1, keepdims=True)
        place = jnp.where(rank < paired, rank, SIDE + slots - 1.0 - rank)
        place = jnp.where(rank < slots, place, -1.0)
        hot = jnp.where(place == across.astype(jnp.float32), 1.0, 0.0)
        filled = jnp.sum(hot, axis=0, keepdims=True)
        values = jnp.sum(hot * column, axis=0, keepdims=True)
        values = jnp.where(filled > 0.5, values, 2.0 * M)
        sorted_rows[group] = jnp.broadcast_to(values, sorted_rows.shape[1:])

        @pl.when(group == lat_index)
        def _():
            mine_ref[:1] = values
            mine_ref[1:] = plain

    for step in range(groups):
        row = sorted_rows[partner(("lat",), (groups,), step), :1]
        wave_ref[:, step * LANES : (step + 1) * LANES] = row


def prepare_places(slot_wave, groups):
    width = groups * LANES
    return pl.pallas_call(
        functools.partial(places_kernel, groups),
        out_shape=[
            jax.ShapeDtypeStruct((1, width), jnp.float32),
            jax.ShapeDtypeStruct((2, LANES), jnp.float32),
        ],
        in_specs=[VMEM_SPEC],
        out_specs=[VMEM_SPEC] * 2,
        scratch_shapes=[pltpu.VMEM((groups, 8, LANES), jnp.float32)],
        compiler_params=pltpu.CompilerParams(vmem_limit_bytes=MIDDLE_BYTES),
        cost_estimate=pl.CostEstimate(flops=2 * 10**9, bytes_accessed=2**20, transcendentals=0),
    )(slot_wave[None])


def lane_pairs(row):
    lane = lax.broadcasted_iota(jnp.int32, row.shape, 1)
    other = pltpu.roll(row, SIDE, 1)
    return jnp.where(lane < SIDE, row, other), jnp.where(lane < SIDE, other, row)


def block_count(wave):
    return jnp.floor((jnp.maximum(M - wave, 0.0) + (BLOCK - 1)) * (1.0 / BLOCK))


def sweep_kernel(
    mine_ref, lat_ref,
    beta_ref, scale_ref, growth_ref, start_ref, state_ref, values_ref, back_ref,
):
    shape = (LANES, LANES)
    same = lax.broadcasted_iota(jnp.int32, shape, 0) == lax.broadcasted_iota(jnp.int32, shape, 1)
    plain = jnp.broadcast_to(mine_ref[1:], shape)
    plain = jnp.sum(jnp.where(same, plain, 0.0), axis=1, keepdims=True)
    hot = (plain == mine_ref[:1]) & (plain < 2.0 * M)
    back_ref[...] = jnp.where(hot, 1.0, 0.0).astype(jnp.bfloat16)
    pair = lane_pairs(jnp.broadcast_to(mine_ref[:1], (8, LANES)))
    one, two = pair[0][:1], pair[1][:1]
    blocks = growth_ref.shape[0]
    turn = block_count(one)
    block = lax.broadcasted_iota(jnp.int32, (blocks, LANES), 0).astype(jnp.float32)
    second = block >= turn
    wave = jnp.where(second, two, one)
    limit = M - wave
    wave = jnp.minimum(wave, M - 1.0)
    first = (block - jnp.where(second, turn, 0.0)) * BLOCK

    scale = jnp.ones((blocks, LANES), jnp.float32)
    for index in range(BLOCK + 1):
        order = first + index
        degree = wave + order
        square = 4.0 * degree * degree - 1.0
        spread = 4.0 * order * (degree + wave)
        if index > 0:
            scale = scale * jnp.sqrt(square / spread)
        if index < BLOCK:
            beta_ref[pl.ds(index, blocks, stride=BLOCK)] = spread / jnp.maximum(square, 1.0)
            scale_ref[pl.ds(index, blocks, stride=BLOCK)] = jnp.where(order < limit, scale, 0.0)
    growth_ref[...] = scale

    counter = lax.broadcasted_iota(jnp.int32, (M, LANES), 0).astype(jnp.float32) + 1.0
    terms = jnp.log(1.0 + 0.5 / counter) * (1.0 / math.log(2.0))
    for kind, wave in enumerate((one, two)):
        wave = jnp.minimum(wave, M - 1.0)
        norm = jnp.sum(jnp.where(counter <= wave, terms, 0.0), axis=0, keepdims=True)
        coarse = lat_ref[1] * wave
        whole = jnp.floor(coarse)
        start_ref[2 * kind] = jnp.exp2(
            (coarse - whole) + lat_ref[2] * wave + 0.5 * (norm - 1.0)
        )
        start_ref[2 * kind + 1] = whole

    state_ref[0] = jnp.zeros_like(state_ref[0])
    state_ref[1] = start_ref[0]
    state_ref[2] = start_ref[1]
    points = lat_ref.shape[1]

    def step(block, carry):
        first = 0
        for chunk in (points // 16 * 8, points - points // 16 * 8):
            rows = slice(first, first + chunk)

            def keep(order, value):
                values_ref[block, order, rows] = value

            sweep_block(block, turn, rows, lat_ref, beta_ref, growth_ref, start_ref, state_ref, keep)
            first += chunk
        return carry

    total = jnp.max(turn + block_count(two)).astype(jnp.int32)
    lax.fori_loop(0, jnp.minimum(total, HELD), step, 0)


def sweep_block(block, turn, rows, lat_ref, beta_ref, growth_ref, start_ref, state_ref, use):
    base = pl.multiple_of(block * BLOCK, BLOCK)
    begins = block.astype(jnp.float32) == turn
    grow = growth_ref[pl.ds(block, 1)]
    cosine = lat_ref[0, rows]
    height = jnp.where(begins, start_ref[3, rows], state_ref[2, rows])
    factor = jnp.exp2(height)
    old = jnp.where(begins, 0.0, state_ref[0, rows])
    new = jnp.where(begins, start_ref[2, rows], state_ref[1, rows])
    for order in range(BLOCK):
        use(order, new * factor)
        beta = beta_ref[pl.ds(base + order, 1)]
        old, new = new, cosine * new - beta * old
    biggest = jnp.maximum(jnp.abs(old), jnp.abs(new)) * grow
    shift = jnp.floor(jnp.log(biggest) * (1.0 / math.log(2.0)))
    factor = grow * jnp.exp2(-shift)
    state_ref[0, rows] = old * factor
    state_ref[1, rows] = new * factor
    state_ref[2, rows] = height + shift


def prepare_recurrence(mine, pieces):
    latitudes = latitude_table()
    points = latitudes.shape[1]
    blocks = 2 * SPAN
    orders = jax.ShapeDtypeStruct((blocks * BLOCK, LANES), jnp.float32)
    return pl.pallas_call(
        sweep_kernel,
        out_shape=[
            orders,
            orders,
            jax.ShapeDtypeStruct((blocks, LANES), jnp.float32),
            jax.ShapeDtypeStruct((4, points, LANES), jnp.float32),
            jax.ShapeDtypeStruct((3, points, LANES), jnp.float32),
            jax.ShapeDtypeStruct((HELD, BLOCK, points, LANES), jnp.float32),
            jax.ShapeDtypeStruct((LANES, LANES), jnp.bfloat16),
        ],
        in_specs=[VMEM_SPEC] * 2,
        out_specs=[VMEM_SPEC] * 7,
        compiler_params=pltpu.CompilerParams(vmem_limit_bytes=late_bytes(pieces)),
        cost_estimate=pl.CostEstimate(
            flops=5 * 10**9, bytes_accessed=25 * 2**20, transcendentals=0
        ),
    )(mine, latitudes)


def resampled(first, fields, table, total):
    for piece, field in enumerate(fields):
        values = from_int16(field[...])
        values = values * scale_of(values[field.shape[0] - 1 :])
        high, low = split_bf16(values)
        spot = partner(("lat",), table.shape[:1], first + piece)
        both = jnp.concatenate([high, low], axis=1)
        part = jnp.dot(table[spot, 0], both, preferred_element_type=jnp.float32)
        part = part[:, : high.shape[1]] + part[:, high.shape[1] :]
        part += jnp.dot(table[spot, 1], high, preferred_element_type=jnp.float32)
        total = part if total is None else total + part
    return total


def resample_kernel(table_ref, *rest):
    rest[-1][...] = resampled(0, rest[:-1], table_ref, None)


def late_bytes(pieces):
    return LATE_BYTES if pieces <= 4 else VMEM_BYTES


def resample(fields, table):
    count, _, height, _ = table.shape
    span = fields[0].shape[1]
    return pl.pallas_call(
        resample_kernel,
        out_shape=jax.ShapeDtypeStruct((height, span), jnp.float32),
        in_specs=[VMEM_SPEC] * (1 + len(fields)),
        out_specs=VMEM_SPEC,
        compiler_params=pltpu.CompilerParams(vmem_limit_bytes=late_bytes(count)),
        cost_estimate=pl.CostEstimate(
            flops=10**9, bytes_accessed=4 * 2**20, transcendentals=0
        ),
    )(table, *fields)


def legendre_kernel(early, *rest):
    table, lat_ref, beta_ref, scale_ref, growth_ref, start_ref, left_ref, values_ref, back_ref = rest[:9]
    total_ref, mine_ref = rest[9:11]
    fields, (out_ref, weights, state_ref, sums, result, final) = rest[11:-6], rest[-6:]
    points = lat_ref.shape[1]
    slots = out_ref.shape[0]
    mine = mine_ref[:1]
    odd = mine - 2.0 * jnp.floor(mine * 0.5) > 0.5
    pair = lane_pairs(jnp.broadcast_to(mine, (8, LANES)))
    turn = block_count(pair[0][:1])
    block_total = jnp.max(turn + block_count(pair[1][:1])).astype(jnp.int32)

    total = resampled(early, fields, table, total_ref[...])
    totals = [total[2 * points * kind : 2 * points * (kind + 1)] for kind in range(4)]
    left = lax.broadcasted_iota(jnp.int32, (points, LANES), 1) < SIDE
    for parity in range(2):
        for comp in range(2):
            cols = slice(comp * LANES, (comp + 1) * LANES)
            value = jnp.where(odd, totals[2 + parity][:, cols], totals[parity][:, cols])
            top, bottom = value[:points], value[points:]
            kind = 2 * parity + comp
            weights[0, kind] = jnp.where(left, top, pltpu.roll(bottom, SIDE, 1))
            weights[1, kind] = jnp.where(left, pltpu.roll(top, SIDE, 1), bottom)
    result[...] = jnp.zeros_like(result)
    state_ref[...] = left_ref[...]

    def reduced(block):
        base = pl.multiple_of(block * BLOCK, BLOCK)
        for comp in range(2):
            total = sums[pl.ds(comp * 8, BLOCK, stride=16)]
            for lane in range(1, 8):
                total += sums[pl.ds(comp * 8 + lane, BLOCK, stride=16)]
            total = total * scale_ref[pl.ds(base, BLOCK)]
            result[comp, pl.ds(base, BLOCK)] = total + pltpu.roll(total, SIDE, 1)

    def held_step(block, carry):
        second = block.astype(jnp.float32) >= turn
        for parity in range(2):
            scaled = [
                jnp.where(second, weights[1, 2 * parity + comp], weights[0, 2 * parity + comp])
                for comp in range(2)
            ]
            for order in range(parity, BLOCK, 2):
                value = values_ref[block, order]
                for comp in range(2):
                    product = (value * scaled[comp]).reshape(points // 8, 8, LANES)
                    sums[pl.ds((order * 2 + comp) * 8, 8)] = product.sum(axis=0)
        reduced(block)
        return carry

    def step(block, carry):
        second = block.astype(jnp.float32) >= turn
        first = 0
        for chunk in CHUNKS:
            rows = slice(first, first + chunk)
            scaled = [jnp.where(second, weights[1, k, rows], weights[0, k, rows]) for k in range(4)]

            def add(order, value):
                for comp in range(2):
                    product = value * scaled[2 * (order % 2) + comp]
                    partial = product.reshape(chunk // 8, 8, LANES).sum(axis=0)
                    place = pl.ds((order * 2 + comp) * 8, 8)
                    if first == 0:
                        sums[place] = partial
                    else:
                        sums[place] += partial

            sweep_block(block, turn, rows, lat_ref, beta_ref, growth_ref, start_ref, state_ref, add)
            first += chunk
        reduced(block)
        return carry

    lax.fori_loop(0, jnp.minimum(block_total, HELD), held_step, 0)
    lax.fori_loop(HELD, block_total, step, 0)

    left = lax.broadcasted_iota(jnp.int32, (BLOCK, LANES), 1) < SIDE
    spots = SPAN
    chosen = [jnp.broadcast_to(turn, (8, LANES)) == value for value in range(spots + 1)]
    chosen = [jnp.concatenate([mask] * (BLOCK // 8), axis=0) for mask in chosen]
    for place in range(spots):
        rows = slice(place * BLOCK, (place + 1) * BLOCK)
        for comp in range(2):
            early_part = jnp.where(turn > place, result[comp, rows], 0.0)
            later = jnp.zeros((BLOCK, LANES), jnp.float32)
            for value in range(spots + 1):
                base = (place + value) * BLOCK
                if base < result.shape[1]:
                    later = jnp.where(chosen[value], result[comp, base : base + BLOCK], later)
            final[comp, rows] = jnp.where(left, early_part, later)
    back = back_ref[...]
    dims = (((1,), (1,)), ((), ()))
    for comp in range(2):
        high, low = split_bf16(final[comp])
        value = lax.dot_general(back, high, dims, preferred_element_type=jnp.float32)
        value += lax.dot_general(back, low, dims, preferred_element_type=jnp.float32)
        out_ref[:, comp, :] = value[:slots, :M]


def resample_pieces(pieces, rows, padded_rows):
    full = resample_table()
    table = full.reshape(full.shape[0], pieces, rows).transpose(1, 0, 2)
    table = table_bf16(np.pad(table, ((0, 0), (0, 0), (0, padded_rows - rows))))
    return table.reshape(pieces, full.shape[0], 2, padded_rows).transpose(0, 2, 1, 3)


def legendre(fields, mine, prepared, rows, slots):
    pieces = len(fields)
    early = pieces // 2
    latitudes = latitude_table()
    points = latitudes.shape[1]
    table = jnp.asarray(resample_pieces(pieces, rows, fields[0].shape[0]))
    total = resample(fields[:early], table)
    block_rows = SPAN * BLOCK
    return pl.pallas_call(
        functools.partial(legendre_kernel, early),
        out_shape=jax.ShapeDtypeStruct((slots, 2, M), jnp.float32),
        in_specs=[VMEM_SPEC] * (11 + pieces - early),
        out_specs=VMEM_SPEC,
        scratch_shapes=[
            pltpu.VMEM((2, 4, points, LANES), jnp.float32),
            pltpu.VMEM((3, points, LANES), jnp.float32),
            pltpu.VMEM((BLOCK * 16, LANES), jnp.float32),
            pltpu.VMEM((2, 2 * block_rows, LANES), jnp.float32),
            pltpu.VMEM((2, block_rows, LANES), jnp.float32),
        ],
        compiler_params=pltpu.CompilerParams(vmem_limit_bytes=late_bytes(pieces)),
        cost_estimate=pl.CostEstimate(
            flops=8 * 10**9, bytes_accessed=6 * 2**20, transcendentals=0
        ),
    )(table, latitudes, *prepared, total, mine, *fields[early:])


def shards(tracer, wind_east, wind_north, keep_m, slot_wave):
    rows = tracer.shape[1]
    lat_count = lax.axis_size("lat")
    slots = slot_wave.shape[0] // lat_count
    axes = ("lev", "fld")
    ring = (axes, tuple(lax.axis_size(axis) for axis in axes))

    blocks, edges = advect(tracer, wind_east, wind_north, keep_m, ring)
    blocks, slot_wave = lax.optimization_barrier((blocks, slot_wave))
    grids = exchange(blocks, axes)
    edges = lax.all_to_all(edges, ("lat", *axes), split_axis=0, concat_axis=0, tiled=True)
    wave_row, mine = prepare_places(slot_wave, lat_count)
    waved = fourier(grids, edges, ring, wave_row, rows, lat_count)
    waved, mine = lax.optimization_barrier((list(waved), mine))
    fields = exchange(waved, "lat")
    prepared = prepare_recurrence(mine, lat_count)
    return legendre(fields, mine, prepared, rows, slots)[None]


def solution(mesh):
    return jax.shard_map(
        shards,
        mesh=mesh,
        in_specs=(
            P("member", "lat", ("lev", "fld")),
            P("member", "lat", ("lev", "fld")),
            P("member", "lat", ("lev", "fld")),
            P("lat"),
            P(),
        ),
        out_specs=P(("member", "lev", "fld"), "lat", None, None),
        check_vma=False,
    )
```

```python
import functools
import math

import jax
import jax.numpy as jnp
import numpy as np
from jax import lax
from jax.experimental import pallas as pl
from jax.experimental.pallas import tpu as pltpu
from jax.sharding import PartitionSpec as P

M = 400
NLAT = 800
NLON = 1600
LANES = 128
BLOCK = 32
CHUNKS = (40, 32, 32)
SPAN = -(-M // BLOCK)
HELD = 13
MORE = 3
SIDE = LANES // 2
TOP = 32767.0
WIND_STEP = 1.5 / TOP
VMEM_BYTES = 60 * 2**20
LATE_BYTES = 10 * 2**20
MIDDLE_BYTES = 16 * 2**20
VMEM_SPEC = pl.BlockSpec(memory_space=pltpu.VMEM)
SMEM_SPEC = pl.BlockSpec(memory_space=pltpu.SMEM)
HBM_SPEC = pl.BlockSpec(memory_space=pltpu.HBM)


def split_bf16(values):
    high = values.astype(jnp.bfloat16)
    low = (values - high.astype(jnp.float32)).astype(jnp.bfloat16)
    return high, low


def table_bf16(table):
    high = table.astype(jnp.bfloat16)
    low = (table - high.astype(np.float64)).astype(jnp.bfloat16)
    return np.concatenate([high, low], axis=-1)


def fourier_tables(pieces):
    quarter = NLON // 4
    spots = np.arange(quarter)[:, None]
    factor = 1.0 / math.sqrt(NLON)

    def parts(waves):
        angles = 2.0 * math.pi / NLON * (spots * waves[None, :] % NLON)
        return factor * np.cos(angles), factor * np.sin(angles)

    def shaped(columns):
        pad = [(0, 0), (0, -columns[0].shape[1] % LANES)]
        table = np.concatenate([np.pad(part, pad) for part in columns], axis=1)
        return table.reshape(share, quarter // share, -1)

    share = pieces // 4
    tables = []
    for first in (0, 2):
        cosine, sine = parts(np.arange(first, M, 4))
        tables.append(shaped([cosine, -sine]))
    waves = np.arange(1, M, 2)
    sign = np.where(waves % 4 == 1, 1.0, -1.0)[None, :]
    cosine, sine = parts(waves)
    return [*tables, shaped([cosine, -sine]), shaped([-sign * sine, -sign * cosine])]


def column_waves(shape):
    row = lax.broadcasted_iota(jnp.int32, shape, 0)
    waves, first = jnp.full(shape, -1, jnp.int32), 0
    for start, step in ((0, 4), (2, 4), (1, 2)):
        count = len(range(start, M, step))
        inside = (row >= first) & (row < first + count)
        waves = jnp.where(inside, start + step * (row - first), waves)
        first += -(-count // LANES) * LANES
    return waves.astype(jnp.float32)


def column_count():
    return sum(-(-len(range(start, M, step)) // LANES) * LANES for start, step in ((0, 4), (2, 4), (1, 2)))


def resample_table():
    half = M // 2
    coarse = math.pi / M * (np.arange(M) + 0.5)
    fine = math.pi / NLAT * (np.arange(NLAT) + 0.5)
    waves = np.arange(M)
    weight = np.where(waves == 0, 1.0, 2.0) / M
    even = (np.cos(np.outer(coarse, waves)) * weight) @ np.cos(np.outer(waves, fine))
    odd = (np.sin(np.outer(coarse, waves)) * weight) @ np.sin(np.outer(waves, fine))
    rows = []
    for full in (even, odd):
        for sign in (1.0, -1.0):
            folded = (full[:half] + sign * full[::-1][:half]).reshape(2, half // 2, NLAT)
            rows.append(np.pad(folded, ((0, 0), (0, -half // 2 % 8), (0, 0))).reshape(-1, NLAT))
    return np.concatenate(rows, axis=0) * (np.sin(fine) * math.sqrt(2.0 / NLAT))


def latitude_table():
    half = M // 2
    angles = math.pi / M * (np.arange(half) + 0.5)
    log_sine = np.log2(np.sin(angles))
    coarse = np.round(log_sine * 1024.0) / 1024.0
    rows = np.stack([2.0 * np.cos(angles), coarse, log_sine - coarse]).reshape(3, 2, half // 2)
    rows = np.pad(rows, ((0, 0), (0, 0), (0, -half // 2 % 8)))
    return np.repeat(rows.transpose(0, 2, 1), SIDE, axis=2).astype(np.float32)


def scale_code(biggest):
    wanted = jnp.maximum(biggest, 1e-30) * (1.0 / TOP)
    exponent = jnp.floor(jnp.log(wanted) * (1.0 / math.log(2.0)))
    return exponent * 128.0 + jnp.ceil((wanted * jnp.exp2(-exponent) - 1.0) * 128.0)


def scale_of(code):
    exponent = jnp.floor(code * (1.0 / 128.0))
    rest = code - 128.0 * exponent
    return jnp.exp2(exponent) * (1.0 + rest * (1.0 / 128.0))


def coded(values, inverse):
    return jnp.floor(values * inverse + 0.5)


def as_int16(values):
    return values.astype(jnp.int32).astype(jnp.int16)


def from_int16(codes):
    return codes.astype(jnp.int32).astype(jnp.float32)


def partner(axes, sizes, step):
    count = math.prod(sizes)
    if count != 4:
        return step
    index = lax.axis_index(axes[0])
    for axis, size in zip(axes[1:], sizes[1:]):
        index = index * size + lax.axis_index(axis)
    return index ^ step


def exchange(blocks, axis):
    count = len(blocks)
    if count != 4:
        return list(lax.all_to_all(jnp.stack(blocks), axis, split_axis=0, concat_axis=0, tiled=True))
    pairs = [[(i, i ^ step) for i in range(count)] for step in range(count)]
    return [blocks[0]] + [lax.ppermute(blocks[step], axis, pairs[step]) for step in range(1, count)]


def advect_kernel(ring, lat_count, keep_hbm, tracer_hbm, east_hbm, north_hbm, *rest):
    levels, rows, lons = tracer_hbm.shape
    outs, (edge_ref, tracer, east_wind, north_wind, keep_ref, sems, keep_sem) = rest[:levels], rest[levels:]
    chosen = [partner(*ring, step) for step in range(levels)]
    copies = [None] * levels
    order = (*range(levels // 2, levels), *range(levels // 2))
    for step in order:
        copies[step] = [
            pltpu.make_async_copy(source.at[chosen[step]], target.at[step], sems.at[kind, step])
            for kind, (source, target) in enumerate(
                ((tracer_hbm, tracer), (east_hbm, east_wind), (north_hbm, north_wind))
            )
        ]
        for copy in copies[step]:
            copy.start()
    keep_copy = pltpu.make_async_copy(keep_hbm, keep_ref, keep_sem)
    keep_copy.start()
    padded_rows = outs[0].shape[0]
    keep_copy.wait()
    same = (rows, rows)
    same = lax.broadcasted_iota(jnp.int32, same, 0) == lax.broadcasted_iota(jnp.int32, same, 1)
    keep = jnp.broadcast_to(keep_ref[...].astype(jnp.float32), (rows, rows))
    keep = jnp.sum(jnp.where(same, keep, 0.0), axis=1, keepdims=True)
    end = (lons - 1) // LANES * LANES
    spare = lons - end
    lane = lax.broadcasted_iota(jnp.int32, (rows, LANES), 1)
    lat_index = lax.axis_index("lat")
    edge_ref[...] = jnp.zeros_like(edge_ref)
    for step in order:
        level = chosen[step]
        for copy in copies[step]:
            copy.wait()
        field = tracer[step].astype(jnp.float32)

        @pl.when(lat_index < lat_count - 1)
        def _():
            edge_ref[(lat_index + 1) * levels + level] = field[rows - 1 :]

        @pl.when(lat_index > 0)
        def _():
            edge_ref[(lat_index - 1) * levels + level] = field[:1]

        blank = jnp.zeros((rows, 1), jnp.float32)
        west = jnp.concatenate([blank, field[:, :-1]], axis=1)
        east = jnp.concatenate([field[:, 1:], blank], axis=1)
        blank = jnp.zeros((1, lons), jnp.float32)
        north = jnp.concatenate([blank, field[:-1]], axis=0)
        south = jnp.concatenate([field[1:], blank], axis=0)
        eastward = 0.5 * east_wind[step].astype(jnp.float32)
        northward = 0.5 * north_wind[step].astype(jnp.float32)
        moved = field - eastward * (east - west) - northward * (south - north)
        first, last = field[:, :1], field[:, lons - 1 :]
        biggest = jnp.max(jnp.abs(moved), axis=1, keepdims=True)
        biggest = jnp.maximum(biggest, jnp.maximum(jnp.abs(first), jnp.abs(last)))
        code = scale_code(biggest)
        inverse = 1.0 / scale_of(code)
        filler = jnp.zeros((rows, LANES - spare), jnp.float32)
        tile = jnp.concatenate([moved[:, end:], filler], axis=1)
        tile = jnp.where(lane == spare + 1, first, jnp.where(lane == spare + 2, last, tile))
        tile = coded(tile, inverse)
        tile = jnp.where(lane == spare, code, tile)
        winds = jnp.where(lane == spare + 3, eastward[:, :1], eastward[:, lons - 1 :])
        winds = coded(winds, 1.0 / WIND_STEP)
        tile = jnp.where((lane == spare + 3) | (lane == spare + 4), winds, tile)
        tile = jnp.where(lane == spare + 5, keep, tile)
        wind_rows = jnp.concatenate([northward[:1], northward[rows - 1 :]], axis=0)
        wind_rows = coded(wind_rows, 1.0 / WIND_STEP)
        blank = jnp.zeros((padded_rows - rows - 2, lons), jnp.float32)
        wind_rows = jnp.concatenate([wind_rows, blank], axis=0)
        filler = jnp.zeros((padded_rows - rows, LANES - spare), jnp.float32)
        wind_tile = jnp.concatenate([wind_rows[:, end:], filler], axis=1)
        steps = jnp.concatenate([coded(moved[:, :end], inverse), wind_rows[:, :end]], axis=0)
        outs[step][:, :end] = as_int16(steps)
        outs[step][:, end:] = as_int16(jnp.concatenate([tile, wind_tile], axis=0))


def advect(tracer, east_wind, north_wind, keep_m, ring):
    levels, rows, lons = tracer.shape
    lat_count = lax.axis_size("lat")
    width = (lons - 1) // LANES * LANES + LANES
    padded_rows = -(-(rows + 2) // 16) * 16
    held = pltpu.VMEM((levels, rows, lons), jnp.bfloat16)
    result = pl.pallas_call(
        functools.partial(advect_kernel, ring, lat_count),
        out_shape=[jax.ShapeDtypeStruct((padded_rows, width), jnp.int16)] * levels
        + [jax.ShapeDtypeStruct((lat_count * levels, 1, lons), jnp.float32)],
        in_specs=[HBM_SPEC] * 4,
        out_specs=[VMEM_SPEC] * (levels + 1),
        scratch_shapes=[
            held,
            held,
            held,
            pltpu.VMEM((1, rows), jnp.int32),
            pltpu.SemaphoreType.DMA((3, levels)),
            pltpu.SemaphoreType.DMA,
        ],
        compiler_params=pltpu.CompilerParams(vmem_limit_bytes=VMEM_BYTES),
        cost_estimate=pl.CostEstimate(
            flops=5 * 10**9, bytes_accessed=8 * levels * rows * lons, transcendentals=0
        ),
    )(keep_m[None], tracer, east_wind, north_wind)
    return list(result[:levels]), result[levels]


def fourier_kernel(ring, lat_count, pieces, *rest):
    grids, (edge_ref, table_ref, wave_ref) = rest[:pieces], rest[pieces : pieces + 3]
    outs, field = rest[pieces + 3 : -1], rest[-1]
    _, rows, width = field.shape
    lons = table_ref.shape[1]
    share = pieces // 4

    end = width - LANES
    spare = lons - end
    lane = lax.broadcasted_iota(jnp.int32, (rows, LANES), 1)
    winds = (lane == spare + 3) | (lane == spare + 4)
    lat_index = lax.axis_index("lat")
    for piece in range(pieces):
        spot = partner(*ring, piece)
        values = from_int16(grids[piece][...])
        tile = values[:rows, end:]
        scale = scale_of(tile[:, spare : spare + 1])
        keep = tile[:, spare + 5 : spare + 6]
        field[spot, :, :end] = values[:rows, :end] * scale
        field[spot, :, end:] = tile * jnp.where(winds, WIND_STEP, scale)
        wind_rows = values[rows : rows + 2, :lons] * WIND_STEP

        @pl.when(lat_index > 0)
        def _():
            above = edge_ref[(lat_index - 1) * pieces + spot]
            field[spot, :1, :lons] += wind_rows[:1] * above

        @pl.when(lat_index < lat_count - 1)
        def _():
            below = edge_ref[(lat_index + 1) * pieces + spot]
            field[spot, rows - 1 :, :lons] -= wind_rows[1:] * below

    for spot in range(pieces):
        tile = field[spot, :, end:]
        before = field[(spot - 1) % pieces, :, end:]
        after = field[(spot + 1) % pieces, :, end:]
        shift = LANES - spare
        gain = pltpu.roll(tile, shift - 3, 1) * pltpu.roll(before, shift - 2, 1)
        loss = pltpu.roll(tile, LANES - 5, 1) * pltpu.roll(after, LANES - 2, 1)
        field[spot, :, end:] = tile - jnp.where(lane == spare - 1, loss, 0.0)
        field[spot, :, :LANES] += jnp.where(lane == 0, gain, 0.0)

    spans = [2 * LANES, 2 * LANES, 4 * LANES, 4 * LANES]

    def product(kind, value, spot):
        high, low = split_bf16(value)
        first, span = 2 * sum(spans[:kind]), spans[kind]
        both = jnp.dot(high, table_ref[spot, :, first : first + 2 * span], preferred_element_type=jnp.float32)
        part = jnp.dot(low, table_ref[spot, :, first : first + span], preferred_element_type=jnp.float32)
        return part + both[:, :span] + both[:, span:]

    sums = [None, None, None]
    for spot in range(share):
        quarters = [field[quarter * share + spot, :, :lons] for quarter in range(4)]
        sum02, dif02 = quarters[0] + quarters[2], quarters[0] - quarters[2]
        sum13, dif13 = quarters[1] + quarters[3], quarters[1] - quarters[3]
        parts = []
        for kind, value in enumerate((sum02 + sum13, sum02 - sum13, dif02, dif13)):
            parts.append(product(kind, value, spot))
        parts = [parts[0], parts[1], parts[2] + parts[3]]
        sums = [part if total is None else total + part for total, part in zip(sums, parts)]
    slot_waves = wave_ref[...]
    waves = column_waves((column_count(), LANES))
    places = [
        jnp.where(waves == slot_waves[:, first : first + LANES], 1.0, 0.0).astype(jnp.bfloat16)
        for first in range(0, slot_waves.shape[1], LANES)
    ]
    places = jnp.concatenate(places, axis=1)
    placed = []
    for part in range(2):
        columns = []
        for total in sums:
            half = total.shape[1] // 2
            columns.append(total[:, part * half : (part + 1) * half])
        high, low = split_bf16(jnp.concatenate(columns, axis=1))
        value = jnp.dot(high, places, preferred_element_type=jnp.float32)
        value += jnp.dot(low, places, preferred_element_type=jnp.float32)
        kept = jnp.where(slot_waves < keep, value, 0.0)
        code = scale_code(jnp.max(jnp.abs(kept), axis=0, keepdims=True))
        steps = coded(kept, 1.0 / scale_of(code))
        codes = jnp.broadcast_to(code, (outs[0].shape[0] - rows, code.shape[1]))
        placed.append(as_int16(jnp.concatenate([steps, codes], axis=0)))
    for target in range(lat_count):
        for part in range(2):
            cols = slice(target * LANES, (target + 1) * LANES)
            outs[target][:, part * LANES : (part + 1) * LANES] = placed[part][:, cols]


def fourier(grids, edges, ring, wave_row, rows, lat_count):
    pieces = len(grids)
    width = grids[0].shape[1]
    padded_rows = -(-(rows + 1) // 16) * 16
    tables = [table_bf16(table) for table in fourier_tables(pieces)]
    return pl.pallas_call(
        functools.partial(fourier_kernel, ring, lat_count, pieces),
        out_shape=[jax.ShapeDtypeStruct((padded_rows, 2 * LANES), jnp.int16)] * lat_count,
        in_specs=[VMEM_SPEC] * (pieces + 3),
        out_specs=[VMEM_SPEC] * lat_count,
        scratch_shapes=[pltpu.VMEM((pieces, rows, width), jnp.float32)],
        compiler_params=pltpu.CompilerParams(vmem_limit_bytes=MIDDLE_BYTES),
        cost_estimate=pl.CostEstimate(
            flops=4 * 10**9, bytes_accessed=6 * 2**20, transcendentals=0
        ),
    )(*grids, edges, np.concatenate(tables, axis=-1), wave_row)


def places_kernel(groups, slot_ref, wave_ref, mine_ref, sorted_rows):
    lat_index = lax.axis_index("lat")
    slots = slot_ref.shape[1] // groups
    paired = (slots + 1) // 2
    shape = (LANES, LANES)
    down = lax.broadcasted_iota(jnp.int32, shape, 0)
    across = lax.broadcasted_iota(jnp.int32, shape, 1)
    filler = jnp.full((1, LANES - slots), 2.0 * M, jnp.float32)
    for group in range(groups):
        plain = slot_ref[:, group * slots : (group + 1) * slots].astype(jnp.float32)
        plain = jnp.concatenate([plain, filler], axis=1)
        row = jnp.broadcast_to(plain, shape)
        column = jnp.sum(jnp.where(down == across, row, 0.0), axis=1, keepdims=True)
        ahead = (row < column) | ((row == column) & (across < down))
        rank = jnp.sum(jnp.where(ahead, 1.0, 0.0), axis=1, keepdims=True)
        place = jnp.where(rank < paired, rank, SIDE + slots - 1.0 - rank)
        place = jnp.where(rank < slots, place, -1.0)
        hot = jnp.where(place == across.astype(jnp.float32), 1.0, 0.0)
        filled = jnp.sum(hot, axis=0, keepdims=True)
        values = jnp.sum(hot * column, axis=0, keepdims=True)
        values = jnp.where(filled > 0.5, values, 2.0 * M)
        sorted_rows[group] = jnp.broadcast_to(values, sorted_rows.shape[1:])

        @pl.when(group == lat_index)
        def _():
            mine_ref[:1] = values
            mine_ref[1:] = plain

    for step in range(groups):
        row = sorted_rows[partner(("lat",), (groups,), step), :1]
        wave_ref[:, step * LANES : (step + 1) * LANES] = row


def prepare_places(slot_wave, groups):
    width = groups * LANES
    return pl.pallas_call(
        functools.partial(places_kernel, groups),
        out_shape=[
            jax.ShapeDtypeStruct((1, width), jnp.float32),
            jax.ShapeDtypeStruct((2, LANES), jnp.float32),
        ],
        in_specs=[VMEM_SPEC],
        out_specs=[VMEM_SPEC] * 2,
        scratch_shapes=[pltpu.VMEM((groups, 8, LANES), jnp.float32)],
        compiler_params=pltpu.CompilerParams(vmem_limit_bytes=MIDDLE_BYTES),
        cost_estimate=pl.CostEstimate(flops=2 * 10**9, bytes_accessed=2**20, transcendentals=0),
    )(slot_wave[None])


def lane_pairs(row):
    lane = lax.broadcasted_iota(jnp.int32, row.shape, 1)
    other = pltpu.roll(row, SIDE, 1)
    return jnp.where(lane < SIDE, row, other), jnp.where(lane < SIDE, other, row)


def block_count(wave):
    return jnp.floor((jnp.maximum(M - wave, 0.0) + (BLOCK - 1)) * (1.0 / BLOCK))


def sweep_kernel(
    mine_ref, lat_ref,
    beta_ref, scale_ref, growth_ref, start_ref, state_ref, values_ref, more_ref, back_ref,
):
    shape = (LANES, LANES)
    same = lax.broadcasted_iota(jnp.int32, shape, 0) == lax.broadcasted_iota(jnp.int32, shape, 1)
    plain = jnp.broadcast_to(mine_ref[1:], shape)
    plain = jnp.sum(jnp.where(same, plain, 0.0), axis=1, keepdims=True)
    hot = (plain == mine_ref[:1]) & (plain < 2.0 * M)
    back_ref[...] = jnp.where(hot, 1.0, 0.0).astype(jnp.bfloat16)
    pair = lane_pairs(jnp.broadcast_to(mine_ref[:1], (8, LANES)))
    one, two = pair[0][:1], pair[1][:1]
    blocks = growth_ref.shape[0]
    turn = block_count(one)
    block = lax.broadcasted_iota(jnp.int32, (blocks, LANES), 0).astype(jnp.float32)
    second = block >= turn
    wave = jnp.where(second, two, one)
    limit = M - wave
    wave = jnp.minimum(wave, M - 1.0)
    first = (block - jnp.where(second, turn, 0.0)) * BLOCK

    scale = jnp.ones((blocks, LANES), jnp.float32)
    for index in range(BLOCK + 1):
        order = first + index
        degree = wave + order
        square = 4.0 * degree * degree - 1.0
        spread = 4.0 * order * (degree + wave)
        if index > 0:
            scale = scale * jnp.sqrt(square / spread)
        if index < BLOCK:
            beta_ref[pl.ds(index, blocks, stride=BLOCK)] = spread / jnp.maximum(square, 1.0)
            scale_ref[pl.ds(index, blocks, stride=BLOCK)] = jnp.where(order < limit, scale, 0.0)
    growth_ref[...] = scale

    counter = lax.broadcasted_iota(jnp.int32, (M, LANES), 0).astype(jnp.float32) + 1.0
    terms = jnp.log(1.0 + 0.5 / counter) * (1.0 / math.log(2.0))
    for kind, wave in enumerate((one, two)):
        wave = jnp.minimum(wave, M - 1.0)
        norm = jnp.sum(jnp.where(counter <= wave, terms, 0.0), axis=0, keepdims=True)
        coarse = lat_ref[1] * wave
        whole = jnp.floor(coarse)
        start_ref[2 * kind] = jnp.exp2(
            (coarse - whole) + lat_ref[2] * wave + 0.5 * (norm - 1.0)
        )
        start_ref[2 * kind + 1] = whole

    state_ref[0] = jnp.zeros_like(state_ref[0])
    state_ref[1] = start_ref[0]
    state_ref[2] = start_ref[1]
    points = lat_ref.shape[1]

    def step(target_ref, start, block, carry):
        first = 0
        for chunk in (points // 16 * 8, points - points // 16 * 8):
            rows = slice(first, first + chunk)

            def keep(order, value):
                target_ref[block - start, order, rows] = value

            sweep_block(block, turn, rows, lat_ref, beta_ref, growth_ref, start_ref, state_ref, keep)
            first += chunk
        return carry

    total = jnp.max(turn + block_count(two)).astype(jnp.int32)
    lax.fori_loop(0, jnp.minimum(total, HELD), functools.partial(step, values_ref, 0), 0)
    more = functools.partial(step, more_ref, HELD)
    lax.fori_loop(HELD, jnp.minimum(total, HELD + MORE), more, 0)


def sweep_block(block, turn, rows, lat_ref, beta_ref, growth_ref, start_ref, state_ref, use):
    base = pl.multiple_of(block * BLOCK, BLOCK)
    begins = block.astype(jnp.float32) == turn
    grow = growth_ref[pl.ds(block, 1)]
    cosine = lat_ref[0, rows]
    height = jnp.where(begins, start_ref[3, rows], state_ref[2, rows])
    factor = jnp.exp2(height)
    old = jnp.where(begins, 0.0, state_ref[0, rows])
    new = jnp.where(begins, start_ref[2, rows], state_ref[1, rows])
    for order in range(BLOCK):
        use(order, new * factor)
        beta = beta_ref[pl.ds(base + order, 1)]
        old, new = new, cosine * new - beta * old
    biggest = jnp.maximum(jnp.abs(old), jnp.abs(new)) * grow
    shift = jnp.floor(jnp.log(biggest) * (1.0 / math.log(2.0)))
    factor = grow * jnp.exp2(-shift)
    state_ref[0, rows] = old * factor
    state_ref[1, rows] = new * factor
    state_ref[2, rows] = height + shift


def prepare_recurrence(mine, pieces):
    latitudes = latitude_table()
    points = latitudes.shape[1]
    blocks = 2 * SPAN
    orders = jax.ShapeDtypeStruct((blocks * BLOCK, LANES), jnp.float32)
    return pl.pallas_call(
        sweep_kernel,
        out_shape=[
            orders,
            orders,
            jax.ShapeDtypeStruct((blocks, LANES), jnp.float32),
            jax.ShapeDtypeStruct((4, points, LANES), jnp.float32),
            jax.ShapeDtypeStruct((3, points, LANES), jnp.float32),
            jax.ShapeDtypeStruct((HELD, BLOCK, points, LANES), jnp.float32),
            jax.ShapeDtypeStruct((MORE, BLOCK, points, LANES), jnp.float32),
            jax.ShapeDtypeStruct((LANES, LANES), jnp.bfloat16),
        ],
        in_specs=[VMEM_SPEC] * 2,
        out_specs=[VMEM_SPEC] * 8,
        compiler_params=pltpu.CompilerParams(vmem_limit_bytes=late_bytes(pieces)),
        cost_estimate=pl.CostEstimate(
            flops=5 * 10**9, bytes_accessed=25 * 2**20, transcendentals=0
        ),
    )(mine, latitudes)


def resampled(first, fields, table, total):
    for piece, field in enumerate(fields):
        values = from_int16(field[...])
        values = values * scale_of(values[field.shape[0] - 1 :])
        high, low = split_bf16(values)
        spot = partner(("lat",), table.shape[:1], first + piece)
        both = jnp.concatenate([high, low], axis=1)
        part = jnp.dot(table[spot, 0], both, preferred_element_type=jnp.float32)
        part = part[:, : high.shape[1]] + part[:, high.shape[1] :]
        part += jnp.dot(table[spot, 1], high, preferred_element_type=jnp.float32)
        total = part if total is None else total + part
    return total


def resample_kernel(table_ref, *rest):
    rest[-1][...] = resampled(0, rest[:-1], table_ref, None)


def late_bytes(pieces):
    return LATE_BYTES if pieces <= 4 else VMEM_BYTES


def resample(fields, table):
    count, _, height, _ = table.shape
    span = fields[0].shape[1]
    return pl.pallas_call(
        resample_kernel,
        out_shape=jax.ShapeDtypeStruct((height, span), jnp.float32),
        in_specs=[VMEM_SPEC] * (1 + len(fields)),
        out_specs=VMEM_SPEC,
        compiler_params=pltpu.CompilerParams(vmem_limit_bytes=late_bytes(count)),
        cost_estimate=pl.CostEstimate(
            flops=10**9, bytes_accessed=4 * 2**20, transcendentals=0
        ),
    )(table, *fields)


def legendre_kernel(early, *rest):
    table, lat_ref, beta_ref, scale_ref, growth_ref, start_ref, left_ref, values_ref = rest[:8]
    more_ref, back_ref, total_ref, mine_ref = rest[8:12]
    fields, (out_ref, weights, state_ref, sums, result, final) = rest[12:-6], rest[-6:]
    points = lat_ref.shape[1]
    slots = out_ref.shape[0]
    mine = mine_ref[:1]
    odd = mine - 2.0 * jnp.floor(mine * 0.5) > 0.5
    pair = lane_pairs(jnp.broadcast_to(mine, (8, LANES)))
    turn = block_count(pair[0][:1])
    block_total = jnp.max(turn + block_count(pair[1][:1])).astype(jnp.int32)

    total = resampled(early, fields, table, total_ref[...])
    totals = [total[2 * points * kind : 2 * points * (kind + 1)] for kind in range(4)]
    left = lax.broadcasted_iota(jnp.int32, (points, LANES), 1) < SIDE
    for parity in range(2):
        for comp in range(2):
            cols = slice(comp * LANES, (comp + 1) * LANES)
            value = jnp.where(odd, totals[2 + parity][:, cols], totals[parity][:, cols])
            top, bottom = value[:points], value[points:]
            kind = 2 * parity + comp
            weights[0, kind] = jnp.where(left, top, pltpu.roll(bottom, SIDE, 1))
            weights[1, kind] = jnp.where(left, pltpu.roll(top, SIDE, 1), bottom)
    result[...] = jnp.zeros_like(result)
    state_ref[...] = left_ref[...]

    def reduced(block):
        base = pl.multiple_of(block * BLOCK, BLOCK)
        for comp in range(2):
            total = sums[pl.ds(comp * 8, BLOCK, stride=16)]
            for lane in range(1, 8):
                total += sums[pl.ds(comp * 8 + lane, BLOCK, stride=16)]
            total = total * scale_ref[pl.ds(base, BLOCK)]
            result[comp, pl.ds(base, BLOCK)] = total + pltpu.roll(total, SIDE, 1)

    def held_step(source_ref, start, block, carry):
        second = block.astype(jnp.float32) >= turn
        for parity in range(2):
            scaled = [
                jnp.where(second, weights[1, 2 * parity + comp], weights[0, 2 * parity + comp])
                for comp in range(2)
            ]
            for order in range(parity, BLOCK, 2):
                value = source_ref[block - start, order]
                for comp in range(2):
                    product = (value * scaled[comp]).reshape(points // 8, 8, LANES)
                    sums[pl.ds((order * 2 + comp) * 8, 8)] = product.sum(axis=0)
        reduced(block)
        return carry

    def step(block, carry):
        second = block.astype(jnp.float32) >= turn
        first = 0
        for chunk in CHUNKS:
            rows = slice(first, first + chunk)
            scaled = [jnp.where(second, weights[1, k, rows], weights[0, k, rows]) for k in range(4)]

            def add(order, value):
                for comp in range(2):
                    product = value * scaled[2 * (order % 2) + comp]
                    partial = product.reshape(chunk // 8, 8, LANES).sum(axis=0)
                    place = pl.ds((order * 2 + comp) * 8, 8)
                    if first == 0:
                        sums[place] = partial
                    else:
                        sums[place] += partial

            sweep_block(block, turn, rows, lat_ref, beta_ref, growth_ref, start_ref, state_ref, add)
            first += chunk
        reduced(block)
        return carry

    held = functools.partial(held_step, values_ref, 0)
    lax.fori_loop(0, jnp.minimum(block_total, HELD), held, 0)
    held = functools.partial(held_step, more_ref, HELD)
    lax.fori_loop(HELD, jnp.minimum(block_total, HELD + MORE), held, 0)
    lax.fori_loop(HELD + MORE, block_total, step, 0)

    left = lax.broadcasted_iota(jnp.int32, (BLOCK, LANES), 1) < SIDE
    spots = SPAN
    chosen = [jnp.broadcast_to(turn, (8, LANES)) == value for value in range(spots + 1)]
    chosen = [jnp.concatenate([mask] * (BLOCK // 8), axis=0) for mask in chosen]
    for place in range(spots):
        rows = slice(place * BLOCK, (place + 1) * BLOCK)
        for comp in range(2):
            early_part = jnp.where(turn > place, result[comp, rows], 0.0)
            later = jnp.zeros((BLOCK, LANES), jnp.float32)
            for value in range(spots + 1):
                base = (place + value) * BLOCK
                if base < result.shape[1]:
                    later = jnp.where(chosen[value], result[comp, base : base + BLOCK], later)
            final[comp, rows] = jnp.where(left, early_part, later)
    back = back_ref[...]
    dims = (((1,), (1,)), ((), ()))
    for comp in range(2):
        high, low = split_bf16(final[comp])
        value = lax.dot_general(back, high, dims, preferred_element_type=jnp.float32)
        value += lax.dot_general(back, low, dims, preferred_element_type=jnp.float32)
        out_ref[:, comp, :] = value[:slots, :M]


def resample_pieces(pieces, rows, padded_rows):
    full = resample_table()
    table = full.reshape(full.shape[0], pieces, rows).transpose(1, 0, 2)
    table = table_bf16(np.pad(table, ((0, 0), (0, 0), (0, padded_rows - rows))))
    return table.reshape(pieces, full.shape[0], 2, padded_rows).transpose(0, 2, 1, 3)


def legendre(fields, mine, prepared, rows, slots):
    pieces = len(fields)
    early = pieces // 2
    latitudes = latitude_table()
    points = latitudes.shape[1]
    table = jnp.asarray(resample_pieces(pieces, rows, fields[0].shape[0]))
    total = resample(fields[:early], table)
    block_rows = SPAN * BLOCK
    return pl.pallas_call(
        functools.partial(legendre_kernel, early),
        out_shape=jax.ShapeDtypeStruct((slots, 2, M), jnp.float32),
        in_specs=[VMEM_SPEC] * (12 + pieces - early),
        out_specs=VMEM_SPEC,
        scratch_shapes=[
            pltpu.VMEM((2, 4, points, LANES), jnp.float32),
            pltpu.VMEM((3, points, LANES), jnp.float32),
            pltpu.VMEM((BLOCK * 16, LANES), jnp.float32),
            pltpu.VMEM((2, 2 * block_rows, LANES), jnp.float32),
            pltpu.VMEM((2, block_rows, LANES), jnp.float32),
        ],
        compiler_params=pltpu.CompilerParams(vmem_limit_bytes=late_bytes(pieces)),
        cost_estimate=pl.CostEstimate(
            flops=8 * 10**9, bytes_accessed=6 * 2**20, transcendentals=0
        ),
    )(table, latitudes, *prepared, total, mine, *fields[early:])


def shards(tracer, wind_east, wind_north, keep_m, slot_wave):
    rows = tracer.shape[1]
    lat_count = lax.axis_size("lat")
    slots = slot_wave.shape[0] // lat_count
    axes = ("lev", "fld")
    ring = (axes, tuple(lax.axis_size(axis) for axis in axes))

    blocks, edges = advect(tracer, wind_east, wind_north, keep_m, ring)
    blocks, slot_wave = lax.optimization_barrier((blocks, slot_wave))
    grids = exchange(blocks, axes)
    edges = lax.all_to_all(edges, ("lat", *axes), split_axis=0, concat_axis=0, tiled=True)
    wave_row, mine = prepare_places(slot_wave, lat_count)
    waved = fourier(grids, edges, ring, wave_row, rows, lat_count)
    waved, mine = lax.optimization_barrier((list(waved), mine))
    fields = exchange(waved, "lat")
    prepared = prepare_recurrence(mine, lat_count)
    return legendre(fields, mine, prepared, rows, slots)[None]


def solution(mesh):
    return jax.shard_map(
        shards,
        mesh=mesh,
        in_specs=(
            P("member", "lat", ("lev", "fld")),
            P("member", "lat", ("lev", "fld")),
            P("member", "lat", ("lev", "fld")),
            P("lat"),
            P(),
        ),
        out_specs=P(("member", "lev", "fld"), "lat", None, None),
        check_vma=False,
    )
```

```python
import functools
import math

import jax
import jax.numpy as jnp
import numpy as np
from jax import lax
from jax.experimental import pallas as pl
from jax.experimental.pallas import tpu as pltpu
from jax.sharding import PartitionSpec as P

M = 400
NLAT = 800
NLON = 1600
LANES = 128
BLOCK = 32
CHUNKS = (40, 32, 32)
SPAN = -(-M // BLOCK)
HELD = 13
MORE = 3
SIDE = LANES // 2
TOP = 32767.0
WIND_STEP = 1.5 / TOP
VMEM_BYTES = 60 * 2**20
LATE_BYTES = 10 * 2**20
MIDDLE_BYTES = 16 * 2**20
VMEM_SPEC = pl.BlockSpec(memory_space=pltpu.VMEM)
SMEM_SPEC = pl.BlockSpec(memory_space=pltpu.SMEM)
HBM_SPEC = pl.BlockSpec(memory_space=pltpu.HBM)


def split_bf16(values):
    high = values.astype(jnp.bfloat16)
    low = (values - high.astype(jnp.float32)).astype(jnp.bfloat16)
    return high, low


def table_bf16(table):
    high = table.astype(jnp.bfloat16)
    low = (table - high.astype(np.float64)).astype(jnp.bfloat16)
    return np.concatenate([high, low], axis=-1)


def fourier_tables(pieces):
    quarter = NLON // 4
    spots = np.arange(quarter)[:, None]
    factor = 1.0 / math.sqrt(NLON)

    def parts(waves):
        angles = 2.0 * math.pi / NLON * (spots * waves[None, :] % NLON)
        return factor * np.cos(angles), factor * np.sin(angles)

    def shaped(columns):
        pad = [(0, 0), (0, -columns[0].shape[1] % LANES)]
        table = np.concatenate([np.pad(part, pad) for part in columns], axis=1)
        return table.reshape(share, quarter // share, -1)

    share = pieces // 4
    tables = []
    for first in (0, 2):
        cosine, sine = parts(np.arange(first, M, 4))
        tables.append(shaped([cosine, -sine]))
    waves = np.arange(1, M, 2)
    sign = np.where(waves % 4 == 1, 1.0, -1.0)[None, :]
    cosine, sine = parts(waves)
    return [*tables, shaped([cosine, -sine]), shaped([-sign * sine, -sign * cosine])]


def column_waves(shape):
    row = lax.broadcasted_iota(jnp.int32, shape, 0)
    waves, first = jnp.full(shape, -1, jnp.int32), 0
    for start, step in ((0, 4), (2, 4), (1, 2)):
        count = len(range(start, M, step))
        inside = (row >= first) & (row < first + count)
        waves = jnp.where(inside, start + step * (row - first), waves)
        first += -(-count // LANES) * LANES
    return waves.astype(jnp.float32)


def column_count():
    return sum(-(-len(range(start, M, step)) // LANES) * LANES for start, step in ((0, 4), (2, 4), (1, 2)))


def resample_table():
    half = M // 2
    coarse = math.pi / M * (np.arange(M) + 0.5)
    fine = math.pi / NLAT * (np.arange(NLAT) + 0.5)
    waves = np.arange(M)
    weight = np.where(waves == 0, 1.0, 2.0) / M
    even = (np.cos(np.outer(coarse, waves)) * weight) @ np.cos(np.outer(waves, fine))
    odd = (np.sin(np.outer(coarse, waves)) * weight) @ np.sin(np.outer(waves, fine))
    rows = []
    for full in (even, odd):
        for sign in (1.0, -1.0):
            folded = (full[:half] + sign * full[::-1][:half]).reshape(2, half // 2, NLAT)
            rows.append(np.pad(folded, ((0, 0), (0, -half // 2 % 8), (0, 0))).reshape(-1, NLAT))
    return np.concatenate(rows, axis=0) * (np.sin(fine) * math.sqrt(2.0 / NLAT))


def latitude_table():
    half = M // 2
    angles = math.pi / M * (np.arange(half) + 0.5)
    log_sine = np.log2(np.sin(angles))
    coarse = np.round(log_sine * 1024.0) / 1024.0
    rows = np.stack([2.0 * np.cos(angles), coarse, log_sine - coarse]).reshape(3, 2, half // 2)
    rows = np.pad(rows, ((0, 0), (0, 0), (0, -half // 2 % 8)))
    return np.repeat(rows.transpose(0, 2, 1), SIDE, axis=2).astype(np.float32)


def scale_code(biggest):
    wanted = jnp.maximum(biggest, 1e-30) * (1.0 / TOP)
    exponent = jnp.floor(jnp.log(wanted) * (1.0 / math.log(2.0)))
    return exponent * 128.0 + jnp.ceil((wanted * jnp.exp2(-exponent) - 1.0) * 128.0)


def scale_of(code):
    exponent = jnp.floor(code * (1.0 / 128.0))
    rest = code - 128.0 * exponent
    return jnp.exp2(exponent) * (1.0 + rest * (1.0 / 128.0))


def coded(values, inverse):
    return jnp.floor(values * inverse + 0.5)


def as_int16(values):
    return values.astype(jnp.int32).astype(jnp.int16)


def from_int16(codes):
    return codes.astype(jnp.int32).astype(jnp.float32)


def partner(axes, sizes, step):
    count = math.prod(sizes)
    if count != 4:
        return step
    index = lax.axis_index(axes[0])
    for axis, size in zip(axes[1:], sizes[1:]):
        index = index * size + lax.axis_index(axis)
    return index ^ step


def exchange(blocks, axis):
    count = len(blocks)
    if count != 4:
        return list(lax.all_to_all(jnp.stack(blocks), axis, split_axis=0, concat_axis=0, tiled=True))
    pairs = [[(i, i ^ step) for i in range(count)] for step in range(count)]
    return [blocks[0]] + [lax.ppermute(blocks[step], axis, pairs[step]) for step in range(1, count)]


def advect_kernel(ring, lat_count, keep_hbm, tracer_hbm, east_hbm, north_hbm, *rest):
    levels, rows, lons = tracer_hbm.shape
    outs, (edge_ref, tracer, east_wind, north_wind, keep_ref, sems, keep_sem) = rest[:levels], rest[levels:]
    chosen = [partner(*ring, step) for step in range(levels)]
    copies = [None] * levels
    order = (*range(levels // 2, levels), *range(levels // 2))
    for step in order:
        copies[step] = [
            pltpu.make_async_copy(source.at[chosen[step]], target.at[step], sems.at[kind, step])
            for kind, (source, target) in enumerate(
                ((tracer_hbm, tracer), (east_hbm, east_wind), (north_hbm, north_wind))
            )
        ]
        for copy in copies[step]:
            copy.start()
    keep_copy = pltpu.make_async_copy(keep_hbm, keep_ref, keep_sem)
    keep_copy.start()
    padded_rows = outs[0].shape[0]
    keep_copy.wait()
    same = (rows, rows)
    same = lax.broadcasted_iota(jnp.int32, same, 0) == lax.broadcasted_iota(jnp.int32, same, 1)
    keep = jnp.broadcast_to(keep_ref[...].astype(jnp.float32), (rows, rows))
    keep = jnp.sum(jnp.where(same, keep, 0.0), axis=1, keepdims=True)
    end = (lons - 1) // LANES * LANES
    spare = lons - end
    lane = lax.broadcasted_iota(jnp.int32, (rows, LANES), 1)
    lat_index = lax.axis_index("lat")
    edge_ref[...] = jnp.zeros_like(edge_ref)
    for step in order:
        level = chosen[step]
        for copy in copies[step]:
            copy.wait()
        field = tracer[step].astype(jnp.float32)

        @pl.when(lat_index < lat_count - 1)
        def _():
            edge_ref[(lat_index + 1) * levels + level] = field[rows - 1 :]

        @pl.when(lat_index > 0)
        def _():
            edge_ref[(lat_index - 1) * levels + level] = field[:1]

        blank = jnp.zeros((rows, 1), jnp.float32)
        west = jnp.concatenate([blank, field[:, :-1]], axis=1)
        east = jnp.concatenate([field[:, 1:], blank], axis=1)
        blank = jnp.zeros((1, lons), jnp.float32)
        north = jnp.concatenate([blank, field[:-1]], axis=0)
        south = jnp.concatenate([field[1:], blank], axis=0)
        eastward = 0.5 * east_wind[step].astype(jnp.float32)
        northward = 0.5 * north_wind[step].astype(jnp.float32)
        moved = field - eastward * (east - west) - northward * (south - north)
        first, last = field[:, :1], field[:, lons - 1 :]
        biggest = jnp.max(jnp.abs(moved), axis=1, keepdims=True)
        biggest = jnp.maximum(biggest, jnp.maximum(jnp.abs(first), jnp.abs(last)))
        code = scale_code(biggest)
        inverse = 1.0 / scale_of(code)
        filler = jnp.zeros((rows, LANES - spare), jnp.float32)
        tile = jnp.concatenate([moved[:, end:], filler], axis=1)
        tile = jnp.where(lane == spare + 1, first, jnp.where(lane == spare + 2, last, tile))
        tile = coded(tile, inverse)
        tile = jnp.where(lane == spare, code, tile)
        winds = jnp.where(lane == spare + 3, eastward[:, :1], eastward[:, lons - 1 :])
        winds = coded(winds, 1.0 / WIND_STEP)
        tile = jnp.where((lane == spare + 3) | (lane == spare + 4), winds, tile)
        tile = jnp.where(lane == spare + 5, keep, tile)
        wind_rows = jnp.concatenate([northward[:1], northward[rows - 1 :]], axis=0)
        wind_rows = coded(wind_rows, 1.0 / WIND_STEP)
        blank = jnp.zeros((padded_rows - rows - 2, lons), jnp.float32)
        wind_rows = jnp.concatenate([wind_rows, blank], axis=0)
        filler = jnp.zeros((padded_rows - rows, LANES - spare), jnp.float32)
        wind_tile = jnp.concatenate([wind_rows[:, end:], filler], axis=1)
        steps = jnp.concatenate([coded(moved[:, :end], inverse), wind_rows[:, :end]], axis=0)
        outs[step][:, :end] = as_int16(steps)
        outs[step][:, end:] = as_int16(jnp.concatenate([tile, wind_tile], axis=0))


def advect(tracer, east_wind, north_wind, keep_m, ring):
    levels, rows, lons = tracer.shape
    lat_count = lax.axis_size("lat")
    width = (lons - 1) // LANES * LANES + LANES
    padded_rows = -(-(rows + 2) // 16) * 16
    held = pltpu.VMEM((levels, rows, lons), jnp.bfloat16)
    result = pl.pallas_call(
        functools.partial(advect_kernel, ring, lat_count),
        out_shape=[jax.ShapeDtypeStruct((padded_rows, width), jnp.int16)] * levels
        + [jax.ShapeDtypeStruct((lat_count * levels, 1, lons), jnp.float32)],
        in_specs=[HBM_SPEC] * 4,
        out_specs=[VMEM_SPEC] * (levels + 1),
        scratch_shapes=[
            held,
            held,
            held,
            pltpu.VMEM((1, rows), jnp.int32),
            pltpu.SemaphoreType.DMA((3, levels)),
            pltpu.SemaphoreType.DMA,
        ],
        compiler_params=pltpu.CompilerParams(vmem_limit_bytes=VMEM_BYTES),
        cost_estimate=pl.CostEstimate(
            flops=5 * 10**9, bytes_accessed=8 * levels * rows * lons, transcendentals=0
        ),
    )(keep_m[None], tracer, east_wind, north_wind)
    return list(result[:levels]), result[levels]


def fourier_kernel(ring, lat_count, pieces, *rest):
    grids, (edge_ref, *tables, wave_ref) = rest[:pieces], rest[pieces : pieces + 6]
    outs, field = rest[pieces + 6 : -1], rest[-1]
    _, rows, width = field.shape
    lons = tables[0].shape[1]
    share = pieces // 4

    end = width - LANES
    spare = lons - end
    lane = lax.broadcasted_iota(jnp.int32, (rows, LANES), 1)
    winds = (lane == spare + 3) | (lane == spare + 4)
    lat_index = lax.axis_index("lat")
    for piece in range(pieces):
        spot = partner(*ring, piece)
        values = from_int16(grids[piece][...])
        tile = values[:rows, end:]
        scale = scale_of(tile[:, spare : spare + 1])
        keep = tile[:, spare + 5 : spare + 6]
        field[spot, :, :end] = values[:rows, :end] * scale
        field[spot, :, end:] = tile * jnp.where(winds, WIND_STEP, scale)
        wind_rows = values[rows : rows + 2, :lons] * WIND_STEP

        @pl.when(lat_index > 0)
        def _():
            above = edge_ref[(lat_index - 1) * pieces + spot]
            field[spot, :1, :lons] += wind_rows[:1] * above

        @pl.when(lat_index < lat_count - 1)
        def _():
            below = edge_ref[(lat_index + 1) * pieces + spot]
            field[spot, rows - 1 :, :lons] -= wind_rows[1:] * below

    for spot in range(pieces):
        tile = field[spot, :, end:]
        before = field[(spot - 1) % pieces, :, end:]
        after = field[(spot + 1) % pieces, :, end:]
        shift = LANES - spare
        gain = pltpu.roll(tile, shift - 3, 1) * pltpu.roll(before, shift - 2, 1)
        loss = pltpu.roll(tile, LANES - 5, 1) * pltpu.roll(after, LANES - 2, 1)
        field[spot, :, end:] = tile - jnp.where(lane == spare - 1, loss, 0.0)
        field[spot, :, :LANES] += jnp.where(lane == 0, gain, 0.0)

    def product(kind, value, spot):
        high, low = split_bf16(value)
        table = tables[kind]
        span = table.shape[2] // 2
        both = jnp.dot(high, table[spot], preferred_element_type=jnp.float32)
        part = jnp.dot(low, table[spot, :, :span], preferred_element_type=jnp.float32)
        return part + both[:, :span] + both[:, span:]

    sums = [None, None, None]
    for spot in range(share):
        quarters = [field[quarter * share + spot, :, :lons] for quarter in range(4)]
        sum02, dif02 = quarters[0] + quarters[2], quarters[0] - quarters[2]
        sum13, dif13 = quarters[1] + quarters[3], quarters[1] - quarters[3]
        parts = []
        for kind, value in enumerate((sum02 + sum13, sum02 - sum13, dif02, dif13)):
            parts.append(product(kind, value, spot))
        parts = [parts[0], parts[1], parts[2] + parts[3]]
        sums = [part if total is None else total + part for total, part in zip(sums, parts)]
    slot_waves = wave_ref[...]
    waves = column_waves((column_count(), LANES))
    places = [
        jnp.where(waves == slot_waves[:, first : first + LANES], 1.0, 0.0).astype(jnp.bfloat16)
        for first in range(0, slot_waves.shape[1], LANES)
    ]
    places = jnp.concatenate(places, axis=1)
    placed = []
    for part in range(2):
        columns = []
        for total in sums:
            half = total.shape[1] // 2
            columns.append(total[:, part * half : (part + 1) * half])
        high, low = split_bf16(jnp.concatenate(columns, axis=1))
        value = jnp.dot(high, places, preferred_element_type=jnp.float32)
        value += jnp.dot(low, places, preferred_element_type=jnp.float32)
        kept = jnp.where(slot_waves < keep, value, 0.0)
        code = scale_code(jnp.max(jnp.abs(kept), axis=0, keepdims=True))
        steps = coded(kept, 1.0 / scale_of(code))
        codes = jnp.broadcast_to(code, (outs[0].shape[0] - rows, code.shape[1]))
        placed.append(as_int16(jnp.concatenate([steps, codes], axis=0)))
    for target in range(lat_count):
        for part in range(2):
            cols = slice(target * LANES, (target + 1) * LANES)
            outs[target][:, part * LANES : (part + 1) * LANES] = placed[part][:, cols]


def fourier(grids, edges, ring, wave_row, rows, lat_count):
    pieces = len(grids)
    width = grids[0].shape[1]
    padded_rows = -(-(rows + 1) // 16) * 16
    tables = [table_bf16(table) for table in fourier_tables(pieces)]
    return pl.pallas_call(
        functools.partial(fourier_kernel, ring, lat_count, pieces),
        out_shape=[jax.ShapeDtypeStruct((padded_rows, 2 * LANES), jnp.int16)] * lat_count,
        in_specs=[VMEM_SPEC] * (pieces + 6),
        out_specs=[VMEM_SPEC] * lat_count,
        scratch_shapes=[pltpu.VMEM((pieces, rows, width), jnp.float32)],
        compiler_params=pltpu.CompilerParams(vmem_limit_bytes=MIDDLE_BYTES),
        cost_estimate=pl.CostEstimate(
            flops=4 * 10**9, bytes_accessed=6 * 2**20, transcendentals=0
        ),
    )(*grids, edges, *tables, wave_row)


def places_kernel(groups, slot_ref, wave_ref, mine_ref, sorted_rows):
    lat_index = lax.axis_index("lat")
    slots = slot_ref.shape[1] // groups
    paired = (slots + 1) // 2
    shape = (LANES, LANES)
    down = lax.broadcasted_iota(jnp.int32, shape, 0)
    across = lax.broadcasted_iota(jnp.int32, shape, 1)
    filler = jnp.full((1, LANES - slots), 2.0 * M, jnp.float32)
    for group in range(groups):
        plain = slot_ref[:, group * slots : (group + 1) * slots].astype(jnp.float32)
        plain = jnp.concatenate([plain, filler], axis=1)
        row = jnp.broadcast_to(plain, shape)
        column = jnp.sum(jnp.where(down == across, row, 0.0), axis=1, keepdims=True)
        ahead = (row < column) | ((row == column) & (across < down))
        rank = jnp.sum(jnp.where(ahead, 1.0, 0.0), axis=1, keepdims=True)
        place = jnp.where(rank < paired, rank, SIDE + slots - 1.0 - rank)
        place = jnp.where(rank < slots, place, -1.0)
        hot = jnp.where(place == across.astype(jnp.float32), 1.0, 0.0)
        filled = jnp.sum(hot, axis=0, keepdims=True)
        values = jnp.sum(hot * column, axis=0, keepdims=True)
        values = jnp.where(filled > 0.5, values, 2.0 * M)
        sorted_rows[group] = jnp.broadcast_to(values, sorted_rows.shape[1:])

        @pl.when(group == lat_index)
        def _():
            mine_ref[:1] = values
            mine_ref[1:] = plain

    for step in range(groups):
        row = sorted_rows[partner(("lat",), (groups,), step), :1]
        wave_ref[:, step * LANES : (step + 1) * LANES] = row


def prepare_places(slot_wave, groups):
    width = groups * LANES
    return pl.pallas_call(
        functools.partial(places_kernel, groups),
        out_shape=[
            jax.ShapeDtypeStruct((1, width), jnp.float32),
            jax.ShapeDtypeStruct((2, LANES), jnp.float32),
        ],
        in_specs=[VMEM_SPEC],
        out_specs=[VMEM_SPEC] * 2,
        scratch_shapes=[pltpu.VMEM((groups, 8, LANES), jnp.float32)],
        compiler_params=pltpu.CompilerParams(vmem_limit_bytes=MIDDLE_BYTES),
        cost_estimate=pl.CostEstimate(flops=2 * 10**9, bytes_accessed=2**20, transcendentals=0),
    )(slot_wave[None])


def lane_pairs(row):
    lane = lax.broadcasted_iota(jnp.int32, row.shape, 1)
    other = pltpu.roll(row, SIDE, 1)
    return jnp.where(lane < SIDE, row, other), jnp.where(lane < SIDE, other, row)


def block_count(wave):
    return jnp.floor((jnp.maximum(M - wave, 0.0) + (BLOCK - 1)) * (1.0 / BLOCK))


def sweep_kernel(
    mine_ref, lat_ref,
    beta_ref, scale_ref, growth_ref, start_ref, state_ref, values_ref, more_ref, back_ref,
):
    shape = (LANES, LANES)
    same = lax.broadcasted_iota(jnp.int32, shape, 0) == lax.broadcasted_iota(jnp.int32, shape, 1)
    plain = jnp.broadcast_to(mine_ref[1:], shape)
    plain = jnp.sum(jnp.where(same, plain, 0.0), axis=1, keepdims=True)
    hot = (plain == mine_ref[:1]) & (plain < 2.0 * M)
    back_ref[...] = jnp.where(hot, 1.0, 0.0).astype(jnp.bfloat16)
    pair = lane_pairs(jnp.broadcast_to(mine_ref[:1], (8, LANES)))
    one, two = pair[0][:1], pair[1][:1]
    blocks = growth_ref.shape[0]
    turn = block_count(one)
    block = lax.broadcasted_iota(jnp.int32, (blocks, LANES), 0).astype(jnp.float32)
    second = block >= turn
    wave = jnp.where(second, two, one)
    limit = M - wave
    wave = jnp.minimum(wave, M - 1.0)
    first = (block - jnp.where(second, turn, 0.0)) * BLOCK

    scale = jnp.ones((blocks, LANES), jnp.float32)
    for index in range(BLOCK + 1):
        order = first + index
        degree = wave + order
        square = 4.0 * degree * degree - 1.0
        spread = 4.0 * order * (degree + wave)
        if index > 0:
            scale = scale * jnp.sqrt(square / spread)
        if index < BLOCK:
            beta_ref[pl.ds(index, blocks, stride=BLOCK)] = spread / jnp.maximum(square, 1.0)
            scale_ref[pl.ds(index, blocks, stride=BLOCK)] = jnp.where(order < limit, scale, 0.0)
    growth_ref[...] = scale

    counter = lax.broadcasted_iota(jnp.int32, (M, LANES), 0).astype(jnp.float32) + 1.0
    terms = jnp.log(1.0 + 0.5 / counter) * (1.0 / math.log(2.0))
    for kind, wave in enumerate((one, two)):
        wave = jnp.minimum(wave, M - 1.0)
        norm = jnp.sum(jnp.where(counter <= wave, terms, 0.0), axis=0, keepdims=True)
        coarse = lat_ref[1] * wave
        whole = jnp.floor(coarse)
        start_ref[2 * kind] = jnp.exp2(
            (coarse - whole) + lat_ref[2] * wave + 0.5 * (norm - 1.0)
        )
        start_ref[2 * kind + 1] = whole

    state_ref[0] = jnp.zeros_like(state_ref[0])
    state_ref[1] = start_ref[0]
    state_ref[2] = start_ref[1]
    points = lat_ref.shape[1]

    def step(target_ref, start, block, carry):
        first = 0
        for chunk in (points // 16 * 8, points - points // 16 * 8):
            rows = slice(first, first + chunk)

            def keep(order, value):
                target_ref[block - start, order, rows] = value

            sweep_block(block, turn, rows, lat_ref, beta_ref, growth_ref, start_ref, state_ref, keep)
            first += chunk
        return carry

    total = jnp.max(turn + block_count(two)).astype(jnp.int32)
    lax.fori_loop(0, jnp.minimum(total, HELD), functools.partial(step, values_ref, 0), 0)
    more = functools.partial(step, more_ref, HELD)
    lax.fori_loop(HELD, jnp.minimum(total, HELD + MORE), more, 0)


def sweep_block(block, turn, rows, lat_ref, beta_ref, growth_ref, start_ref, state_ref, use):
    base = pl.multiple_of(block * BLOCK, BLOCK)
    begins = block.astype(jnp.float32) == turn
    grow = growth_ref[pl.ds(block, 1)]
    cosine = lat_ref[0, rows]
    height = jnp.where(begins, start_ref[3, rows], state_ref[2, rows])
    factor = jnp.exp2(height)
    old = jnp.where(begins, 0.0, state_ref[0, rows])
    new = jnp.where(begins, start_ref[2, rows], state_ref[1, rows])
    for order in range(BLOCK):
        use(order, new * factor)
        beta = beta_ref[pl.ds(base + order, 1)]
        old, new = new, cosine * new - beta * old
    biggest = jnp.maximum(jnp.abs(old), jnp.abs(new)) * grow
    shift = jnp.floor(jnp.log(biggest) * (1.0 / math.log(2.0)))
    factor = grow * jnp.exp2(-shift)
    state_ref[0, rows] = old * factor
    state_ref[1, rows] = new * factor
    state_ref[2, rows] = height + shift


def prepare_recurrence(mine, pieces):
    latitudes = latitude_table()
    points = latitudes.shape[1]
    blocks = 2 * SPAN
    orders = jax.ShapeDtypeStruct((blocks * BLOCK, LANES), jnp.float32)
    return pl.pallas_call(
        sweep_kernel,
        out_shape=[
            orders,
            orders,
            jax.ShapeDtypeStruct((blocks, LANES), jnp.float32),
            jax.ShapeDtypeStruct((4, points, LANES), jnp.float32),
            jax.ShapeDtypeStruct((3, points, LANES), jnp.float32),
            jax.ShapeDtypeStruct((HELD, BLOCK, points, LANES), jnp.float32),
            jax.ShapeDtypeStruct((MORE, BLOCK, points, LANES), jnp.float32),
            jax.ShapeDtypeStruct((LANES, LANES), jnp.bfloat16),
        ],
        in_specs=[VMEM_SPEC] * 2,
        out_specs=[VMEM_SPEC] * 8,
        compiler_params=pltpu.CompilerParams(vmem_limit_bytes=late_bytes(pieces)),
        cost_estimate=pl.CostEstimate(
            flops=5 * 10**9, bytes_accessed=25 * 2**20, transcendentals=0
        ),
    )(mine, latitudes)


def resampled(first, fields, table, total):
    for piece, field in enumerate(fields):
        values = from_int16(field[...])
        values = values * scale_of(values[field.shape[0] - 1 :])
        high, low = split_bf16(values)
        spot = partner(("lat",), table.shape[:1], first + piece)
        both = jnp.concatenate([high, low], axis=1)
        part = jnp.dot(table[spot, 0], both, preferred_element_type=jnp.float32)
        part = part[:, : high.shape[1]] + part[:, high.shape[1] :]
        part += jnp.dot(table[spot, 1], high, preferred_element_type=jnp.float32)
        total = part if total is None else total + part
    return total


def resample_kernel(table_ref, *rest):
    rest[-1][...] = resampled(0, rest[:-1], table_ref, None)


def late_bytes(pieces):
    return LATE_BYTES if pieces <= 4 else VMEM_BYTES


def resample(fields, table):
    count, _, height, _ = table.shape
    span = fields[0].shape[1]
    return pl.pallas_call(
        resample_kernel,
        out_shape=jax.ShapeDtypeStruct((height, span), jnp.float32),
        in_specs=[VMEM_SPEC] * (1 + len(fields)),
        out_specs=VMEM_SPEC,
        compiler_params=pltpu.CompilerParams(vmem_limit_bytes=late_bytes(count)),
        cost_estimate=pl.CostEstimate(
            flops=10**9, bytes_accessed=4 * 2**20, transcendentals=0
        ),
    )(table, *fields)


def legendre_kernel(early, *rest):
    table, lat_ref, beta_ref, scale_ref, growth_ref, start_ref, left_ref, values_ref = rest[:8]
    more_ref, back_ref, total_ref, mine_ref = rest[8:12]
    fields, (out_ref, weights, state_ref, sums, result, final) = rest[12:-6], rest[-6:]
    points = lat_ref.shape[1]
    slots = out_ref.shape[0]
    mine = mine_ref[:1]
    odd = mine - 2.0 * jnp.floor(mine * 0.5) > 0.5
    pair = lane_pairs(jnp.broadcast_to(mine, (8, LANES)))
    turn = block_count(pair[0][:1])
    block_total = jnp.max(turn + block_count(pair[1][:1])).astype(jnp.int32)

    total = resampled(early, fields, table, total_ref[...])
    totals = [total[2 * points * kind : 2 * points * (kind + 1)] for kind in range(4)]
    left = lax.broadcasted_iota(jnp.int32, (points, LANES), 1) < SIDE
    for parity in range(2):
        for comp in range(2):
            cols = slice(comp * LANES, (comp + 1) * LANES)
            value = jnp.where(odd, totals[2 + parity][:, cols], totals[parity][:, cols])
            top, bottom = value[:points], value[points:]
            kind = 2 * parity + comp
            weights[0, kind] = jnp.where(left, top, pltpu.roll(bottom, SIDE, 1))
            weights[1, kind] = jnp.where(left, pltpu.roll(top, SIDE, 1), bottom)
    result[...] = jnp.zeros_like(result)
    state_ref[...] = left_ref[...]

    def reduced(block):
        base = pl.multiple_of(block * BLOCK, BLOCK)
        for comp in range(2):
            total = sums[pl.ds(comp * 8, BLOCK, stride=16)]
            for lane in range(1, 8):
                total += sums[pl.ds(comp * 8 + lane, BLOCK, stride=16)]
            total = total * scale_ref[pl.ds(base, BLOCK)]
            result[comp, pl.ds(base, BLOCK)] = total + pltpu.roll(total, SIDE, 1)

    def held_step(source_ref, start, block, carry):
        second = block.astype(jnp.float32) >= turn
        for parity in range(2):
            scaled = [
                jnp.where(second, weights[1, 2 * parity + comp], weights[0, 2 * parity + comp])
                for comp in range(2)
            ]
            for order in range(parity, BLOCK, 2):
                value = source_ref[block - start, order]
                for comp in range(2):
                    product = (value * scaled[comp]).reshape(points // 8, 8, LANES)
                    sums[pl.ds((order * 2 + comp) * 8, 8)] = product.sum(axis=0)
        reduced(block)
        return carry

    def step(block, carry):
        second = block.astype(jnp.float32) >= turn
        first = 0
        for chunk in CHUNKS:
            rows = slice(first, first + chunk)
            scaled = [jnp.where(second, weights[1, k, rows], weights[0, k, rows]) for k in range(4)]

            def add(order, value):
                for comp in range(2):
                    product = value * scaled[2 * (order % 2) + comp]
                    partial = product.reshape(chunk // 8, 8, LANES).sum(axis=0)
                    place = pl.ds((order * 2 + comp) * 8, 8)
                    if first == 0:
                        sums[place] = partial
                    else:
                        sums[place] += partial

            sweep_block(block, turn, rows, lat_ref, beta_ref, growth_ref, start_ref, state_ref, add)
            first += chunk
        reduced(block)
        return carry

    held = functools.partial(held_step, values_ref, 0)
    lax.fori_loop(0, jnp.minimum(block_total, HELD), held, 0)
    held = functools.partial(held_step, more_ref, HELD)
    lax.fori_loop(HELD, jnp.minimum(block_total, HELD + MORE), held, 0)
    lax.fori_loop(HELD + MORE, block_total, step, 0)

    left = lax.broadcasted_iota(jnp.int32, (BLOCK, LANES), 1) < SIDE
    spots = SPAN
    chosen = [jnp.broadcast_to(turn, (8, LANES)) == value for value in range(spots + 1)]
    chosen = [jnp.concatenate([mask] * (BLOCK // 8), axis=0) for mask in chosen]
    for place in range(spots):
        rows = slice(place * BLOCK, (place + 1) * BLOCK)
        for comp in range(2):
            early_part = jnp.where(turn > place, result[comp, rows], 0.0)
            later = jnp.zeros((BLOCK, LANES), jnp.float32)
            for value in range(spots + 1):
                base = (place + value) * BLOCK
                if base < result.shape[1]:
                    later = jnp.where(chosen[value], result[comp, base : base + BLOCK], later)
            final[comp, rows] = jnp.where(left, early_part, later)
    back = back_ref[...]
    dims = (((1,), (1,)), ((), ()))
    for comp in range(2):
        high, low = split_bf16(final[comp])
        value = lax.dot_general(back, high, dims, preferred_element_type=jnp.float32)
        value += lax.dot_general(back, low, dims, preferred_element_type=jnp.float32)
        out_ref[:, comp, :] = value[:slots, :M]


def resample_pieces(pieces, rows, padded_rows):
    full = resample_table()
    table = full.reshape(full.shape[0], pieces, rows).transpose(1, 0, 2)
    table = table_bf16(np.pad(table, ((0, 0), (0, 0), (0, padded_rows - rows))))
    return table.reshape(pieces, full.shape[0], 2, padded_rows).transpose(0, 2, 1, 3)


def legendre(fields, mine, prepared, table, slots):
    pieces = len(fields)
    early = pieces // 2
    latitudes = latitude_table()
    points = latitudes.shape[1]
    total = resample(fields[:early], table)
    block_rows = SPAN * BLOCK
    return pl.pallas_call(
        functools.partial(legendre_kernel, early),
        out_shape=jax.ShapeDtypeStruct((slots, 2, M), jnp.float32),
        in_specs=[VMEM_SPEC] * (12 + pieces - early),
        out_specs=VMEM_SPEC,
        scratch_shapes=[
            pltpu.VMEM((2, 4, points, LANES), jnp.float32),
            pltpu.VMEM((3, points, LANES), jnp.float32),
            pltpu.VMEM((BLOCK * 16, LANES), jnp.float32),
            pltpu.VMEM((2, 2 * block_rows, LANES), jnp.float32),
            pltpu.VMEM((2, block_rows, LANES), jnp.float32),
        ],
        compiler_params=pltpu.CompilerParams(vmem_limit_bytes=late_bytes(pieces)),
        cost_estimate=pl.CostEstimate(
            flops=8 * 10**9, bytes_accessed=6 * 2**20, transcendentals=0
        ),
    )(table, latitudes, *prepared, total, mine, *fields[early:])


def shards(tracer, wind_east, wind_north, keep_m, slot_wave):
    rows = tracer.shape[1]
    lat_count = lax.axis_size("lat")
    slots = slot_wave.shape[0] // lat_count
    axes = ("lev", "fld")
    ring = (axes, tuple(lax.axis_size(axis) for axis in axes))

    blocks, edges = advect(tracer, wind_east, wind_north, keep_m, ring)
    blocks, slot_wave = lax.optimization_barrier((blocks, slot_wave))
    grids = exchange(blocks, axes)
    edges = lax.all_to_all(edges, ("lat", *axes), split_axis=0, concat_axis=0, tiled=True)
    wave_row, mine = prepare_places(slot_wave, lat_count)
    waved = fourier(grids, edges, ring, wave_row, rows, lat_count)
    table = jnp.asarray(resample_pieces(lat_count, rows, waved[0].shape[0]))
    waved, mine, table = lax.optimization_barrier((list(waved), mine, table))
    fields = exchange(waved, "lat")
    prepared = prepare_recurrence(mine, lat_count)
    return legendre(fields, mine, prepared, table, slots)[None]


def solution(mesh):
    return jax.shard_map(
        shards,
        mesh=mesh,
        in_specs=(
            P("member", "lat", ("lev", "fld")),
            P("member", "lat", ("lev", "fld")),
            P("member", "lat", ("lev", "fld")),
            P("lat"),
            P(),
        ),
        out_specs=P(("member", "lev", "fld"), "lat", None, None),
        check_vma=False,
    )
```

```python
import functools
import math

import jax
import jax.numpy as jnp
import numpy as np
from jax import lax
from jax.experimental import pallas as pl
from jax.experimental.pallas import tpu as pltpu
from jax.sharding import PartitionSpec as P

M = 400
NLAT = 800
NLON = 1600
LANES = 128
BLOCK = 32
CHUNKS = (40, 32, 32)
SPAN = -(-M // BLOCK)
HELD = 13
MORE = 3
SIDE = LANES // 2
TOP = 32767.0
WIND_STEP = 1.5 / TOP
VMEM_BYTES = 60 * 2**20
LATE_BYTES = 10 * 2**20
MIDDLE_BYTES = 16 * 2**20
VMEM_SPEC = pl.BlockSpec(memory_space=pltpu.VMEM)
SMEM_SPEC = pl.BlockSpec(memory_space=pltpu.SMEM)
HBM_SPEC = pl.BlockSpec(memory_space=pltpu.HBM)


def split_bf16(values):
    high = values.astype(jnp.bfloat16)
    low = (values - high.astype(jnp.float32)).astype(jnp.bfloat16)
    return high, low


def table_bf16(table):
    high = table.astype(jnp.bfloat16)
    low = (table - high.astype(np.float64)).astype(jnp.bfloat16)
    return np.concatenate([high, low], axis=-1)


def fourier_tables(pieces):
    quarter = NLON // 4
    spots = np.arange(quarter)[:, None]
    factor = 1.0 / math.sqrt(NLON)

    def parts(waves):
        angles = 2.0 * math.pi / NLON * (spots * waves[None, :] % NLON)
        return factor * np.cos(angles), factor * np.sin(angles)

    def shaped(columns):
        pad = [(0, 0), (0, -columns[0].shape[1] % LANES)]
        table = np.concatenate([np.pad(part, pad) for part in columns], axis=1)
        return table.reshape(share, quarter // share, -1)

    share = pieces // 4
    tables = []
    for first in (0, 2):
        cosine, sine = parts(np.arange(first, M, 4))
        tables.append(shaped([cosine, -sine]))
    waves = np.arange(1, M, 2)
    sign = np.where(waves % 4 == 1, 1.0, -1.0)[None, :]
    cosine, sine = parts(waves)
    return [*tables, shaped([cosine, -sine]), shaped([-sign * sine, -sign * cosine])]


def column_waves(shape):
    row = lax.broadcasted_iota(jnp.int32, shape, 0)
    waves, first = jnp.full(shape, -1, jnp.int32), 0
    for start, step in ((0, 4), (2, 4), (1, 2)):
        count = len(range(start, M, step))
        inside = (row >= first) & (row < first + count)
        waves = jnp.where(inside, start + step * (row - first), waves)
        first += -(-count // LANES) * LANES
    return waves.astype(jnp.float32)


def column_count():
    return sum(-(-len(range(start, M, step)) // LANES) * LANES for start, step in ((0, 4), (2, 4), (1, 2)))


def resample_table():
    half = M // 2
    coarse = math.pi / M * (np.arange(M) + 0.5)
    fine = math.pi / NLAT * (np.arange(NLAT) + 0.5)
    waves = np.arange(M)
    weight = np.where(waves == 0, 1.0, 2.0) / M
    even = (np.cos(np.outer(coarse, waves)) * weight) @ np.cos(np.outer(waves, fine))
    odd = (np.sin(np.outer(coarse, waves)) * weight) @ np.sin(np.outer(waves, fine))
    rows = []
    for full in (even, odd):
        for sign in (1.0, -1.0):
            folded = (full[:half] + sign * full[::-1][:half]).reshape(2, half // 2, NLAT)
            rows.append(np.pad(folded, ((0, 0), (0, -half // 2 % 8), (0, 0))).reshape(-1, NLAT))
    return np.concatenate(rows, axis=0) * (np.sin(fine) * math.sqrt(2.0 / NLAT))


def latitude_table():
    half = M // 2
    angles = math.pi / M * (np.arange(half) + 0.5)
    log_sine = np.log2(np.sin(angles))
    coarse = np.round(log_sine * 1024.0) / 1024.0
    rows = np.stack([2.0 * np.cos(angles), coarse, log_sine - coarse]).reshape(3, 2, half // 2)
    rows = np.pad(rows, ((0, 0), (0, 0), (0, -half // 2 % 8)))
    return np.repeat(rows.transpose(0, 2, 1), SIDE, axis=2).astype(np.float32)


def scale_code(biggest):
    wanted = jnp.maximum(biggest, 1e-30) * (1.0 / TOP)
    exponent = jnp.floor(jnp.log(wanted) * (1.0 / math.log(2.0)))
    return exponent * 128.0 + jnp.ceil((wanted * jnp.exp2(-exponent) - 1.0) * 128.0)


def scale_of(code):
    exponent = jnp.floor(code * (1.0 / 128.0))
    rest = code - 128.0 * exponent
    return jnp.exp2(exponent) * (1.0 + rest * (1.0 / 128.0))


def coded(values, inverse):
    return jnp.floor(values * inverse + 0.5)


def as_int16(values):
    return values.astype(jnp.int32).astype(jnp.int16)


def from_int16(codes):
    return codes.astype(jnp.int32).astype(jnp.float32)


def partner(axes, sizes, step):
    count = math.prod(sizes)
    if count != 4:
        return step
    index = lax.axis_index(axes[0])
    for axis, size in zip(axes[1:], sizes[1:]):
        index = index * size + lax.axis_index(axis)
    return index ^ step


def exchange(blocks, axis):
    count = len(blocks)
    if count != 4:
        return list(lax.all_to_all(jnp.stack(blocks), axis, split_axis=0, concat_axis=0, tiled=True))
    pairs = [[(i, i ^ step) for i in range(count)] for step in range(count)]
    return [blocks[0]] + [lax.ppermute(blocks[step], axis, pairs[step]) for step in range(1, count)]


def advect_kernel(ring, lat_count, keep_hbm, tracer_hbm, east_hbm, north_hbm, *rest):
    levels, rows, lons = tracer_hbm.shape
    outs, (edge_ref, tracer, east_wind, north_wind, keep_ref, sems, keep_sem) = rest[:levels], rest[levels:]
    chosen = [partner(*ring, step) for step in range(levels)]
    copies = [None] * levels
    order = (*range(levels // 2, levels), *range(levels // 2))
    for step in order:
        copies[step] = [
            pltpu.make_async_copy(source.at[chosen[step]], target.at[step], sems.at[kind, step])
            for kind, (source, target) in enumerate(
                ((tracer_hbm, tracer), (east_hbm, east_wind), (north_hbm, north_wind))
            )
        ]
        for copy in copies[step]:
            copy.start()
    keep_copy = pltpu.make_async_copy(keep_hbm, keep_ref, keep_sem)
    keep_copy.start()
    padded_rows = outs[0].shape[0]
    keep_copy.wait()
    same = (rows, rows)
    same = lax.broadcasted_iota(jnp.int32, same, 0) == lax.broadcasted_iota(jnp.int32, same, 1)
    keep = jnp.broadcast_to(keep_ref[...].astype(jnp.float32), (rows, rows))
    keep = jnp.sum(jnp.where(same, keep, 0.0), axis=1, keepdims=True)
    end = (lons - 1) // LANES * LANES
    spare = lons - end
    lane = lax.broadcasted_iota(jnp.int32, (rows, LANES), 1)
    lat_index = lax.axis_index("lat")
    edge_ref[...] = jnp.zeros_like(edge_ref)
    for step in order:
        level = chosen[step]
        for copy in copies[step]:
            copy.wait()
        field = tracer[step].astype(jnp.float32)

        @pl.when(lat_index < lat_count - 1)
        def _():
            edge_ref[(lat_index + 1) * levels + level] = field[rows - 1 :]

        @pl.when(lat_index > 0)
        def _():
            edge_ref[(lat_index - 1) * levels + level] = field[:1]

        blank = jnp.zeros((rows, 1), jnp.float32)
        west = jnp.concatenate([blank, field[:, :-1]], axis=1)
        east = jnp.concatenate([field[:, 1:], blank], axis=1)
        blank = jnp.zeros((1, lons), jnp.float32)
        north = jnp.concatenate([blank, field[:-1]], axis=0)
        south = jnp.concatenate([field[1:], blank], axis=0)
        eastward = 0.5 * east_wind[step].astype(jnp.float32)
        northward = 0.5 * north_wind[step].astype(jnp.float32)
        moved = field - eastward * (east - west) - northward * (south - north)
        first, last = field[:, :1], field[:, lons - 1 :]
        biggest = jnp.max(jnp.abs(moved), axis=1, keepdims=True)
        biggest = jnp.maximum(biggest, jnp.maximum(jnp.abs(first), jnp.abs(last)))
        code = scale_code(biggest)
        inverse = 1.0 / scale_of(code)
        filler = jnp.zeros((rows, LANES - spare), jnp.float32)
        tile = jnp.concatenate([moved[:, end:], filler], axis=1)
        tile = jnp.where(lane == spare + 1, first, jnp.where(lane == spare + 2, last, tile))
        tile = coded(tile, inverse)
        tile = jnp.where(lane == spare, code, tile)
        winds = jnp.where(lane == spare + 3, eastward[:, :1], eastward[:, lons - 1 :])
        winds = coded(winds, 1.0 / WIND_STEP)
        tile = jnp.where((lane == spare + 3) | (lane == spare + 4), winds, tile)
        tile = jnp.where(lane == spare + 5, keep, tile)
        wind_rows = jnp.concatenate([northward[:1], northward[rows - 1 :]], axis=0)
        wind_rows = coded(wind_rows, 1.0 / WIND_STEP)
        blank = jnp.zeros((padded_rows - rows - 2, lons), jnp.float32)
        wind_rows = jnp.concatenate([wind_rows, blank], axis=0)
        filler = jnp.zeros((padded_rows - rows, LANES - spare), jnp.float32)
        wind_tile = jnp.concatenate([wind_rows[:, end:], filler], axis=1)
        steps = jnp.concatenate([coded(moved[:, :end], inverse), wind_rows[:, :end]], axis=0)
        outs[step][:, :end] = as_int16(steps)
        outs[step][:, end:] = as_int16(jnp.concatenate([tile, wind_tile], axis=0))


def advect(tracer, east_wind, north_wind, keep_m, ring):
    levels, rows, lons = tracer.shape
    lat_count = lax.axis_size("lat")
    width = (lons - 1) // LANES * LANES + LANES
    padded_rows = -(-(rows + 2) // 16) * 16
    held = pltpu.VMEM((levels, rows, lons), jnp.bfloat16)
    result = pl.pallas_call(
        functools.partial(advect_kernel, ring, lat_count),
        out_shape=[jax.ShapeDtypeStruct((padded_rows, width), jnp.int16)] * levels
        + [jax.ShapeDtypeStruct((lat_count * levels, 1, lons), jnp.float32)],
        in_specs=[HBM_SPEC] * 4,
        out_specs=[VMEM_SPEC] * (levels + 1),
        scratch_shapes=[
            held,
            held,
            held,
            pltpu.VMEM((1, rows), jnp.int32),
            pltpu.SemaphoreType.DMA((3, levels)),
            pltpu.SemaphoreType.DMA,
        ],
        compiler_params=pltpu.CompilerParams(vmem_limit_bytes=VMEM_BYTES),
        cost_estimate=pl.CostEstimate(
            flops=5 * 10**9, bytes_accessed=8 * levels * rows * lons, transcendentals=0
        ),
    )(keep_m[None], tracer, east_wind, north_wind)
    return list(result[:levels]), result[levels]


def exchanged_rows(rows):
    return -(-(rows + 1) // 16) * 16


def folded_rows(rows, slots):
    if 2 * slots <= LANES:
        return rows
    fits = 2 * slots <= LANES + SIDE + 8 and rows % 16 == 0 and rows <= 16 * 16
    return -(-(rows + rows // 2 + 16) // 16) * 16 if fits else 0


def fold(one, two, slots):
    rows = one.shape[0]
    total = folded_rows(rows, slots)
    if not total:
        return jnp.concatenate([one, two], axis=1)
    lane = lax.broadcasted_iota(jnp.int32, one.shape, 1)
    turned = pltpu.roll(two, slots, 1)
    whole = jnp.where(lane < slots, one, turned)
    if total == rows:
        return whole
    half = rows // 2
    halves = jnp.where(lane[:half] < SIDE, turned[:half], pltpu.roll(turned[half:], SIDE, 1))
    last = jnp.zeros((16, LANES), jnp.float32)
    for group in range(rows // 16):
        part = pltpu.roll(turned[16 * group : 16 * group + 16], (8 * group - SIDE) % LANES, 1)
        last = jnp.where(lane[:16] // 8 == group, part, last)
    filler = jnp.zeros((total - rows - half - 16, LANES), jnp.float32)
    return jnp.concatenate([whole, halves, last, filler], axis=0)


def unfold(block, rows, slots):
    total = folded_rows(rows, slots)
    if not total:
        return block[:, :LANES], block[:, LANES:]
    whole = block[:rows]
    lane = lax.broadcasted_iota(jnp.int32, whole.shape, 1)
    two = pltpu.roll(whole, (LANES - slots) % LANES, 1)
    if total != rows:
        half = rows // 2
        halves = block[rows : rows + half]
        last = block[rows + half : rows + half + 16]
        last = [pltpu.roll(last, (SIDE - 8 * group) % LANES, 1) for group in range(rows // 16)]
        halves = jnp.concatenate([halves, pltpu.roll(halves, SIDE, 1)], axis=0)
        rest = jnp.where(lane < SIDE, halves, jnp.concatenate(last, axis=0))
        two = jnp.where(lane < LANES - slots, two, pltpu.roll(rest, LANES - slots, 1))
    inside = lane < slots
    return jnp.where(inside, whole, 0.0), jnp.where(inside, two, 0.0)


def fourier_kernel(ring, lat_count, pieces, slots, *rest):
    grids, (edge_ref, *tables, wave_ref) = rest[:pieces], rest[pieces : pieces + 6]
    outs, field = rest[pieces + 6 : -1], rest[-1]
    _, rows, width = field.shape
    lons = tables[0].shape[1]
    share = pieces // 4

    end = width - LANES
    spare = lons - end
    lane = lax.broadcasted_iota(jnp.int32, (rows, LANES), 1)
    winds = (lane == spare + 3) | (lane == spare + 4)
    lat_index = lax.axis_index("lat")
    for piece in range(pieces):
        spot = partner(*ring, piece)
        values = from_int16(grids[piece][...])
        tile = values[:rows, end:]
        scale = scale_of(tile[:, spare : spare + 1])
        keep = tile[:, spare + 5 : spare + 6]
        field[spot, :, :end] = values[:rows, :end] * scale
        field[spot, :, end:] = tile * jnp.where(winds, WIND_STEP, scale)
        wind_rows = values[rows : rows + 2, :lons] * WIND_STEP

        @pl.when(lat_index > 0)
        def _():
            above = edge_ref[(lat_index - 1) * pieces + spot]
            field[spot, :1, :lons] += wind_rows[:1] * above

        @pl.when(lat_index < lat_count - 1)
        def _():
            below = edge_ref[(lat_index + 1) * pieces + spot]
            field[spot, rows - 1 :, :lons] -= wind_rows[1:] * below

    for spot in range(pieces):
        tile = field[spot, :, end:]
        before = field[(spot - 1) % pieces, :, end:]
        after = field[(spot + 1) % pieces, :, end:]
        shift = LANES - spare
        gain = pltpu.roll(tile, shift - 3, 1) * pltpu.roll(before, shift - 2, 1)
        loss = pltpu.roll(tile, LANES - 5, 1) * pltpu.roll(after, LANES - 2, 1)
        field[spot, :, end:] = tile - jnp.where(lane == spare - 1, loss, 0.0)
        field[spot, :, :LANES] += jnp.where(lane == 0, gain, 0.0)

    def product(kind, value, spot):
        high, low = split_bf16(value)
        table = tables[kind]
        span = table.shape[2] // 2
        both = jnp.dot(high, table[spot], preferred_element_type=jnp.float32)
        part = jnp.dot(low, table[spot, :, :span], preferred_element_type=jnp.float32)
        return part + both[:, :span] + both[:, span:]

    sums = [None, None, None]
    for spot in range(share):
        quarters = [field[quarter * share + spot, :, :lons] for quarter in range(4)]
        sum02, dif02 = quarters[0] + quarters[2], quarters[0] - quarters[2]
        sum13, dif13 = quarters[1] + quarters[3], quarters[1] - quarters[3]
        parts = []
        for kind, value in enumerate((sum02 + sum13, sum02 - sum13, dif02, dif13)):
            parts.append(product(kind, value, spot))
        parts = [parts[0], parts[1], parts[2] + parts[3]]
        sums = [part if total is None else total + part for total, part in zip(sums, parts)]
    slot_waves = wave_ref[...]
    waves = column_waves((column_count(), LANES))
    places = [
        jnp.where(waves == slot_waves[:, first : first + LANES], 1.0, 0.0).astype(jnp.bfloat16)
        for first in range(0, slot_waves.shape[1], LANES)
    ]
    places = jnp.concatenate(places, axis=1)
    placed = []
    for part in range(2):
        columns = []
        for total in sums:
            half = total.shape[1] // 2
            columns.append(total[:, part * half : (part + 1) * half])
        high, low = split_bf16(jnp.concatenate(columns, axis=1))
        value = jnp.dot(high, places, preferred_element_type=jnp.float32)
        value += jnp.dot(low, places, preferred_element_type=jnp.float32)
        kept = jnp.where(slot_waves < keep, value, 0.0)
        code = scale_code(jnp.max(jnp.abs(kept), axis=0, keepdims=True))
        steps = coded(kept, 1.0 / scale_of(code))
        codes = jnp.broadcast_to(code, (exchanged_rows(rows) - rows, code.shape[1]))
        placed.append(jnp.concatenate([steps, codes], axis=0))
    for target in range(lat_count):
        cols = slice(target * LANES, (target + 1) * LANES)
        outs[target][...] = as_int16(fold(placed[0][:, cols], placed[1][:, cols], slots))


def fourier(grids, edges, ring, wave_row, rows, slots, lat_count):
    pieces = len(grids)
    width = grids[0].shape[1]
    full = exchanged_rows(rows)
    folded = folded_rows(full, slots)
    shape = (folded, LANES) if folded else (full, 2 * LANES)
    tables = [table_bf16(table) for table in fourier_tables(pieces)]
    return pl.pallas_call(
        functools.partial(fourier_kernel, ring, lat_count, pieces, slots),
        out_shape=[jax.ShapeDtypeStruct(shape, jnp.int16)] * lat_count,
        in_specs=[VMEM_SPEC] * (pieces + 6),
        out_specs=[VMEM_SPEC] * lat_count,
        scratch_shapes=[pltpu.VMEM((pieces, rows, width), jnp.float32)],
        compiler_params=pltpu.CompilerParams(vmem_limit_bytes=MIDDLE_BYTES),
        cost_estimate=pl.CostEstimate(
            flops=4 * 10**9, bytes_accessed=6 * 2**20, transcendentals=0
        ),
    )(*grids, edges, *tables, wave_row)


def places_kernel(groups, slot_ref, wave_ref, mine_ref, sorted_rows):
    lat_index = lax.axis_index("lat")
    slots = slot_ref.shape[1] // groups
    paired = (slots + 1) // 2
    shape = (LANES, LANES)
    down = lax.broadcasted_iota(jnp.int32, shape, 0)
    across = lax.broadcasted_iota(jnp.int32, shape, 1)
    filler = jnp.full((1, LANES - slots), 2.0 * M, jnp.float32)
    for group in range(groups):
        plain = slot_ref[:, group * slots : (group + 1) * slots].astype(jnp.float32)
        plain = jnp.concatenate([plain, filler], axis=1)
        row = jnp.broadcast_to(plain, shape)
        column = jnp.sum(jnp.where(down == across, row, 0.0), axis=1, keepdims=True)
        ahead = (row < column) | ((row == column) & (across < down))
        rank = jnp.sum(jnp.where(ahead, 1.0, 0.0), axis=1, keepdims=True)
        def ordered(side):
            place = jnp.where(rank < paired, rank, side + slots - 1.0 - rank)
            place = jnp.where(rank < slots, place, -1.0)
            hot = jnp.where(place == across.astype(jnp.float32), 1.0, 0.0)
            filled = jnp.sum(hot, axis=0, keepdims=True)
            values = jnp.sum(hot * column, axis=0, keepdims=True)
            return jnp.where(filled > 0.5, values, 2.0 * M)

        sorted_rows[group] = jnp.broadcast_to(ordered(paired), sorted_rows.shape[1:])

        @pl.when(group == lat_index)
        def _():
            mine_ref[:1] = ordered(SIDE)
            mine_ref[1:] = plain

    for step in range(groups):
        row = sorted_rows[partner(("lat",), (groups,), step), :1]
        wave_ref[:, step * LANES : (step + 1) * LANES] = row


def prepare_places(slot_wave, groups):
    width = groups * LANES
    return pl.pallas_call(
        functools.partial(places_kernel, groups),
        out_shape=[
            jax.ShapeDtypeStruct((1, width), jnp.float32),
            jax.ShapeDtypeStruct((2, LANES), jnp.float32),
        ],
        in_specs=[VMEM_SPEC],
        out_specs=[VMEM_SPEC] * 2,
        scratch_shapes=[pltpu.VMEM((groups, 8, LANES), jnp.float32)],
        compiler_params=pltpu.CompilerParams(vmem_limit_bytes=MIDDLE_BYTES),
        cost_estimate=pl.CostEstimate(flops=2 * 10**9, bytes_accessed=2**20, transcendentals=0),
    )(slot_wave[None])


def lane_pairs(row):
    lane = lax.broadcasted_iota(jnp.int32, row.shape, 1)
    other = pltpu.roll(row, SIDE, 1)
    return jnp.where(lane < SIDE, row, other), jnp.where(lane < SIDE, other, row)


def block_count(wave):
    return jnp.floor((jnp.maximum(M - wave, 0.0) + (BLOCK - 1)) * (1.0 / BLOCK))


def sweep_kernel(
    mine_ref, lat_ref,
    beta_ref, scale_ref, growth_ref, start_ref, state_ref, values_ref, more_ref, back_ref,
):
    shape = (LANES, LANES)
    same = lax.broadcasted_iota(jnp.int32, shape, 0) == lax.broadcasted_iota(jnp.int32, shape, 1)
    plain = jnp.broadcast_to(mine_ref[1:], shape)
    plain = jnp.sum(jnp.where(same, plain, 0.0), axis=1, keepdims=True)
    hot = (plain == mine_ref[:1]) & (plain < 2.0 * M)
    back_ref[...] = jnp.where(hot, 1.0, 0.0).astype(jnp.bfloat16)
    pair = lane_pairs(jnp.broadcast_to(mine_ref[:1], (8, LANES)))
    one, two = pair[0][:1], pair[1][:1]
    blocks = growth_ref.shape[0]
    turn = block_count(one)
    block = lax.broadcasted_iota(jnp.int32, (blocks, LANES), 0).astype(jnp.float32)
    second = block >= turn
    wave = jnp.where(second, two, one)
    limit = M - wave
    wave = jnp.minimum(wave, M - 1.0)
    first = (block - jnp.where(second, turn, 0.0)) * BLOCK

    scale = jnp.ones((blocks, LANES), jnp.float32)
    for index in range(BLOCK + 1):
        order = first + index
        degree = wave + order
        square = 4.0 * degree * degree - 1.0
        spread = 4.0 * order * (degree + wave)
        if index > 0:
            scale = scale * jnp.sqrt(square / spread)
        if index < BLOCK:
            beta_ref[pl.ds(index, blocks, stride=BLOCK)] = spread / jnp.maximum(square, 1.0)
            scale_ref[pl.ds(index, blocks, stride=BLOCK)] = jnp.where(order < limit, scale, 0.0)
    growth_ref[...] = scale

    counter = lax.broadcasted_iota(jnp.int32, (M, LANES), 0).astype(jnp.float32) + 1.0
    terms = jnp.log(1.0 + 0.5 / counter) * (1.0 / math.log(2.0))
    for kind, wave in enumerate((one, two)):
        wave = jnp.minimum(wave, M - 1.0)
        norm = jnp.sum(jnp.where(counter <= wave, terms, 0.0), axis=0, keepdims=True)
        coarse = lat_ref[1] * wave
        whole = jnp.floor(coarse)
        start_ref[2 * kind] = jnp.exp2(
            (coarse - whole) + lat_ref[2] * wave + 0.5 * (norm - 1.0)
        )
        start_ref[2 * kind + 1] = whole

    state_ref[0] = jnp.zeros_like(state_ref[0])
    state_ref[1] = start_ref[0]
    state_ref[2] = start_ref[1]
    points = lat_ref.shape[1]

    def step(target_ref, start, block, carry):
        first = 0
        for chunk in (points // 16 * 8, points - points // 16 * 8):
            rows = slice(first, first + chunk)

            def keep(order, value):
                target_ref[block - start, order, rows] = value

            sweep_block(block, turn, rows, lat_ref, beta_ref, growth_ref, start_ref, state_ref, keep)
            first += chunk
        return carry

    total = jnp.max(turn + block_count(two)).astype(jnp.int32)
    lax.fori_loop(0, jnp.minimum(total, HELD), functools.partial(step, values_ref, 0), 0)
    more = functools.partial(step, more_ref, HELD)
    lax.fori_loop(HELD, jnp.minimum(total, HELD + MORE), more, 0)


def sweep_block(block, turn, rows, lat_ref, beta_ref, growth_ref, start_ref, state_ref, use):
    base = pl.multiple_of(block * BLOCK, BLOCK)
    begins = block.astype(jnp.float32) == turn
    grow = growth_ref[pl.ds(block, 1)]
    cosine = lat_ref[0, rows]
    height = jnp.where(begins, start_ref[3, rows], state_ref[2, rows])
    factor = jnp.exp2(height)
    old = jnp.where(begins, 0.0, state_ref[0, rows])
    new = jnp.where(begins, start_ref[2, rows], state_ref[1, rows])
    for order in range(BLOCK):
        use(order, new * factor)
        beta = beta_ref[pl.ds(base + order, 1)]
        old, new = new, cosine * new - beta * old
    biggest = jnp.maximum(jnp.abs(old), jnp.abs(new)) * grow
    shift = jnp.floor(jnp.log(biggest) * (1.0 / math.log(2.0)))
    factor = grow * jnp.exp2(-shift)
    state_ref[0, rows] = old * factor
    state_ref[1, rows] = new * factor
    state_ref[2, rows] = height + shift


def prepare_recurrence(mine, pieces):
    latitudes = latitude_table()
    points = latitudes.shape[1]
    blocks = 2 * SPAN
    orders = jax.ShapeDtypeStruct((blocks * BLOCK, LANES), jnp.float32)
    return pl.pallas_call(
        sweep_kernel,
        out_shape=[
            orders,
            orders,
            jax.ShapeDtypeStruct((blocks, LANES), jnp.float32),
            jax.ShapeDtypeStruct((4, points, LANES), jnp.float32),
            jax.ShapeDtypeStruct((3, points, LANES), jnp.float32),
            jax.ShapeDtypeStruct((HELD, BLOCK, points, LANES), jnp.float32),
            jax.ShapeDtypeStruct((MORE, BLOCK, points, LANES), jnp.float32),
            jax.ShapeDtypeStruct((LANES, LANES), jnp.bfloat16),
        ],
        in_specs=[VMEM_SPEC] * 2,
        out_specs=[VMEM_SPEC] * 8,
        compiler_params=pltpu.CompilerParams(vmem_limit_bytes=late_bytes(pieces)),
        cost_estimate=pl.CostEstimate(
            flops=5 * 10**9, bytes_accessed=25 * 2**20, transcendentals=0
        ),
    )(mine, latitudes)


def resampled(first, fields, table, slots, total):
    for piece, field in enumerate(fields):
        rows = table.shape[3]
        parts = []
        for part in unfold(from_int16(field[...]), rows, slots):
            part = part * scale_of(part[rows - 1 :])
            lane = lax.broadcasted_iota(jnp.int32, part.shape, 1)
            shift = SIDE - (slots + 1) // 2
            parts.append(jnp.where(lane < SIDE, part, pltpu.roll(part, shift, 1)))
        values = jnp.concatenate(parts, axis=1)
        high, low = split_bf16(values)
        spot = partner(("lat",), table.shape[:1], first + piece)
        both = jnp.concatenate([high, low], axis=1)
        part = jnp.dot(table[spot, 0], both, preferred_element_type=jnp.float32)
        part = part[:, : high.shape[1]] + part[:, high.shape[1] :]
        part += jnp.dot(table[spot, 1], high, preferred_element_type=jnp.float32)
        total = part if total is None else total + part
    return total


def resample_kernel(slots, table_ref, *rest):
    rest[-1][...] = resampled(0, rest[:-1], table_ref, slots, None)


def late_bytes(pieces):
    return LATE_BYTES if pieces <= 4 else VMEM_BYTES


def resample(fields, table, slots):
    count, _, height, _ = table.shape
    span = 2 * LANES
    return pl.pallas_call(
        functools.partial(resample_kernel, slots),
        out_shape=jax.ShapeDtypeStruct((height, span), jnp.float32),
        in_specs=[VMEM_SPEC] * (1 + len(fields)),
        out_specs=VMEM_SPEC,
        compiler_params=pltpu.CompilerParams(vmem_limit_bytes=late_bytes(count)),
        cost_estimate=pl.CostEstimate(
            flops=10**9, bytes_accessed=4 * 2**20, transcendentals=0
        ),
    )(table, *fields)


def legendre_kernel(early, *rest):
    table, lat_ref, beta_ref, scale_ref, growth_ref, start_ref, left_ref, values_ref = rest[:8]
    more_ref, back_ref, total_ref, mine_ref = rest[8:12]
    fields, (out_ref, weights, state_ref, sums, result, final) = rest[12:-6], rest[-6:]
    points = lat_ref.shape[1]
    slots = out_ref.shape[0]
    mine = mine_ref[:1]
    odd = mine - 2.0 * jnp.floor(mine * 0.5) > 0.5
    pair = lane_pairs(jnp.broadcast_to(mine, (8, LANES)))
    turn = block_count(pair[0][:1])
    block_total = jnp.max(turn + block_count(pair[1][:1])).astype(jnp.int32)

    total = resampled(early, fields, table, slots, total_ref[...])
    totals = [total[2 * points * kind : 2 * points * (kind + 1)] for kind in range(4)]
    left = lax.broadcasted_iota(jnp.int32, (points, LANES), 1) < SIDE
    for parity in range(2):
        for comp in range(2):
            cols = slice(comp * LANES, (comp + 1) * LANES)
            value = jnp.where(odd, totals[2 + parity][:, cols], totals[parity][:, cols])
            top, bottom = value[:points], value[points:]
            kind = 2 * parity + comp
            weights[0, kind] = jnp.where(left, top, pltpu.roll(bottom, SIDE, 1))
            weights[1, kind] = jnp.where(left, pltpu.roll(top, SIDE, 1), bottom)
    result[...] = jnp.zeros_like(result)
    state_ref[...] = left_ref[...]

    def reduced(block):
        base = pl.multiple_of(block * BLOCK, BLOCK)
        for comp in range(2):
            total = sums[pl.ds(comp * 8, BLOCK, stride=16)]
            for lane in range(1, 8):
                total += sums[pl.ds(comp * 8 + lane, BLOCK, stride=16)]
            total = total * scale_ref[pl.ds(base, BLOCK)]
            result[comp, pl.ds(base, BLOCK)] = total + pltpu.roll(total, SIDE, 1)

    def held_step(source_ref, start, block, carry):
        second = block.astype(jnp.float32) >= turn
        for parity in range(2):
            scaled = [
                jnp.where(second, weights[1, 2 * parity + comp], weights[0, 2 * parity + comp])
                for comp in range(2)
            ]
            for order in range(parity, BLOCK, 2):
                value = source_ref[block - start, order]
                for comp in range(2):
                    product = (value * scaled[comp]).reshape(points // 8, 8, LANES)
                    sums[pl.ds((order * 2 + comp) * 8, 8)] = product.sum(axis=0)
        reduced(block)
        return carry

    def step(block, carry):
        second = block.astype(jnp.float32) >= turn
        first = 0
        for chunk in CHUNKS:
            rows = slice(first, first + chunk)
            scaled = [jnp.where(second, weights[1, k, rows], weights[0, k, rows]) for k in range(4)]

            def add(order, value):
                for comp in range(2):
                    product = value * scaled[2 * (order % 2) + comp]
                    partial = product.reshape(chunk // 8, 8, LANES).sum(axis=0)
                    place = pl.ds((order * 2 + comp) * 8, 8)
                    if first == 0:
                        sums[place] = partial
                    else:
                        sums[place] += partial

            sweep_block(block, turn, rows, lat_ref, beta_ref, growth_ref, start_ref, state_ref, add)
            first += chunk
        reduced(block)
        return carry

    held = functools.partial(held_step, values_ref, 0)
    lax.fori_loop(0, jnp.minimum(block_total, HELD), held, 0)
    held = functools.partial(held_step, more_ref, HELD)
    lax.fori_loop(HELD, jnp.minimum(block_total, HELD + MORE), held, 0)
    lax.fori_loop(HELD + MORE, block_total, step, 0)

    left = lax.broadcasted_iota(jnp.int32, (BLOCK, LANES), 1) < SIDE
    spots = SPAN
    chosen = [jnp.broadcast_to(turn, (8, LANES)) == value for value in range(spots + 1)]
    chosen = [jnp.concatenate([mask] * (BLOCK // 8), axis=0) for mask in chosen]
    for place in range(spots):
        rows = slice(place * BLOCK, (place + 1) * BLOCK)
        for comp in range(2):
            early_part = jnp.where(turn > place, result[comp, rows], 0.0)
            later = jnp.zeros((BLOCK, LANES), jnp.float32)
            for value in range(spots + 1):
                base = (place + value) * BLOCK
                if base < result.shape[1]:
                    later = jnp.where(chosen[value], result[comp, base : base + BLOCK], later)
            final[comp, rows] = jnp.where(left, early_part, later)
    back = back_ref[...]
    dims = (((1,), (1,)), ((), ()))
    for comp in range(2):
        high, low = split_bf16(final[comp])
        value = lax.dot_general(back, high, dims, preferred_element_type=jnp.float32)
        value += lax.dot_general(back, low, dims, preferred_element_type=jnp.float32)
        out_ref[:, comp, :] = value[:slots, :M]


def resample_pieces(pieces, rows, padded_rows):
    full = resample_table()
    table = full.reshape(full.shape[0], pieces, rows).transpose(1, 0, 2)
    table = table_bf16(np.pad(table, ((0, 0), (0, 0), (0, padded_rows - rows))))
    return table.reshape(pieces, full.shape[0], 2, padded_rows).transpose(0, 2, 1, 3)


def legendre(fields, mine, prepared, table, slots):
    pieces = len(fields)
    early = pieces // 2
    latitudes = latitude_table()
    points = latitudes.shape[1]
    total = resample(fields[:early], table, slots)
    block_rows = SPAN * BLOCK
    return pl.pallas_call(
        functools.partial(legendre_kernel, early),
        out_shape=jax.ShapeDtypeStruct((slots, 2, M), jnp.float32),
        in_specs=[VMEM_SPEC] * (12 + pieces - early),
        out_specs=VMEM_SPEC,
        scratch_shapes=[
            pltpu.VMEM((2, 4, points, LANES), jnp.float32),
            pltpu.VMEM((3, points, LANES), jnp.float32),
            pltpu.VMEM((BLOCK * 16, LANES), jnp.float32),
            pltpu.VMEM((2, 2 * block_rows, LANES), jnp.float32),
            pltpu.VMEM((2, block_rows, LANES), jnp.float32),
        ],
        compiler_params=pltpu.CompilerParams(vmem_limit_bytes=late_bytes(pieces)),
        cost_estimate=pl.CostEstimate(
            flops=8 * 10**9, bytes_accessed=6 * 2**20, transcendentals=0
        ),
    )(table, latitudes, *prepared, total, mine, *fields[early:])


def shards(tracer, wind_east, wind_north, keep_m, slot_wave):
    rows = tracer.shape[1]
    lat_count = lax.axis_size("lat")
    slots = slot_wave.shape[0] // lat_count
    axes = ("lev", "fld")
    ring = (axes, tuple(lax.axis_size(axis) for axis in axes))

    blocks, edges = advect(tracer, wind_east, wind_north, keep_m, ring)
    blocks, slot_wave = lax.optimization_barrier((blocks, slot_wave))
    grids = exchange(blocks, axes)
    edges = lax.all_to_all(edges, ("lat", *axes), split_axis=0, concat_axis=0, tiled=True)
    wave_row, mine = prepare_places(slot_wave, lat_count)
    waved = fourier(grids, edges, ring, wave_row, rows, slots, lat_count)
    table = jnp.asarray(resample_pieces(lat_count, rows, exchanged_rows(rows)))
    waved, mine, table = lax.optimization_barrier((list(waved), mine, table))
    fields = exchange(waved, "lat")
    prepared = prepare_recurrence(mine, lat_count)
    return legendre(fields, mine, prepared, table, slots)[None]


def solution(mesh):
    return jax.shard_map(
        shards,
        mesh=mesh,
        in_specs=(
            P("member", "lat", ("lev", "fld")),
            P("member", "lat", ("lev", "fld")),
            P("member", "lat", ("lev", "fld")),
            P("lat"),
            P(),
        ),
        out_specs=P(("member", "lev", "fld"), "lat", None, None),
        check_vma=False,
    )
```

```python
import functools
import math

import jax
import jax.numpy as jnp
import numpy as np
from jax import lax
from jax.experimental import pallas as pl
from jax.experimental.pallas import tpu as pltpu
from jax.sharding import PartitionSpec as P

M = 400
NLAT = 800
NLON = 1600
LANES = 128
BLOCK = 32
CHUNKS = (40, 32, 32)
SPAN = -(-M // BLOCK)
HELD = 13
MORE = 3
SIDE = LANES // 2
TOP = 32767.0
WIND_STEP = 1.5 / TOP
VMEM_BYTES = 60 * 2**20
LATE_BYTES = 10 * 2**20
MIDDLE_BYTES = 16 * 2**20
VMEM_SPEC = pl.BlockSpec(memory_space=pltpu.VMEM)
SMEM_SPEC = pl.BlockSpec(memory_space=pltpu.SMEM)
HBM_SPEC = pl.BlockSpec(memory_space=pltpu.HBM)


def split_bf16(values):
    high = values.astype(jnp.bfloat16)
    low = (values - high.astype(jnp.float32)).astype(jnp.bfloat16)
    return high, low


def table_bf16(table):
    high = table.astype(jnp.bfloat16)
    low = (table - high.astype(np.float64)).astype(jnp.bfloat16)
    return np.concatenate([high, low], axis=-1)


def fourier_tables(pieces):
    quarter = NLON // 4
    spots = np.arange(quarter)[:, None]
    factor = 1.0 / math.sqrt(NLON)

    def parts(waves):
        angles = 2.0 * math.pi / NLON * (spots * waves[None, :] % NLON)
        return factor * np.cos(angles), factor * np.sin(angles)

    def shaped(columns):
        pad = [(0, 0), (0, -columns[0].shape[1] % LANES)]
        table = np.concatenate([np.pad(part, pad) for part in columns], axis=1)
        return table.reshape(share, quarter // share, -1)

    share = pieces // 4
    tables = []
    for first in (0, 2):
        cosine, sine = parts(np.arange(first, M, 4))
        tables.append(shaped([cosine, -sine]))
    cosine, sine = parts(np.arange(1, M, 2))
    return [*tables, shaped([cosine, -sine])]


def column_waves(shape):
    row = lax.broadcasted_iota(jnp.int32, shape, 0)
    waves, first = jnp.full(shape, -1, jnp.int32), 0
    for start, step in ((0, 4), (2, 4), (1, 2)):
        count = len(range(start, M, step))
        inside = (row >= first) & (row < first + count)
        waves = jnp.where(inside, start + step * (row - first), waves)
        first += -(-count // LANES) * LANES
    return waves.astype(jnp.float32)


def column_count():
    return sum(-(-len(range(start, M, step)) // LANES) * LANES for start, step in ((0, 4), (2, 4), (1, 2)))


def resample_table():
    half = M // 2
    coarse = math.pi / M * (np.arange(M) + 0.5)
    fine = math.pi / NLAT * (np.arange(NLAT) + 0.5)
    waves = np.arange(M)
    weight = np.where(waves == 0, 1.0, 2.0) / M
    even = (np.cos(np.outer(coarse, waves)) * weight) @ np.cos(np.outer(waves, fine))
    odd = (np.sin(np.outer(coarse, waves)) * weight) @ np.sin(np.outer(waves, fine))
    rows = []
    for full in (even, odd):
        for sign in (1.0, -1.0):
            folded = (full[:half] + sign * full[::-1][:half]).reshape(2, half // 2, NLAT)
            rows.append(np.pad(folded, ((0, 0), (0, -half // 2 % 8), (0, 0))).reshape(-1, NLAT))
    return np.concatenate(rows, axis=0) * (np.sin(fine) * math.sqrt(2.0 / NLAT))


def latitude_table():
    half = M // 2
    angles = math.pi / M * (np.arange(half) + 0.5)
    log_sine = np.log2(np.sin(angles))
    coarse = np.round(log_sine * 1024.0) / 1024.0
    rows = np.stack([2.0 * np.cos(angles), coarse, log_sine - coarse]).reshape(3, 2, half // 2)
    rows = np.pad(rows, ((0, 0), (0, 0), (0, -half // 2 % 8)))
    return np.repeat(rows.transpose(0, 2, 1), SIDE, axis=2).astype(np.float32)


def scale_code(biggest):
    wanted = jnp.maximum(biggest, 1e-30) * (1.0 / TOP)
    exponent = jnp.floor(jnp.log(wanted) * (1.0 / math.log(2.0)))
    return exponent * 128.0 + jnp.ceil((wanted * jnp.exp2(-exponent) - 1.0) * 128.0)


def scale_of(code):
    exponent = jnp.floor(code * (1.0 / 128.0))
    rest = code - 128.0 * exponent
    return jnp.exp2(exponent) * (1.0 + rest * (1.0 / 128.0))


def coded(values, inverse):
    return jnp.floor(values * inverse + 0.5)


def as_int16(values):
    return values.astype(jnp.int32).astype(jnp.int16)


def from_int16(codes):
    return codes.astype(jnp.int32).astype(jnp.float32)


def partner(axes, sizes, step):
    count = math.prod(sizes)
    if count != 4:
        return step
    index = lax.axis_index(axes[0])
    for axis, size in zip(axes[1:], sizes[1:]):
        index = index * size + lax.axis_index(axis)
    return index ^ step


def exchange(blocks, axis):
    count = len(blocks)
    if count != 4:
        return list(lax.all_to_all(jnp.stack(blocks), axis, split_axis=0, concat_axis=0, tiled=True))
    pairs = [[(i, i ^ step) for i in range(count)] for step in range(count)]
    return [blocks[0]] + [lax.ppermute(blocks[step], axis, pairs[step]) for step in range(1, count)]


def advect_kernel(ring, lat_count, keep_hbm, tracer_hbm, east_hbm, north_hbm, *rest):
    levels, rows, lons = tracer_hbm.shape
    outs, (edge_ref, tracer, east_wind, north_wind, keep_ref, sems, keep_sem) = rest[:levels], rest[levels:]
    chosen = [partner(*ring, step) for step in range(levels)]
    copies = [None] * levels
    order = (*range(levels // 2, levels), *range(levels // 2))
    for step in order:
        copies[step] = [
            pltpu.make_async_copy(source.at[chosen[step]], target.at[step], sems.at[kind, step])
            for kind, (source, target) in enumerate(
                ((tracer_hbm, tracer), (east_hbm, east_wind), (north_hbm, north_wind))
            )
        ]
        for copy in copies[step]:
            copy.start()
    keep_copy = pltpu.make_async_copy(keep_hbm, keep_ref, keep_sem)
    keep_copy.start()
    padded_rows = outs[0].shape[0]
    keep_copy.wait()
    same = (rows, rows)
    same = lax.broadcasted_iota(jnp.int32, same, 0) == lax.broadcasted_iota(jnp.int32, same, 1)
    keep = jnp.broadcast_to(keep_ref[...].astype(jnp.float32), (rows, rows))
    keep = jnp.sum(jnp.where(same, keep, 0.0), axis=1, keepdims=True)
    end = (lons - 1) // LANES * LANES
    spare = lons - end
    lane = lax.broadcasted_iota(jnp.int32, (rows, LANES), 1)
    lat_index = lax.axis_index("lat")
    edge_ref[...] = jnp.zeros_like(edge_ref)
    for step in order:
        level = chosen[step]
        for copy in copies[step]:
            copy.wait()
        field = tracer[step].astype(jnp.float32)

        @pl.when(lat_index < lat_count - 1)
        def _():
            edge_ref[(lat_index + 1) * levels + level] = field[rows - 1 :]

        @pl.when(lat_index > 0)
        def _():
            edge_ref[(lat_index - 1) * levels + level] = field[:1]

        blank = jnp.zeros((rows, 1), jnp.float32)
        west = jnp.concatenate([blank, field[:, :-1]], axis=1)
        east = jnp.concatenate([field[:, 1:], blank], axis=1)
        blank = jnp.zeros((1, lons), jnp.float32)
        north = jnp.concatenate([blank, field[:-1]], axis=0)
        south = jnp.concatenate([field[1:], blank], axis=0)
        eastward = 0.5 * east_wind[step].astype(jnp.float32)
        northward = 0.5 * north_wind[step].astype(jnp.float32)
        moved = field - eastward * (east - west) - northward * (south - north)
        first, last = field[:, :1], field[:, lons - 1 :]
        biggest = jnp.max(jnp.abs(moved), axis=1, keepdims=True)
        biggest = jnp.maximum(biggest, jnp.maximum(jnp.abs(first), jnp.abs(last)))
        code = scale_code(biggest)
        inverse = 1.0 / scale_of(code)
        filler = jnp.zeros((rows, LANES - spare), jnp.float32)
        tile = jnp.concatenate([moved[:, end:], filler], axis=1)
        tile = jnp.where(lane == spare + 1, first, jnp.where(lane == spare + 2, last, tile))
        tile = coded(tile, inverse)
        tile = jnp.where(lane == spare, code, tile)
        winds = jnp.where(lane == spare + 3, eastward[:, :1], eastward[:, lons - 1 :])
        winds = coded(winds, 1.0 / WIND_STEP)
        tile = jnp.where((lane == spare + 3) | (lane == spare + 4), winds, tile)
        tile = jnp.where(lane == spare + 5, keep, tile)
        wind_rows = jnp.concatenate([northward[:1], northward[rows - 1 :]], axis=0)
        wind_rows = coded(wind_rows, 1.0 / WIND_STEP)
        blank = jnp.zeros((padded_rows - rows - 2, lons), jnp.float32)
        wind_rows = jnp.concatenate([wind_rows, blank], axis=0)
        filler = jnp.zeros((padded_rows - rows, LANES - spare), jnp.float32)
        wind_tile = jnp.concatenate([wind_rows[:, end:], filler], axis=1)
        steps = jnp.concatenate([coded(moved[:, :end], inverse), wind_rows[:, :end]], axis=0)
        outs[step][:, :end] = as_int16(steps)
        outs[step][:, end:] = as_int16(jnp.concatenate([tile, wind_tile], axis=0))


def advect(tracer, east_wind, north_wind, keep_m, ring):
    levels, rows, lons = tracer.shape
    lat_count = lax.axis_size("lat")
    width = (lons - 1) // LANES * LANES + LANES
    padded_rows = -(-(rows + 2) // 16) * 16
    held = pltpu.VMEM((levels, rows, lons), jnp.bfloat16)
    result = pl.pallas_call(
        functools.partial(advect_kernel, ring, lat_count),
        out_shape=[jax.ShapeDtypeStruct((padded_rows, width), jnp.int16)] * levels
        + [jax.ShapeDtypeStruct((lat_count * levels, 1, lons), jnp.float32)],
        in_specs=[HBM_SPEC] * 4,
        out_specs=[VMEM_SPEC] * (levels + 1),
        scratch_shapes=[
            held,
            held,
            held,
            pltpu.VMEM((1, rows), jnp.int32),
            pltpu.SemaphoreType.DMA((3, levels)),
            pltpu.SemaphoreType.DMA,
        ],
        compiler_params=pltpu.CompilerParams(vmem_limit_bytes=VMEM_BYTES),
        cost_estimate=pl.CostEstimate(
            flops=5 * 10**9, bytes_accessed=8 * levels * rows * lons, transcendentals=0
        ),
    )(keep_m[None], tracer, east_wind, north_wind)
    return list(result[:levels]), result[levels]


def exchanged_rows(rows):
    return -(-(rows + 1) // 16) * 16


def folded_rows(rows, slots):
    if 2 * slots <= LANES:
        return rows
    fits = 2 * slots <= LANES + SIDE + 8 and rows % 16 == 0 and rows <= 16 * 16
    return -(-(rows + rows // 2 + 16) // 16) * 16 if fits else 0


def fold(one, two, slots):
    rows = one.shape[0]
    total = folded_rows(rows, slots)
    if not total:
        return jnp.concatenate([one, two], axis=1)
    lane = lax.broadcasted_iota(jnp.int32, one.shape, 1)
    turned = pltpu.roll(two, slots, 1)
    whole = jnp.where(lane < slots, one, turned)
    if total == rows:
        return whole
    half = rows // 2
    halves = jnp.where(lane[:half] < SIDE, turned[:half], pltpu.roll(turned[half:], SIDE, 1))
    last = jnp.zeros((16, LANES), jnp.float32)
    for group in range(rows // 16):
        part = pltpu.roll(turned[16 * group : 16 * group + 16], (8 * group - SIDE) % LANES, 1)
        last = jnp.where(lane[:16] // 8 == group, part, last)
    filler = jnp.zeros((total - rows - half - 16, LANES), jnp.float32)
    return jnp.concatenate([whole, halves, last, filler], axis=0)


def unfold(block, rows, slots):
    total = folded_rows(rows, slots)
    if not total:
        return block[:, :LANES], block[:, LANES:]
    whole = block[:rows]
    lane = lax.broadcasted_iota(jnp.int32, whole.shape, 1)
    two = pltpu.roll(whole, (LANES - slots) % LANES, 1)
    if total != rows:
        half = rows // 2
        halves = block[rows : rows + half]
        last = block[rows + half : rows + half + 16]
        last = [pltpu.roll(last, (SIDE - 8 * group) % LANES, 1) for group in range(rows // 16)]
        halves = jnp.concatenate([halves, pltpu.roll(halves, SIDE, 1)], axis=0)
        rest = jnp.where(lane < SIDE, halves, jnp.concatenate(last, axis=0))
        two = jnp.where(lane < LANES - slots, two, pltpu.roll(rest, LANES - slots, 1))
    inside = lane < slots
    return jnp.where(inside, whole, 0.0), jnp.where(inside, two, 0.0)


def fourier_kernel(ring, lat_count, pieces, slots, *rest):
    grids, (edge_ref, *tables, wave_ref) = rest[:pieces], rest[pieces : pieces + 5]
    outs, field = rest[pieces + 5 : -1], rest[-1]
    _, rows, width = field.shape
    lons = tables[0].shape[1]
    share = pieces // 4

    end = width - LANES
    spare = lons - end
    lane = lax.broadcasted_iota(jnp.int32, (rows, LANES), 1)
    winds = (lane == spare + 3) | (lane == spare + 4)
    lat_index = lax.axis_index("lat")
    for piece in range(pieces):
        spot = partner(*ring, piece)
        values = from_int16(grids[piece][...])
        tile = values[:rows, end:]
        scale = scale_of(tile[:, spare : spare + 1])
        keep = tile[:, spare + 5 : spare + 6]
        field[spot, :, :end] = values[:rows, :end] * scale
        field[spot, :, end:] = tile * jnp.where(winds, WIND_STEP, scale)
        wind_rows = values[rows : rows + 2, :lons] * WIND_STEP

        @pl.when(lat_index > 0)
        def _():
            above = edge_ref[(lat_index - 1) * pieces + spot]
            field[spot, :1, :lons] += wind_rows[:1] * above

        @pl.when(lat_index < lat_count - 1)
        def _():
            below = edge_ref[(lat_index + 1) * pieces + spot]
            field[spot, rows - 1 :, :lons] -= wind_rows[1:] * below

    for spot in range(pieces):
        tile = field[spot, :, end:]
        before = field[(spot - 1) % pieces, :, end:]
        after = field[(spot + 1) % pieces, :, end:]
        shift = LANES - spare
        gain = pltpu.roll(tile, shift - 3, 1) * pltpu.roll(before, shift - 2, 1)
        loss = pltpu.roll(tile, LANES - 5, 1) * pltpu.roll(after, LANES - 2, 1)
        field[spot, :, end:] = tile - jnp.where(lane == spare - 1, loss, 0.0)
        field[spot, :, :LANES] += jnp.where(lane == 0, gain, 0.0)

    def product(kind, value, spot):
        high, low = split_bf16(value)
        table = tables[kind]
        span = table.shape[2] // 2
        both = jnp.dot(high, table[spot], preferred_element_type=jnp.float32)
        part = jnp.dot(low, table[spot, :, :span], preferred_element_type=jnp.float32)
        return part + both[:, :span] + both[:, span:]

    sums = [None, None, None]
    for spot in range(share):
        quarters = [field[quarter * share + spot, :, :lons] for quarter in range(4)]
        sum02, dif02 = quarters[0] + quarters[2], quarters[0] - quarters[2]
        sum13, dif13 = quarters[1] + quarters[3], quarters[1] - quarters[3]
        odd, turned = product(2, dif02, spot), product(2, dif13, spot)
        half = odd.shape[1] // 2
        cosine, sine = turned[:, :half], turned[:, half:]
        even = lax.broadcasted_iota(jnp.int32, cosine.shape, 1) % 2 == 0
        turned = [jnp.where(even, sine, -sine), jnp.where(even, -cosine, cosine)]
        odd = odd + jnp.concatenate(turned, axis=1)
        parts = [product(0, sum02 + sum13, spot), product(1, sum02 - sum13, spot), odd]
        sums = [part if total is None else total + part for total, part in zip(sums, parts)]
    slot_waves = wave_ref[...]
    waves = column_waves((column_count(), LANES))
    places = [
        jnp.where(waves == slot_waves[:, first : first + LANES], 1.0, 0.0).astype(jnp.bfloat16)
        for first in range(0, slot_waves.shape[1], LANES)
    ]
    places = jnp.concatenate(places, axis=1)
    placed = []
    for part in range(2):
        columns = []
        for total in sums:
            half = total.shape[1] // 2
            columns.append(total[:, part * half : (part + 1) * half])
        high, low = split_bf16(jnp.concatenate(columns, axis=1))
        value = jnp.dot(high, places, preferred_element_type=jnp.float32)
        value += jnp.dot(low, places, preferred_element_type=jnp.float32)
        kept = jnp.where(slot_waves < keep, value, 0.0)
        code = scale_code(jnp.max(jnp.abs(kept), axis=0, keepdims=True))
        steps = coded(kept, 1.0 / scale_of(code))
        codes = jnp.broadcast_to(code, (exchanged_rows(rows) - rows, code.shape[1]))
        placed.append(jnp.concatenate([steps, codes], axis=0))
    for target in range(lat_count):
        cols = slice(target * LANES, (target + 1) * LANES)
        outs[target][...] = as_int16(fold(placed[0][:, cols], placed[1][:, cols], slots))


def fourier(grids, edges, ring, wave_row, rows, slots, lat_count):
    pieces = len(grids)
    width = grids[0].shape[1]
    full = exchanged_rows(rows)
    folded = folded_rows(full, slots)
    shape = (folded, LANES) if folded else (full, 2 * LANES)
    tables = [table_bf16(table) for table in fourier_tables(pieces)]
    return pl.pallas_call(
        functools.partial(fourier_kernel, ring, lat_count, pieces, slots),
        out_shape=[jax.ShapeDtypeStruct(shape, jnp.int16)] * lat_count,
        in_specs=[VMEM_SPEC] * (pieces + 5),
        out_specs=[VMEM_SPEC] * lat_count,
        scratch_shapes=[pltpu.VMEM((pieces, rows, width), jnp.float32)],
        compiler_params=pltpu.CompilerParams(vmem_limit_bytes=MIDDLE_BYTES),
        cost_estimate=pl.CostEstimate(
            flops=4 * 10**9, bytes_accessed=6 * 2**20, transcendentals=0
        ),
    )(*grids, edges, *tables, wave_row)


def places_kernel(
    groups, slot_ref, lat_ref, wave_ref, mine_ref, beta_ref, start_ref, back_ref, sorted_rows
):
    lat_index = lax.axis_index("lat")
    slots = slot_ref.shape[1] // groups
    paired = (slots + 1) // 2
    shape = (LANES, LANES)
    down = lax.broadcasted_iota(jnp.int32, shape, 0)
    across = lax.broadcasted_iota(jnp.int32, shape, 1)
    filler = jnp.full((1, LANES - slots), 2.0 * M, jnp.float32)
    for group in range(groups):
        plain = slot_ref[:, group * slots : (group + 1) * slots].astype(jnp.float32)
        plain = jnp.concatenate([plain, filler], axis=1)
        row = jnp.broadcast_to(plain, shape)
        column = jnp.sum(jnp.where(down == across, row, 0.0), axis=1, keepdims=True)
        ahead = (row < column) | ((row == column) & (across < down))
        rank = jnp.sum(jnp.where(ahead, 1.0, 0.0), axis=1, keepdims=True)
        def ordered(side):
            place = jnp.where(rank < paired, rank, side + slots - 1.0 - rank)
            place = jnp.where(rank < slots, place, -1.0)
            hot = jnp.where(place == across.astype(jnp.float32), 1.0, 0.0)
            filled = jnp.sum(hot, axis=0, keepdims=True)
            values = jnp.sum(hot * column, axis=0, keepdims=True)
            return jnp.where(filled > 0.5, values, 2.0 * M)

        sorted_rows[group] = jnp.broadcast_to(ordered(paired), sorted_rows.shape[1:])

        @pl.when(group == lat_index)
        def _():
            mine_ref[:1] = ordered(SIDE)
            mine_ref[1:] = plain

    for step in range(groups):
        row = sorted_rows[partner(("lat",), (groups,), step), :1]
        wave_ref[:, step * LANES : (step + 1) * LANES] = row
    recurrence_tables(mine_ref, lat_ref, beta_ref, start_ref, back_ref)


def prepare_places(slot_wave, groups, latitudes):
    width = groups * LANES
    blocks = 2 * SPAN
    orders = jax.ShapeDtypeStruct((blocks * BLOCK, LANES), jnp.float32)
    return pl.pallas_call(
        functools.partial(places_kernel, groups),
        out_shape=[
            jax.ShapeDtypeStruct((1, width), jnp.float32),
            jax.ShapeDtypeStruct((2, LANES), jnp.float32),
            orders,
            jax.ShapeDtypeStruct((4, latitudes.shape[1], LANES), jnp.float32),
            jax.ShapeDtypeStruct((LANES, LANES), jnp.bfloat16),
        ],
        in_specs=[VMEM_SPEC] * 2,
        out_specs=[VMEM_SPEC] * 5,
        scratch_shapes=[pltpu.VMEM((groups, 8, LANES), jnp.float32)],
        compiler_params=pltpu.CompilerParams(vmem_limit_bytes=MIDDLE_BYTES),
        cost_estimate=pl.CostEstimate(flops=2 * 10**9, bytes_accessed=2**20, transcendentals=0),
    )(slot_wave[None], latitudes)


def lane_pairs(row):
    lane = lax.broadcasted_iota(jnp.int32, row.shape, 1)
    other = pltpu.roll(row, SIDE, 1)
    return jnp.where(lane < SIDE, row, other), jnp.where(lane < SIDE, other, row)


def block_count(wave):
    return jnp.floor((jnp.maximum(M - wave, 0.0) + (BLOCK - 1)) * (1.0 / BLOCK))


def lane_orders(one, two, blocks):
    turn = block_count(one)
    block = lax.broadcasted_iota(jnp.int32, (blocks, LANES), 0).astype(jnp.float32)
    second = block >= turn
    return jnp.where(second, two, one), (block - jnp.where(second, turn, 0.0)) * BLOCK


def recurrence_tables(mine_ref, lat_ref, beta_ref, start_ref, back_ref):
    shape = (LANES, LANES)
    same = lax.broadcasted_iota(jnp.int32, shape, 0) == lax.broadcasted_iota(jnp.int32, shape, 1)
    plain = jnp.broadcast_to(mine_ref[1:], shape)
    plain = jnp.sum(jnp.where(same, plain, 0.0), axis=1, keepdims=True)
    hot = (plain == mine_ref[:1]) & (plain < 2.0 * M)
    back_ref[...] = jnp.where(hot, 1.0, 0.0).astype(jnp.bfloat16)
    pair = lane_pairs(jnp.broadcast_to(mine_ref[:1], (8, LANES)))
    one, two = pair[0][:1], pair[1][:1]
    blocks = beta_ref.shape[0] // BLOCK
    wave, first = lane_orders(one, two, blocks)
    wave = jnp.minimum(wave, M - 1.0)
    for index in range(BLOCK):
        order = first + index
        degree = wave + order
        square = 4.0 * degree * degree - 1.0
        spread = 4.0 * order * (degree + wave)
        beta_ref[pl.ds(index, blocks, stride=BLOCK)] = spread / jnp.maximum(square, 1.0)

    counter = lax.broadcasted_iota(jnp.int32, (M, LANES), 0).astype(jnp.float32) + 1.0
    terms = jnp.log(1.0 + 0.5 / counter) * (1.0 / math.log(2.0))
    for kind, wave in enumerate((one, two)):
        wave = jnp.minimum(wave, M - 1.0)
        norm = jnp.sum(jnp.where(counter <= wave, terms, 0.0), axis=0, keepdims=True)
        coarse = lat_ref[1] * wave
        whole = jnp.floor(coarse)
        start_ref[2 * kind] = jnp.exp2(
            (coarse - whole) + lat_ref[2] * wave + 0.5 * (norm - 1.0)
        )
        start_ref[2 * kind + 1] = whole


def sweep_kernel(
    mine_ref, lat_ref, beta_ref, start_ref,
    scale_ref, growth_ref, state_ref, values_ref, more_ref,
):
    pair = lane_pairs(jnp.broadcast_to(mine_ref[:1], (8, LANES)))
    one, two = pair[0][:1], pair[1][:1]
    turn = block_count(one)

    blocks = growth_ref.shape[0]
    wave, first_order = lane_orders(one, two, blocks)
    limit = M - wave
    scale = jnp.ones((blocks, LANES), jnp.float32)
    for index in range(BLOCK):
        if index > 0:
            beta = beta_ref[pl.ds(index, blocks, stride=BLOCK)]
            scale = scale * lax.rsqrt(jnp.maximum(beta, 1e-6))
        inside = first_order + index < limit
        scale_ref[pl.ds(index, blocks, stride=BLOCK)] = jnp.where(inside, scale, 0.0)
    beta = beta_ref[pl.ds(BLOCK, blocks - 1, stride=BLOCK)]
    beta = jnp.concatenate([beta, jnp.ones((1, LANES), jnp.float32)], axis=0)
    growth_ref[...] = scale * lax.rsqrt(jnp.maximum(beta, 1e-6))

    state_ref[0] = jnp.zeros_like(state_ref[0])
    state_ref[1] = start_ref[0]
    state_ref[2] = start_ref[1]
    points = lat_ref.shape[1]

    def step(target_ref, start, block, carry):
        first = 0
        for chunk in (points // 16 * 8, points - points // 16 * 8):
            rows = slice(first, first + chunk)

            def keep(order, value):
                target_ref[block - start, order, rows] = value

            sweep_block(block, turn, rows, lat_ref, beta_ref, growth_ref, start_ref, state_ref, keep)
            first += chunk
        return carry

    total = jnp.max(turn + block_count(two)).astype(jnp.int32)
    lax.fori_loop(0, jnp.minimum(total, HELD), functools.partial(step, values_ref, 0), 0)
    more = functools.partial(step, more_ref, HELD)
    lax.fori_loop(HELD, jnp.minimum(total, HELD + MORE), more, 0)


def sweep_block(block, turn, rows, lat_ref, beta_ref, growth_ref, start_ref, state_ref, use):
    base = pl.multiple_of(block * BLOCK, BLOCK)
    begins = block.astype(jnp.float32) == turn
    grow = growth_ref[pl.ds(block, 1)]
    cosine = lat_ref[0, rows]
    height = jnp.where(begins, start_ref[3, rows], state_ref[2, rows])
    factor = jnp.exp2(height)
    old = jnp.where(begins, 0.0, state_ref[0, rows])
    new = jnp.where(begins, start_ref[2, rows], state_ref[1, rows])
    for order in range(BLOCK):
        use(order, new * factor)
        beta = beta_ref[pl.ds(base + order, 1)]
        old, new = new, cosine * new - beta * old
    biggest = jnp.maximum(jnp.abs(old), jnp.abs(new)) * grow
    shift = jnp.floor(jnp.log(biggest) * (1.0 / math.log(2.0)))
    factor = grow * jnp.exp2(-shift)
    state_ref[0, rows] = old * factor
    state_ref[1, rows] = new * factor
    state_ref[2, rows] = height + shift


def sweep(mine, latitudes, beta, start, pieces):
    points = latitudes.shape[1]
    blocks = beta.shape[0] // BLOCK
    return pl.pallas_call(
        sweep_kernel,
        out_shape=[
            jax.ShapeDtypeStruct(beta.shape, jnp.float32),
            jax.ShapeDtypeStruct((blocks, LANES), jnp.float32),
            jax.ShapeDtypeStruct((3, points, LANES), jnp.float32),
            jax.ShapeDtypeStruct((HELD, BLOCK, points, LANES), jnp.float32),
            jax.ShapeDtypeStruct((MORE, BLOCK, points, LANES), jnp.float32),
        ],
        in_specs=[VMEM_SPEC] * 4,
        out_specs=[VMEM_SPEC] * 5,
        compiler_params=pltpu.CompilerParams(vmem_limit_bytes=late_bytes(pieces)),
        cost_estimate=pl.CostEstimate(
            flops=5 * 10**9, bytes_accessed=25 * 2**20, transcendentals=0
        ),
    )(mine, latitudes, beta, start)


def resampled(first, fields, table, slots, total):
    for piece, field in enumerate(fields):
        rows = table.shape[3]
        parts = []
        for part in unfold(from_int16(field[...]), rows, slots):
            part = part * scale_of(part[rows - 1 :])
            lane = lax.broadcasted_iota(jnp.int32, part.shape, 1)
            shift = SIDE - (slots + 1) // 2
            parts.append(jnp.where(lane < SIDE, part, pltpu.roll(part, shift, 1)))
        values = jnp.concatenate(parts, axis=1)
        high, low = split_bf16(values)
        spot = partner(("lat",), table.shape[:1], first + piece)
        both = jnp.concatenate([high, low], axis=1)
        part = jnp.dot(table[spot, 0], both, preferred_element_type=jnp.float32)
        part = part[:, : high.shape[1]] + part[:, high.shape[1] :]
        part += jnp.dot(table[spot, 1], high, preferred_element_type=jnp.float32)
        total = part if total is None else total + part
    return total


def resample_kernel(slots, table_ref, *rest):
    rest[-1][...] = resampled(0, rest[:-1], table_ref, slots, None)


def late_bytes(pieces):
    return LATE_BYTES if pieces <= 4 else VMEM_BYTES


def resample(fields, table, slots):
    count, _, height, _ = table.shape
    span = 2 * LANES
    return pl.pallas_call(
        functools.partial(resample_kernel, slots),
        out_shape=jax.ShapeDtypeStruct((height, span), jnp.float32),
        in_specs=[VMEM_SPEC] * (1 + len(fields)),
        out_specs=VMEM_SPEC,
        compiler_params=pltpu.CompilerParams(vmem_limit_bytes=late_bytes(count)),
        cost_estimate=pl.CostEstimate(
            flops=10**9, bytes_accessed=4 * 2**20, transcendentals=0
        ),
    )(table, *fields)


def legendre_kernel(early, *rest):
    table, lat_ref, beta_ref, scale_ref, growth_ref, start_ref, left_ref, values_ref = rest[:8]
    more_ref, back_ref, total_ref, mine_ref = rest[8:12]
    fields, (out_ref, weights, state_ref, sums, result, final) = rest[12:-6], rest[-6:]
    points = lat_ref.shape[1]
    slots = out_ref.shape[0]
    mine = mine_ref[:1]
    odd = mine - 2.0 * jnp.floor(mine * 0.5) > 0.5
    pair = lane_pairs(jnp.broadcast_to(mine, (8, LANES)))
    turn = block_count(pair[0][:1])
    block_total = jnp.max(turn + block_count(pair[1][:1])).astype(jnp.int32)

    total = resampled(early, fields, table, slots, total_ref[...])
    totals = [total[2 * points * kind : 2 * points * (kind + 1)] for kind in range(4)]
    left = lax.broadcasted_iota(jnp.int32, (points, LANES), 1) < SIDE
    for parity in range(2):
        for comp in range(2):
            cols = slice(comp * LANES, (comp + 1) * LANES)
            value = jnp.where(odd, totals[2 + parity][:, cols], totals[parity][:, cols])
            top, bottom = value[:points], value[points:]
            kind = 2 * parity + comp
            weights[0, kind] = jnp.where(left, top, pltpu.roll(bottom, SIDE, 1))
            weights[1, kind] = jnp.where(left, pltpu.roll(top, SIDE, 1), bottom)
    result[...] = jnp.zeros_like(result)
    state_ref[...] = left_ref[...]

    def reduced(block):
        base = pl.multiple_of(block * BLOCK, BLOCK)
        for comp in range(2):
            total = sums[pl.ds(comp * 8, BLOCK, stride=16)]
            for lane in range(1, 8):
                total += sums[pl.ds(comp * 8 + lane, BLOCK, stride=16)]
            total = total * scale_ref[pl.ds(base, BLOCK)]
            result[comp, pl.ds(base, BLOCK)] = total + pltpu.roll(total, SIDE, 1)

    def held_step(source_ref, start, block, carry):
        second = block.astype(jnp.float32) >= turn
        for parity in range(2):
            scaled = [
                jnp.where(second, weights[1, 2 * parity + comp], weights[0, 2 * parity + comp])
                for comp in range(2)
            ]
            for order in range(parity, BLOCK, 2):
                value = source_ref[block - start, order]
                for comp in range(2):
                    product = (value * scaled[comp]).reshape(points // 8, 8, LANES)
                    sums[pl.ds((order * 2 + comp) * 8, 8)] = product.sum(axis=0)
        reduced(block)
        return carry

    def step(block, carry):
        second = block.astype(jnp.float32) >= turn
        first = 0
        for chunk in CHUNKS:
            rows = slice(first, first + chunk)
            scaled = [jnp.where(second, weights[1, k, rows], weights[0, k, rows]) for k in range(4)]

            def add(order, value):
                for comp in range(2):
                    product = value * scaled[2 * (order % 2) + comp]
                    partial = product.reshape(chunk // 8, 8, LANES).sum(axis=0)
                    place = pl.ds((order * 2 + comp) * 8, 8)
                    if first == 0:
                        sums[place] = partial
                    else:
                        sums[place] += partial

            sweep_block(block, turn, rows, lat_ref, beta_ref, growth_ref, start_ref, state_ref, add)
            first += chunk
        reduced(block)
        return carry

    held = functools.partial(held_step, values_ref, 0)
    lax.fori_loop(0, jnp.minimum(block_total, HELD), held, 0)
    held = functools.partial(held_step, more_ref, HELD)
    lax.fori_loop(HELD, jnp.minimum(block_total, HELD + MORE), held, 0)
    lax.fori_loop(HELD + MORE, block_total, step, 0)

    left = lax.broadcasted_iota(jnp.int32, (BLOCK, LANES), 1) < SIDE
    spots = SPAN
    chosen = [jnp.broadcast_to(turn, (8, LANES)) == value for value in range(spots + 1)]
    chosen = [jnp.concatenate([mask] * (BLOCK // 8), axis=0) for mask in chosen]
    for place in range(spots):
        rows = slice(place * BLOCK, (place + 1) * BLOCK)
        for comp in range(2):
            early_part = jnp.where(turn > place, result[comp, rows], 0.0)
            later = jnp.zeros((BLOCK, LANES), jnp.float32)
            for value in range(spots + 1):
                base = (place + value) * BLOCK
                if base < result.shape[1]:
                    later = jnp.where(chosen[value], result[comp, base : base + BLOCK], later)
            final[comp, rows] = jnp.where(left, early_part, later)
    back = back_ref[...]
    dims = (((1,), (1,)), ((), ()))
    for comp in range(2):
        high, low = split_bf16(final[comp])
        value = lax.dot_general(back, high, dims, preferred_element_type=jnp.float32)
        value += lax.dot_general(back, low, dims, preferred_element_type=jnp.float32)
        out_ref[:, comp, :] = value[:slots, :M]


def resample_pieces(pieces, rows, padded_rows):
    full = resample_table()
    table = full.reshape(full.shape[0], pieces, rows).transpose(1, 0, 2)
    table = table_bf16(np.pad(table, ((0, 0), (0, 0), (0, padded_rows - rows))))
    return table.reshape(pieces, full.shape[0], 2, padded_rows).transpose(0, 2, 1, 3)


def legendre(fields, mine, latitudes, prepared, table, slots):
    pieces = len(fields)
    early = pieces // 2
    points = latitudes.shape[1]
    total = resample(fields[:early], table, slots)
    block_rows = SPAN * BLOCK
    return pl.pallas_call(
        functools.partial(legendre_kernel, early),
        out_shape=jax.ShapeDtypeStruct((slots, 2, M), jnp.float32),
        in_specs=[VMEM_SPEC] * (12 + pieces - early),
        out_specs=VMEM_SPEC,
        scratch_shapes=[
            pltpu.VMEM((2, 4, points, LANES), jnp.float32),
            pltpu.VMEM((3, points, LANES), jnp.float32),
            pltpu.VMEM((BLOCK * 16, LANES), jnp.float32),
            pltpu.VMEM((2, 2 * block_rows, LANES), jnp.float32),
            pltpu.VMEM((2, block_rows, LANES), jnp.float32),
        ],
        compiler_params=pltpu.CompilerParams(vmem_limit_bytes=late_bytes(pieces)),
        cost_estimate=pl.CostEstimate(
            flops=8 * 10**9, bytes_accessed=6 * 2**20, transcendentals=0
        ),
    )(table, latitudes, *prepared, total, mine, *fields[early:])


def shards(tracer, wind_east, wind_north, keep_m, slot_wave):
    rows = tracer.shape[1]
    lat_count = lax.axis_size("lat")
    slots = slot_wave.shape[0] // lat_count
    axes = ("lev", "fld")
    ring = (axes, tuple(lax.axis_size(axis) for axis in axes))

    blocks, edges = advect(tracer, wind_east, wind_north, keep_m, ring)
    blocks, slot_wave = lax.optimization_barrier((blocks, slot_wave))
    grids = exchange(blocks, axes)
    edges = lax.all_to_all(edges, ("lat", *axes), split_axis=0, concat_axis=0, tiled=True)
    latitudes = jnp.asarray(latitude_table())
    wave_row, mine, beta, start, back = prepare_places(slot_wave, lat_count, latitudes)
    waved = fourier(grids, edges, ring, wave_row, rows, slots, lat_count)
    table = jnp.asarray(resample_pieces(lat_count, rows, exchanged_rows(rows)))
    waved, mine, table = lax.optimization_barrier((list(waved), mine, table))
    fields = exchange(waved, "lat")
    scale, growth, state, values, more = sweep(mine, latitudes, beta, start, lat_count)
    prepared = (beta, scale, growth, start, state, values, more, back)
    return legendre(fields, mine, latitudes, prepared, table, slots)[None]


def solution(mesh):
    return jax.shard_map(
        shards,
        mesh=mesh,
        in_specs=(
            P("member", "lat", ("lev", "fld")),
            P("member", "lat", ("lev", "fld")),
            P("member", "lat", ("lev", "fld")),
            P("lat"),
            P(),
        ),
        out_specs=P(("member", "lev", "fld"), "lat", None, None),
        check_vma=False,
    )
```

```python
import functools
import math

import jax
import jax.numpy as jnp
import numpy as np
from jax import lax
from jax.experimental import pallas as pl
from jax.experimental.pallas import tpu as pltpu
from jax.sharding import PartitionSpec as P

M = 400
NLAT = 800
NLON = 1600
LANES = 128
BLOCK = 32
CHUNKS = (40, 32, 32)
SPAN = -(-M // BLOCK)
HELD = 13
MORE = 3
SIDE = LANES // 2
TOP = 32767.0
WIND_STEP = 1.5 / TOP
VMEM_BYTES = 60 * 2**20
LATE_BYTES = 10 * 2**20
MIDDLE_BYTES = 16 * 2**20
VMEM_SPEC = pl.BlockSpec(memory_space=pltpu.VMEM)
SMEM_SPEC = pl.BlockSpec(memory_space=pltpu.SMEM)
HBM_SPEC = pl.BlockSpec(memory_space=pltpu.HBM)


def split_bf16(values):
    high = values.astype(jnp.bfloat16)
    low = (values - high.astype(jnp.float32)).astype(jnp.bfloat16)
    return high, low


def table_bf16(table):
    high = table.astype(jnp.bfloat16)
    low = (table - high.astype(np.float64)).astype(jnp.bfloat16)
    return np.concatenate([high, low], axis=-1)


def fourier_tables(pieces):
    quarter = NLON // 4
    spots = np.arange(quarter)[:, None]
    factor = 1.0 / math.sqrt(NLON)

    def parts(waves):
        angles = 2.0 * math.pi / NLON * (spots * waves[None, :] % NLON)
        return factor * np.cos(angles), factor * np.sin(angles)

    def shaped(columns):
        pad = [(0, 0), (0, -columns[0].shape[1] % LANES)]
        table = np.concatenate([np.pad(part, pad) for part in columns], axis=1)
        return table.reshape(share, quarter // share, -1)

    share = pieces // 4
    tables = []
    for first in (0, 2):
        cosine, sine = parts(np.arange(first, M, 4))
        tables.append(shaped([cosine, -sine]))
    cosine, sine = parts(np.arange(1, M, 2))
    return [*tables, shaped([cosine, -sine])]


def column_waves(shape):
    row = lax.broadcasted_iota(jnp.int32, shape, 0)
    waves, first = jnp.full(shape, -1, jnp.int32), 0
    for start, step in ((0, 4), (2, 4), (1, 2)):
        count = len(range(start, M, step))
        inside = (row >= first) & (row < first + count)
        waves = jnp.where(inside, start + step * (row - first), waves)
        first += -(-count // LANES) * LANES
    return waves.astype(jnp.float32)


def column_count():
    return sum(-(-len(range(start, M, step)) // LANES) * LANES for start, step in ((0, 4), (2, 4), (1, 2)))


def resample_table():
    half = M // 2
    coarse = math.pi / M * (np.arange(M) + 0.5)
    fine = math.pi / NLAT * (np.arange(NLAT) + 0.5)
    waves = np.arange(M)
    weight = np.where(waves == 0, 1.0, 2.0) / M
    even = (np.cos(np.outer(coarse, waves)) * weight) @ np.cos(np.outer(waves, fine))
    odd = (np.sin(np.outer(coarse, waves)) * weight) @ np.sin(np.outer(waves, fine))
    rows = []
    for full in (even, odd):
        for sign in (1.0, -1.0):
            folded = (full[:half] + sign * full[::-1][:half]).reshape(2, half // 2, NLAT)
            rows.append(np.pad(folded, ((0, 0), (0, -half // 2 % 8), (0, 0))).reshape(-1, NLAT))
    return np.concatenate(rows, axis=0) * (np.sin(fine) * math.sqrt(2.0 / NLAT))


def latitude_table():
    half = M // 2
    angles = math.pi / M * (np.arange(half) + 0.5)
    log_sine = np.log2(np.sin(angles))
    coarse = np.round(log_sine * 1024.0) / 1024.0
    rows = np.stack([2.0 * np.cos(angles), coarse, log_sine - coarse]).reshape(3, 2, half // 2)
    rows = np.pad(rows, ((0, 0), (0, 0), (0, -half // 2 % 8)))
    return np.repeat(rows.transpose(0, 2, 1), SIDE, axis=2).astype(np.float32)


def scale_code(biggest):
    wanted = jnp.maximum(biggest, 1e-30) * (1.0 / TOP)
    exponent = jnp.floor(jnp.log(wanted) * (1.0 / math.log(2.0)))
    return exponent * 128.0 + jnp.ceil((wanted * jnp.exp2(-exponent) - 1.0) * 128.0)


def scale_of(code):
    exponent = jnp.floor(code * (1.0 / 128.0))
    rest = code - 128.0 * exponent
    return jnp.exp2(exponent) * (1.0 + rest * (1.0 / 128.0))


def coded(values, inverse):
    return jnp.floor(values * inverse + 0.5)


def as_int16(values):
    return values.astype(jnp.int32).astype(jnp.int16)


def from_int16(codes):
    return codes.astype(jnp.int32).astype(jnp.float32)


def group_index(axes, sizes):
    index = lax.axis_index(axes[0])
    for axis, size in zip(axes[1:], sizes[1:]):
        index = index * size + lax.axis_index(axis)
    return index


def mask(step):
    return -step % 4


def partner(axes, sizes, step):
    return group_index(axes, sizes) ^ mask(step) if math.prod(sizes) == 4 else step


def exchange(blocks, axis):
    count = len(blocks)
    if count != 4:
        return list(lax.all_to_all(jnp.stack(blocks), axis, split_axis=0, concat_axis=0, tiled=True))
    pairs = [[(i, i ^ mask(step)) for i in range(count)] for step in range(count)]
    return [blocks[0]] + [lax.ppermute(blocks[step], axis, pairs[step]) for step in range(1, count)]


def advect_kernel(ring, lat_count, keep_hbm, tracer_hbm, east_hbm, north_hbm, *rest):
    levels, rows, lons = tracer_hbm.shape
    outs, (edge_ref, tracer, east_wind, north_wind, keep_ref, sems, keep_sem) = rest[:levels], rest[levels:]
    chosen = [partner(*ring, step) for step in range(levels)]
    copies = [None] * levels
    order = (*range(levels // 2, levels), *range(levels // 2))
    for step in order:
        copies[step] = [
            pltpu.make_async_copy(source.at[chosen[step]], target.at[step], sems.at[kind, step])
            for kind, (source, target) in enumerate(
                ((tracer_hbm, tracer), (east_hbm, east_wind), (north_hbm, north_wind))
            )
        ]
        for copy in copies[step]:
            copy.start()
    keep_copy = pltpu.make_async_copy(keep_hbm, keep_ref, keep_sem)
    keep_copy.start()
    padded_rows = outs[0].shape[0]
    keep_copy.wait()
    same = (rows, rows)
    same = lax.broadcasted_iota(jnp.int32, same, 0) == lax.broadcasted_iota(jnp.int32, same, 1)
    keep = jnp.broadcast_to(keep_ref[...].astype(jnp.float32), (rows, rows))
    keep = jnp.sum(jnp.where(same, keep, 0.0), axis=1, keepdims=True)
    end = (lons - 1) // LANES * LANES
    spare = lons - end
    lane = lax.broadcasted_iota(jnp.int32, (rows, LANES), 1)
    lat_index = lax.axis_index("lat")
    edge_ref[...] = jnp.zeros_like(edge_ref)
    for step in order:
        level = chosen[step]
        for copy in copies[step]:
            copy.wait()
        field = tracer[step].astype(jnp.float32)

        @pl.when(lat_index < lat_count - 1)
        def _():
            edge_ref[(lat_index + 1) * levels + level] = field[rows - 1 :]

        @pl.when(lat_index > 0)
        def _():
            edge_ref[(lat_index - 1) * levels + level] = field[:1]

        blank = jnp.zeros((rows, 1), jnp.float32)
        west = jnp.concatenate([blank, field[:, :-1]], axis=1)
        east = jnp.concatenate([field[:, 1:], blank], axis=1)
        blank = jnp.zeros((1, lons), jnp.float32)
        north = jnp.concatenate([blank, field[:-1]], axis=0)
        south = jnp.concatenate([field[1:], blank], axis=0)
        eastward = 0.5 * east_wind[step].astype(jnp.float32)
        northward = 0.5 * north_wind[step].astype(jnp.float32)
        moved = field - eastward * (east - west) - northward * (south - north)
        first, last = field[:, :1], field[:, lons - 1 :]
        biggest = jnp.max(jnp.abs(moved), axis=1, keepdims=True)
        biggest = jnp.maximum(biggest, jnp.maximum(jnp.abs(first), jnp.abs(last)))
        code = scale_code(biggest)
        inverse = 1.0 / scale_of(code)
        filler = jnp.zeros((rows, LANES - spare), jnp.float32)
        tile = jnp.concatenate([moved[:, end:], filler], axis=1)
        tile = jnp.where(lane == spare + 1, first, jnp.where(lane == spare + 2, last, tile))
        tile = coded(tile, inverse)
        tile = jnp.where(lane == spare, code, tile)
        winds = jnp.where(lane == spare + 3, eastward[:, :1], eastward[:, lons - 1 :])
        winds = coded(winds, 1.0 / WIND_STEP)
        tile = jnp.where((lane == spare + 3) | (lane == spare + 4), winds, tile)
        tile = jnp.where(lane == spare + 5, keep, tile)
        wind_rows = jnp.concatenate([northward[:1], northward[rows - 1 :]], axis=0)
        wind_rows = coded(wind_rows, 1.0 / WIND_STEP)
        blank = jnp.zeros((padded_rows - rows - 2, lons), jnp.float32)
        wind_rows = jnp.concatenate([wind_rows, blank], axis=0)
        filler = jnp.zeros((padded_rows - rows, LANES - spare), jnp.float32)
        wind_tile = jnp.concatenate([wind_rows[:, end:], filler], axis=1)
        steps = jnp.concatenate([coded(moved[:, :end], inverse), wind_rows[:, :end]], axis=0)
        outs[step][:, :end] = as_int16(steps)
        outs[step][:, end:] = as_int16(jnp.concatenate([tile, wind_tile], axis=0))


def advect(tracer, east_wind, north_wind, keep_m, ring):
    levels, rows, lons = tracer.shape
    lat_count = lax.axis_size("lat")
    width = (lons - 1) // LANES * LANES + LANES
    padded_rows = -(-(rows + 2) // 16) * 16
    held = pltpu.VMEM((levels, rows, lons), jnp.bfloat16)
    result = pl.pallas_call(
        functools.partial(advect_kernel, ring, lat_count),
        out_shape=[jax.ShapeDtypeStruct((padded_rows, width), jnp.int16)] * levels
        + [jax.ShapeDtypeStruct((lat_count * levels, 1, lons), jnp.float32)],
        in_specs=[HBM_SPEC] * 4,
        out_specs=[VMEM_SPEC] * (levels + 1),
        scratch_shapes=[
            held,
            held,
            held,
            pltpu.VMEM((1, rows), jnp.int32),
            pltpu.SemaphoreType.DMA((3, levels)),
            pltpu.SemaphoreType.DMA,
        ],
        compiler_params=pltpu.CompilerParams(vmem_limit_bytes=VMEM_BYTES),
        cost_estimate=pl.CostEstimate(
            flops=5 * 10**9, bytes_accessed=8 * levels * rows * lons, transcendentals=0
        ),
    )(keep_m[None], tracer, east_wind, north_wind)
    return list(result[:levels]), result[levels]


def exchanged_rows(rows):
    return -(-(rows + 1) // 16) * 16


def folded_rows(rows, slots):
    if 2 * slots <= LANES:
        return rows
    fits = 2 * slots <= LANES + SIDE + 8 and rows % 16 == 0 and rows <= 16 * 16
    return -(-(rows + rows // 2 + 16) // 16) * 16 if fits else 0


def fold(one, two, slots):
    rows = one.shape[0]
    total = folded_rows(rows, slots)
    if not total:
        return jnp.concatenate([one, two], axis=1)
    lane = lax.broadcasted_iota(jnp.int32, one.shape, 1)
    turned = pltpu.roll(two, slots, 1)
    whole = jnp.where(lane < slots, one, turned)
    if total == rows:
        return whole
    half = rows // 2
    halves = jnp.where(lane[:half] < SIDE, turned[:half], pltpu.roll(turned[half:], SIDE, 1))
    last = jnp.zeros((16, LANES), jnp.float32)
    for group in range(rows // 16):
        part = pltpu.roll(turned[16 * group : 16 * group + 16], (8 * group - SIDE) % LANES, 1)
        last = jnp.where(lane[:16] // 8 == group, part, last)
    filler = jnp.zeros((total - rows - half - 16, LANES), jnp.float32)
    return jnp.concatenate([whole, halves, last, filler], axis=0)


def unfold(block, rows, slots):
    total = folded_rows(rows, slots)
    if not total:
        return block[:, :LANES], block[:, LANES:]
    whole = block[:rows]
    lane = lax.broadcasted_iota(jnp.int32, whole.shape, 1)
    two = pltpu.roll(whole, (LANES - slots) % LANES, 1)
    if total != rows:
        half = rows // 2
        halves = block[rows : rows + half]
        last = block[rows + half : rows + half + 16]
        last = [pltpu.roll(last, (SIDE - 8 * group) % LANES, 1) for group in range(rows // 16)]
        halves = jnp.concatenate([halves, pltpu.roll(halves, SIDE, 1)], axis=0)
        rest = jnp.where(lane < SIDE, halves, jnp.concatenate(last, axis=0))
        two = jnp.where(lane < LANES - slots, two, pltpu.roll(rest, LANES - slots, 1))
    inside = lane < slots
    return jnp.where(inside, whole, 0.0), jnp.where(inside, two, 0.0)


def fourier_kernel(ring, lat_count, pieces, slots, *rest):
    grids, (edge_ref, *tables, wave_ref) = rest[:pieces], rest[pieces : pieces + 5]
    outs, field = rest[pieces + 5 : -1], rest[-1]
    _, rows, width = field.shape
    lons = tables[0].shape[1]
    share = pieces // 4

    end = width - LANES
    spare = lons - end
    lane = lax.broadcasted_iota(jnp.int32, (rows, LANES), 1)
    winds = (lane == spare + 3) | (lane == spare + 4)
    lat_index = lax.axis_index("lat")
    for piece in range(pieces):
        spot = partner(*ring, piece)
        values = from_int16(grids[piece][...])
        tile = values[:rows, end:]
        scale = scale_of(tile[:, spare : spare + 1])
        keep = tile[:, spare + 5 : spare + 6]
        field[spot, :, :end] = values[:rows, :end] * scale
        field[spot, :, end:] = tile * jnp.where(winds, WIND_STEP, scale)
        wind_rows = values[rows : rows + 2, :lons] * WIND_STEP

        @pl.when(lat_index > 0)
        def _():
            above = edge_ref[(lat_index - 1) * pieces + spot]
            field[spot, :1, :lons] += wind_rows[:1] * above

        @pl.when(lat_index < lat_count - 1)
        def _():
            below = edge_ref[(lat_index + 1) * pieces + spot]
            field[spot, rows - 1 :, :lons] -= wind_rows[1:] * below

    for spot in range(pieces):
        tile = field[spot, :, end:]
        before = field[(spot - 1) % pieces, :, end:]
        after = field[(spot + 1) % pieces, :, end:]
        shift = LANES - spare
        gain = pltpu.roll(tile, shift - 3, 1) * pltpu.roll(before, shift - 2, 1)
        loss = pltpu.roll(tile, LANES - 5, 1) * pltpu.roll(after, LANES - 2, 1)
        field[spot, :, end:] = tile - jnp.where(lane == spare - 1, loss, 0.0)
        field[spot, :, :LANES] += jnp.where(lane == 0, gain, 0.0)

    def product(kind, value, spot):
        high, low = split_bf16(value)
        table = tables[kind]
        span = table.shape[2] // 2
        both = jnp.dot(high, table[spot], preferred_element_type=jnp.float32)
        part = jnp.dot(low, table[spot, :, :span], preferred_element_type=jnp.float32)
        return part + both[:, :span] + both[:, span:]

    sums = [None, None, None]
    for spot in range(share):
        quarters = [field[quarter * share + spot, :, :lons] for quarter in range(4)]
        sum02, dif02 = quarters[0] + quarters[2], quarters[0] - quarters[2]
        sum13, dif13 = quarters[1] + quarters[3], quarters[1] - quarters[3]
        odd, turned = product(2, dif02, spot), product(2, dif13, spot)
        half = odd.shape[1] // 2
        cosine, sine = turned[:, :half], turned[:, half:]
        even = lax.broadcasted_iota(jnp.int32, cosine.shape, 1) % 2 == 0
        turned = [jnp.where(even, sine, -sine), jnp.where(even, -cosine, cosine)]
        odd = odd + jnp.concatenate(turned, axis=1)
        parts = [product(0, sum02 + sum13, spot), product(1, sum02 - sum13, spot), odd]
        sums = [part if total is None else total + part for total, part in zip(sums, parts)]
    slot_waves = wave_ref[...]
    waves = column_waves((column_count(), LANES))
    places = [
        jnp.where(waves == slot_waves[:, first : first + LANES], 1.0, 0.0).astype(jnp.bfloat16)
        for first in range(0, slot_waves.shape[1], LANES)
    ]
    places = jnp.concatenate(places, axis=1)
    placed = []
    for part in range(2):
        columns = []
        for total in sums:
            half = total.shape[1] // 2
            columns.append(total[:, part * half : (part + 1) * half])
        high, low = split_bf16(jnp.concatenate(columns, axis=1))
        value = jnp.dot(high, places, preferred_element_type=jnp.float32)
        value += jnp.dot(low, places, preferred_element_type=jnp.float32)
        kept = jnp.where(slot_waves < keep, value, 0.0)
        code = scale_code(jnp.max(jnp.abs(kept), axis=0, keepdims=True))
        steps = coded(kept, 1.0 / scale_of(code))
        codes = jnp.broadcast_to(code, (exchanged_rows(rows) - rows, code.shape[1]))
        placed.append(jnp.concatenate([steps, codes], axis=0))
    for target in range(lat_count):
        cols = slice(target * LANES, (target + 1) * LANES)
        outs[target][...] = as_int16(fold(placed[0][:, cols], placed[1][:, cols], slots))


def fourier(grids, edges, ring, wave_row, rows, slots, lat_count):
    pieces = len(grids)
    width = grids[0].shape[1]
    full = exchanged_rows(rows)
    folded = folded_rows(full, slots)
    shape = (folded, LANES) if folded else (full, 2 * LANES)
    tables = [table_bf16(table) for table in fourier_tables(pieces)]
    return pl.pallas_call(
        functools.partial(fourier_kernel, ring, lat_count, pieces, slots),
        out_shape=[jax.ShapeDtypeStruct(shape, jnp.int16)] * lat_count,
        in_specs=[VMEM_SPEC] * (pieces + 5),
        out_specs=[VMEM_SPEC] * lat_count,
        scratch_shapes=[pltpu.VMEM((pieces, rows, width), jnp.float32)],
        compiler_params=pltpu.CompilerParams(vmem_limit_bytes=MIDDLE_BYTES),
        cost_estimate=pl.CostEstimate(
            flops=4 * 10**9, bytes_accessed=6 * 2**20, transcendentals=0
        ),
    )(*grids, edges, *tables, wave_row)


def places_kernel(
    groups, slot_ref, lat_ref, wave_ref, mine_ref, beta_ref, start_ref, back_ref, sorted_rows
):
    lat_index = lax.axis_index("lat")
    slots = slot_ref.shape[1] // groups
    paired = (slots + 1) // 2
    shape = (LANES, LANES)
    down = lax.broadcasted_iota(jnp.int32, shape, 0)
    across = lax.broadcasted_iota(jnp.int32, shape, 1)
    filler = jnp.full((1, LANES - slots), 2.0 * M, jnp.float32)
    for group in range(groups):
        plain = slot_ref[:, group * slots : (group + 1) * slots].astype(jnp.float32)
        plain = jnp.concatenate([plain, filler], axis=1)
        row = jnp.broadcast_to(plain, shape)
        column = jnp.sum(jnp.where(down == across, row, 0.0), axis=1, keepdims=True)
        ahead = (row < column) | ((row == column) & (across < down))
        rank = jnp.sum(jnp.where(ahead, 1.0, 0.0), axis=1, keepdims=True)
        def ordered(side):
            place = jnp.where(rank < paired, rank, side + slots - 1.0 - rank)
            place = jnp.where(rank < slots, place, -1.0)
            hot = jnp.where(place == across.astype(jnp.float32), 1.0, 0.0)
            filled = jnp.sum(hot, axis=0, keepdims=True)
            values = jnp.sum(hot * column, axis=0, keepdims=True)
            return jnp.where(filled > 0.5, values, 2.0 * M)

        sorted_rows[group] = jnp.broadcast_to(ordered(paired), sorted_rows.shape[1:])

        @pl.when(group == lat_index)
        def _():
            mine_ref[:1] = ordered(SIDE)
            mine_ref[1:] = plain

    for step in range(groups):
        row = sorted_rows[partner(("lat",), (groups,), step), :1]
        wave_ref[:, step * LANES : (step + 1) * LANES] = row
    recurrence_tables(mine_ref, lat_ref, beta_ref, start_ref, back_ref)


def prepare_places(slot_wave, groups, latitudes):
    width = groups * LANES
    blocks = 2 * SPAN
    orders = jax.ShapeDtypeStruct((blocks * BLOCK, LANES), jnp.float32)
    return pl.pallas_call(
        functools.partial(places_kernel, groups),
        out_shape=[
            jax.ShapeDtypeStruct((1, width), jnp.float32),
            jax.ShapeDtypeStruct((2, LANES), jnp.float32),
            orders,
            jax.ShapeDtypeStruct((4, latitudes.shape[1], LANES), jnp.float32),
            jax.ShapeDtypeStruct((LANES, LANES), jnp.bfloat16),
        ],
        in_specs=[VMEM_SPEC] * 2,
        out_specs=[VMEM_SPEC] * 5,
        scratch_shapes=[pltpu.VMEM((groups, 8, LANES), jnp.float32)],
        compiler_params=pltpu.CompilerParams(vmem_limit_bytes=MIDDLE_BYTES),
        cost_estimate=pl.CostEstimate(flops=2 * 10**9, bytes_accessed=2**20, transcendentals=0),
    )(slot_wave[None], latitudes)


def lane_pairs(row):
    lane = lax.broadcasted_iota(jnp.int32, row.shape, 1)
    other = pltpu.roll(row, SIDE, 1)
    return jnp.where(lane < SIDE, row, other), jnp.where(lane < SIDE, other, row)


def block_count(wave):
    return jnp.floor((jnp.maximum(M - wave, 0.0) + (BLOCK - 1)) * (1.0 / BLOCK))


def lane_orders(one, two, blocks):
    turn = block_count(one)
    block = lax.broadcasted_iota(jnp.int32, (blocks, LANES), 0).astype(jnp.float32)
    second = block >= turn
    return jnp.where(second, two, one), (block - jnp.where(second, turn, 0.0)) * BLOCK


def recurrence_tables(mine_ref, lat_ref, beta_ref, start_ref, back_ref):
    shape = (LANES, LANES)
    same = lax.broadcasted_iota(jnp.int32, shape, 0) == lax.broadcasted_iota(jnp.int32, shape, 1)
    plain = jnp.broadcast_to(mine_ref[1:], shape)
    plain = jnp.sum(jnp.where(same, plain, 0.0), axis=1, keepdims=True)
    hot = (plain == mine_ref[:1]) & (plain < 2.0 * M)
    back_ref[...] = jnp.where(hot, 1.0, 0.0).astype(jnp.bfloat16)
    pair = lane_pairs(jnp.broadcast_to(mine_ref[:1], (8, LANES)))
    one, two = pair[0][:1], pair[1][:1]
    blocks = beta_ref.shape[0] // BLOCK
    wave, first = lane_orders(one, two, blocks)
    wave = jnp.minimum(wave, M - 1.0)
    for index in range(BLOCK):
        order = first + index
        degree = wave + order
        square = 4.0 * degree * degree - 1.0
        spread = 4.0 * order * (degree + wave)
        beta_ref[pl.ds(index, blocks, stride=BLOCK)] = spread / jnp.maximum(square, 1.0)

    counter = lax.broadcasted_iota(jnp.int32, (M, LANES), 0).astype(jnp.float32) + 1.0
    terms = jnp.log(1.0 + 0.5 / counter) * (1.0 / math.log(2.0))
    for kind, wave in enumerate((one, two)):
        wave = jnp.minimum(wave, M - 1.0)
        norm = jnp.sum(jnp.where(counter <= wave, terms, 0.0), axis=0, keepdims=True)
        coarse = lat_ref[1] * wave
        whole = jnp.floor(coarse)
        start_ref[2 * kind] = jnp.exp2(
            (coarse - whole) + lat_ref[2] * wave + 0.5 * (norm - 1.0)
        )
        start_ref[2 * kind + 1] = whole


def sweep_kernel(
    mine_ref, lat_ref, beta_ref, start_ref,
    scale_ref, growth_ref, state_ref, values_ref, more_ref,
):
    pair = lane_pairs(jnp.broadcast_to(mine_ref[:1], (8, LANES)))
    one, two = pair[0][:1], pair[1][:1]
    turn = block_count(one)

    blocks = growth_ref.shape[0]
    wave, first_order = lane_orders(one, two, blocks)
    limit = M - wave
    scale = jnp.ones((blocks, LANES), jnp.float32)
    for index in range(BLOCK):
        if index > 0:
            beta = beta_ref[pl.ds(index, blocks, stride=BLOCK)]
            scale = scale * lax.rsqrt(jnp.maximum(beta, 1e-6))
        inside = first_order + index < limit
        scale_ref[pl.ds(index, blocks, stride=BLOCK)] = jnp.where(inside, scale, 0.0)
    beta = beta_ref[pl.ds(BLOCK, blocks - 1, stride=BLOCK)]
    beta = jnp.concatenate([beta, jnp.ones((1, LANES), jnp.float32)], axis=0)
    growth_ref[...] = scale * lax.rsqrt(jnp.maximum(beta, 1e-6))

    state_ref[0] = jnp.zeros_like(state_ref[0])
    state_ref[1] = start_ref[0]
    state_ref[2] = start_ref[1]
    points = lat_ref.shape[1]

    def step(target_ref, start, block, carry):
        first = 0
        for chunk in (points // 16 * 8, points - points // 16 * 8):
            rows = slice(first, first + chunk)

            def keep(order, value):
                target_ref[block - start, order, rows] = value

            sweep_block(block, turn, rows, lat_ref, beta_ref, growth_ref, start_ref, state_ref, keep)
            first += chunk
        return carry

    total = jnp.max(turn + block_count(two)).astype(jnp.int32)
    lax.fori_loop(0, jnp.minimum(total, HELD), functools.partial(step, values_ref, 0), 0)
    more = functools.partial(step, more_ref, HELD)
    lax.fori_loop(HELD, jnp.minimum(total, HELD + MORE), more, 0)


def sweep_block(block, turn, rows, lat_ref, beta_ref, growth_ref, start_ref, state_ref, use):
    base = pl.multiple_of(block * BLOCK, BLOCK)
    begins = block.astype(jnp.float32) == turn
    grow = growth_ref[pl.ds(block, 1)]
    cosine = lat_ref[0, rows]
    height = jnp.where(begins, start_ref[3, rows], state_ref[2, rows])
    factor = jnp.exp2(height)
    old = jnp.where(begins, 0.0, state_ref[0, rows])
    new = jnp.where(begins, start_ref[2, rows], state_ref[1, rows])
    for order in range(BLOCK):
        use(order, new * factor)
        beta = beta_ref[pl.ds(base + order, 1)]
        old, new = new, cosine * new - beta * old
    biggest = jnp.maximum(jnp.abs(old), jnp.abs(new)) * grow
    shift = jnp.floor(jnp.log(biggest) * (1.0 / math.log(2.0)))
    factor = grow * jnp.exp2(-shift)
    state_ref[0, rows] = old * factor
    state_ref[1, rows] = new * factor
    state_ref[2, rows] = height + shift


def sweep(mine, latitudes, beta, start, pieces):
    points = latitudes.shape[1]
    blocks = beta.shape[0] // BLOCK
    return pl.pallas_call(
        sweep_kernel,
        out_shape=[
            jax.ShapeDtypeStruct(beta.shape, jnp.float32),
            jax.ShapeDtypeStruct((blocks, LANES), jnp.float32),
            jax.ShapeDtypeStruct((3, points, LANES), jnp.float32),
            jax.ShapeDtypeStruct((HELD, BLOCK, points, LANES), jnp.float32),
            jax.ShapeDtypeStruct((MORE, BLOCK, points, LANES), jnp.float32),
        ],
        in_specs=[VMEM_SPEC] * 4,
        out_specs=[VMEM_SPEC] * 5,
        compiler_params=pltpu.CompilerParams(vmem_limit_bytes=late_bytes(pieces)),
        cost_estimate=pl.CostEstimate(
            flops=5 * 10**9, bytes_accessed=25 * 2**20, transcendentals=0
        ),
    )(mine, latitudes, beta, start)


def resampled(first, fields, table, slots, total):
    for piece, field in enumerate(fields):
        rows = table.shape[3]
        parts = []
        for part in unfold(from_int16(field[...]), rows, slots):
            part = part * scale_of(part[rows - 1 :])
            lane = lax.broadcasted_iota(jnp.int32, part.shape, 1)
            shift = SIDE - (slots + 1) // 2
            parts.append(jnp.where(lane < SIDE, part, pltpu.roll(part, shift, 1)))
        values = jnp.concatenate(parts, axis=1)
        high, low = split_bf16(values)
        spot = partner(("lat",), table.shape[:1], first + piece)
        both = jnp.concatenate([high, low], axis=1)
        part = jnp.dot(table[spot, 0], both, preferred_element_type=jnp.float32)
        part = part[:, : high.shape[1]] + part[:, high.shape[1] :]
        part += jnp.dot(table[spot, 1], high, preferred_element_type=jnp.float32)
        total = part if total is None else total + part
    return total


def resample_kernel(slots, table_ref, *rest):
    rest[-1][...] = resampled(0, rest[:-1], table_ref, slots, None)


def late_bytes(pieces):
    return LATE_BYTES if pieces <= 4 else VMEM_BYTES


def resample(fields, table, slots):
    count, _, height, _ = table.shape
    span = 2 * LANES
    return pl.pallas_call(
        functools.partial(resample_kernel, slots),
        out_shape=jax.ShapeDtypeStruct((height, span), jnp.float32),
        in_specs=[VMEM_SPEC] * (1 + len(fields)),
        out_specs=VMEM_SPEC,
        compiler_params=pltpu.CompilerParams(vmem_limit_bytes=late_bytes(count)),
        cost_estimate=pl.CostEstimate(
            flops=10**9, bytes_accessed=4 * 2**20, transcendentals=0
        ),
    )(table, *fields)


def legendre_kernel(early, *rest):
    table, lat_ref, beta_ref, scale_ref, growth_ref, start_ref, left_ref, values_ref = rest[:8]
    more_ref, back_ref, total_ref, mine_ref = rest[8:12]
    fields, (out_ref, weights, state_ref, sums, result, final) = rest[12:-6], rest[-6:]
    points = lat_ref.shape[1]
    slots = out_ref.shape[0]
    mine = mine_ref[:1]
    odd = mine - 2.0 * jnp.floor(mine * 0.5) > 0.5
    pair = lane_pairs(jnp.broadcast_to(mine, (8, LANES)))
    turn = block_count(pair[0][:1])
    block_total = jnp.max(turn + block_count(pair[1][:1])).astype(jnp.int32)

    total = resampled(early, fields, table, slots, total_ref[...])
    totals = [total[2 * points * kind : 2 * points * (kind + 1)] for kind in range(4)]
    left = lax.broadcasted_iota(jnp.int32, (points, LANES), 1) < SIDE
    for parity in range(2):
        for comp in range(2):
            cols = slice(comp * LANES, (comp + 1) * LANES)
            value = jnp.where(odd, totals[2 + parity][:, cols], totals[parity][:, cols])
            top, bottom = value[:points], value[points:]
            kind = 2 * parity + comp
            weights[0, kind] = jnp.where(left, top, pltpu.roll(bottom, SIDE, 1))
            weights[1, kind] = jnp.where(left, pltpu.roll(top, SIDE, 1), bottom)
    result[...] = jnp.zeros_like(result)
    state_ref[...] = left_ref[...]

    def reduced(block):
        base = pl.multiple_of(block * BLOCK, BLOCK)
        for comp in range(2):
            total = sums[pl.ds(comp * 8, BLOCK, stride=16)]
            for lane in range(1, 8):
                total += sums[pl.ds(comp * 8 + lane, BLOCK, stride=16)]
            total = total * scale_ref[pl.ds(base, BLOCK)]
            result[comp, pl.ds(base, BLOCK)] = total + pltpu.roll(total, SIDE, 1)

    def held_step(source_ref, start, block, carry):
        second = block.astype(jnp.float32) >= turn
        for parity in range(2):
            scaled = [
                jnp.where(second, weights[1, 2 * parity + comp], weights[0, 2 * parity + comp])
                for comp in range(2)
            ]
            for order in range(parity, BLOCK, 2):
                value = source_ref[block - start, order]
                for comp in range(2):
                    product = (value * scaled[comp]).reshape(points // 8, 8, LANES)
                    sums[pl.ds((order * 2 + comp) * 8, 8)] = product.sum(axis=0)
        reduced(block)
        return carry

    def step(block, carry):
        second = block.astype(jnp.float32) >= turn
        first = 0
        for chunk in CHUNKS:
            rows = slice(first, first + chunk)
            scaled = [jnp.where(second, weights[1, k, rows], weights[0, k, rows]) for k in range(4)]

            def add(order, value):
                for comp in range(2):
                    product = value * scaled[2 * (order % 2) + comp]
                    partial = product.reshape(chunk // 8, 8, LANES).sum(axis=0)
                    place = pl.ds((order * 2 + comp) * 8, 8)
                    if first == 0:
                        sums[place] = partial
                    else:
                        sums[place] += partial

            sweep_block(block, turn, rows, lat_ref, beta_ref, growth_ref, start_ref, state_ref, add)
            first += chunk
        reduced(block)
        return carry

    held = functools.partial(held_step, values_ref, 0)
    lax.fori_loop(0, jnp.minimum(block_total, HELD), held, 0)
    held = functools.partial(held_step, more_ref, HELD)
    lax.fori_loop(HELD, jnp.minimum(block_total, HELD + MORE), held, 0)
    lax.fori_loop(HELD + MORE, block_total, step, 0)

    left = lax.broadcasted_iota(jnp.int32, (BLOCK, LANES), 1) < SIDE
    spots = SPAN
    chosen = [jnp.broadcast_to(turn, (8, LANES)) == value for value in range(spots + 1)]
    chosen = [jnp.concatenate([mask] * (BLOCK // 8), axis=0) for mask in chosen]
    for place in range(spots):
        rows = slice(place * BLOCK, (place + 1) * BLOCK)
        for comp in range(2):
            early_part = jnp.where(turn > place, result[comp, rows], 0.0)
            later = jnp.zeros((BLOCK, LANES), jnp.float32)
            for value in range(spots + 1):
                base = (place + value) * BLOCK
                if base < result.shape[1]:
                    later = jnp.where(chosen[value], result[comp, base : base + BLOCK], later)
            final[comp, rows] = jnp.where(left, early_part, later)
    back = back_ref[...]
    dims = (((1,), (1,)), ((), ()))
    for comp in range(2):
        high, low = split_bf16(final[comp])
        value = lax.dot_general(back, high, dims, preferred_element_type=jnp.float32)
        value += lax.dot_general(back, low, dims, preferred_element_type=jnp.float32)
        out_ref[:, comp, :] = value[:slots, :M]


def resample_pieces(pieces, rows, padded_rows):
    full = resample_table()
    table = full.reshape(full.shape[0], pieces, rows).transpose(1, 0, 2)
    table = table_bf16(np.pad(table, ((0, 0), (0, 0), (0, padded_rows - rows))))
    return table.reshape(pieces, full.shape[0], 2, padded_rows).transpose(0, 2, 1, 3)


def legendre(fields, mine, latitudes, prepared, table, slots):
    pieces = len(fields)
    early = pieces // 2
    points = latitudes.shape[1]
    total = resample(fields[:early], table, slots)
    block_rows = SPAN * BLOCK
    return pl.pallas_call(
        functools.partial(legendre_kernel, early),
        out_shape=jax.ShapeDtypeStruct((slots, 2, M), jnp.float32),
        in_specs=[VMEM_SPEC] * (12 + pieces - early),
        out_specs=VMEM_SPEC,
        scratch_shapes=[
            pltpu.VMEM((2, 4, points, LANES), jnp.float32),
            pltpu.VMEM((3, points, LANES), jnp.float32),
            pltpu.VMEM((BLOCK * 16, LANES), jnp.float32),
            pltpu.VMEM((2, 2 * block_rows, LANES), jnp.float32),
            pltpu.VMEM((2, block_rows, LANES), jnp.float32),
        ],
        compiler_params=pltpu.CompilerParams(vmem_limit_bytes=late_bytes(pieces)),
        cost_estimate=pl.CostEstimate(
            flops=8 * 10**9, bytes_accessed=6 * 2**20, transcendentals=0
        ),
    )(table, latitudes, *prepared, total, mine, *fields[early:])


def shards(tracer, wind_east, wind_north, keep_m, slot_wave):
    rows = tracer.shape[1]
    lat_count = lax.axis_size("lat")
    slots = slot_wave.shape[0] // lat_count
    axes = ("lev", "fld")
    ring = (axes, tuple(lax.axis_size(axis) for axis in axes))

    blocks, edges = advect(tracer, wind_east, wind_north, keep_m, ring)
    blocks, slot_wave = lax.optimization_barrier((blocks, slot_wave))
    grids = exchange(blocks, axes)
    edges = lax.all_to_all(edges, ("lat", *axes), split_axis=0, concat_axis=0, tiled=True)
    latitudes = jnp.asarray(latitude_table())
    wave_row, mine, beta, start, back = prepare_places(slot_wave, lat_count, latitudes)
    waved = fourier(grids, edges, ring, wave_row, rows, slots, lat_count)
    table = jnp.asarray(resample_pieces(lat_count, rows, exchanged_rows(rows)))
    waved, mine, table = lax.optimization_barrier((list(waved), mine, table))
    fields = exchange(waved, "lat")
    scale, growth, state, values, more = sweep(mine, latitudes, beta, start, lat_count)
    prepared = (beta, scale, growth, start, state, values, more, back)
    return legendre(fields, mine, latitudes, prepared, table, slots)[None]


def solution(mesh):
    return jax.shard_map(
        shards,
        mesh=mesh,
        in_specs=(
            P("member", "lat", ("lev", "fld")),
            P("member", "lat", ("lev", "fld")),
            P("member", "lat", ("lev", "fld")),
            P("lat"),
            P(),
        ),
        out_specs=P(("member", "lev", "fld"), "lat", None, None),
        check_vma=False,
    )
```

```python
import functools
import math

import jax
import jax.numpy as jnp
import numpy as np
from jax import lax
from jax.experimental import pallas as pl
from jax.experimental.pallas import tpu as pltpu
from jax.sharding import PartitionSpec as P

M = 400
NLAT = 800
NLON = 1600
LANES = 128
BLOCK = 32
CHUNKS = (40, 32, 32)
SPAN = -(-M // BLOCK)
HELD = 13
MORE = 3
SIDE = LANES // 2
TOP = 32767.0
WIND_STEP = 1.5 / TOP
VMEM_BYTES = 60 * 2**20
LATE_BYTES = 10 * 2**20
MIDDLE_BYTES = 16 * 2**20
VMEM_SPEC = pl.BlockSpec(memory_space=pltpu.VMEM)
SMEM_SPEC = pl.BlockSpec(memory_space=pltpu.SMEM)
HBM_SPEC = pl.BlockSpec(memory_space=pltpu.HBM)


def split_bf16(values):
    high = values.astype(jnp.bfloat16)
    low = (values - high.astype(jnp.float32)).astype(jnp.bfloat16)
    return high, low


def table_bf16(table):
    high = table.astype(jnp.bfloat16)
    low = (table - high.astype(np.float64)).astype(jnp.bfloat16)
    return np.concatenate([high, low], axis=-1)


def fourier_tables(pieces):
    quarter = NLON // 4
    spots = np.arange(quarter)[:, None]
    factor = 1.0 / math.sqrt(NLON)

    def parts(waves):
        angles = 2.0 * math.pi / NLON * (spots * waves[None, :] % NLON)
        return factor * np.cos(angles), factor * np.sin(angles)

    def shaped(columns):
        pad = [(0, 0), (0, -columns[0].shape[1] % LANES)]
        table = np.concatenate([np.pad(part, pad) for part in columns], axis=1)
        return table.reshape(share, quarter // share, -1)

    share = pieces // 4
    tables = []
    for first in (0, 2):
        cosine, sine = parts(np.arange(first, M, 4))
        tables.append(shaped([cosine, -sine]))
    cosine, sine = parts(np.arange(1, M, 2))
    return [*tables, shaped([cosine, -sine])]


def column_waves(shape):
    row = lax.broadcasted_iota(jnp.int32, shape, 0)
    waves, first = jnp.full(shape, -1, jnp.int32), 0
    for start, step in ((0, 4), (2, 4), (1, 2)):
        count = len(range(start, M, step))
        inside = (row >= first) & (row < first + count)
        waves = jnp.where(inside, start + step * (row - first), waves)
        first += -(-count // LANES) * LANES
    return waves.astype(jnp.float32)


def column_count():
    return sum(-(-len(range(start, M, step)) // LANES) * LANES for start, step in ((0, 4), (2, 4), (1, 2)))


def resample_table():
    half = M // 2
    coarse = math.pi / M * (np.arange(M) + 0.5)
    fine = math.pi / NLAT * (np.arange(NLAT) + 0.5)
    waves = np.arange(M)
    weight = np.where(waves == 0, 1.0, 2.0) / M
    even = (np.cos(np.outer(coarse, waves)) * weight) @ np.cos(np.outer(waves, fine))
    odd = (np.sin(np.outer(coarse, waves)) * weight) @ np.sin(np.outer(waves, fine))
    rows = []
    for full in (even, odd):
        for sign in (1.0, -1.0):
            folded = (full[:half] + sign * full[::-1][:half]).reshape(2, half // 2, NLAT)
            rows.append(np.pad(folded, ((0, 0), (0, -half // 2 % 8), (0, 0))).reshape(-1, NLAT))
    return np.concatenate(rows, axis=0) * (np.sin(fine) * math.sqrt(2.0 / NLAT))


def latitude_table():
    half = M // 2
    angles = math.pi / M * (np.arange(half) + 0.5)
    log_sine = np.log2(np.sin(angles))
    coarse = np.round(log_sine * 1024.0) / 1024.0
    rows = np.stack([2.0 * np.cos(angles), coarse, log_sine - coarse]).reshape(3, 2, half // 2)
    rows = np.pad(rows, ((0, 0), (0, 0), (0, -half // 2 % 8)))
    return np.repeat(rows.transpose(0, 2, 1), SIDE, axis=2).astype(np.float32)


def scale_code(biggest):
    wanted = jnp.maximum(biggest, 1e-30) * (1.0 / TOP)
    exponent = jnp.floor(jnp.log(wanted) * (1.0 / math.log(2.0)))
    return exponent * 128.0 + jnp.ceil((wanted * jnp.exp2(-exponent) - 1.0) * 128.0)


def scale_of(code):
    exponent = jnp.floor(code * (1.0 / 128.0))
    rest = code - 128.0 * exponent
    return jnp.exp2(exponent) * (1.0 + rest * (1.0 / 128.0))


def coded(values, inverse):
    return jnp.floor(values * inverse + 0.5)


def as_int16(values):
    return values.astype(jnp.int32).astype(jnp.int16)


def from_int16(codes):
    return codes.astype(jnp.int32).astype(jnp.float32)


def group_index(axes, sizes):
    index = lax.axis_index(axes[0])
    for axis, size in zip(axes[1:], sizes[1:]):
        index = index * size + lax.axis_index(axis)
    return index


def mask(step):
    return -step % 4


def partner(axes, sizes, step):
    return group_index(axes, sizes) ^ mask(step) if math.prod(sizes) == 4 else step


def exchange(blocks, axis):
    count = len(blocks)
    if count != 4:
        return list(lax.all_to_all(jnp.stack(blocks), axis, split_axis=0, concat_axis=0, tiled=True))
    pairs = [[(i, i ^ mask(step)) for i in range(count)] for step in range(count)]
    return [blocks[0]] + [lax.ppermute(blocks[step], axis, pairs[step]) for step in range(1, count)]


def advect_kernel(ring, lat_count, keep_hbm, tracer_hbm, east_hbm, north_hbm, *rest):
    levels, rows, lons = tracer_hbm.shape
    outs, (edge_ref, tracer, east_wind, north_wind, keep_ref, sems, keep_sem) = rest[:levels], rest[levels:]
    chosen = [partner(*ring, step) for step in range(levels)]
    copies = [None] * levels
    order = (*range(levels // 2, levels), *range(levels // 2))
    for step in order:
        copies[step] = [
            pltpu.make_async_copy(source.at[chosen[step]], target.at[step], sems.at[kind, step])
            for kind, (source, target) in enumerate(
                ((tracer_hbm, tracer), (east_hbm, east_wind), (north_hbm, north_wind))
            )
        ]
        for copy in copies[step]:
            copy.start()
    keep_copy = pltpu.make_async_copy(keep_hbm, keep_ref, keep_sem)
    keep_copy.start()
    padded_rows = outs[0].shape[0]
    keep_copy.wait()
    same = (rows, rows)
    same = lax.broadcasted_iota(jnp.int32, same, 0) == lax.broadcasted_iota(jnp.int32, same, 1)
    keep = jnp.broadcast_to(keep_ref[...].astype(jnp.float32), (rows, rows))
    keep = jnp.sum(jnp.where(same, keep, 0.0), axis=1, keepdims=True)
    end = (lons - 1) // LANES * LANES
    spare = lons - end
    lane = lax.broadcasted_iota(jnp.int32, (rows, LANES), 1)
    lat_index = lax.axis_index("lat")
    edge_ref[...] = jnp.zeros_like(edge_ref)
    for step in order:
        level = chosen[step]
        for copy in copies[step]:
            copy.wait()
        field = tracer[step].astype(jnp.float32)

        @pl.when(lat_index < lat_count - 1)
        def _():
            edge_ref[(lat_index + 1) * levels + level] = field[rows - 1 :]

        @pl.when(lat_index > 0)
        def _():
            edge_ref[(lat_index - 1) * levels + level] = field[:1]

        blank = jnp.zeros((rows, 1), jnp.float32)
        west = jnp.concatenate([blank, field[:, :-1]], axis=1)
        east = jnp.concatenate([field[:, 1:], blank], axis=1)
        blank = jnp.zeros((1, lons), jnp.float32)
        north = jnp.concatenate([blank, field[:-1]], axis=0)
        south = jnp.concatenate([field[1:], blank], axis=0)
        eastward = 0.5 * east_wind[step].astype(jnp.float32)
        northward = 0.5 * north_wind[step].astype(jnp.float32)
        moved = field - eastward * (east - west) - northward * (south - north)
        first, last = field[:, :1], field[:, lons - 1 :]
        biggest = jnp.max(jnp.abs(moved), axis=1, keepdims=True)
        biggest = jnp.maximum(biggest, jnp.maximum(jnp.abs(first), jnp.abs(last)))
        code = scale_code(biggest)
        inverse = 1.0 / scale_of(code)
        filler = jnp.zeros((rows, LANES - spare), jnp.float32)
        tile = jnp.concatenate([moved[:, end:], filler], axis=1)
        tile = jnp.where(lane == spare + 1, first, jnp.where(lane == spare + 2, last, tile))
        tile = coded(tile, inverse)
        tile = jnp.where(lane == spare, code, tile)
        winds = jnp.where(lane == spare + 3, eastward[:, :1], eastward[:, lons - 1 :])
        winds = coded(winds, 1.0 / WIND_STEP)
        tile = jnp.where((lane == spare + 3) | (lane == spare + 4), winds, tile)
        tile = jnp.where(lane == spare + 5, keep, tile)
        wind_rows = jnp.concatenate([northward[:1], northward[rows - 1 :]], axis=0)
        wind_rows = coded(wind_rows, 1.0 / WIND_STEP)
        blank = jnp.zeros((padded_rows - rows - 2, lons), jnp.float32)
        wind_rows = jnp.concatenate([wind_rows, blank], axis=0)
        filler = jnp.zeros((padded_rows - rows, LANES - spare), jnp.float32)
        wind_tile = jnp.concatenate([wind_rows[:, end:], filler], axis=1)
        steps = jnp.concatenate([coded(moved[:, :end], inverse), wind_rows[:, :end]], axis=0)
        outs[step][:, :end] = as_int16(steps)
        outs[step][:, end:] = as_int16(jnp.concatenate([tile, wind_tile], axis=0))


def advect(tracer, east_wind, north_wind, keep_m, ring):
    levels, rows, lons = tracer.shape
    lat_count = lax.axis_size("lat")
    width = (lons - 1) // LANES * LANES + LANES
    padded_rows = -(-(rows + 2) // 16) * 16
    held = pltpu.VMEM((levels, rows, lons), jnp.bfloat16)
    result = pl.pallas_call(
        functools.partial(advect_kernel, ring, lat_count),
        out_shape=[jax.ShapeDtypeStruct((padded_rows, width), jnp.int16)] * levels
        + [jax.ShapeDtypeStruct((lat_count * levels, 1, lons), jnp.float32)],
        in_specs=[HBM_SPEC] * 4,
        out_specs=[VMEM_SPEC] * (levels + 1),
        scratch_shapes=[
            held,
            held,
            held,
            pltpu.VMEM((1, rows), jnp.int32),
            pltpu.SemaphoreType.DMA((3, levels)),
            pltpu.SemaphoreType.DMA,
        ],
        compiler_params=pltpu.CompilerParams(vmem_limit_bytes=VMEM_BYTES),
        cost_estimate=pl.CostEstimate(
            flops=5 * 10**9, bytes_accessed=8 * levels * rows * lons, transcendentals=0
        ),
    )(keep_m[None], tracer, east_wind, north_wind)
    return list(result[:levels]), result[levels]


def exchanged_rows(rows):
    return -(-(rows + 1) // 16) * 16


def fourier_kernel(ring, lat_count, pieces, *rest):
    grids, (edge_ref, *tables, wave_ref) = rest[:pieces], rest[pieces : pieces + 5]
    outs, field = rest[pieces + 5 : -1], rest[-1]
    _, rows, width = field.shape
    lons = tables[0].shape[1]
    share = pieces // 4

    end = width - LANES
    spare = lons - end
    lane = lax.broadcasted_iota(jnp.int32, (rows, LANES), 1)
    winds = (lane == spare + 3) | (lane == spare + 4)
    lat_index = lax.axis_index("lat")
    for piece in range(pieces):
        spot = partner(*ring, piece)
        values = from_int16(grids[piece][...])
        tile = values[:rows, end:]
        scale = scale_of(tile[:, spare : spare + 1])
        keep = tile[:, spare + 5 : spare + 6]
        field[spot, :, :end] = values[:rows, :end] * scale
        field[spot, :, end:] = tile * jnp.where(winds, WIND_STEP, scale)
        wind_rows = values[rows : rows + 2, :lons] * WIND_STEP

        @pl.when(lat_index > 0)
        def _():
            above = edge_ref[(lat_index - 1) * pieces + spot]
            field[spot, :1, :lons] += wind_rows[:1] * above

        @pl.when(lat_index < lat_count - 1)
        def _():
            below = edge_ref[(lat_index + 1) * pieces + spot]
            field[spot, rows - 1 :, :lons] -= wind_rows[1:] * below

    for spot in range(pieces):
        tile = field[spot, :, end:]
        before = field[(spot - 1) % pieces, :, end:]
        after = field[(spot + 1) % pieces, :, end:]
        shift = LANES - spare
        gain = pltpu.roll(tile, shift - 3, 1) * pltpu.roll(before, shift - 2, 1)
        loss = pltpu.roll(tile, LANES - 5, 1) * pltpu.roll(after, LANES - 2, 1)
        field[spot, :, end:] = tile - jnp.where(lane == spare - 1, loss, 0.0)
        field[spot, :, :LANES] += jnp.where(lane == 0, gain, 0.0)

    def product(kind, value, spot):
        high, low = split_bf16(value)
        table = tables[kind]
        span = table.shape[2] // 2
        both = jnp.dot(high, table[spot], preferred_element_type=jnp.float32)
        part = jnp.dot(low, table[spot, :, :span], preferred_element_type=jnp.float32)
        return part + both[:, :span] + both[:, span:]

    sums = [None, None, None]
    for spot in range(share):
        quarters = [field[quarter * share + spot, :, :lons] for quarter in range(4)]
        sum02, dif02 = quarters[0] + quarters[2], quarters[0] - quarters[2]
        sum13, dif13 = quarters[1] + quarters[3], quarters[1] - quarters[3]
        odd, turned = product(2, dif02, spot), product(2, dif13, spot)
        half = odd.shape[1] // 2
        cosine, sine = turned[:, :half], turned[:, half:]
        even = lax.broadcasted_iota(jnp.int32, cosine.shape, 1) % 2 == 0
        turned = [jnp.where(even, sine, -sine), jnp.where(even, -cosine, cosine)]
        odd = odd + jnp.concatenate(turned, axis=1)
        parts = [product(0, sum02 + sum13, spot), product(1, sum02 - sum13, spot), odd]
        sums = [part if total is None else total + part for total, part in zip(sums, parts)]
    slot_waves = wave_ref[...]
    waves = column_waves((column_count(), LANES))
    places = [
        jnp.where(waves == slot_waves[:, first : first + LANES], 1.0, 0.0).astype(jnp.bfloat16)
        for first in range(0, slot_waves.shape[1], LANES)
    ]
    places = jnp.concatenate(places, axis=1)
    placed = []
    for part in range(2):
        columns = []
        for total in sums:
            half = total.shape[1] // 2
            columns.append(total[:, part * half : (part + 1) * half])
        high, low = split_bf16(jnp.concatenate(columns, axis=1))
        value = jnp.dot(high, places, preferred_element_type=jnp.float32)
        value += jnp.dot(low, places, preferred_element_type=jnp.float32)
        kept = jnp.where(slot_waves < keep, value, 0.0)
        code = scale_code(jnp.max(jnp.abs(kept), axis=0, keepdims=True))
        steps = coded(kept, 1.0 / scale_of(code))
        codes = jnp.broadcast_to(code, (exchanged_rows(rows) - rows, code.shape[1]))
        placed.append(jnp.concatenate([steps, codes], axis=0))
    for target in range(lat_count):
        cols = slice(target * LANES, (target + 1) * LANES)
        for part in range(2):
            outs[target][:, part * LANES : (part + 1) * LANES] = as_int16(placed[part][:, cols])


def fourier(grids, edges, ring, wave_row, rows, lat_count):
    pieces = len(grids)
    width = grids[0].shape[1]
    shape = (exchanged_rows(rows), 2 * LANES)
    tables = [table_bf16(table) for table in fourier_tables(pieces)]
    return pl.pallas_call(
        functools.partial(fourier_kernel, ring, lat_count, pieces),
        out_shape=[jax.ShapeDtypeStruct(shape, jnp.int16)] * lat_count,
        in_specs=[VMEM_SPEC] * (pieces + 5),
        out_specs=[VMEM_SPEC] * lat_count,
        scratch_shapes=[pltpu.VMEM((pieces, rows, width), jnp.float32)],
        compiler_params=pltpu.CompilerParams(vmem_limit_bytes=MIDDLE_BYTES),
        cost_estimate=pl.CostEstimate(
            flops=4 * 10**9, bytes_accessed=6 * 2**20, transcendentals=0
        ),
    )(*grids, edges, *tables, wave_row)


def places_kernel(
    groups, slot_ref, lat_ref, wave_ref, mine_ref, beta_ref, start_ref, back_ref, sorted_rows
):
    lat_index = lax.axis_index("lat")
    slots = slot_ref.shape[1] // groups
    paired = (slots + 1) // 2
    shape = (LANES, LANES)
    down = lax.broadcasted_iota(jnp.int32, shape, 0)
    across = lax.broadcasted_iota(jnp.int32, shape, 1)
    filler = jnp.full((1, LANES - slots), 2.0 * M, jnp.float32)
    for group in range(groups):
        plain = slot_ref[:, group * slots : (group + 1) * slots].astype(jnp.float32)
        plain = jnp.concatenate([plain, filler], axis=1)
        row = jnp.broadcast_to(plain, shape)
        column = jnp.sum(jnp.where(down == across, row, 0.0), axis=1, keepdims=True)
        ahead = (row < column) | ((row == column) & (across < down))
        rank = jnp.sum(jnp.where(ahead, 1.0, 0.0), axis=1, keepdims=True)
        place = jnp.where(rank < paired, rank, SIDE + slots - 1.0 - rank)
        place = jnp.where(rank < slots, place, -1.0)
        hot = jnp.where(place == across.astype(jnp.float32), 1.0, 0.0)
        filled = jnp.sum(hot, axis=0, keepdims=True)
        values = jnp.sum(hot * column, axis=0, keepdims=True)
        values = jnp.where(filled > 0.5, values, 2.0 * M)
        sorted_rows[group] = jnp.broadcast_to(values, sorted_rows.shape[1:])

        @pl.when(group == lat_index)
        def _():
            mine_ref[:1] = values
            mine_ref[1:] = plain

    for step in range(groups):
        row = sorted_rows[partner(("lat",), (groups,), step), :1]
        wave_ref[:, step * LANES : (step + 1) * LANES] = row
    recurrence_tables(mine_ref, lat_ref, beta_ref, start_ref, back_ref)


def prepare_places(slot_wave, groups, latitudes):
    width = groups * LANES
    blocks = 2 * SPAN
    orders = jax.ShapeDtypeStruct((blocks * BLOCK, LANES), jnp.float32)
    return pl.pallas_call(
        functools.partial(places_kernel, groups),
        out_shape=[
            jax.ShapeDtypeStruct((1, width), jnp.float32),
            jax.ShapeDtypeStruct((2, LANES), jnp.float32),
            orders,
            jax.ShapeDtypeStruct((4, latitudes.shape[1], LANES), jnp.float32),
            jax.ShapeDtypeStruct((LANES, LANES), jnp.bfloat16),
        ],
        in_specs=[VMEM_SPEC] * 2,
        out_specs=[VMEM_SPEC] * 5,
        scratch_shapes=[pltpu.VMEM((groups, 8, LANES), jnp.float32)],
        compiler_params=pltpu.CompilerParams(vmem_limit_bytes=MIDDLE_BYTES),
        cost_estimate=pl.CostEstimate(flops=2 * 10**9, bytes_accessed=2**20, transcendentals=0),
    )(slot_wave[None], latitudes)


def lane_pairs(row):
    lane = lax.broadcasted_iota(jnp.int32, row.shape, 1)
    other = pltpu.roll(row, SIDE, 1)
    return jnp.where(lane < SIDE, row, other), jnp.where(lane < SIDE, other, row)


def block_count(wave):
    return jnp.floor((jnp.maximum(M - wave, 0.0) + (BLOCK - 1)) * (1.0 / BLOCK))


def lane_orders(one, two, blocks):
    turn = block_count(one)
    block = lax.broadcasted_iota(jnp.int32, (blocks, LANES), 0).astype(jnp.float32)
    second = block >= turn
    return jnp.where(second, two, one), (block - jnp.where(second, turn, 0.0)) * BLOCK


def recurrence_tables(mine_ref, lat_ref, beta_ref, start_ref, back_ref):
    shape = (LANES, LANES)
    same = lax.broadcasted_iota(jnp.int32, shape, 0) == lax.broadcasted_iota(jnp.int32, shape, 1)
    plain = jnp.broadcast_to(mine_ref[1:], shape)
    plain = jnp.sum(jnp.where(same, plain, 0.0), axis=1, keepdims=True)
    hot = (plain == mine_ref[:1]) & (plain < 2.0 * M)
    back_ref[...] = jnp.where(hot, 1.0, 0.0).astype(jnp.bfloat16)
    pair = lane_pairs(jnp.broadcast_to(mine_ref[:1], (8, LANES)))
    one, two = pair[0][:1], pair[1][:1]
    blocks = beta_ref.shape[0] // BLOCK
    wave, first = lane_orders(one, two, blocks)
    wave = jnp.minimum(wave, M - 1.0)
    for index in range(BLOCK):
        order = first + index
        degree = wave + order
        square = 4.0 * degree * degree - 1.0
        spread = 4.0 * order * (degree + wave)
        beta_ref[pl.ds(index, blocks, stride=BLOCK)] = spread / jnp.maximum(square, 1.0)

    counter = lax.broadcasted_iota(jnp.int32, (M, LANES), 0).astype(jnp.float32) + 1.0
    terms = jnp.log(1.0 + 0.5 / counter) * (1.0 / math.log(2.0))
    for kind, wave in enumerate((one, two)):
        wave = jnp.minimum(wave, M - 1.0)
        norm = jnp.sum(jnp.where(counter <= wave, terms, 0.0), axis=0, keepdims=True)
        coarse = lat_ref[1] * wave
        whole = jnp.floor(coarse)
        start_ref[2 * kind] = jnp.exp2(
            (coarse - whole) + lat_ref[2] * wave + 0.5 * (norm - 1.0)
        )
        start_ref[2 * kind + 1] = whole


def sweep_kernel(
    mine_ref, lat_ref, beta_ref, start_ref,
    scale_ref, growth_ref, state_ref, values_ref, more_ref,
):
    pair = lane_pairs(jnp.broadcast_to(mine_ref[:1], (8, LANES)))
    one, two = pair[0][:1], pair[1][:1]
    turn = block_count(one)

    blocks = growth_ref.shape[0]
    wave, first_order = lane_orders(one, two, blocks)
    limit = M - wave
    scale = jnp.ones((blocks, LANES), jnp.float32)
    for index in range(BLOCK):
        if index > 0:
            beta = beta_ref[pl.ds(index, blocks, stride=BLOCK)]
            scale = scale * lax.rsqrt(jnp.maximum(beta, 1e-6))
        inside = first_order + index < limit
        scale_ref[pl.ds(index, blocks, stride=BLOCK)] = jnp.where(inside, scale, 0.0)
    beta = beta_ref[pl.ds(BLOCK, blocks - 1, stride=BLOCK)]
    beta = jnp.concatenate([beta, jnp.ones((1, LANES), jnp.float32)], axis=0)
    growth_ref[...] = scale * lax.rsqrt(jnp.maximum(beta, 1e-6))

    state_ref[0] = jnp.zeros_like(state_ref[0])
    state_ref[1] = start_ref[0]
    state_ref[2] = start_ref[1]
    points = lat_ref.shape[1]

    def step(target_ref, start, block, carry):
        first = 0
        for chunk in (points // 16 * 8, points - points // 16 * 8):
            rows = slice(first, first + chunk)

            def keep(order, value):
                target_ref[block - start, order, rows] = value

            sweep_block(block, turn, rows, lat_ref, beta_ref, growth_ref, start_ref, state_ref, keep)
            first += chunk
        return carry

    total = jnp.max(turn + block_count(two)).astype(jnp.int32)
    lax.fori_loop(0, jnp.minimum(total, HELD), functools.partial(step, values_ref, 0), 0)
    more = functools.partial(step, more_ref, HELD)
    lax.fori_loop(HELD, jnp.minimum(total, HELD + MORE), more, 0)


def sweep_block(block, turn, rows, lat_ref, beta_ref, growth_ref, start_ref, state_ref, use):
    base = pl.multiple_of(block * BLOCK, BLOCK)
    begins = block.astype(jnp.float32) == turn
    grow = growth_ref[pl.ds(block, 1)]
    cosine = lat_ref[0, rows]
    height = jnp.where(begins, start_ref[3, rows], state_ref[2, rows])
    factor = jnp.exp2(height)
    old = jnp.where(begins, 0.0, state_ref[0, rows])
    new = jnp.where(begins, start_ref[2, rows], state_ref[1, rows])
    for order in range(BLOCK):
        use(order, new * factor)
        beta = beta_ref[pl.ds(base + order, 1)]
        old, new = new, cosine * new - beta * old
    biggest = jnp.maximum(jnp.abs(old), jnp.abs(new)) * grow
    shift = jnp.floor(jnp.log(biggest) * (1.0 / math.log(2.0)))
    factor = grow * jnp.exp2(-shift)
    state_ref[0, rows] = old * factor
    state_ref[1, rows] = new * factor
    state_ref[2, rows] = height + shift


def sweep(mine, latitudes, beta, start, pieces):
    points = latitudes.shape[1]
    blocks = beta.shape[0] // BLOCK
    return pl.pallas_call(
        sweep_kernel,
        out_shape=[
            jax.ShapeDtypeStruct(beta.shape, jnp.float32),
            jax.ShapeDtypeStruct((blocks, LANES), jnp.float32),
            jax.ShapeDtypeStruct((3, points, LANES), jnp.float32),
            jax.ShapeDtypeStruct((HELD, BLOCK, points, LANES), jnp.float32),
            jax.ShapeDtypeStruct((MORE, BLOCK, points, LANES), jnp.float32),
        ],
        in_specs=[VMEM_SPEC] * 4,
        out_specs=[VMEM_SPEC] * 5,
        compiler_params=pltpu.CompilerParams(vmem_limit_bytes=late_bytes(pieces)),
        cost_estimate=pl.CostEstimate(
            flops=5 * 10**9, bytes_accessed=25 * 2**20, transcendentals=0
        ),
    )(mine, latitudes, beta, start)


def resampled(first, fields, table, total):
    for piece, field in enumerate(fields):
        values = from_int16(field[...])
        values = values * scale_of(values[field.shape[0] - 1 :])
        high, low = split_bf16(values)
        spot = partner(("lat",), table.shape[:1], first + piece)
        both = jnp.concatenate([high, low], axis=1)
        part = jnp.dot(table[spot, 0], both, preferred_element_type=jnp.float32)
        part = part[:, : high.shape[1]] + part[:, high.shape[1] :]
        part += jnp.dot(table[spot, 1], high, preferred_element_type=jnp.float32)
        total = part if total is None else total + part
    return total


def resample_kernel(table_ref, *rest):
    rest[-1][...] = resampled(0, rest[:-1], table_ref, None)


def late_bytes(pieces):
    return LATE_BYTES if pieces <= 4 else VMEM_BYTES


def resample(fields, table):
    count, _, height, _ = table.shape
    span = 2 * LANES
    return pl.pallas_call(
        resample_kernel,
        out_shape=jax.ShapeDtypeStruct((height, span), jnp.float32),
        in_specs=[VMEM_SPEC] * (1 + len(fields)),
        out_specs=VMEM_SPEC,
        compiler_params=pltpu.CompilerParams(vmem_limit_bytes=late_bytes(count)),
        cost_estimate=pl.CostEstimate(
            flops=10**9, bytes_accessed=4 * 2**20, transcendentals=0
        ),
    )(table, *fields)


def legendre_kernel(early, *rest):
    table, lat_ref, beta_ref, scale_ref, growth_ref, start_ref, left_ref, values_ref = rest[:8]
    more_ref, back_ref, total_ref, mine_ref = rest[8:12]
    fields, (out_ref, weights, state_ref, sums, result, final) = rest[12:-6], rest[-6:]
    points = lat_ref.shape[1]
    slots = out_ref.shape[0]
    mine = mine_ref[:1]
    odd = mine - 2.0 * jnp.floor(mine * 0.5) > 0.5
    pair = lane_pairs(jnp.broadcast_to(mine, (8, LANES)))
    turn = block_count(pair[0][:1])
    block_total = jnp.max(turn + block_count(pair[1][:1])).astype(jnp.int32)

    total = resampled(early, fields, table, total_ref[...])
    totals = [total[2 * points * kind : 2 * points * (kind + 1)] for kind in range(4)]
    left = lax.broadcasted_iota(jnp.int32, (points, LANES), 1) < SIDE
    for parity in range(2):
        for comp in range(2):
            cols = slice(comp * LANES, (comp + 1) * LANES)
            value = jnp.where(odd, totals[2 + parity][:, cols], totals[parity][:, cols])
            top, bottom = value[:points], value[points:]
            kind = 2 * parity + comp
            weights[0, kind] = jnp.where(left, top, pltpu.roll(bottom, SIDE, 1))
            weights[1, kind] = jnp.where(left, pltpu.roll(top, SIDE, 1), bottom)
    result[...] = jnp.zeros_like(result)
    state_ref[...] = left_ref[...]

    def reduced(block):
        base = pl.multiple_of(block * BLOCK, BLOCK)
        for comp in range(2):
            total = sums[pl.ds(comp * 8, BLOCK, stride=16)]
            for lane in range(1, 8):
                total += sums[pl.ds(comp * 8 + lane, BLOCK, stride=16)]
            total = total * scale_ref[pl.ds(base, BLOCK)]
            result[comp, pl.ds(base, BLOCK)] = total + pltpu.roll(total, SIDE, 1)

    def held_step(source_ref, start, block, carry):
        second = block.astype(jnp.float32) >= turn
        for parity in range(2):
            scaled = [
                jnp.where(second, weights[1, 2 * parity + comp], weights[0, 2 * parity + comp])
                for comp in range(2)
            ]
            for order in range(parity, BLOCK, 2):
                value = source_ref[block - start, order]
                for comp in range(2):
                    product = (value * scaled[comp]).reshape(points // 8, 8, LANES)
                    sums[pl.ds((order * 2 + comp) * 8, 8)] = product.sum(axis=0)
        reduced(block)
        return carry

    def step(block, carry):
        second = block.astype(jnp.float32) >= turn
        first = 0
        for chunk in CHUNKS:
            rows = slice(first, first + chunk)
            scaled = [jnp.where(second, weights[1, k, rows], weights[0, k, rows]) for k in range(4)]

            def add(order, value):
                for comp in range(2):
                    product = value * scaled[2 * (order % 2) + comp]
                    partial = product.reshape(chunk // 8, 8, LANES).sum(axis=0)
                    place = pl.ds((order * 2 + comp) * 8, 8)
                    if first == 0:
                        sums[place] = partial
                    else:
                        sums[place] += partial

            sweep_block(block, turn, rows, lat_ref, beta_ref, growth_ref, start_ref, state_ref, add)
            first += chunk
        reduced(block)
        return carry

    held = functools.partial(held_step, values_ref, 0)
    lax.fori_loop(0, jnp.minimum(block_total, HELD), held, 0)
    held = functools.partial(held_step, more_ref, HELD)
    lax.fori_loop(HELD, jnp.minimum(block_total, HELD + MORE), held, 0)
    lax.fori_loop(HELD + MORE, block_total, step, 0)

    left = lax.broadcasted_iota(jnp.int32, (BLOCK, LANES), 1) < SIDE
    spots = SPAN
    chosen = [jnp.broadcast_to(turn, (8, LANES)) == value for value in range(spots + 1)]
    chosen = [jnp.concatenate([mask] * (BLOCK // 8), axis=0) for mask in chosen]
    for place in range(spots):
        rows = slice(place * BLOCK, (place + 1) * BLOCK)
        for comp in range(2):
            early_part = jnp.where(turn > place, result[comp, rows], 0.0)
            later = jnp.zeros((BLOCK, LANES), jnp.float32)
            for value in range(spots + 1):
                base = (place + value) * BLOCK
                if base < result.shape[1]:
                    later = jnp.where(chosen[value], result[comp, base : base + BLOCK], later)
            final[comp, rows] = jnp.where(left, early_part, later)
    back = back_ref[...]
    dims = (((1,), (1,)), ((), ()))
    for comp in range(2):
        high, low = split_bf16(final[comp])
        value = lax.dot_general(back, high, dims, preferred_element_type=jnp.float32)
        value += lax.dot_general(back, low, dims, preferred_element_type=jnp.float32)
        out_ref[:, comp, :] = value[:slots, :M]


def resample_pieces(pieces, rows, padded_rows):
    full = resample_table()
    table = full.reshape(full.shape[0], pieces, rows).transpose(1, 0, 2)
    table = table_bf16(np.pad(table, ((0, 0), (0, 0), (0, padded_rows - rows))))
    return table.reshape(pieces, full.shape[0], 2, padded_rows).transpose(0, 2, 1, 3)


def legendre(fields, mine, latitudes, prepared, table, slots):
    pieces = len(fields)
    early = pieces // 2
    points = latitudes.shape[1]
    total = resample(fields[:early], table)
    block_rows = SPAN * BLOCK
    return pl.pallas_call(
        functools.partial(legendre_kernel, early),
        out_shape=jax.ShapeDtypeStruct((slots, 2, M), jnp.float32),
        in_specs=[VMEM_SPEC] * (12 + pieces - early),
        out_specs=VMEM_SPEC,
        scratch_shapes=[
            pltpu.VMEM((2, 4, points, LANES), jnp.float32),
            pltpu.VMEM((3, points, LANES), jnp.float32),
            pltpu.VMEM((BLOCK * 16, LANES), jnp.float32),
            pltpu.VMEM((2, 2 * block_rows, LANES), jnp.float32),
            pltpu.VMEM((2, block_rows, LANES), jnp.float32),
        ],
        compiler_params=pltpu.CompilerParams(vmem_limit_bytes=late_bytes(pieces)),
        cost_estimate=pl.CostEstimate(
            flops=8 * 10**9, bytes_accessed=6 * 2**20, transcendentals=0
        ),
    )(table, latitudes, *prepared, total, mine, *fields[early:])


def shards(tracer, wind_east, wind_north, keep_m, slot_wave):
    rows = tracer.shape[1]
    lat_count = lax.axis_size("lat")
    slots = slot_wave.shape[0] // lat_count
    axes = ("lev", "fld")
    ring = (axes, tuple(lax.axis_size(axis) for axis in axes))

    blocks, edges = advect(tracer, wind_east, wind_north, keep_m, ring)
    blocks, slot_wave = lax.optimization_barrier((blocks, slot_wave))
    grids = exchange(blocks, axes)
    edges = lax.all_to_all(edges, ("lat", *axes), split_axis=0, concat_axis=0, tiled=True)
    latitudes = jnp.asarray(latitude_table())
    wave_row, mine, beta, start, back = prepare_places(slot_wave, lat_count, latitudes)
    waved = fourier(grids, edges, ring, wave_row, rows, lat_count)
    table = jnp.asarray(resample_pieces(lat_count, rows, exchanged_rows(rows)))
    waved, mine, table = lax.optimization_barrier((list(waved), mine, table))
    fields = exchange(waved, "lat")
    scale, growth, state, values, more = sweep(mine, latitudes, beta, start, lat_count)
    prepared = (beta, scale, growth, start, state, values, more, back)
    return legendre(fields, mine, latitudes, prepared, table, slots)[None]


def solution(mesh):
    return jax.shard_map(
        shards,
        mesh=mesh,
        in_specs=(
            P("member", "lat", ("lev", "fld")),
            P("member", "lat", ("lev", "fld")),
            P("member", "lat", ("lev", "fld")),
            P("lat"),
            P(),
        ),
        out_specs=P(("member", "lev", "fld"), "lat", None, None),
        check_vma=False,
    )
```

```python
import functools
import math

import jax
import jax.numpy as jnp
import numpy as np
from jax import lax
from jax.experimental import pallas as pl
from jax.experimental.pallas import tpu as pltpu
from jax.sharding import PartitionSpec as P

M = 400
NLAT = 800
NLON = 1600
LANES = 128
BLOCK = 32
CHUNKS = (40, 32, 32)
SPAN = -(-M // BLOCK)
HELD = 13
MORE = 3
SIDE = LANES // 2
TOP = 32767.0
WIND_STEP = 1.5 / TOP
VMEM_BYTES = 60 * 2**20
LATE_BYTES = 10 * 2**20
MIDDLE_BYTES = 16 * 2**20
VMEM_SPEC = pl.BlockSpec(memory_space=pltpu.VMEM)
SMEM_SPEC = pl.BlockSpec(memory_space=pltpu.SMEM)
HBM_SPEC = pl.BlockSpec(memory_space=pltpu.HBM)


def split_bf16(values):
    high = values.astype(jnp.bfloat16)
    low = (values - high.astype(jnp.float32)).astype(jnp.bfloat16)
    return high, low


def table_bf16(table):
    high = table.astype(jnp.bfloat16)
    low = (table - high.astype(np.float64)).astype(jnp.bfloat16)
    return np.concatenate([high, low], axis=-1)


def fourier_tables(pieces):
    quarter = NLON // 4
    spots = np.arange(quarter)[:, None]
    factor = 1.0 / math.sqrt(NLON)

    def parts(waves):
        angles = 2.0 * math.pi / NLON * (spots * waves[None, :] % NLON)
        return factor * np.cos(angles), factor * np.sin(angles)

    def shaped(columns):
        pad = [(0, 0), (0, -columns[0].shape[1] % LANES)]
        table = np.concatenate([np.pad(part, pad) for part in columns], axis=1)
        return table.reshape(share, quarter // share, -1)

    share = pieces // 4
    tables = []
    for first in (0, 2):
        cosine, sine = parts(np.arange(first, M, 4))
        tables.append(shaped([cosine, -sine]))
    cosine, sine = parts(np.arange(1, M, 2))
    return [*tables, shaped([cosine, -sine])]


def column_waves(shape):
    row = lax.broadcasted_iota(jnp.int32, shape, 0)
    waves, first = jnp.full(shape, -1, jnp.int32), 0
    for start, step in ((0, 4), (2, 4), (1, 2)):
        count = len(range(start, M, step))
        inside = (row >= first) & (row < first + count)
        waves = jnp.where(inside, start + step * (row - first), waves)
        first += -(-count // LANES) * LANES
    return waves.astype(jnp.float32)


def column_count():
    return sum(-(-len(range(start, M, step)) // LANES) * LANES for start, step in ((0, 4), (2, 4), (1, 2)))


def resample_table():
    half = M // 2
    coarse = math.pi / M * (np.arange(M) + 0.5)
    fine = math.pi / NLAT * (np.arange(NLAT) + 0.5)
    waves = np.arange(M)
    weight = np.where(waves == 0, 1.0, 2.0) / M
    even = (np.cos(np.outer(coarse, waves)) * weight) @ np.cos(np.outer(waves, fine))
    odd = (np.sin(np.outer(coarse, waves)) * weight) @ np.sin(np.outer(waves, fine))
    rows = []
    for full in (even, odd):
        for sign in (1.0, -1.0):
            folded = (full[:half] + sign * full[::-1][:half]).reshape(2, half // 2, NLAT)
            rows.append(np.pad(folded, ((0, 0), (0, -half // 2 % 8), (0, 0))).reshape(-1, NLAT))
    return np.concatenate(rows, axis=0) * (np.sin(fine) * math.sqrt(2.0 / NLAT))


def latitude_table():
    half = M // 2
    angles = math.pi / M * (np.arange(half) + 0.5)
    log_sine = np.log2(np.sin(angles))
    coarse = np.round(log_sine * 1024.0) / 1024.0
    rows = np.stack([2.0 * np.cos(angles), coarse, log_sine - coarse]).reshape(3, 2, half // 2)
    rows = np.pad(rows, ((0, 0), (0, 0), (0, -half // 2 % 8)))
    return np.repeat(rows.transpose(0, 2, 1), SIDE, axis=2).astype(np.float32)


def scale_code(biggest):
    wanted = jnp.maximum(biggest, 1e-30) * (1.0 / TOP)
    exponent = jnp.floor(jnp.log(wanted) * (1.0 / math.log(2.0)))
    return exponent * 128.0 + jnp.ceil((wanted * jnp.exp2(-exponent) - 1.0) * 128.0)


def scale_of(code):
    exponent = jnp.floor(code * (1.0 / 128.0))
    rest = code - 128.0 * exponent
    return jnp.exp2(exponent) * (1.0 + rest * (1.0 / 128.0))


def coded(values, inverse):
    return jnp.floor(values * inverse + 0.5)


def as_int16(values):
    return values.astype(jnp.int32).astype(jnp.int16)


def from_int16(codes):
    return codes.astype(jnp.int32).astype(jnp.float32)


def partner(axes, sizes, step):
    count = math.prod(sizes)
    if count != 4:
        return step
    index = lax.axis_index(axes[0])
    for axis, size in zip(axes[1:], sizes[1:]):
        index = index * size + lax.axis_index(axis)
    return index ^ step


def exchange(blocks, axis):
    count = len(blocks)
    if count != 4:
        return list(lax.all_to_all(jnp.stack(blocks), axis, split_axis=0, concat_axis=0, tiled=True))
    pairs = [[(i, i ^ step) for i in range(count)] for step in range(count)]
    return [blocks[0]] + [lax.ppermute(blocks[step], axis, pairs[step]) for step in range(1, count)]


def advect_kernel(ring, lat_count, keep_hbm, tracer_hbm, east_hbm, north_hbm, *rest):
    levels, rows, lons = tracer_hbm.shape
    outs, (edge_ref, tracer, east_wind, north_wind, keep_ref, sems, keep_sem) = rest[:levels], rest[levels:]
    chosen = [partner(*ring, step) for step in range(levels)]
    copies = [None] * levels
    order = (*range(levels // 2, levels), *range(levels // 2))
    for step in order:
        copies[step] = [
            pltpu.make_async_copy(source.at[chosen[step]], target.at[step], sems.at[kind, step])
            for kind, (source, target) in enumerate(
                ((tracer_hbm, tracer), (east_hbm, east_wind), (north_hbm, north_wind))
            )
        ]
        for copy in copies[step]:
            copy.start()
    keep_copy = pltpu.make_async_copy(keep_hbm, keep_ref, keep_sem)
    keep_copy.start()
    padded_rows = outs[0].shape[0]
    keep_copy.wait()
    same = (rows, rows)
    same = lax.broadcasted_iota(jnp.int32, same, 0) == lax.broadcasted_iota(jnp.int32, same, 1)
    keep = jnp.broadcast_to(keep_ref[...].astype(jnp.float32), (rows, rows))
    keep = jnp.sum(jnp.where(same, keep, 0.0), axis=1, keepdims=True)
    end = (lons - 1) // LANES * LANES
    spare = lons - end
    lane = lax.broadcasted_iota(jnp.int32, (rows, LANES), 1)
    lat_index = lax.axis_index("lat")
    edge_ref[...] = jnp.zeros_like(edge_ref)
    for step in order:
        level = chosen[step]
        for copy in copies[step]:
            copy.wait()
        field = tracer[step].astype(jnp.float32)

        @pl.when(lat_index < lat_count - 1)
        def _():
            edge_ref[(lat_index + 1) * levels + level] = field[rows - 1 :]

        @pl.when(lat_index > 0)
        def _():
            edge_ref[(lat_index - 1) * levels + level] = field[:1]

        blank = jnp.zeros((rows, 1), jnp.float32)
        west = jnp.concatenate([blank, field[:, :-1]], axis=1)
        east = jnp.concatenate([field[:, 1:], blank], axis=1)
        blank = jnp.zeros((1, lons), jnp.float32)
        north = jnp.concatenate([blank, field[:-1]], axis=0)
        south = jnp.concatenate([field[1:], blank], axis=0)
        eastward = 0.5 * east_wind[step].astype(jnp.float32)
        northward = 0.5 * north_wind[step].astype(jnp.float32)
        moved = field - eastward * (east - west) - northward * (south - north)
        first, last = field[:, :1], field[:, lons - 1 :]
        biggest = jnp.max(jnp.abs(moved), axis=1, keepdims=True)
        biggest = jnp.maximum(biggest, jnp.maximum(jnp.abs(first), jnp.abs(last)))
        code = scale_code(biggest)
        inverse = 1.0 / scale_of(code)
        filler = jnp.zeros((rows, LANES - spare), jnp.float32)
        tile = jnp.concatenate([moved[:, end:], filler], axis=1)
        tile = jnp.where(lane == spare + 1, first, jnp.where(lane == spare + 2, last, tile))
        tile = coded(tile, inverse)
        tile = jnp.where(lane == spare, code, tile)
        winds = jnp.where(lane == spare + 3, eastward[:, :1], eastward[:, lons - 1 :])
        winds = coded(winds, 1.0 / WIND_STEP)
        tile = jnp.where((lane == spare + 3) | (lane == spare + 4), winds, tile)
        tile = jnp.where(lane == spare + 5, keep, tile)
        wind_rows = jnp.concatenate([northward[:1], northward[rows - 1 :]], axis=0)
        wind_rows = coded(wind_rows, 1.0 / WIND_STEP)
        blank = jnp.zeros((padded_rows - rows - 2, lons), jnp.float32)
        wind_rows = jnp.concatenate([wind_rows, blank], axis=0)
        filler = jnp.zeros((padded_rows - rows, LANES - spare), jnp.float32)
        wind_tile = jnp.concatenate([wind_rows[:, end:], filler], axis=1)
        steps = jnp.concatenate([coded(moved[:, :end], inverse), wind_rows[:, :end]], axis=0)
        outs[step][:, :end] = as_int16(steps)
        outs[step][:, end:] = as_int16(jnp.concatenate([tile, wind_tile], axis=0))


def advect(tracer, east_wind, north_wind, keep_m, ring):
    levels, rows, lons = tracer.shape
    lat_count = lax.axis_size("lat")
    width = (lons - 1) // LANES * LANES + LANES
    padded_rows = -(-(rows + 2) // 16) * 16
    held = pltpu.VMEM((levels, rows, lons), jnp.bfloat16)
    result = pl.pallas_call(
        functools.partial(advect_kernel, ring, lat_count),
        out_shape=[jax.ShapeDtypeStruct((padded_rows, width), jnp.int16)] * levels
        + [jax.ShapeDtypeStruct((lat_count * levels, 1, lons), jnp.float32)],
        in_specs=[HBM_SPEC] * 4,
        out_specs=[VMEM_SPEC] * (levels + 1),
        scratch_shapes=[
            held,
            held,
            held,
            pltpu.VMEM((1, rows), jnp.int32),
            pltpu.SemaphoreType.DMA((3, levels)),
            pltpu.SemaphoreType.DMA,
        ],
        compiler_params=pltpu.CompilerParams(vmem_limit_bytes=VMEM_BYTES),
        cost_estimate=pl.CostEstimate(
            flops=5 * 10**9, bytes_accessed=8 * levels * rows * lons, transcendentals=0
        ),
    )(keep_m[None], tracer, east_wind, north_wind)
    return list(result[:levels]), result[levels]


def exchanged_rows(rows):
    return -(-(rows + 1) // 16) * 16


def folded_rows(rows, slots):
    if 2 * slots <= LANES:
        return rows
    fits = 2 * slots <= LANES + SIDE + 8 and rows % 16 == 0 and rows <= 16 * 16
    return -(-(rows + rows // 2 + 16) // 16) * 16 if fits else 0


def fold(one, two, slots):
    rows = one.shape[0]
    total = folded_rows(rows, slots)
    if not total:
        return jnp.concatenate([one, two], axis=1)
    lane = lax.broadcasted_iota(jnp.int32, one.shape, 1)
    turned = pltpu.roll(two, slots, 1)
    whole = jnp.where(lane < slots, one, turned)
    if total == rows:
        return whole
    half = rows // 2
    halves = jnp.where(lane[:half] < SIDE, turned[:half], pltpu.roll(turned[half:], SIDE, 1))
    last = jnp.zeros((16, LANES), jnp.float32)
    for group in range(rows // 16):
        part = pltpu.roll(turned[16 * group : 16 * group + 16], (8 * group - SIDE) % LANES, 1)
        last = jnp.where(lane[:16] // 8 == group, part, last)
    filler = jnp.zeros((total - rows - half - 16, LANES), jnp.float32)
    return jnp.concatenate([whole, halves, last, filler], axis=0)


def unfold(block, rows, slots):
    total = folded_rows(rows, slots)
    if not total:
        return block[:, :LANES], block[:, LANES:]
    whole = block[:rows]
    lane = lax.broadcasted_iota(jnp.int32, whole.shape, 1)
    two = pltpu.roll(whole, (LANES - slots) % LANES, 1)
    if total != rows:
        half = rows // 2
        halves = block[rows : rows + half]
        last = block[rows + half : rows + half + 16]
        last = [pltpu.roll(last, (SIDE - 8 * group) % LANES, 1) for group in range(rows // 16)]
        halves = jnp.concatenate([halves, pltpu.roll(halves, SIDE, 1)], axis=0)
        rest = jnp.where(lane < SIDE, halves, jnp.concatenate(last, axis=0))
        two = jnp.where(lane < LANES - slots, two, pltpu.roll(rest, LANES - slots, 1))
    inside = lane < slots
    return jnp.where(inside, whole, 0.0), jnp.where(inside, two, 0.0)


def fourier_kernel(ring, lat_count, pieces, slots, *rest):
    grids, (edge_ref, *tables, wave_ref) = rest[:pieces], rest[pieces : pieces + 5]
    outs, field = rest[pieces + 5 : -1], rest[-1]
    _, rows, width = field.shape
    lons = tables[0].shape[1]
    share = pieces // 4

    end = width - LANES
    spare = lons - end
    lane = lax.broadcasted_iota(jnp.int32, (rows, LANES), 1)
    winds = (lane == spare + 3) | (lane == spare + 4)
    lat_index = lax.axis_index("lat")
    for piece in range(pieces):
        spot = partner(*ring, piece)
        values = from_int16(grids[piece][...])
        tile = values[:rows, end:]
        scale = scale_of(tile[:, spare : spare + 1])
        keep = tile[:, spare + 5 : spare + 6]
        field[spot, :, :end] = values[:rows, :end] * scale
        field[spot, :, end:] = tile * jnp.where(winds, WIND_STEP, scale)
        wind_rows = values[rows : rows + 2, :lons] * WIND_STEP

        @pl.when(lat_index > 0)
        def _():
            above = edge_ref[(lat_index - 1) * pieces + spot]
            field[spot, :1, :lons] += wind_rows[:1] * above

        @pl.when(lat_index < lat_count - 1)
        def _():
            below = edge_ref[(lat_index + 1) * pieces + spot]
            field[spot, rows - 1 :, :lons] -= wind_rows[1:] * below

    for spot in range(pieces):
        tile = field[spot, :, end:]
        before = field[(spot - 1) % pieces, :, end:]
        after = field[(spot + 1) % pieces, :, end:]
        shift = LANES - spare
        gain = pltpu.roll(tile, shift - 3, 1) * pltpu.roll(before, shift - 2, 1)
        loss = pltpu.roll(tile, LANES - 5, 1) * pltpu.roll(after, LANES - 2, 1)
        field[spot, :, end:] = tile - jnp.where(lane == spare - 1, loss, 0.0)
        field[spot, :, :LANES] += jnp.where(lane == 0, gain, 0.0)

    def product(kind, value, spot):
        high, low = split_bf16(value)
        table = tables[kind]
        span = table.shape[2] // 2
        both = jnp.dot(high, table[spot], preferred_element_type=jnp.float32)
        part = jnp.dot(low, table[spot, :, :span], preferred_element_type=jnp.float32)
        return part + both[:, :span] + both[:, span:]

    sums = [None, None, None]
    for spot in range(share):
        quarters = [field[quarter * share + spot, :, :lons] for quarter in range(4)]
        sum02, dif02 = quarters[0] + quarters[2], quarters[0] - quarters[2]
        sum13, dif13 = quarters[1] + quarters[3], quarters[1] - quarters[3]
        odd, turned = product(2, dif02, spot), product(2, dif13, spot)
        half = odd.shape[1] // 2
        cosine, sine = turned[:, :half], turned[:, half:]
        even = lax.broadcasted_iota(jnp.int32, cosine.shape, 1) % 2 == 0
        turned = [jnp.where(even, sine, -sine), jnp.where(even, -cosine, cosine)]
        odd = odd + jnp.concatenate(turned, axis=1)
        parts = [product(0, sum02 + sum13, spot), product(1, sum02 - sum13, spot), odd]
        sums = [part if total is None else total + part for total, part in zip(sums, parts)]
    slot_waves = wave_ref[...]
    waves = column_waves((column_count(), LANES))
    places = [
        jnp.where(waves == slot_waves[:, first : first + LANES], 1.0, 0.0).astype(jnp.bfloat16)
        for first in range(0, slot_waves.shape[1], LANES)
    ]
    places = jnp.concatenate(places, axis=1)
    placed = []
    for part in range(2):
        columns = []
        for total in sums:
            half = total.shape[1] // 2
            columns.append(total[:, part * half : (part + 1) * half])
        high, low = split_bf16(jnp.concatenate(columns, axis=1))
        value = jnp.dot(high, places, preferred_element_type=jnp.float32)
        value += jnp.dot(low, places, preferred_element_type=jnp.float32)
        kept = jnp.where(slot_waves < keep, value, 0.0)
        code = scale_code(jnp.max(jnp.abs(kept), axis=0, keepdims=True))
        steps = coded(kept, 1.0 / scale_of(code))
        codes = jnp.broadcast_to(code, (exchanged_rows(rows) - rows, code.shape[1]))
        placed.append(jnp.concatenate([steps, codes], axis=0))
    for target in range(lat_count):
        cols = slice(target * LANES, (target + 1) * LANES)
        outs[target][...] = as_int16(fold(placed[0][:, cols], placed[1][:, cols], slots))


def fourier(grids, edges, ring, wave_row, rows, slots, lat_count):
    pieces = len(grids)
    width = grids[0].shape[1]
    full = exchanged_rows(rows)
    folded = folded_rows(full, slots)
    shape = (folded, LANES) if folded else (full, 2 * LANES)
    tables = [table_bf16(table) for table in fourier_tables(pieces)]
    return pl.pallas_call(
        functools.partial(fourier_kernel, ring, lat_count, pieces, slots),
        out_shape=[jax.ShapeDtypeStruct(shape, jnp.int16)] * lat_count,
        in_specs=[VMEM_SPEC] * (pieces + 5),
        out_specs=[VMEM_SPEC] * lat_count,
        scratch_shapes=[pltpu.VMEM((pieces, rows, width), jnp.float32)],
        compiler_params=pltpu.CompilerParams(vmem_limit_bytes=MIDDLE_BYTES),
        cost_estimate=pl.CostEstimate(
            flops=4 * 10**9, bytes_accessed=6 * 2**20, transcendentals=0
        ),
    )(*grids, edges, *tables, wave_row)


def places_kernel(
    groups, slot_ref, lat_ref, wave_ref, mine_ref, beta_ref, start_ref, back_ref, sorted_rows
):
    lat_index = lax.axis_index("lat")
    slots = slot_ref.shape[1] // groups
    paired = (slots + 1) // 2
    shape = (LANES, LANES)
    down = lax.broadcasted_iota(jnp.int32, shape, 0)
    across = lax.broadcasted_iota(jnp.int32, shape, 1)
    filler = jnp.full((1, LANES - slots), 2.0 * M, jnp.float32)
    for group in range(groups):
        plain = slot_ref[:, group * slots : (group + 1) * slots].astype(jnp.float32)
        plain = jnp.concatenate([plain, filler], axis=1)
        row = jnp.broadcast_to(plain, shape)
        column = jnp.sum(jnp.where(down == across, row, 0.0), axis=1, keepdims=True)
        ahead = (row < column) | ((row == column) & (across < down))
        rank = jnp.sum(jnp.where(ahead, 1.0, 0.0), axis=1, keepdims=True)
        def ordered(side):
            place = jnp.where(rank < paired, rank, side + slots - 1.0 - rank)
            place = jnp.where(rank < slots, place, -1.0)
            hot = jnp.where(place == across.astype(jnp.float32), 1.0, 0.0)
            filled = jnp.sum(hot, axis=0, keepdims=True)
            values = jnp.sum(hot * column, axis=0, keepdims=True)
            return jnp.where(filled > 0.5, values, 2.0 * M)

        sorted_rows[group] = jnp.broadcast_to(ordered(paired), sorted_rows.shape[1:])

        @pl.when(group == lat_index)
        def _():
            mine_ref[:1] = ordered(SIDE)
            mine_ref[1:] = plain

    for step in range(groups):
        row = sorted_rows[partner(("lat",), (groups,), step), :1]
        wave_ref[:, step * LANES : (step + 1) * LANES] = row
    recurrence_tables(mine_ref, lat_ref, beta_ref, start_ref, back_ref)


def prepare_places(slot_wave, groups, latitudes):
    width = groups * LANES
    blocks = 2 * SPAN
    orders = jax.ShapeDtypeStruct((blocks * BLOCK, LANES), jnp.float32)
    return pl.pallas_call(
        functools.partial(places_kernel, groups),
        out_shape=[
            jax.ShapeDtypeStruct((1, width), jnp.float32),
            jax.ShapeDtypeStruct((2, LANES), jnp.float32),
            orders,
            jax.ShapeDtypeStruct((4, latitudes.shape[1], LANES), jnp.float32),
            jax.ShapeDtypeStruct((LANES, LANES), jnp.bfloat16),
        ],
        in_specs=[VMEM_SPEC] * 2,
        out_specs=[VMEM_SPEC] * 5,
        scratch_shapes=[pltpu.VMEM((groups, 8, LANES), jnp.float32)],
        compiler_params=pltpu.CompilerParams(vmem_limit_bytes=MIDDLE_BYTES),
        cost_estimate=pl.CostEstimate(flops=2 * 10**9, bytes_accessed=2**20, transcendentals=0),
    )(slot_wave[None], latitudes)


def lane_pairs(row):
    lane = lax.broadcasted_iota(jnp.int32, row.shape, 1)
    other = pltpu.roll(row, SIDE, 1)
    return jnp.where(lane < SIDE, row, other), jnp.where(lane < SIDE, other, row)


def block_count(wave):
    return jnp.floor((jnp.maximum(M - wave, 0.0) + (BLOCK - 1)) * (1.0 / BLOCK))


def lane_orders(one, two, blocks):
    turn = block_count(one)
    block = lax.broadcasted_iota(jnp.int32, (blocks, LANES), 0).astype(jnp.float32)
    second = block >= turn
    return jnp.where(second, two, one), (block - jnp.where(second, turn, 0.0)) * BLOCK


def recurrence_tables(mine_ref, lat_ref, beta_ref, start_ref, back_ref):
    shape = (LANES, LANES)
    same = lax.broadcasted_iota(jnp.int32, shape, 0) == lax.broadcasted_iota(jnp.int32, shape, 1)
    plain = jnp.broadcast_to(mine_ref[1:], shape)
    plain = jnp.sum(jnp.where(same, plain, 0.0), axis=1, keepdims=True)
    hot = (plain == mine_ref[:1]) & (plain < 2.0 * M)
    back_ref[...] = jnp.where(hot, 1.0, 0.0).astype(jnp.bfloat16)
    pair = lane_pairs(jnp.broadcast_to(mine_ref[:1], (8, LANES)))
    one, two = pair[0][:1], pair[1][:1]
    blocks = beta_ref.shape[0] // BLOCK
    wave, first = lane_orders(one, two, blocks)
    wave = jnp.minimum(wave, M - 1.0)
    for index in range(BLOCK):
        order = first + index
        degree = wave + order
        square = 4.0 * degree * degree - 1.0
        spread = 4.0 * order * (degree + wave)
        beta_ref[pl.ds(index, blocks, stride=BLOCK)] = spread / jnp.maximum(square, 1.0)

    counter = lax.broadcasted_iota(jnp.int32, (M, LANES), 0).astype(jnp.float32) + 1.0
    terms = jnp.log(1.0 + 0.5 / counter) * (1.0 / math.log(2.0))
    for kind, wave in enumerate((one, two)):
        wave = jnp.minimum(wave, M - 1.0)
        norm = jnp.sum(jnp.where(counter <= wave, terms, 0.0), axis=0, keepdims=True)
        coarse = lat_ref[1] * wave
        whole = jnp.floor(coarse)
        start_ref[2 * kind] = jnp.exp2(
            (coarse - whole) + lat_ref[2] * wave + 0.5 * (norm - 1.0)
        )
        start_ref[2 * kind + 1] = whole


def sweep_kernel(
    mine_ref, lat_ref, beta_ref, start_ref,
    scale_ref, growth_ref, state_ref, values_ref, more_ref,
):
    pair = lane_pairs(jnp.broadcast_to(mine_ref[:1], (8, LANES)))
    one, two = pair[0][:1], pair[1][:1]
    turn = block_count(one)

    blocks = growth_ref.shape[0]
    wave, first_order = lane_orders(one, two, blocks)
    limit = M - wave
    scale = jnp.ones((blocks, LANES), jnp.float32)
    for index in range(BLOCK):
        if index > 0:
            beta = beta_ref[pl.ds(index, blocks, stride=BLOCK)]
            scale = scale * lax.rsqrt(jnp.maximum(beta, 1e-6))
        inside = first_order + index < limit
        scale_ref[pl.ds(index, blocks, stride=BLOCK)] = jnp.where(inside, scale, 0.0)
    beta = beta_ref[pl.ds(BLOCK, blocks - 1, stride=BLOCK)]
    beta = jnp.concatenate([beta, jnp.ones((1, LANES), jnp.float32)], axis=0)
    growth_ref[...] = scale * lax.rsqrt(jnp.maximum(beta, 1e-6))

    state_ref[0] = jnp.zeros_like(state_ref[0])
    state_ref[1] = start_ref[0]
    state_ref[2] = start_ref[1]
    points = lat_ref.shape[1]

    def step(target_ref, start, block, carry):
        first = 0
        for chunk in (points // 16 * 8, points - points // 16 * 8):
            rows = slice(first, first + chunk)

            def keep(order, value):
                target_ref[block - start, order, rows] = value

            sweep_block(block, turn, rows, lat_ref, beta_ref, growth_ref, start_ref, state_ref, keep)
            first += chunk
        return carry

    total = jnp.max(turn + block_count(two)).astype(jnp.int32)
    lax.fori_loop(0, jnp.minimum(total, HELD), functools.partial(step, values_ref, 0), 0)
    more = functools.partial(step, more_ref, HELD)
    lax.fori_loop(HELD, jnp.minimum(total, HELD + MORE), more, 0)


def sweep_block(block, turn, rows, lat_ref, beta_ref, growth_ref, start_ref, state_ref, use):
    base = pl.multiple_of(block * BLOCK, BLOCK)
    begins = block.astype(jnp.float32) == turn
    grow = growth_ref[pl.ds(block, 1)]
    cosine = lat_ref[0, rows]
    height = jnp.where(begins, start_ref[3, rows], state_ref[2, rows])
    factor = jnp.exp2(height)
    old = jnp.where(begins, 0.0, state_ref[0, rows])
    new = jnp.where(begins, start_ref[2, rows], state_ref[1, rows])
    for order in range(BLOCK):
        use(order, new * factor)
        beta = beta_ref[pl.ds(base + order, 1)]
        old, new = new, cosine * new - beta * old
    biggest = jnp.maximum(jnp.abs(old), jnp.abs(new)) * grow
    shift = jnp.floor(jnp.log(biggest) * (1.0 / math.log(2.0)))
    factor = grow * jnp.exp2(-shift)
    state_ref[0, rows] = old * factor
    state_ref[1, rows] = new * factor
    state_ref[2, rows] = height + shift


def sweep(mine, latitudes, beta, start, pieces):
    points = latitudes.shape[1]
    blocks = beta.shape[0] // BLOCK
    return pl.pallas_call(
        sweep_kernel,
        out_shape=[
            jax.ShapeDtypeStruct(beta.shape, jnp.float32),
            jax.ShapeDtypeStruct((blocks, LANES), jnp.float32),
            jax.ShapeDtypeStruct((3, points, LANES), jnp.float32),
            jax.ShapeDtypeStruct((HELD, BLOCK, points, LANES), jnp.float32),
            jax.ShapeDtypeStruct((MORE, BLOCK, points, LANES), jnp.float32),
        ],
        in_specs=[VMEM_SPEC] * 4,
        out_specs=[VMEM_SPEC] * 5,
        compiler_params=pltpu.CompilerParams(vmem_limit_bytes=late_bytes(pieces)),
        cost_estimate=pl.CostEstimate(
            flops=5 * 10**9, bytes_accessed=25 * 2**20, transcendentals=0
        ),
    )(mine, latitudes, beta, start)


def resampled(first, fields, table, slots, total):
    for piece, field in enumerate(fields):
        rows = table.shape[3]
        parts = []
        for part in unfold(from_int16(field[...]), rows, slots):
            part = part * scale_of(part[rows - 1 :])
            lane = lax.broadcasted_iota(jnp.int32, part.shape, 1)
            shift = SIDE - (slots + 1) // 2
            parts.append(jnp.where(lane < SIDE, part, pltpu.roll(part, shift, 1)))
        values = jnp.concatenate(parts, axis=1)
        high, low = split_bf16(values)
        spot = partner(("lat",), table.shape[:1], first + piece)
        both = jnp.concatenate([high, low], axis=1)
        part = jnp.dot(table[spot, 0], both, preferred_element_type=jnp.float32)
        part = part[:, : high.shape[1]] + part[:, high.shape[1] :]
        part += jnp.dot(table[spot, 1], high, preferred_element_type=jnp.float32)
        total = part if total is None else total + part
    return total


def resample_kernel(slots, table_ref, *rest):
    rest[-1][...] = resampled(0, rest[:-1], table_ref, slots, None)


def late_bytes(pieces):
    return LATE_BYTES if pieces <= 4 else VMEM_BYTES


def resample(fields, table, slots):
    count, _, height, _ = table.shape
    span = 2 * LANES
    return pl.pallas_call(
        functools.partial(resample_kernel, slots),
        out_shape=jax.ShapeDtypeStruct((height, span), jnp.float32),
        in_specs=[VMEM_SPEC] * (1 + len(fields)),
        out_specs=VMEM_SPEC,
        compiler_params=pltpu.CompilerParams(vmem_limit_bytes=late_bytes(count)),
        cost_estimate=pl.CostEstimate(
            flops=10**9, bytes_accessed=4 * 2**20, transcendentals=0
        ),
    )(table, *fields)


def legendre_kernel(early, *rest):
    table, lat_ref, beta_ref, scale_ref, growth_ref, start_ref, left_ref, values_ref = rest[:8]
    more_ref, back_ref, total_ref, mine_ref = rest[8:12]
    fields, (out_ref, weights, state_ref, sums, result, final) = rest[12:-6], rest[-6:]
    points = lat_ref.shape[1]
    slots = out_ref.shape[0]
    mine = mine_ref[:1]
    odd = mine - 2.0 * jnp.floor(mine * 0.5) > 0.5
    pair = lane_pairs(jnp.broadcast_to(mine, (8, LANES)))
    turn = block_count(pair[0][:1])
    block_total = jnp.max(turn + block_count(pair[1][:1])).astype(jnp.int32)

    total = resampled(early, fields, table, slots, total_ref[...])
    totals = [total[2 * points * kind : 2 * points * (kind + 1)] for kind in range(4)]
    left = lax.broadcasted_iota(jnp.int32, (points, LANES), 1) < SIDE
    for parity in range(2):
        for comp in range(2):
            cols = slice(comp * LANES, (comp + 1) * LANES)
            value = jnp.where(odd, totals[2 + parity][:, cols], totals[parity][:, cols])
            top, bottom = value[:points], value[points:]
            kind = 2 * parity + comp
            weights[0, kind] = jnp.where(left, top, pltpu.roll(bottom, SIDE, 1))
            weights[1, kind] = jnp.where(left, pltpu.roll(top, SIDE, 1), bottom)
    result[...] = jnp.zeros_like(result)
    state_ref[...] = left_ref[...]

    def reduced(block):
        base = pl.multiple_of(block * BLOCK, BLOCK)
        for comp in range(2):
            total = sums[pl.ds(comp * 8, BLOCK, stride=16)]
            for lane in range(1, 8):
                total += sums[pl.ds(comp * 8 + lane, BLOCK, stride=16)]
            total = total * scale_ref[pl.ds(base, BLOCK)]
            result[comp, pl.ds(base, BLOCK)] = total + pltpu.roll(total, SIDE, 1)

    def held_step(source_ref, start, block, carry):
        second = block.astype(jnp.float32) >= turn
        for parity in range(2):
            scaled = [
                jnp.where(second, weights[1, 2 * parity + comp], weights[0, 2 * parity + comp])
                for comp in range(2)
            ]
            for order in range(parity, BLOCK, 2):
                value = source_ref[block - start, order]
                for comp in range(2):
                    product = (value * scaled[comp]).reshape(points // 8, 8, LANES)
                    middle = (points // 8 + 1) // 2
                    total = product[:middle].sum(axis=0) + product[middle:].sum(axis=0)
                    sums[pl.ds((order * 2 + comp) * 8, 8)] = total
        reduced(block)
        return carry

    def step(block, carry):
        second = block.astype(jnp.float32) >= turn
        first = 0
        for chunk in CHUNKS:
            rows = slice(first, first + chunk)
            scaled = [jnp.where(second, weights[1, k, rows], weights[0, k, rows]) for k in range(4)]

            def add(order, value):
                for comp in range(2):
                    product = value * scaled[2 * (order % 2) + comp]
                    partial = product.reshape(chunk // 8, 8, LANES).sum(axis=0)
                    place = pl.ds((order * 2 + comp) * 8, 8)
                    if first == 0:
                        sums[place] = partial
                    else:
                        sums[place] += partial

            sweep_block(block, turn, rows, lat_ref, beta_ref, growth_ref, start_ref, state_ref, add)
            first += chunk
        reduced(block)
        return carry

    held = functools.partial(held_step, values_ref, 0)
    lax.fori_loop(0, jnp.minimum(block_total, HELD), held, 0)
    held = functools.partial(held_step, more_ref, HELD)
    lax.fori_loop(HELD, jnp.minimum(block_total, HELD + MORE), held, 0)
    lax.fori_loop(HELD + MORE, block_total, step, 0)

    left = lax.broadcasted_iota(jnp.int32, (BLOCK, LANES), 1) < SIDE
    spots = SPAN
    chosen = [jnp.broadcast_to(turn, (8, LANES)) == value for value in range(spots + 1)]
    chosen = [jnp.concatenate([mask] * (BLOCK // 8), axis=0) for mask in chosen]
    for place in range(spots):
        rows = slice(place * BLOCK, (place + 1) * BLOCK)
        for comp in range(2):
            early_part = jnp.where(turn > place, result[comp, rows], 0.0)
            later = jnp.zeros((BLOCK, LANES), jnp.float32)
            for value in range(spots + 1):
                base = (place + value) * BLOCK
                if base < result.shape[1]:
                    later = jnp.where(chosen[value], result[comp, base : base + BLOCK], later)
            final[comp, rows] = jnp.where(left, early_part, later)
    back = back_ref[...]
    dims = (((1,), (1,)), ((), ()))
    for comp in range(2):
        high, low = split_bf16(final[comp])
        value = lax.dot_general(back, high, dims, preferred_element_type=jnp.float32)
        value += lax.dot_general(back, low, dims, preferred_element_type=jnp.float32)
        out_ref[:, comp, :] = value[:slots, :M]


def resample_pieces(pieces, rows, padded_rows):
    full = resample_table()
    table = full.reshape(full.shape[0], pieces, rows).transpose(1, 0, 2)
    table = table_bf16(np.pad(table, ((0, 0), (0, 0), (0, padded_rows - rows))))
    return table.reshape(pieces, full.shape[0], 2, padded_rows).transpose(0, 2, 1, 3)


def legendre(fields, mine, latitudes, prepared, table, slots):
    pieces = len(fields)
    early = pieces // 2
    points = latitudes.shape[1]
    total = resample(fields[:early], table, slots)
    block_rows = SPAN * BLOCK
    return pl.pallas_call(
        functools.partial(legendre_kernel, early),
        out_shape=jax.ShapeDtypeStruct((slots, 2, M), jnp.float32),
        in_specs=[VMEM_SPEC] * (12 + pieces - early),
        out_specs=VMEM_SPEC,
        scratch_shapes=[
            pltpu.VMEM((2, 4, points, LANES), jnp.float32),
            pltpu.VMEM((3, points, LANES), jnp.float32),
            pltpu.VMEM((BLOCK * 16, LANES), jnp.float32),
            pltpu.VMEM((2, 2 * block_rows, LANES), jnp.float32),
            pltpu.VMEM((2, block_rows, LANES), jnp.float32),
        ],
        compiler_params=pltpu.CompilerParams(vmem_limit_bytes=late_bytes(pieces)),
        cost_estimate=pl.CostEstimate(
            flops=8 * 10**9, bytes_accessed=6 * 2**20, transcendentals=0
        ),
    )(table, latitudes, *prepared, total, mine, *fields[early:])


def shards(tracer, wind_east, wind_north, keep_m, slot_wave):
    rows = tracer.shape[1]
    lat_count = lax.axis_size("lat")
    slots = slot_wave.shape[0] // lat_count
    axes = ("lev", "fld")
    ring = (axes, tuple(lax.axis_size(axis) for axis in axes))

    blocks, edges = advect(tracer, wind_east, wind_north, keep_m, ring)
    blocks, slot_wave = lax.optimization_barrier((blocks, slot_wave))
    grids = exchange(blocks, axes)
    edges = lax.all_to_all(edges, ("lat", *axes), split_axis=0, concat_axis=0, tiled=True)
    latitudes = jnp.asarray(latitude_table())
    wave_row, mine, beta, start, back = prepare_places(slot_wave, lat_count, latitudes)
    waved = fourier(grids, edges, ring, wave_row, rows, slots, lat_count)
    table = jnp.asarray(resample_pieces(lat_count, rows, exchanged_rows(rows)))
    waved, mine, table = lax.optimization_barrier((list(waved), mine, table))
    fields = exchange(waved, "lat")
    scale, growth, state, values, more = sweep(mine, latitudes, beta, start, lat_count)
    prepared = (beta, scale, growth, start, state, values, more, back)
    return legendre(fields, mine, latitudes, prepared, table, slots)[None]


def solution(mesh):
    return jax.shard_map(
        shards,
        mesh=mesh,
        in_specs=(
            P("member", "lat", ("lev", "fld")),
            P("member", "lat", ("lev", "fld")),
            P("member", "lat", ("lev", "fld")),
            P("lat"),
            P(),
        ),
        out_specs=P(("member", "lev", "fld"), "lat", None, None),
        check_vma=False,
    )
```
